32 devices in a mesh: dp: 16 (over z, y, x), mp: 2 (over core).
Axes of the slice: x: 2, y: 2, z: 4, core: 2. Of those that a mesh axis runs over, the one named last changes fastest.
Arguments:
- hidden_in: float32 [128, 198, 384], P('dp'), may hold values from -6 to 6
- keep_mask: int32 [128, 198], P('dp'), may hold values from 0 to 1, as said below
- cotangent: float32 [128, 198, 384], P('dp'), may hold values from -6 to 6
- slot_block: int32 [2, 384], replicated, may hold values from 0 to 383, each once within a row
- master: float32 [2, 2, 384, 6, 384], P('mp', None, 'dp'), may hold values from -0.375 to 0.375
- moment_one: float32 [2, 2, 384, 6, 384], P('mp', None, 'dp')
- moment_two: float32 [2, 2, 384, 6, 384], P('mp', None, 'dp'), as said below
- vector_master: float32 [2, 2, 6, 384], P('mp')
- vector_one: float32 [2, 2, 6, 384], P('mp')
- vector_two: float32 [2, 2, 6, 384], P('mp'), as said below
Outputs:
- activations: float32 [128, 198, 384], P('dp')
- input_grad: float32 [128, 198, 384], P('dp')
- matrix_grad: float32 [2, 2, 384, 6, 384], P('mp', None, 'dp')
- matrix_two: float32 [2, 2, 384, 6, 384], P('mp', None, 'dp')
- matrix_new: float32 [2, 2, 384, 6, 384], P('mp', None, 'dp')
- vector_grad: float32 [2, 2, 6, 384], P('mp')
- vector_two_new: float32 [2, 2, 6, 384], P('mp')
- vector_new: float32 [2, 2, 6, 384], P('mp')
The draws below stay inside these ranges and needn't reach their ends.
Inputs may be any that keep to these rules, and one draw needn't show every extreme that they name: `keep_mask`: positions 0 and 1 of every image are 1; one image in every draw keeps all 198 tokens. `slot_block`: each layer's row is a permutation of the 384 blocks. `moment_two`: positive. `vector_two`: positive.
All inputs are finite; a program needn't handle non-finite values.
Results may differ from the reference program's by a relative error of at most 0.018.
Values may be sent and summed in bfloat16 or wider, within the bound.
A program may use at most 192 MiB of HBM per device.

```python
import math
import jax
import jax.numpy as jnp
from jax import lax

D = 384
HEADS = 6
HD = 64
FF = 1536
SEQ = 198
IMG_DEV = 8
LAYERS = 2
BR = 6
STEP = 10
IMAGES = 128
HL = 3
FL = 768
ROWS_L = 2304
NBL = 384
VR = 6
N_MP = 2


def grad_size():
    return 0.25 * math.sqrt(IMAGES * SEQ)


def draw_keep_mask(key, part):
    key = jax.random.fold_in(key, 11)
    key_first, key_second, key_third, key_fourth = jax.random.split(key, 4)
    first_draw = jax.random.randint(key_first, (IMAGES,), 0, 1024)
    second_draw = jax.random.randint(key_second, (IMAGES,), 0, 1024)
    extra_kept = (SEQ - 2) * first_draw * second_draw // (1024 * 1024)
    full_image = jax.random.randint(key_fourth, (), 0, IMAGES)
    extra_kept = jnp.where(jnp.arange(IMAGES) == full_image, SEQ - 2, extra_kept)
    scores = jax.random.randint(key_third, (IMAGES, SEQ - 2), 0, 1 << 20) * SEQ + jnp.arange(SEQ - 2)
    rank_of = jnp.argsort(jnp.argsort(scores, axis=1, stable=True), axis=1, stable=True)
    kept_bits = (rank_of < extra_kept[:, None]).astype(jnp.int32)
    return jnp.concatenate([jnp.ones((IMAGES, 2), jnp.int32), kept_bits], 1)


def draw_moment_one(key, part):
    key = jax.random.fold_in(key, 12)
    shape_all = (N_MP, LAYERS, NBL, BR, D)
    return jax.random.normal(key, shape_all, jnp.float32) * (9.0 * grad_size())


def draw_moment_two(key, part):
    key = jax.random.fold_in(key, 13)
    shape_all = (N_MP, LAYERS, NBL, BR, D)
    spread = jax.random.uniform(key, shape_all, jnp.float32, math.log(0.5), math.log(8.0))
    return jnp.exp(spread) * (0.001 * grad_size() ** 2)


def draw_vector_master(key, part):
    key = jax.random.fold_in(key, 14)
    key_first, key_second = jax.random.split(key)
    shape_all = (N_MP, LAYERS, VR, D)
    row_ids = jnp.arange(VR)[None, None, :, None]
    gain_rows = 1.0 + jax.random.uniform(key_first, shape_all, jnp.float32, -0.25, 0.25)
    shift_rows = 0.3 * jax.random.normal(key_second, shape_all, jnp.float32)
    return jnp.where(row_ids == VR - 3, gain_rows, shift_rows)


def draw_vector_one(key, part):
    key = jax.random.fold_in(key, 15)
    shape_all = (N_MP, LAYERS, VR, D)
    return jax.random.normal(key, shape_all, jnp.float32) * (18.0 * grad_size())


def draw_vector_two(key, part):
    key = jax.random.fold_in(key, 16)
    shape_all = (N_MP, LAYERS, VR, D)
    spread = jax.random.uniform(key, shape_all, jnp.float32, math.log(0.5), math.log(8.0))
    return jnp.exp(spread) * (0.004 * grad_size() ** 2)


def levels(rng, dims, cuts, smallest, largest):
    level, own = 1.0, jax.random.fold_in(rng, 6)
    for position, shards_of in cuts:
        steps = jnp.exp(jax.random.uniform(jax.random.fold_in(own, position), (shards_of,), jnp.float32, smallest / len(cuts), largest / len(cuts)))
        level = level * jnp.repeat(steps, dims[position] // shards_of).reshape([-1 if axis == position else 1 for axis in range(len(dims))])
    return level


def bell_draw(stream_key, dims, scale, most, cuts=(), held_as=jnp.bfloat16):
    level = levels(stream_key, dims, cuts, -0.22, 0.18) if cuts else 1.0
    result = jax.random.normal(stream_key, dims, jnp.float32) * scale * level
    return jnp.minimum(jnp.maximum(result, -most), most).astype(held_as)


def setup_inputs(seed: int = 0) -> dict:
    keys = jax.random.split(jax.random.key(seed), 11)
    hidden_in = bell_draw(keys[0], (IMAGES, SEQ, D), 1.0, 6.0, ((0, 16),), jnp.float32)
    keep_mask = draw_keep_mask(jax.random.fold_in(keys[10], 71), 0)
    cotangent = bell_draw(keys[2], (IMAGES, SEQ, D), 1.0, 6.0, ((0, 16),), jnp.float32)
    slot_block = jax.vmap(lambda own: jax.random.permutation(own, NBL))(jax.random.split(keys[3], LAYERS)).reshape((LAYERS, NBL)).astype(jnp.int32)
    master = bell_draw(keys[4], (N_MP, LAYERS, NBL, BR, D), (D * 10 // 17) ** -0.5, 0.375, ((0, 2), (2, 16)), jnp.float32)
    moment_one = draw_moment_one(jax.random.fold_in(keys[10], 71), 0)
    moment_two = draw_moment_two(jax.random.fold_in(keys[10], 71), 0)
    vector_master = draw_vector_master(jax.random.fold_in(keys[10], 71), 0)
    vector_one = draw_vector_one(jax.random.fold_in(keys[10], 71), 0)
    vector_two = draw_vector_two(jax.random.fold_in(keys[10], 71), 0)
    return dict(hidden_in=hidden_in, keep_mask=keep_mask, cotangent=cotangent, slot_block=slot_block, master=master, moment_one=moment_one, moment_two=moment_two, vector_master=vector_master, vector_one=vector_one, vector_two=vector_two)


@jax.custom_vjp
def low(v):
    return lax.optimization_barrier(v.astype(jnp.bfloat16)).astype(jnp.float32)

@jax.custom_vjp
def low_back(v):
    return v

def low_keep(v):
    return (low(v), None)

def low_pass(kept, grad):
    return (grad,)

def back_keep(v):
    return (v, None)

def back_low(kept, grad):
    return (low(grad),)
low.defvjp(low_keep, low_pass)
low_back.defvjp(back_keep, back_low)
EPS_NORM = 1e-06
BETA_ONE = 0.9
BETA_TWO = 0.999
RATE_MATRIX = 0.003
RATE_VECTOR = 0.01
DECAY_MATRIX = 0.05
EPS_ADAM = 1e-08
NEG_FILL = -1e+30

def matmul_high(left, right):
    return jnp.dot(left, right, precision=lax.Precision.HIGHEST)

def layer_norm(values, gain_vec, shift_vec):
    average = lax.optimization_barrier(jnp.mean(values, -1, keepdims=True))
    centred = values - average
    return centred * lax.rsqrt(lax.optimization_barrier(jnp.mean(centred * centred, -1, keepdims=True)) + EPS_NORM) * gain_vec + shift_vec

def softmax_rows(scores):
    row_top = lax.optimization_barrier(jnp.max(scores, -1, keepdims=True))
    exponent = jnp.exp(scores - row_top)
    return exponent / lax.optimization_barrier(jnp.sum(exponent, -1, keepdims=True))

def forward(tokens_in, keep_group, master_in, vectors_in, slot_block):
    images = tokens_in.shape[0]
    head_cols = HL * HD
    layer_ids = jnp.arange(LAYERS, dtype=jnp.int32)[:, None]
    inverse = jnp.zeros((LAYERS, NBL), jnp.int32).at[layer_ids, slot_block.astype(jnp.int32)].set(jnp.broadcast_to(jnp.arange(NBL, dtype=jnp.int32), (LAYERS, NBL)))
    tables = low(master_in)[:, layer_ids, inverse].reshape(N_MP, LAYERS, ROWS_L, D)
    keep_float = keep_group.astype(jnp.float32).reshape(-1, 1)
    key_mask = (keep_group > 0)[:, None, None, :]
    hidden = tokens_in.reshape(images * SEQ, D)
    for number in range(LAYERS):
        rows_now = tables[:, number]
        w_query = rows_now[:, :head_cols].reshape(HEADS * HD, D)
        w_key = rows_now[:, head_cols:2 * head_cols].reshape(HEADS * HD, D)
        w_value = rows_now[:, 2 * head_cols:3 * head_cols].reshape(HEADS * HD, D)
        w_out = rows_now[:, 3 * head_cols:4 * head_cols].reshape(HEADS * HD, D)
        w_up = rows_now[:, 4 * head_cols:4 * head_cols + FL].reshape(FF, D)
        w_down = rows_now[:, 4 * head_cols + FL:].reshape(FF, D)
        flat_bias = vectors_in[:, number, :VR - 3].reshape(N_MP, (VR - 3) * D)
        bias_query = flat_bias[:, :head_cols].reshape(HEADS * HD)
        bias_value = flat_bias[:, head_cols:2 * head_cols].reshape(HEADS * HD)
        bias_up = flat_bias[:, 2 * head_cols:].reshape(FF)
        shared_first = vectors_in[0, number]
        shared_second = vectors_in[1, number]
        normed_a = low(layer_norm(hidden, shared_first[VR - 3], shared_first[VR - 2]))
        queries = low(low_back(matmul_high(normed_a, w_query.T) + bias_query)).reshape(images, SEQ, HEADS, HD)
        keys_all = low(low_back(matmul_high(normed_a, w_key.T))).reshape(images, SEQ, HEADS, HD)
        values_all = low(low_back(matmul_high(normed_a, w_value.T) + bias_value)).reshape(images, SEQ, HEADS, HD)
        raw_scores = low_back(jnp.einsum('iqhe,ikhe->ihqk', queries, keys_all, precision=lax.Precision.HIGHEST))
        probabilities = softmax_rows(jnp.where(key_mask, raw_scores * HD ** (-0.5), NEG_FILL))
        attended = jnp.einsum('ihqk,ikhe->iqhe', low(probabilities), values_all, precision=lax.Precision.HIGHEST)
        attended = low(low_back(attended.reshape(images * SEQ, HEADS * HD)))
        middle = hidden + low_back(matmul_high(attended, w_out) + shared_first[VR - 1])
        normed_b = low(layer_norm(middle, shared_second[VR - 3], shared_second[VR - 2]))
        up_pre = low_back(matmul_high(normed_b, w_up.T) + bias_up)
        activated = low(jax.nn.gelu(up_pre, approximate=False))
        hidden = middle + low_back(matmul_high(activated, w_down) + shared_second[VR - 1])
    return (hidden * keep_float).reshape(images, SEQ, D)

def adam_step(weight, grad_sum, first_old, second_old, rate, decay):
    first_new = BETA_ONE * first_old + (1.0 - BETA_ONE) * grad_sum
    second_new = BETA_TWO * second_old + (1.0 - BETA_TWO) * grad_sum * grad_sum
    first_hat = first_new / (1.0 - BETA_ONE ** STEP)
    second_hat = second_new / (1.0 - BETA_TWO ** STEP)
    return (second_new, weight - rate * (first_hat / (jnp.sqrt(second_hat) + EPS_ADAM) + decay * weight))

def reference(hidden_in, keep_mask, cotangent, slot_block, master, moment_one, moment_two, vector_master, vector_one, vector_two):
    groups = IMAGES // IMG_DEV

    def group_step(carry, inputs):
        tokens_group, keep_group, cot_group = inputs

        def apply(tokens_in, master_in, vectors_in):
            return forward(tokens_in, keep_group, master_in, vectors_in, slot_block)
        outputs, pullback = jax.vjp(apply, tokens_group, master, vector_master)
        grad_tokens, grad_master, grad_vectors = pullback(cot_group)
        return ((carry[0] + grad_master, carry[1] + grad_vectors), (outputs, grad_tokens))
    start = (jnp.zeros(master.shape, jnp.float32), jnp.zeros(vector_master.shape, jnp.float32))
    sliced = (hidden_in.reshape(groups, IMG_DEV, SEQ, D), keep_mask.reshape(groups, IMG_DEV, SEQ), cotangent.reshape(groups, IMG_DEV, SEQ, D))
    (matrix_grad, vector_grad), (outputs, grad_tokens) = lax.scan(group_step, start, sliced)
    matrix_two, matrix_new = adam_step(master, matrix_grad, moment_one, moment_two, RATE_MATRIX, DECAY_MATRIX)
    vector_two_new, vector_new = adam_step(vector_master, vector_grad, vector_one, vector_two, RATE_VECTOR, 0.0)
    return (outputs.reshape(IMAGES, SEQ, D), grad_tokens.reshape(IMAGES, SEQ, D), matrix_grad, matrix_two, matrix_new, vector_grad, vector_two_new, vector_new)
```

```python
import functools

import jax
import jax.numpy as jnp
from jax import lax
from jax.experimental import pallas as pl
from jax.experimental.pallas import tpu as pltpu
from jax.sharding import PartitionSpec as P

HEADS = 6
HD = 64
FF = 1536
STEP = 10

EPS_NORM = 1e-06
BETA_ONE = 0.9
BETA_TWO = 0.999
RATE_MATRIX = 0.003
RATE_VECTOR = 0.01
DECAY_MATRIX = 0.05
EPS_ADAM = 1e-08
NEG_FILL = -1e30

F32 = jnp.float32
MESH = pl.DeviceIdType.MESH
BF16 = jnp.bfloat16


def dot_nn(left, right):
    return lax.dot_general(left, right, (((1,), (0,)), ((), ())), preferred_element_type=F32)


def dot_nt(left, right):
    return lax.dot_general(left, right, (((1,), (1,)), ((), ())), preferred_element_type=F32)


def dot_tn(left, right):
    return lax.dot_general(left, right, (((0,), (0,)), ((), ())), preferred_element_type=F32)


def fold_rows(values):
    rows, cols = values.shape
    return jnp.sum(values.reshape(rows // 8, 8, cols), 0)


def loop(count, body):
    lax.fori_loop(0, count, lambda i, c: (body(i), c)[1], 0)


def gelu_pair(u):
    cdf = 0.5 + 0.5 * lax.erf(u * (0.5**0.5))
    slope = cdf + u * (jnp.exp(-0.5 * u * u) * 0.3989422804014327)
    return u * cdf, slope


class Dims:
    def __init__(self, layers, images, seq, width, halves, ranks, blocks, block_rows):
        self.layers, self.images, self.seq, self.width = layers, images, seq, width
        self.halves, self.ranks, self.blocks, self.block_rows = halves, ranks, blocks, block_rows
        self.pad_seq = -(-seq // 16) * 16
        self.tokens = images * self.pad_seq
        self.slots = blocks // ranks
        side = 1
        while side**3 * 8 <= ranks:
            side *= 2
        self.axes = (ranks // (side * side), side, side)
        self.shard_rows = -(-block_rows * self.slots // 16) * 16
        self.first_rows = -(-self.shard_rows // 32) * 16
        self.groups = block_rows // 2 if 2 * self.slots % 16 == 0 else 1
        self.group = self.shard_rows // self.groups
        self.group_js = block_rows // self.groups
        self.keys = ranks * self.group
        self.half_cols = HEADS * HD // halves
        self.half_units = FF // halves
        self.natural = 4 * self.half_cols
        self.unit_blocks = self.half_units // block_rows
        self.group_units = self.group_js * self.unit_blocks
        self.half_rows = self.natural + 2 * self.half_units


def divide(values, number):
    return jnp.floor((values.astype(F32) + 0.5) * (1.0 / number))


def one_hot(rows, codes, axis):
    start, count = rows
    shape = (count, codes.shape[1]) if axis == 0 else (codes.shape[0], count)
    here = lax.broadcasted_iota(jnp.int32, shape, axis) + start
    return (here == codes.astype(jnp.int32)).astype(F32).astype(BF16)


def permute_in(dm, layer, half, s):
    cols, units = dm.half_cols, dm.half_units
    shards = [
        s.gath[layer, :, :, :, g * dm.group : (g + 1) * dm.group, :].reshape(dm.keys, dm.width)
        for g in range(dm.groups)
    ]
    code = s.codes[layer]
    for kind in range(4):
        total = None
        for g in range(dm.groups):
            part = dot_nn(one_hot((kind * cols, cols), code[g : g + 1, :], 0), shards[g])
            total = part if total is None else total + part
        total = total.astype(BF16)
        if kind < 3:
            s.w_qkv[layer, pl.ds(pl.multiple_of(kind * HEADS * HD + half * cols, 16), cols), :] = total
        else:
            s.w_out[layer, pl.ds(pl.multiple_of(half * cols, 16), cols), :] = total
    yield
    tile = min(256, dm.group_units)
    for g in range(dm.groups):
        for target, first in ((s.w_up, 0), (s.w_down, dm.group_units)):
            for start in range(0, dm.group_units, tile):
                chosen = one_hot((first + start, tile), code[dm.groups : dm.groups + 1, :], 0)
                at = pl.multiple_of(half * units + g * dm.group_units + start, 16)
                target[layer, pl.ds(at, tile), :] = dot_nn(chosen, shards[g]).astype(BF16)


def permute_out(dm, layer, half, s):
    natural, units, size = dm.natural, dm.half_units, dm.group_units

    def summed(start, count):
        rows = slice(start, start + count)
        return (s.grads[half, rows, :].astype(F32) + s.grads_in[rows, :].astype(F32)).astype(BF16)

    qkvo = summed(0, natural)
    per = dm.axes[1] * dm.axes[2] * dm.group
    for g in range(dm.groups):
        both = jnp.concatenate(
            [summed(natural + g * size, size), summed(natural + units + g * size, size)], 0
        )
        for z in range(dm.axes[0]):
            codes = jnp.transpose(s.codes[layer, :, z * per : (z + 1) * per])
            rows = dot_nn(one_hot((0, natural), codes[:, g : g + 1], 1), qkvo)
            rows = rows + dot_nn(one_hot((0, 2 * size), codes[:, dm.groups : dm.groups + 1], 1), both)
            s.gath[layer, z, :, :, g * dm.group : (g + 1) * dm.group, :] = rows.astype(BF16).reshape(
                dm.axes[1], dm.axes[2], dm.group, dm.width
            )


def prepare_codes(dm, slot_block, s):
    layers, blocks, group = dm.layers, dm.blocks, dm.group
    block = slot_block[...].astype(F32)
    high = divide(block, 16)
    zero = jnp.zeros((16 - 2 * layers, blocks), F32)
    halves = jnp.concatenate([high, block - 16.0 * high, zero], 0).astype(BF16)
    first = dm.natural // dm.block_rows
    size = min(768, dm.keys)
    for start in range(0, dm.keys, size):
        size = min(size, dm.keys - start)

        def place(shape):
            key = lax.broadcasted_iota(jnp.int32, shape, 1) + start
            rank = divide(key, group)
            inside = key.astype(F32) - rank * group
            odd = divide(inside, dm.slots)
            return rank * dm.slots + inside - odd * dm.slots, odd, inside >= dm.group_js * dm.slots

        slot, _, _ = place((blocks, size))
        same = slot == lax.broadcasted_iota(jnp.int32, (blocks, size), 0).astype(F32)
        parts = dot_nn(halves, same.astype(F32).astype(BF16))
        _, odd, padding = place((1, size))
        for layer in range(layers):
            block = 16.0 * parts[layer : layer + 1] + parts[layers + layer : layers + layer + 1]
            rows = []
            for g in range(dm.groups):
                at = block * dm.block_rows + g * dm.group_js + odd
                rows.append(jnp.where(padding | (block >= first), -1.0, at))
            inner = block - first
            at = odd * dm.unit_blocks + inner
            at = jnp.where(inner < dm.unit_blocks, at, at - dm.unit_blocks + dm.group_units)
            rows.append(jnp.where(padding | (inner < 0), -1.0, at))
            rows.append(jnp.zeros((8 - len(rows), size), F32))
            s.codes[layer, :, start : start + size] = jnp.concatenate(rows, 0)


def unit_order(dm):
    units = dm.half_units
    here = lax.broadcasted_iota(jnp.int32, (units, units), 1)
    inner = divide(here, dm.unit_blocks)
    source = (here.astype(F32) - inner * dm.unit_blocks) * dm.block_rows + inner
    same = source == lax.broadcasted_iota(jnp.int32, (units, units), 0).astype(F32)
    return same.astype(F32).astype(BF16)


def reorder(dot, row, order):
    high = row.astype(BF16)
    rest = row - high.astype(F32)
    middle = rest.astype(BF16)
    low = (rest - middle.astype(F32)).astype(BF16)
    parts = [high.astype(F32), middle.astype(F32), low.astype(F32)]
    parts.append(jnp.zeros((13, row.shape[1]), F32))
    out = dot(jnp.concatenate(parts, 0).astype(BF16), order)
    return out[0:1] + (out[1:2] + out[2:3])


def pack_vectors(dm, vectors, first, s):
    cols, units, width = dm.half_cols, dm.half_units, dm.width
    wide = HEADS * HD
    order = unit_order(dm)
    for layer in range(dm.layers):
        rows = jnp.concatenate([vectors[0, r, layer : layer + 1, :] for r in range(6)], 0)
        flat = rows[0:1]
        q, v = flat[:, :cols], flat[:, cols : 2 * cols]
        none, mid = jnp.zeros((1, cols), F32), jnp.zeros((1, wide), F32)
        tail = jnp.zeros((1, FF - 3 * wide), F32)
        zero_half = jnp.concatenate([q, none, mid, v, none, tail], 1)
        one_half = jnp.concatenate([none, q, mid, none, v, tail], 1)
        s.vec_own[layer, 0:1, :] = jnp.where(first, zero_half, one_half)
        up = reorder(dot_nn, jnp.concatenate([rows[1:2], rows[2:3]], 1), order)
        none = jnp.zeros((1, units), F32)
        s.vec_own[layer, 1:2, :] = jnp.where(
            first, jnp.concatenate([up, none], 1), jnp.concatenate([none, up], 1)
        )
        own = jnp.concatenate([rows[3:6], jnp.zeros((3, FF - width), F32)], 1)
        none = jnp.zeros((3, FF), F32)
        s.vec_own[layer, 2:5, :] = jnp.where(first, own, none)
        s.vec_own[layer, 5:8, :] = jnp.where(first, none, own)


def unpack_vectors(dm, packed, first):
    cols, units, width = dm.half_cols, dm.half_units, dm.width
    wide = HEADS * HD
    flat = packed[0:1]
    zero_half = jnp.concatenate([flat[:, :cols], flat[:, 2 * wide : 2 * wide + cols]], 1)
    one_half = jnp.concatenate([flat[:, cols : 2 * cols], flat[:, 2 * wide + cols : 3 * wide]], 1)
    flat = packed[1:2]
    up = reorder(dot_nt, jnp.where(first, flat[:, :units], flat[:, units:]), unit_order(dm))
    own = jnp.where(first, packed[2:5, :width], packed[5:8, :width])
    return jnp.concatenate(
        [
            jnp.where(first, zero_half, one_half),
            up[:, :width],
            up[:, width:],
            own,
            jnp.zeros((2, width), F32),
        ],
        0,
    )


NORM_ROWS = 64


def norm_forward(dm, layer, source, gain, shift, low_out, hat_out, columns, place):
    def chunk(i):
        rows = pl.ds(pl.multiple_of(i * NORM_ROWS, NORM_ROWS), NORM_ROWS)
        values = source[rows, :]
        centred = values - jnp.mean(values, -1, keepdims=True)
        inv = lax.rsqrt(jnp.mean(centred * centred, -1, keepdims=True) + EPS_NORM)
        hat = centred * inv
        hat_out[layer, rows, :] = hat
        columns[rows, place : place + 1] = inv
        low_out[layer, rows, :] = (hat * gain + shift).astype(BF16)

    loop(dm.tokens // NORM_ROWS, chunk)


def norm_backward(dm, layer, grad, into, gain, hat_in, columns, place):
    def chunk(i, carry):
        rows = pl.ds(pl.multiple_of(i * NORM_ROWS, NORM_ROWS), NORM_ROWS)
        out, hat, inv = grad[rows, :], hat_in[layer, rows, :], columns[rows, place : place + 1]
        scaled = out * gain
        first = jnp.mean(scaled, -1, keepdims=True)
        second = jnp.mean(scaled * hat, -1, keepdims=True)
        into[rows, :] = into[rows, :] + inv * (scaled - first - hat * second)
        return carry[0] + fold_rows(out * hat), carry[1] + fold_rows(out)

    zero = jnp.zeros((8, dm.width), F32)
    gains, shifts = lax.fori_loop(0, dm.tokens // NORM_ROWS, chunk, (zero, zero))
    return jnp.sum(gains, 0, keepdims=True), jnp.sum(shifts, 0, keepdims=True)


def image_rows(dm, image):
    return pl.ds(pl.multiple_of(image * dm.pad_seq, 16), dm.pad_seq)


def forward_layer(dm, layer, vec, s, tick):
    width, tokens = dm.width, dm.tokens
    wide = HEADS * HD
    gain = [vec[layer, row : row + 1, :width] for row in range(2, 8)]
    g1, c1, bo, g2, c2, b2 = gain
    norm_forward(dm, layer, s.hid, g1, c1, s.low_a, s.hat_a, s.columns, 1 + 2 * layer)
    tick('norm')

    def project(image):
        rows = image_rows(dm, image)
        source = s.low_a[layer, rows, :]
        for kind in range(3):
            cols = slice(kind * wide, (kind + 1) * wide)
            value = dot_nt(source, s.w_qkv[layer, cols, :]) + vec[layer, 0:1, cols]
            s.qkv[layer, rows, cols] = value.astype(BF16)

    loop(dm.images, project)
    tick('project')

    def attend(image):
        rows = image_rows(dm, image)
        keep = s.columns[rows, 0:1]
        for head in range(HEADS):
            cols = slice(head * HD, (head + 1) * HD)
            q = s.qkv[layer, rows, cols]
            k = s.qkv[layer, rows, wide + head * HD : wide + (head + 1) * HD]
            v = s.qkv[layer, rows, 2 * wide + head * HD : 2 * wide + (head + 1) * HD]
            scores = dot_nt(k, q)
            scores = jnp.where(keep > 0, scores * HD ** (-0.5), NEG_FILL)
            exponent = jnp.exp(scores - jnp.max(scores, 0, keepdims=True))
            probs = (exponent * (1.0 / jnp.sum(exponent, 0, keepdims=True))).astype(BF16)
            s.probs[layer, image * HEADS + head] = probs
            s.att[layer, rows, cols] = dot_tn(probs, v).astype(BF16)

    loop(dm.images, attend)
    tick('attend')

    def out_project(image):
        rows = image_rows(dm, image)
        s.mid[rows, :] = s.hid[rows, :] + (dot_nn(s.att[layer, rows, :], s.w_out[layer]) + bo)

    loop(dm.images, out_project)
    norm_forward(dm, layer, s.mid, g2, c2, s.low_b, s.hat_b, s.columns, 2 + 2 * layer)
    tick('mid')

    tile = 256

    def up(image):
        rows = image_rows(dm, image)
        source = s.low_b[layer, rows, :]
        for number in range(FF // tile):
            cols = slice(number * tile, (number + 1) * tile)
            u = dot_nt(source, s.w_up[layer, cols, :]) + vec[layer, 1:2, cols]
            act, slope = gelu_pair(u)
            s.act[layer, rows, cols] = act.astype(BF16)
            s.slope[layer, rows, cols] = slope.astype(BF16)

    loop(dm.images, up)
    tick('up')

    def down(image):
        rows = image_rows(dm, image)
        s.hid[rows, :] = s.mid[rows, :] + (dot_nn(s.act[layer, rows, :], s.w_down[layer]) + b2)

    loop(dm.images, down)
    tick('down')


def low_and_sum(dm, source, target):
    def chunk(i, carry):
        rows = pl.ds(pl.multiple_of(i * NORM_ROWS, NORM_ROWS), NORM_ROWS)
        low = source[rows, :].astype(BF16)
        target[rows, :] = low
        return carry + fold_rows(low.astype(F32))

    total = lax.fori_loop(0, dm.tokens // NORM_ROWS, chunk, jnp.zeros((8, dm.width), F32))
    return jnp.sum(total, 0, keepdims=True)


def column_sums(dm, read, cols):
    def chunk(i, carry):
        rows = pl.ds(pl.multiple_of(i * NORM_ROWS, NORM_ROWS), NORM_ROWS)
        return carry + fold_rows(read(rows).astype(F32))

    total = lax.fori_loop(0, dm.tokens // NORM_ROWS, chunk, jnp.zeros((8, cols), F32))
    return jnp.sum(total, 0, keepdims=True)


def backward_layer(dm, layer, vec, vec_grad, s, tick):
    width, tokens = dm.width, dm.tokens
    wide, cols_half, units = HEADS * HD, dm.half_cols, dm.half_units
    tile = 256
    vec_grad[layer, 7:8, :width] = low_and_sum(dm, s.hid, s.low_g)
    tick("start")
    per_half = units // tile

    def unit_tile(number):
        cols = pl.ds(pl.multiple_of(number * tile, tile), tile)
        grad = dot_nt(s.low_g[...], s.w_down[layer, cols, :])
        grad = (grad * s.slope[layer, :, cols].astype(F32)).astype(BF16)
        s.slope[layer, :, cols] = grad
        half, at = number // per_half, pl.multiple_of((number % per_half) * tile, tile)
        s.grads[half, pl.ds(dm.natural + units + at, tile), :] = dot_tn(
            s.act[layer, :, cols], s.low_g[...]
        ).astype(BF16)
        s.grads[half, pl.ds(dm.natural + at, tile), :] = dot_tn(grad, s.low_b[layer]).astype(BF16)

    loop(FF // tile, unit_tile)
    tick("units")
    vec_grad[layer, 1:2, :] = column_sums(dm, lambda rows: s.slope[layer, rows, :], FF)

    def down(image):
        rows = image_rows(dm, image)
        s.mid[rows, :] = dot_nn(s.slope[layer, rows, :], s.w_up[layer])

    loop(dm.images, down)
    tick("down")
    gains, shifts = norm_backward(dm, layer, s.mid, s.hid, vec[layer, 5:6, :width], s.hat_b, s.columns, 2 + 2 * layer)
    vec_grad[layer, 5:6, :width] = gains
    vec_grad[layer, 6:7, :width] = shifts
    vec_grad[layer, 4:5, :width] = low_and_sum(dm, s.hid, s.low_g)
    tick("mid")
    value = dot_tn(s.att[layer], s.low_g[...]).astype(BF16)
    for half in range(dm.halves):
        s.grads[half, 3 * cols_half : dm.natural, :] = value[half * cols_half : (half + 1) * cols_half]

    def out_project(image):
        rows = image_rows(dm, image)
        s.att[layer, rows, :] = dot_nt(s.low_g[rows, :], s.w_out[layer]).astype(BF16)

    loop(dm.images, out_project)
    tick("out")

    def attend(image):
        rows = image_rows(dm, image)
        keep = s.columns[rows, 0:1] * HD ** (-0.5)
        for head in range(HEADS):
            cols = slice(head * HD, (head + 1) * HD)
            k_cols = slice(wide + head * HD, wide + (head + 1) * HD)
            v_cols = slice(2 * wide + head * HD, 2 * wide + (head + 1) * HD)
            q, k, v = (s.qkv[layer, rows, c] for c in (cols, k_cols, v_cols))
            out = s.att[layer, rows, cols]
            probs = s.probs[layer, image * HEADS + head]
            s.qkv[layer, rows, v_cols] = dot_nn(probs, out).astype(BF16)
            grad = dot_nt(v, out)
            wide_probs = probs.astype(F32)
            total = jnp.sum(wide_probs * grad, 0, keepdims=True)
            raw = (wide_probs * (grad - total) * keep).astype(BF16)
            s.qkv[layer, rows, cols] = dot_tn(raw, k).astype(BF16)
            s.qkv[layer, rows, k_cols] = dot_nn(raw, q).astype(BF16)

    loop(dm.images, attend)
    for kind in range(3):
        value = dot_tn(s.qkv[layer, :, kind * wide : (kind + 1) * wide], s.low_a[layer]).astype(BF16)
        for half in range(dm.halves):
            s.grads[half, kind * cols_half : (kind + 1) * cols_half, :] = value[
                half * cols_half : (half + 1) * cols_half
            ]
    tick("attend")
    vec_grad[layer, 0:1, : 3 * wide] = column_sums(dm, lambda rows: s.qkv[layer, rows, :], 3 * wide)

    def project(image):
        rows = image_rows(dm, image)
        s.mid[rows, :] = dot_nn(s.qkv[layer, rows, :], s.w_qkv[layer])

    loop(dm.images, project)
    tick("project")
    gains, shifts = norm_backward(dm, layer, s.mid, s.hid, vec[layer, 2:3, :width], s.hat_a, s.columns, 1 + 2 * layer)
    vec_grad[layer, 2:3, :width] = gains
    vec_grad[layer, 3:4, :width] = shifts
    tick("end")


class Net:
    def __init__(self, dm, s):
        self.dm, self.s, self.used = dm, s, 0
        self.rank, self.core = lax.axis_index("dp"), lax.axis_index("mp")
        _, rows, cols = dm.axes
        self.place = (self.rank // (rows * cols), (self.rank // cols) % rows, self.rank % cols)

    def device(self, axis, offset):
        if axis == 3:
            return (self.rank, 1 - self.core)
        at = list(self.place)
        at[axis] = (at[axis] + offset) % self.dm.axes[axis]
        return ((at[0] * self.dm.axes[1] + at[1]) * self.dm.axes[2] + at[2], self.core)

    def along(self, axis, offset):
        return (self.place[axis] + offset) % self.dm.axes[axis]

    def partners(self):
        found = [self.device(3, 1)]
        for axis in range(3):
            found += [self.device(axis, o) for o in range(1, self.dm.axes[axis])]
        return found

    def greet(self, semaphore):
        for partner in self.partners():
            pl.semaphore_signal(semaphore, inc=1, device_id=partner, device_id_type=MESH)

    def met(self, semaphore):
        pl.semaphore_wait(semaphore, len(self.partners()))

    def send(self, source, target, axis, offset=1):
        number = self.used
        self.used += 1
        copy = pltpu.make_async_remote_copy(
            src_ref=source,
            dst_ref=target,
            send_sem=self.s.send_sems.at[number],
            recv_sem=self.s.recv_sems.at[number],
            device_id=self.device(axis, offset),
            device_id_type=MESH,
        )
        copy.start()
        return copy


def copies_needed(dm):
    depth, rows, cols = dm.axes
    cross = depth * ((cols - 1) + (rows - 1))
    moves = depth - 1 + 2 * cross
    vectors = 1 + (depth - 1) + (rows - 1) + (cols - 1)
    return dm.layers * (2 * moves + 6 + 4 + vectors) + 2 * dm.images + 1


def gather_steps(dm, layer, net, s, sent):
    depth, rows, cols = dm.axes
    z, y, x = net.place
    buf = s.gath.at[layer]
    head, tail = pl.ds(0, dm.first_rows), pl.ds(dm.first_rows, dm.shard_rows - dm.first_rows)
    first, second, third = {}, {}, {}

    def one(offset):
        ref = buf.at[z, y, x]
        first[offset] = net.send(ref, ref, 0, offset)
        sent.append(first[offset])

    def two(piece):
        at = net.along(0, -piece)
        a, b = buf.at[at, y, x, head], buf.at[at, y, x, tail]
        second[piece] = [net.send(a, a, 2, o) for o in range(1, cols)]
        second[piece] += [net.send(b, b, 1, o) for o in range(1, rows)]
        sent.extend(second[piece])

    def three(piece):
        at = net.along(0, -piece)
        a, b = buf.at[at, y, :, head], buf.at[at, :, x, tail]
        third[piece] = [net.send(a, a, 1, o) for o in range(1, rows)]
        third[piece] += [net.send(b, b, 2, o) for o in range(1, cols)]
        sent.extend(third[piece])

    def arrived(copies):
        for copy in copies:
            copy.wait_recv()

    for offset in range(1, depth):
        one(offset)
    two(0)
    yield
    arrived(second[0])
    three(0)
    order = sorted(range(1, depth), key=lambda o: min(o, depth - o))
    for number, piece in enumerate(order):
        arrived([first[piece]])
        two(piece)
        if number > 0:
            arrived(second[order[number - 1]])
            three(order[number - 1])
        yield
    arrived(second[order[-1]])
    three(order[-1])
    yield
    for piece in range(depth):
        arrived(third[piece])


def scatter_steps(dm, layer, net, s, sent):
    depth, rows, cols = dm.axes
    z, y, x = net.place
    buf = s.gath.at[layer]
    head, tail = pl.ds(0, dm.first_rows), pl.ds(dm.first_rows, dm.shard_rows - dm.first_rows)
    order = sorted(range(depth), key=lambda o: -min(o, depth - o))
    first, second, third = {}, {}, {}

    def add(at, parts):
        value = buf[at].astype(F32)
        for part in parts:
            value = value + part.astype(F32)
        buf[at] = value.astype(BF16)

    for piece in order:
        at = net.along(0, piece)
        a, b = [], []
        for o in range(1, rows):
            to = net.along(1, o)
            a.append(net.send(buf.at[at, to, :, head], s.one_a.at[piece, o - 1], 1, o))
        for o in range(1, cols):
            to = net.along(2, o)
            b.append(net.send(buf.at[at, :, to, tail], s.one_b.at[piece, o - 1], 2, o))
        first[piece] = (a, b)
        sent.extend(a + b)
    yield
    for piece in order:
        at = net.along(0, piece)
        for copy in first[piece][0] + first[piece][1]:
            copy.wait_recv()
        add((at, y, slice(None), head), [s.one_a[piece, o] for o in range(rows - 1)])
        add((at, slice(None), x, tail), [s.one_b[piece, o] for o in range(cols - 1)])
        a, b = [], []
        for o in range(1, cols):
            to = net.along(2, o)
            a.append(net.send(buf.at[at, y, to, head], s.two_a.at[piece, o - 1], 2, o))
        for o in range(1, rows):
            to = net.along(1, o)
            b.append(net.send(buf.at[at, to, x, tail], s.two_b.at[piece, o - 1], 1, o))
        second[piece] = (a, b)
        sent.extend(a + b)
        yield
    for piece in order:
        at = net.along(0, piece)
        for copy in second[piece][0] + second[piece][1]:
            copy.wait_recv()
        add((at, y, x, head), [s.two_a[piece, o] for o in range(cols - 1)])
        add((at, y, x, tail), [s.two_b[piece, o] for o in range(rows - 1)])
        if piece > 0:
            third[piece] = net.send(buf.at[at, y, x], s.three.at[piece - 1], 0, piece)
            sent.append(third[piece])
        yield
    value = buf[z, y, x].astype(F32)
    for piece in range(1, depth):
        third[piece].wait_recv()
        value = value + s.three[piece - 1].astype(F32)
    s.rows[...] = value


def vector_steps(dm, layer, net, s, first, sent):
    copy = net.send(s.vec_grad.at[layer], s.vec_back.at[layer], 3)
    sent.append(copy)
    yield
    copy.wait_recv()
    value = unpack_vectors(dm, s.vec_grad[layer] + s.vec_back[layer], first)
    for axis, buf in ((1, s.vec_y), (2, s.vec_x), (0, s.vec_z)):
        here = net.place[axis]
        buf[layer, here] = value
        copies = []
        for o in range(1, dm.axes[axis]):
            copies.append(net.send(buf.at[layer, here], buf.at[layer, here], axis, o))
        sent.extend(copies)
        yield
        for copy in copies:
            copy.wait_recv()
        value = buf[layer, 0]
        for o in range(1, dm.axes[axis]):
            value = value + buf[layer, o]
    s.vec_sum[layer] = value


class Refs:
    pass


def scratch_shapes(dm):
    layers, tokens, width, wide = dm.layers, dm.tokens, dm.width, HEADS * HD
    depth, rows, cols = dm.axes
    head, tail = dm.first_rows, dm.shard_rows - dm.first_rows
    vmem, copies = pltpu.VMEM, copies_needed(dm)
    return dict(
        hid=vmem((tokens, width), F32),
        mid=vmem((tokens, width), F32),
        columns=vmem((tokens, 8), F32),
        low_a=vmem((layers, tokens, width), BF16),
        low_b=vmem((layers, tokens, width), BF16),
        low_g=vmem((tokens, width), BF16),
        hat_a=vmem((layers, tokens, width), F32),
        hat_b=vmem((layers, tokens, width), F32),
        qkv=vmem((layers, tokens, 3 * wide), BF16),
        probs=vmem((layers, dm.images * HEADS, dm.pad_seq, dm.pad_seq), BF16),
        att=vmem((layers, tokens, wide), BF16),
        act=vmem((layers, tokens, FF), BF16),
        slope=vmem((layers, tokens, FF), BF16),
        w_qkv=vmem((layers, 3 * wide, width), BF16),
        w_out=vmem((layers, wide, width), BF16),
        w_up=vmem((layers, FF, width), BF16),
        w_down=vmem((layers, FF, width), BF16),
        grads=vmem((dm.halves, dm.half_rows, width), BF16),
        grads_in=vmem((dm.half_rows, width), BF16),
        gath=vmem((layers, depth, rows, cols, dm.shard_rows, width), BF16),
        one_a=vmem((depth, rows - 1, cols, head, width), BF16),
        one_b=vmem((depth, cols - 1, rows, tail, width), BF16),
        two_a=vmem((depth, cols - 1, head, width), BF16),
        two_b=vmem((depth, rows - 1, tail, width), BF16),
        three=vmem((depth - 1, dm.shard_rows, width), BF16),
        rows=vmem((dm.shard_rows, width), F32),
        tok_in=vmem((dm.images, dm.seq, width), F32),
        tok_out=vmem((dm.images, dm.seq, width), F32),
        codes=vmem((layers, 8, dm.keys), F32),
        vec_own=vmem((layers, 8, FF), F32),
        vec=vmem((layers, 8, FF), F32),
        vec_grad=vmem((layers, 8, FF), F32),
        vec_in=vmem((layers, 8, FF), F32),
        vec_back=vmem((layers, 8, FF), F32),
        vec_z=vmem((layers, depth, 8, width), F32),
        vec_y=vmem((layers, rows, 8, width), F32),
        vec_x=vmem((layers, cols, 8, width), F32),
        vec_sum=vmem((layers, 8, width), F32),
        keep_row=vmem((8, -(-dm.pad_seq // 128) * 128), F32),
        send_sems=pltpu.SemaphoreType.DMA((copies,)),
        recv_sems=pltpu.SemaphoreType.DMA((copies,)),
        local_sems=pltpu.SemaphoreType.DMA((4 * dm.images,)),
        credit=pltpu.SemaphoreType.REGULAR,
    )


def load_tokens(dm, source, target, scale=None):
    tail = dm.pad_seq - 16
    for image in range(dm.images):
        start = image * dm.pad_seq
        target[start + tail : start + dm.pad_seq, :] = jnp.zeros((16, dm.width), F32)
        value = source[image]
        if scale is not None:
            value = value * scale[start : start + dm.seq, 0:1]
        target[start : start + dm.seq, :] = value


class Tokens:
    def __init__(self, dm, net, s):
        self.dm, self.net, self.s, self.used = dm, net, s, 0

    def image(self, ref, number):
        return ref.at[:, self.net.core * self.dm.images + number]

    def start(self, source, target):
        copy = pltpu.make_async_copy(source, target, self.s.local_sems.at[self.used])
        self.used += 1
        copy.start()
        return copy

    def load(self, ref):
        return [self.start(self.image(ref, i), self.s.tok_in.at[i]) for i in range(self.dm.images)]

    def store(self, ref):
        copies = []
        for i in range(self.dm.images):
            copies.append(self.start(self.s.tok_out.at[i], self.image(ref, i)))
            copies.append(self.net.send(self.s.tok_out.at[i], self.image(ref, i), 3))
        return copies


def wait_all(copies):
    for copy in copies:
        copy.wait()


def prepare_keep(dm, keep_mask, first, s):
    kept = keep_mask[...].astype(F32)
    kept = jnp.where(first, kept[: dm.images], kept[dm.images :])
    s.keep_row[...] = jnp.zeros(s.keep_row.shape, F32)
    s.keep_row[: dm.images, : dm.seq] = kept
    columns = jnp.transpose(s.keep_row[...])
    for image in range(dm.images):
        rows = slice(image * dm.pad_seq, (image + 1) * dm.pad_seq)
        s.columns[rows, 0:1] = columns[: dm.pad_seq, image : image + 1]


def own_shard(dm, master, net, s):
    z, y, x = net.place
    if dm.shard_rows > dm.block_rows * dm.slots:
        s.rows[...] = jnp.zeros(s.rows.shape, F32)
    for layer in range(dm.layers):
        for j in range(dm.block_rows):
            s.rows[j * dm.slots : (j + 1) * dm.slots, :] = master[0, layer, j]
        s.gath[layer, z, y, x] = s.rows[...].astype(BF16)


def step_kernel(dm, names, hidden, keep_mask, cotangent, slot_block, master, vectors, acts, grad_in, matrix, vec_out, *scratch):
    s = Refs()
    for name, ref in zip(names, scratch):
        setattr(s, name, ref)
    net = Net(dm, s)
    first = net.core == 0
    tokens = Tokens(dm, net, s)
    sent = []
    barrier = pltpu.get_barrier_semaphore()
    net.greet(barrier)
    load = tokens.load(hidden)
    own_shard(dm, master, net, s)
    net.met(barrier)
    moved = [[] for _ in range(dm.layers)]
    gathers = [gather_steps(dm, 0, net, s, moved[0])]
    next(gathers[0])
    pack_vectors(dm, vectors, first, s)
    other_vec = net.send(s.vec_own, s.vec_in, 3)
    sent.append(other_vec)
    prepare_codes(dm, slot_block, s)
    prepare_keep(dm, keep_mask, first, s)
    wait_all(load)
    load_tokens(dm, s.tok_in, s.hid)
    load = tokens.load(cotangent)
    other_vec.wait_recv()
    s.vec[...] = s.vec_own[...] + s.vec_in[...]
    for _ in gathers[0]:
        pass

    def share(layer):
        cols, units = dm.half_cols, dm.half_units
        parts = permute_in(dm, layer, net.core, s)
        copies = []

        def push(ref, start, count):
            rows = ref.at[layer, pl.ds(pl.multiple_of(start, 16), count)]
            copies.append(net.send(rows, rows, 3))

        for _ in parts:
            for kind in range(3):
                push(s.w_qkv, kind * HEADS * HD + net.core * cols, cols)
            push(s.w_out, net.core * cols, cols)
        push(s.w_up, net.core * units, units)
        push(s.w_down, net.core * units, units)
        sent.extend(copies)
        return copies

    weights = share(0)
    for layer in range(dm.layers):
        following = []
        if layer + 1 < dm.layers:
            following = gather_steps(dm, layer + 1, net, s, moved[layer + 1])

        def tick(name):
            if name == "norm":
                for copy in weights[:3]:
                    copy.wait_recv()
            if name == "attend":
                weights[3].wait_recv()
            if name == "mid":
                weights[4].wait_recv()
            if name == "up":
                weights[5].wait_recv()
            if following:
                next(following, None)

        forward_layer(dm, layer, s.vec, s, tick)
        if following:
            for _ in following:
                pass
            weights = share(layer + 1)
    for image in range(dm.images):
        rows = slice(image * dm.pad_seq, image * dm.pad_seq + dm.seq)
        s.tok_out[image] = s.hid[rows, :] * s.columns[rows, 0:1]
    store = tokens.store(acts)
    wait_all(load)
    load_tokens(dm, s.tok_in, s.hid, s.columns)

    pending = []

    def advance(count):
        for _ in range(count):
            for steps in pending:
                next(steps, None)

    def finish(layer):
        for steps in pending:
            for _ in steps:
                pass
        pending.clear()
        for j in range(dm.block_rows):
            matrix[0, layer, j] = s.rows[j * dm.slots : (j + 1) * dm.slots, :]
        for r in range(vec_out.shape[1]):
            vec_out[0, r, layer : layer + 1, :] = s.vec_sum[layer, r : r + 1, :]

    for layer in reversed(range(dm.layers)):
        last = layer == 0
        shared = []

        def push(start, count):
            rows = pl.ds(start, count)
            shared.append(net.send(s.grads.at[1 - net.core, rows], s.grads_in.at[rows], 3))

        def tick(name):
            if name == "units":
                if layer + 1 < dm.layers:
                    finish_credit()
                push(dm.natural, 2 * dm.half_units)
            if name == "attend":
                push(0, dm.natural)
            if name == "attend" and last:
                scatter()
            if name in ("start", "down", "mid", "out", "project"):
                advance(2)

        def scatter():
            for copy in shared:
                copy.wait_recv()
            for copy in moved[layer]:
                copy.wait_send()
            permute_out(dm, layer, net.core, s)
            pending.append(scatter_steps(dm, layer, net, s, sent))
            advance(1)

        def finish_credit():
            finish(layer + 1)
            net.greet(s.credit)
            net.met(s.credit)

        backward_layer(dm, layer, s.vec, s.vec_grad, s, tick)
        for copy in shared:
            copy.wait_send()
        if not last:
            scatter()
        pending.append(vector_steps(dm, layer, net, s, first, sent))
        advance(1)
    wait_all(store)
    for image in range(dm.images):
        rows = slice(image * dm.pad_seq, image * dm.pad_seq + dm.seq)
        s.tok_out[image] = s.hid[rows, :]
    store = tokens.store(grad_in)
    finish(0)
    wait_all(store)
    for copy in sent:
        copy.wait_send()
    assert net.used <= copies_needed(dm)


def run_step(dm, hidden_in, keep_mask, cotangent, slot_block, master, vector_master):
    shapes = scratch_shapes(dm)
    out_shape = (
        jax.ShapeDtypeStruct(hidden_in.shape, F32),
        jax.ShapeDtypeStruct(hidden_in.shape, F32),
        jax.ShapeDtypeStruct(master.shape, F32),
        jax.ShapeDtypeStruct(vector_master.shape, F32),
    )
    full, far = pl.BlockSpec(memory_space=pltpu.VMEM), pl.BlockSpec(memory_space=pl.ANY)
    return pl.pallas_call(
        functools.partial(step_kernel, dm, tuple(shapes)),
        out_shape=out_shape,
        in_specs=[far, full, far, full, full, full],
        out_specs=[far, far, full, full],
        scratch_shapes=list(shapes.values()),
        compiler_params=pltpu.CompilerParams(
            vmem_limit_bytes=63 * 2**20, collective_id=0, has_side_effects=True
        ),
    )(hidden_in, keep_mask, cotangent, slot_block, master, vector_master)


def adam_step(weight, grad_sum, first_old, second_old, rate, decay):
    first_new = BETA_ONE * first_old + (1.0 - BETA_ONE) * grad_sum
    second_new = BETA_TWO * second_old + (1.0 - BETA_TWO) * grad_sum * grad_sum
    first_hat = first_new / (1.0 - BETA_ONE**STEP)
    second_hat = second_new / (1.0 - BETA_TWO**STEP)
    return (
        second_new,
        weight - rate * (first_hat / (jnp.sqrt(second_hat) + EPS_ADAM) + decay * weight),
    )


def shards(
    hidden_in, keep_mask, cotangent, slot_block, master, moment_one, moment_two, vector_master, vector_one, vector_two
):
    images, seq, width = hidden_in.shape
    halves, ranks = lax.axis_size("mp"), lax.axis_size("dp")
    dm = Dims(
        master.shape[1], images // halves, seq, width, halves, ranks, slot_block.shape[1], master.shape[3]
    )
    activations, input_grad, matrix_grad, vector_grad = run_step(
        dm,
        hidden_in.swapaxes(0, 1),
        keep_mask,
        cotangent.swapaxes(0, 1),
        slot_block,
        master.swapaxes(2, 3),
        vector_master.swapaxes(1, 2),
    )
    activations, input_grad = activations.swapaxes(0, 1), input_grad.swapaxes(0, 1)
    matrix_grad, vector_grad = matrix_grad.swapaxes(2, 3), vector_grad.swapaxes(1, 2)
    matrix_two, matrix_new = adam_step(
        master, matrix_grad, moment_one, moment_two, RATE_MATRIX, DECAY_MATRIX
    )
    vector_two_new, vector_new = adam_step(
        vector_master, vector_grad, vector_one, vector_two, RATE_VECTOR, 0.0
    )
    return (
        activations,
        input_grad,
        matrix_grad,
        matrix_two,
        matrix_new,
        vector_grad,
        vector_two_new,
        vector_new,
    )


def solution(mesh):
    images, rows, copied = P("dp", None, None), P("mp", None, "dp", None, None), P("mp", None, None, None)
    return jax.shard_map(
        shards,
        mesh=mesh,
        in_specs=(images, P("dp", None), images, P(), rows, rows, rows, copied, copied, copied),
        out_specs=(images, images, rows, rows, rows, copied, copied, copied),
        check_vma=False,
    )
```

```python
import functools

import jax
import jax.numpy as jnp
from jax import lax
from jax.experimental import pallas as pl
from jax.experimental.pallas import tpu as pltpu
from jax.sharding import PartitionSpec as P

HEADS = 6
HD = 64
FF = 1536
STEP = 10

EPS_NORM = 1e-06
BETA_ONE = 0.9
BETA_TWO = 0.999
RATE_MATRIX = 0.003
RATE_VECTOR = 0.01
DECAY_MATRIX = 0.05
EPS_ADAM = 1e-08
NEG_FILL = -1e30

F32 = jnp.float32
MESH = pl.DeviceIdType.MESH
BF16 = jnp.bfloat16


def dot_nn(left, right):
    return lax.dot_general(left, right, (((1,), (0,)), ((), ())), preferred_element_type=F32)


def dot_nt(left, right):
    return lax.dot_general(left, right, (((1,), (1,)), ((), ())), preferred_element_type=F32)


def dot_tn(left, right):
    return lax.dot_general(left, right, (((0,), (0,)), ((), ())), preferred_element_type=F32)


def fold_rows(values):
    rows, cols = values.shape
    return jnp.sum(values.reshape(rows // 8, 8, cols), 0)


def loop(count, body):
    lax.fori_loop(0, count, lambda i, c: (body(i), c)[1], 0, unroll=True)


def gelu_pair(u):
    cdf = 0.5 + 0.5 * lax.erf(u * (0.5**0.5))
    slope = cdf + u * (jnp.exp(-0.5 * u * u) * 0.3989422804014327)
    return u * cdf, slope


class Dims:
    def __init__(self, layers, images, seq, width, halves, ranks, blocks, block_rows):
        self.layers, self.images, self.seq, self.width = layers, images, seq, width
        self.halves, self.ranks, self.blocks, self.block_rows = halves, ranks, blocks, block_rows
        self.pad_seq = -(-seq // 16) * 16
        self.tokens = images * self.pad_seq
        self.slots = blocks // ranks
        side = 1
        while side**3 * 8 <= ranks:
            side *= 2
        self.axes = (ranks // (side * side), side, side)
        self.shard_rows = -(-block_rows * self.slots // 16) * 16
        self.first_rows = -(-self.shard_rows // 32) * 16
        self.groups = block_rows // 2 if 2 * self.slots % 16 == 0 else 1
        self.group = self.shard_rows // self.groups
        self.group_js = block_rows // self.groups
        self.keys = ranks * self.group
        self.half_cols = HEADS * HD // halves
        self.half_units = FF // halves
        self.natural = 4 * self.half_cols
        self.unit_blocks = self.half_units // block_rows
        self.group_units = self.group_js * self.unit_blocks
        self.half_rows = self.natural + 2 * self.half_units


def divide(values, number):
    return jnp.floor((values.astype(F32) + 0.5) * (1.0 / number))


def one_hot(rows, codes, axis):
    start, count = rows
    shape = (count, codes.shape[1]) if axis == 0 else (codes.shape[0], count)
    here = lax.broadcasted_iota(jnp.int32, shape, axis) + start
    return (here == codes.astype(jnp.int32)).astype(F32).astype(BF16)


def permute_in(dm, layer, half, s):
    cols, units = dm.half_cols, dm.half_units
    shards = [
        s.gath[layer, :, :, :, g * dm.group : (g + 1) * dm.group, :].reshape(dm.keys, dm.width)
        for g in range(dm.groups)
    ]
    code = jnp.concatenate([s.codes[layer, z] for z in range(dm.axes[0])], 1)
    for kind in range(4):
        total = None
        for g in range(dm.groups):
            part = dot_nn(one_hot((kind * cols, cols), code[g : g + 1, :], 0), shards[g])
            total = part if total is None else total + part
        total = total.astype(BF16)
        if kind < 3:
            s.w_qkv[layer, pl.ds(pl.multiple_of(kind * HEADS * HD + half * cols, 16), cols), :] = total
        else:
            s.w_out[layer, pl.ds(pl.multiple_of(half * cols, 16), cols), :] = total
    yield
    tile = min(256, dm.group_units)
    for g in range(dm.groups):
        for target, first in ((s.w_up, 0), (s.w_down, dm.group_units)):
            for start in range(0, dm.group_units, tile):
                chosen = one_hot((first + start, tile), code[dm.groups : dm.groups + 1, :], 0)
                at = pl.multiple_of(half * units + g * dm.group_units + start, 16)
                target[layer, pl.ds(at, tile), :] = dot_nn(chosen, shards[g]).astype(BF16)


def permute_out(dm, layer, half, s):
    natural, units, size = dm.natural, dm.half_units, dm.group_units

    def add(start, count):
        rows = slice(start, start + count)
        total = s.grads[half, rows, :].astype(F32) + s.grads_in[rows, :].astype(F32)
        s.grads_in[rows, :] = total.astype(BF16)

    for start in range(0, dm.half_rows, 256):
        add(start, min(256, dm.half_rows - start))
    per = dm.axes[1] * dm.axes[2] * dm.group

    def piece(z):
        codes = jnp.transpose(s.codes[layer, z])
        for g in range(dm.groups):
            up, down = natural + g * size, natural + units + g * size
            both = jnp.concatenate([s.grads_in[up : up + size, :], s.grads_in[down : down + size, :]], 0)
            rows = dot_nn(one_hot((0, natural), codes[:, g : g + 1], 1), s.grads_in[:natural, :])
            rows = rows + dot_nn(one_hot((0, 2 * size), codes[:, dm.groups : dm.groups + 1], 1), both)
            s.gath[layer, z, :, :, g * dm.group : (g + 1) * dm.group, :] = rows.astype(BF16).reshape(
                dm.axes[1], dm.axes[2], dm.group, dm.width
            )

    return piece


def prepare_codes(dm, slot_block, s):
    layers, blocks, group = dm.layers, dm.blocks, dm.group
    block = slot_block[...].astype(F32)
    high = divide(block, 16)
    zero = jnp.zeros((16 - 2 * layers, blocks), F32)
    halves = jnp.concatenate([high, block - 16.0 * high, zero], 0).astype(BF16)
    first = dm.natural // dm.block_rows
    per = dm.keys // dm.axes[0]
    size = per * max(1, 768 // per)
    for start in range(0, dm.keys, size):
        size = min(size, dm.keys - start)

        def place(shape):
            key = lax.broadcasted_iota(jnp.int32, shape, 1) + start
            rank = divide(key, group)
            inside = key.astype(F32) - rank * group
            odd = divide(inside, dm.slots)
            return rank * dm.slots + inside - odd * dm.slots, odd, inside >= dm.group_js * dm.slots

        slot, _, _ = place((blocks, size))
        same = slot == lax.broadcasted_iota(jnp.int32, (blocks, size), 0).astype(F32)
        parts = dot_nn(halves, same.astype(F32).astype(BF16))
        _, odd, padding = place((1, size))
        for layer in range(layers):
            block = 16.0 * parts[layer : layer + 1] + parts[layers + layer : layers + layer + 1]
            rows = []
            for g in range(dm.groups):
                at = block * dm.block_rows + g * dm.group_js + odd
                rows.append(jnp.where(padding | (block >= first), -1.0, at))
            inner = block - first
            at = odd * dm.unit_blocks + inner
            at = jnp.where(inner < dm.unit_blocks, at, at - dm.unit_blocks + dm.group_units)
            rows.append(jnp.where(padding | (inner < 0), -1.0, at))
            rows.append(jnp.zeros((8 - len(rows), size), F32))
            rows = jnp.concatenate(rows, 0)
            for z in range(start // per, (start + size) // per):
                s.codes[layer, z] = rows[:, z * per - start : (z + 1) * per - start]


def unit_order(dm):
    units = dm.half_units
    here = lax.broadcasted_iota(jnp.int32, (units, units), 1)
    inner = divide(here, dm.unit_blocks)
    source = (here.astype(F32) - inner * dm.unit_blocks) * dm.block_rows + inner
    same = source == lax.broadcasted_iota(jnp.int32, (units, units), 0).astype(F32)
    return same.astype(F32).astype(BF16)


def reorder(dot, row, order):
    high = row.astype(BF16)
    rest = row - high.astype(F32)
    middle = rest.astype(BF16)
    low = (rest - middle.astype(F32)).astype(BF16)
    parts = [high.astype(F32), middle.astype(F32), low.astype(F32)]
    parts.append(jnp.zeros((13, row.shape[1]), F32))
    out = dot(jnp.concatenate(parts, 0).astype(BF16), order)
    return out[0:1] + (out[1:2] + out[2:3])


def pack_vectors(dm, vectors, first, s):
    cols, units, width = dm.half_cols, dm.half_units, dm.width
    wide = HEADS * HD
    order = unit_order(dm)
    for layer in range(dm.layers):
        rows = jnp.concatenate([vectors[0, r, layer : layer + 1, :] for r in range(6)], 0)
        flat = rows[0:1]
        q, v = flat[:, :cols], flat[:, cols : 2 * cols]
        none, mid = jnp.zeros((1, cols), F32), jnp.zeros((1, wide), F32)
        tail = jnp.zeros((1, FF - 3 * wide), F32)
        zero_half = jnp.concatenate([q, none, mid, v, none, tail], 1)
        one_half = jnp.concatenate([none, q, mid, none, v, tail], 1)
        s.vec_own[layer, 0:1, :] = jnp.where(first, zero_half, one_half)
        up = reorder(dot_nn, jnp.concatenate([rows[1:2], rows[2:3]], 1), order)
        none = jnp.zeros((1, units), F32)
        s.vec_own[layer, 1:2, :] = jnp.where(
            first, jnp.concatenate([up, none], 1), jnp.concatenate([none, up], 1)
        )
        own = jnp.concatenate([rows[3:6], jnp.zeros((3, FF - width), F32)], 1)
        none = jnp.zeros((3, FF), F32)
        s.vec_own[layer, 2:5, :] = jnp.where(first, own, none)
        s.vec_own[layer, 5:8, :] = jnp.where(first, none, own)


def unpack_vectors(dm, packed, first):
    cols, units, width = dm.half_cols, dm.half_units, dm.width
    wide = HEADS * HD
    flat = packed[0:1]
    zero_half = jnp.concatenate([flat[:, :cols], flat[:, 2 * wide : 2 * wide + cols]], 1)
    one_half = jnp.concatenate([flat[:, cols : 2 * cols], flat[:, 2 * wide + cols : 3 * wide]], 1)
    flat = packed[1:2]
    up = reorder(dot_nt, jnp.where(first, flat[:, :units], flat[:, units:]), unit_order(dm))
    own = jnp.where(first, packed[2:5, :width], packed[5:8, :width])
    return jnp.concatenate(
        [
            jnp.where(first, zero_half, one_half),
            up[:, :width],
            up[:, width:],
            own,
            jnp.zeros((2, width), F32),
        ],
        0,
    )


NORM_ROWS = 208


def norm_forward(dm, layer, source, gain, shift, low_out, hat_out, columns, place):
    def chunk(i):
        rows = pl.ds(pl.multiple_of(i * NORM_ROWS, NORM_ROWS), NORM_ROWS)
        values = source[rows, :]
        centred = values - jnp.mean(values, -1, keepdims=True)
        inv = lax.rsqrt(jnp.mean(centred * centred, -1, keepdims=True) + EPS_NORM)
        hat = centred * inv
        hat_out[layer, rows, :] = hat
        columns[rows, place : place + 1] = inv
        low_out[layer, rows, :] = (hat * gain + shift).astype(BF16)

    loop(dm.tokens // NORM_ROWS, chunk)


def norm_backward(dm, layer, grad, into, gain, hat_in, columns, place):
    def chunk(i, carry):
        rows = pl.ds(pl.multiple_of(i * NORM_ROWS, NORM_ROWS), NORM_ROWS)
        out, hat, inv = grad[rows, :], hat_in[layer, rows, :], columns[rows, place : place + 1]
        scaled = out * gain
        first = jnp.mean(scaled, -1, keepdims=True)
        second = jnp.mean(scaled * hat, -1, keepdims=True)
        into[rows, :] = into[rows, :] + inv * (scaled - first - hat * second)
        return carry[0] + fold_rows(out * hat), carry[1] + fold_rows(out)

    zero = jnp.zeros((8, dm.width), F32)
    gains, shifts = lax.fori_loop(0, dm.tokens // NORM_ROWS, chunk, (zero, zero), unroll=True)
    return jnp.sum(gains, 0, keepdims=True), jnp.sum(shifts, 0, keepdims=True)


def lane_halves():
    lane = lax.broadcasted_iota(jnp.int32, (1, 2 * HD), 1)
    return (lane < HD).astype(F32).astype(BF16), (lane >= HD).astype(F32).astype(BF16)


def image_rows(dm, image):
    return pl.ds(pl.multiple_of(image * dm.pad_seq, 16), dm.pad_seq)


def vector_row(dm, layer, s, row, count=None):
    return s.vec[layer, row : row + 1, : count or dm.width]


def forward_norm_a(dm, layer, s):
    gain, shift = vector_row(dm, layer, s, 2), vector_row(dm, layer, s, 3)
    norm_forward(dm, layer, s.hid, gain, shift, s.low_a, s.hat_a, s.columns, 1 + 2 * layer)


def forward_project(dm, layer, s):
    wide = HEADS * HD

    def project(image):
        rows = image_rows(dm, image)
        source = s.low_a[layer, rows, :]
        for kind in range(3):
            cols = slice(kind * wide, (kind + 1) * wide)
            value = dot_nt(source, s.w_qkv[layer, cols, :]) + s.vec[layer, 0:1, cols]
            s.qkv[layer, rows, cols] = value.astype(BF16)

    loop(dm.images, project)


def forward_attend(dm, layer, s):
    wide = HEADS * HD

    halves = lane_halves()

    def attend(image):
        rows = image_rows(dm, image)
        keep = s.columns[rows, 0:1]
        for pair in range(HEADS // 2):
            cols = slice(pair * 2 * HD, (pair + 1) * 2 * HD)
            q, k, v = (s.qkv[layer, rows, n * wide + cols.start : n * wide + cols.stop] for n in range(3))
            out = None
            for side, lanes in enumerate(halves):
                scores = dot_nt(k * lanes, q)
                scores = jnp.where(keep > 0, scores * HD ** (-0.5), NEG_FILL)
                exponent = jnp.exp(scores - jnp.max(scores, 0, keepdims=True))
                probs = (exponent * (1.0 / jnp.sum(exponent, 0, keepdims=True))).astype(BF16)
                s.probs[layer, image * HEADS + 2 * pair + side] = probs
                part = dot_tn(probs, v * lanes)
                out = part if out is None else out + part
            s.att[layer, rows, cols] = out.astype(BF16)

    loop(dm.images, attend)


def forward_out(dm, layer, s):
    bias = vector_row(dm, layer, s, 4)

    def out_project(image):
        rows = image_rows(dm, image)
        s.mid[rows, :] = s.hid[rows, :] + (dot_nn(s.att[layer, rows, :], s.w_out[layer]) + bias)

    loop(dm.images, out_project)


def forward_norm_b(dm, layer, s):
    gain, shift = vector_row(dm, layer, s, 5), vector_row(dm, layer, s, 6)
    norm_forward(dm, layer, s.mid, gain, shift, s.low_b, s.hat_b, s.columns, 2 + 2 * layer)


def forward_up(dm, layer, s):
    tile = 256

    def up(image):
        rows = image_rows(dm, image)
        source = s.low_b[layer, rows, :]
        for number in range(FF // tile):
            cols = slice(number * tile, (number + 1) * tile)
            u = dot_nt(source, s.w_up[layer, cols, :]) + s.vec[layer, 1:2, cols]
            act, slope = gelu_pair(u)
            s.act[layer, rows, cols] = act.astype(BF16)
            s.slope[layer, rows, cols] = slope.astype(BF16)

    loop(dm.images, up)


def forward_down(dm, layer, s):
    bias = vector_row(dm, layer, s, 7)

    def down(image):
        rows = image_rows(dm, image)
        s.hid[rows, :] = s.mid[rows, :] + (dot_nn(s.act[layer, rows, :], s.w_down[layer]) + bias)

    loop(dm.images, down)


FORWARD = (
    ("norm", forward_norm_a),
    ("project", forward_project),
    ("attend", forward_attend),
    ("out", forward_out),
    ("mid", forward_norm_b),
    ("up", forward_up),
    ("down", forward_down),
)


def low_and_sum(dm, source, target):
    def chunk(i, carry):
        rows = pl.ds(pl.multiple_of(i * NORM_ROWS, NORM_ROWS), NORM_ROWS)
        low = source[rows, :].astype(BF16)
        target[rows, :] = low
        return carry + fold_rows(low.astype(F32))

    total = lax.fori_loop(0, dm.tokens // NORM_ROWS, chunk, jnp.zeros((8, dm.width), F32), unroll=True)
    return jnp.sum(total, 0, keepdims=True)


def column_sums(dm, read, cols):
    def chunk(i, carry):
        rows = pl.ds(pl.multiple_of(i * NORM_ROWS, NORM_ROWS), NORM_ROWS)
        return carry + fold_rows(read(rows).astype(F32))

    total = lax.fori_loop(0, dm.tokens // NORM_ROWS, chunk, jnp.zeros((8, cols), F32), unroll=True)
    return jnp.sum(total, 0, keepdims=True)


def backward_start(dm, layer, s):
    s.vec_grad[layer, 7:8, : dm.width] = low_and_sum(dm, s.hid, s.low_g)


def backward_units(dm, layer, s):
    tile, units = 256, dm.half_units
    per_half = units // tile

    def unit_tile(number):
        cols = pl.ds(pl.multiple_of(number * tile, tile), tile)
        grad = dot_nt(s.low_g[...], s.w_down[layer, cols, :])
        grad = (grad * s.slope[layer, :, cols].astype(F32)).astype(BF16)
        s.slope[layer, :, cols] = grad
        half, at = number // per_half, pl.multiple_of((number % per_half) * tile, tile)
        s.grads[half, pl.ds(dm.natural + units + at, tile), :] = dot_tn(
            s.act[layer, :, cols], s.low_g[...]
        ).astype(BF16)
        s.grads[half, pl.ds(dm.natural + at, tile), :] = dot_tn(grad, s.low_b[layer]).astype(BF16)

    loop(FF // tile, unit_tile)


def backward_up_sums(dm, layer, s):
    s.vec_grad[layer, 1:2, :] = column_sums(dm, lambda rows: s.slope[layer, rows, :], FF)


def backward_down(dm, layer, s):
    def down(image):
        rows = image_rows(dm, image)
        s.mid[rows, :] = dot_nn(s.slope[layer, rows, :], s.w_up[layer])

    loop(dm.images, down)


def backward_norm_b(dm, layer, s):
    width = dm.width
    gain = vector_row(dm, layer, s, 5)
    gains, shifts = norm_backward(dm, layer, s.mid, s.hid, gain, s.hat_b, s.columns, 2 + 2 * layer)
    s.vec_grad[layer, 5:6, :width] = gains
    s.vec_grad[layer, 6:7, :width] = shifts
    s.vec_grad[layer, 4:5, :width] = low_and_sum(dm, s.hid, s.low_g)


def backward_out(dm, layer, s):
    cols = dm.half_cols
    value = dot_tn(s.att[layer], s.low_g[...]).astype(BF16)
    for half in range(dm.halves):
        s.grads[half, 3 * cols : dm.natural, :] = value[half * cols : (half + 1) * cols]

    def out_project(image):
        rows = image_rows(dm, image)
        s.att[layer, rows, :] = dot_nt(s.low_g[rows, :], s.w_out[layer]).astype(BF16)

    loop(dm.images, out_project)


def backward_attend(dm, layer, s, part):
    wide = HEADS * HD
    half = dm.images // 2

    halves = lane_halves()

    def attend(image):
        rows = image_rows(dm, image)
        keep = s.columns[rows, 0:1] * HD ** (-0.5)
        for pair in range(HEADS // 2):
            cols = slice(pair * 2 * HD, (pair + 1) * 2 * HD)
            q, k, v = (s.qkv[layer, rows, n * wide + cols.start : n * wide + cols.stop] for n in range(3))
            out = s.att[layer, rows, cols]
            parts = None
            for side, lanes in enumerate(halves):
                probs = s.probs[layer, image * HEADS + 2 * pair + side]
                grad = dot_nt(v * lanes, out)
                wide_probs = probs.astype(F32)
                total = jnp.sum(wide_probs * grad, 0, keepdims=True)
                raw = (wide_probs * (grad - total) * keep).astype(BF16)
                found = dot_tn(raw, k * lanes), dot_nn(raw, q * lanes), dot_nn(probs, out * lanes)
                parts = found if parts is None else [p + f for p, f in zip(parts, found)]
            for n, part in enumerate(parts):
                s.qkv[layer, rows, n * wide + cols.start : n * wide + cols.stop] = part.astype(BF16)

    loop(half, lambda i: attend(part * half + i))


def backward_rows(dm, layer, s):
    wide, cols = HEADS * HD, dm.half_cols
    for kind in range(3):
        value = dot_tn(s.qkv[layer, :, kind * wide : (kind + 1) * wide], s.low_a[layer]).astype(BF16)
        for half in range(dm.halves):
            s.grads[half, kind * cols : (kind + 1) * cols, :] = value[half * cols : (half + 1) * cols]


def backward_sums(dm, layer, s):
    wide = 3 * HEADS * HD
    s.vec_grad[layer, 0:1, :wide] = column_sums(dm, lambda rows: s.qkv[layer, rows, :], wide)


def backward_project(dm, layer, s):
    def project(image):
        rows = image_rows(dm, image)
        s.mid[rows, :] = dot_nn(s.qkv[layer, rows, :], s.w_qkv[layer])

    loop(dm.images, project)


def backward_norm_a(dm, layer, s):
    width = dm.width
    gain = vector_row(dm, layer, s, 2)
    gains, shifts = norm_backward(dm, layer, s.mid, s.hid, gain, s.hat_a, s.columns, 1 + 2 * layer)
    s.vec_grad[layer, 2:3, :width] = gains
    s.vec_grad[layer, 3:4, :width] = shifts


BACKWARD = (
    ("start", backward_start),
    ("units", backward_units),
    ("sums", backward_up_sums),
    ("down", backward_down),
    ("mid", backward_norm_b),
    ("out", backward_out),
    ("attend", functools.partial(backward_attend, part=0)),
    ("attended", functools.partial(backward_attend, part=1)),
    ("rows", backward_rows),
    ("more", backward_sums),
    ("project", backward_project),
    ("end", backward_norm_a),
)


class Net:
    def __init__(self, dm, s):
        self.dm, self.s, self.used = dm, s, 0
        self.rank, self.core = lax.axis_index("dp"), lax.axis_index("mp")
        _, rows, cols = dm.axes
        self.place = (self.rank // (rows * cols), (self.rank // cols) % rows, self.rank % cols)

    def device(self, *offsets):
        z, y, x = ((here + o) % size for here, o, size in zip(self.place, offsets, self.dm.axes))
        return ((z * self.dm.axes[1] + y) * self.dm.axes[2] + x, self.core)

    def sibling(self):
        return (self.rank, 1 - self.core)

    def on_axis(self, axis, offset):
        return self.device(*(offset if axis == k else 0 for k in range(3)))

    def along(self, axis, offset):
        return (self.place[axis] + offset) % self.dm.axes[axis]

    def partners(self):
        depth, rows, cols = self.dm.axes
        found = [self.sibling()]
        found += [self.device(o, 0, 0) for o in range(1, depth)]
        return found + [self.device(0, *o) for o in self.plane()]

    def plane(self):
        _, rows, cols = self.dm.axes
        return [(p, q) for p in range(rows) for q in range(cols) if p or q]

    def greet(self, semaphore):
        for partner in self.partners():
            pl.semaphore_signal(semaphore, inc=1, device_id=partner, device_id_type=MESH)

    def met(self, semaphore):
        pl.semaphore_wait(semaphore, len(self.partners()))

    def send(self, source, target, device):
        number = self.used
        self.used += 1
        copy = pltpu.make_async_remote_copy(
            src_ref=source,
            dst_ref=target,
            send_sem=self.s.send_sems.at[number],
            recv_sem=self.s.recv_sems.at[number],
            device_id=device,
            device_id_type=MESH,
        )
        copy.start()
        return copy


def copies_needed(dm):
    depth, rows, cols = dm.axes
    cross = depth * ((cols - 1) + (rows - 1))
    moves = depth - 1 + 2 * cross
    vectors = 1 + (depth - 1) + (rows * cols - 1)
    return dm.layers * (2 * moves + 6 + 4 + vectors) + 2 * dm.images + 1


def gather_steps(dm, layer, net, s, sent):
    depth, rows, cols = dm.axes
    z, y, x = net.place
    buf = s.gath.at[layer]
    head, tail = pl.ds(0, dm.first_rows), pl.ds(dm.first_rows, dm.shard_rows - dm.first_rows)
    first, second, third = {}, {}, {}

    def one(offset):
        ref = buf.at[z, y, x]
        first[offset] = net.send(ref, ref, net.on_axis(0, offset))
        sent.append(first[offset])

    def two(piece):
        at = net.along(0, -piece)
        a, b = buf.at[at, y, x, head], buf.at[at, y, x, tail]
        second[piece] = [net.send(a, a, net.on_axis(2, o)) for o in range(1, cols)]
        second[piece] += [net.send(b, b, net.on_axis(1, o)) for o in range(1, rows)]
        sent.extend(second[piece])

    def three(piece):
        at = net.along(0, -piece)
        a, b = buf.at[at, y, :, head], buf.at[at, :, x, tail]
        third[piece] = [net.send(a, a, net.on_axis(1, o)) for o in range(1, rows)]
        third[piece] += [net.send(b, b, net.on_axis(2, o)) for o in range(1, cols)]
        sent.extend(third[piece])

    def arrived(copies):
        for copy in copies:
            copy.wait_recv()

    for offset in range(1, depth):
        one(offset)
    two(0)
    yield
    arrived(second[0])
    three(0)
    order = sorted(range(1, depth), key=lambda o: min(o, depth - o))
    for number, piece in enumerate(order):
        arrived([first[piece]])
        two(piece)
        if number > 0:
            arrived(second[order[number - 1]])
            three(order[number - 1])
        yield
    arrived(second[order[-1]])
    three(order[-1])
    yield "sent"
    for piece in range(depth):
        arrived(third[piece])


def scatter_steps(dm, layer, net, s, sent, fill, put):
    depth, rows, cols = dm.axes
    z, y, x = net.place
    buf = s.gath.at[layer]
    head, tail = pl.ds(0, dm.first_rows), pl.ds(dm.first_rows, dm.shard_rows - dm.first_rows)
    order = sorted(range(depth), key=lambda o: -min(o, depth - o))
    first, second, third = {}, {}, {}

    def add(at, parts):
        value = buf[at].astype(F32)
        for part in parts:
            value = value + part.astype(F32)
        buf[at] = value.astype(BF16)

    def send(source, target, axis, offset):
        copy = net.send(source, target, net.on_axis(axis, offset))
        sent.append(copy)
        return copy

    if layer + 1 < dm.layers:
        net.met(s.credit)
    for piece in order:
        at = net.along(0, piece)
        fill(at)
        first[piece] = [
            send(buf.at[at, net.along(1, o), :, head], s.one_a.at[piece, o - 1], 1, o)
            for o in range(1, rows)
        ] + [
            send(buf.at[at, :, net.along(2, o), tail], s.one_b.at[piece, o - 1], 2, o)
            for o in range(1, cols)
        ]
        yield
    for piece in order:
        at = net.along(0, piece)
        for copy in first[piece]:
            copy.wait_recv()
        add((at, y, slice(None), head), [s.one_a[piece, o] for o in range(rows - 1)])
        add((at, slice(None), x, tail), [s.one_b[piece, o] for o in range(cols - 1)])
        second[piece] = [
            send(buf.at[at, y, net.along(2, o), head], s.two_a.at[piece, o - 1], 2, o)
            for o in range(1, cols)
        ] + [
            send(buf.at[at, net.along(1, o), x, tail], s.two_b.at[piece, o - 1], 1, o)
            for o in range(1, rows)
        ]
        yield
    for piece in order:
        at = net.along(0, piece)
        for copy in second[piece]:
            copy.wait_recv()
        add((at, y, x, head), [s.two_a[piece, o] for o in range(cols - 1)])
        add((at, y, x, tail), [s.two_b[piece, o] for o in range(rows - 1)])
        if piece > 0:
            third[piece] = send(buf.at[at, y, x], s.three.at[layer, piece - 1], 0, piece)
        if piece == order[-1] and layer > 0:
            net.greet(s.credit)
        yield
    value = buf[z, y, x].astype(F32)
    for piece in range(1, depth):
        third[piece].wait_recv()
        value = value + s.three[layer, piece - 1].astype(F32)
    put(layer, value)
    yield


def vector_steps(dm, layer, net, s, first, sent):
    depth, rows, cols = dm.axes
    z, y, x = net.place
    copy = net.send(s.vec_grad.at[layer], s.vec_back.at[layer], net.sibling())
    sent.append(copy)
    yield
    copy.wait_recv()
    here = s.vec_p.at[layer, y * cols + x]
    here[...] = unpack_vectors(dm, s.vec_grad[layer] + s.vec_back[layer], first)
    copies = [net.send(here, here, net.device(0, *o)) for o in net.plane()]
    sent.extend(copies)
    yield
    for copy in copies:
        copy.wait_recv()
    value = s.vec_p[layer, 0]
    for o in range(1, rows * cols):
        value = value + s.vec_p[layer, o]
    here = s.vec_z.at[layer, z]
    here[...] = value
    copies = [net.send(here, here, net.on_axis(0, o)) for o in range(1, depth)]
    sent.extend(copies)
    yield
    for copy in copies:
        copy.wait_recv()
    value = s.vec_z[layer, 0]
    for o in range(1, depth):
        value = value + s.vec_z[layer, o]
    s.vec_sum[layer] = value
    yield


class Refs:
    pass


def scratch_shapes(dm):
    layers, tokens, width, wide = dm.layers, dm.tokens, dm.width, HEADS * HD
    depth, rows, cols = dm.axes
    head, tail = dm.first_rows, dm.shard_rows - dm.first_rows
    vmem, copies = pltpu.VMEM, copies_needed(dm)
    return dict(
        hid=vmem((tokens, width), F32),
        mid=vmem((tokens, width), F32),
        columns=vmem((tokens, 8), F32),
        low_a=vmem((layers, tokens, width), BF16),
        low_b=vmem((layers, tokens, width), BF16),
        low_g=vmem((tokens, width), BF16),
        hat_a=vmem((layers, tokens, width), F32),
        hat_b=vmem((layers, tokens, width), F32),
        qkv=vmem((layers, tokens, 3 * wide), BF16),
        probs=vmem((layers, dm.images * HEADS, dm.pad_seq, dm.pad_seq), BF16),
        att=vmem((layers, tokens, wide), BF16),
        act=vmem((layers, tokens, FF), BF16),
        slope=vmem((layers, tokens, FF), BF16),
        w_qkv=vmem((layers, 3 * wide, width), BF16),
        w_out=vmem((layers, wide, width), BF16),
        w_up=vmem((layers, FF, width), BF16),
        w_down=vmem((layers, FF, width), BF16),
        grads=vmem((dm.halves, dm.half_rows, width), BF16),
        grads_in=vmem((dm.half_rows, width), BF16),
        gath=vmem((layers, depth, rows, cols, dm.shard_rows, width), BF16),
        one_a=vmem((depth, rows - 1, cols, head, width), BF16),
        one_b=vmem((depth, cols - 1, rows, tail, width), BF16),
        two_a=vmem((depth, cols - 1, head, width), BF16),
        two_b=vmem((depth, rows - 1, tail, width), BF16),
        three=vmem((layers, depth - 1, dm.shard_rows, width), BF16),
        rows=vmem((dm.shard_rows, width), F32),
        tok_in=vmem((dm.images, dm.seq, width), F32),
        tok_out=vmem((dm.images, dm.seq, width), F32),
        codes=vmem((layers, depth, 8, dm.keys // depth), F32),
        vec_own=vmem((layers, 8, FF), F32),
        vec=vmem((layers, 8, FF), F32),
        vec_grad=vmem((layers, 8, FF), F32),
        vec_in=vmem((layers, 8, FF), F32),
        vec_back=vmem((layers, 8, FF), F32),
        vec_z=vmem((layers, depth, 8, width), F32),
        vec_p=vmem((layers, rows * cols, 8, width), F32),
        vec_sum=vmem((layers, 8, width), F32),
        keep_row=vmem((8, -(-dm.pad_seq // 128) * 128), F32),
        send_sems=pltpu.SemaphoreType.DMA((copies,)),
        recv_sems=pltpu.SemaphoreType.DMA((copies,)),
        local_sems=pltpu.SemaphoreType.DMA((4 * dm.images,)),
        credit=pltpu.SemaphoreType.REGULAR,
        core_credit=pltpu.SemaphoreType.REGULAR,
    )


def load_tokens(dm, source, target, scale=None):
    tail = dm.pad_seq - 16
    for image in range(dm.images):
        start = image * dm.pad_seq
        target[start + tail : start + dm.pad_seq, :] = jnp.zeros((16, dm.width), F32)
        value = source[image]
        if scale is not None:
            value = value * scale[start : start + dm.seq, 0:1]
        target[start : start + dm.seq, :] = value


class Tokens:
    def __init__(self, dm, net, s):
        self.dm, self.net, self.s, self.used = dm, net, s, 0

    def image(self, ref, number):
        return ref.at[:, self.net.core * self.dm.images + number]

    def start(self, source, target):
        copy = pltpu.make_async_copy(source, target, self.s.local_sems.at[self.used])
        self.used += 1
        copy.start()
        return copy

    def load(self, ref):
        return [self.start(self.image(ref, i), self.s.tok_in.at[i]) for i in range(self.dm.images)]

    def store(self, ref):
        copies = []
        for i in range(self.dm.images):
            copies.append(self.start(self.s.tok_out.at[i], self.image(ref, i)))
            copies.append(self.net.send(self.s.tok_out.at[i], self.image(ref, i), self.net.sibling()))
        return copies


def wait_all(copies):
    for copy in copies:
        copy.wait()


def prepare_keep(dm, keep_mask, first, s):
    kept = keep_mask[...].astype(F32)
    kept = jnp.where(first, kept[: dm.images], kept[dm.images :])
    s.keep_row[...] = jnp.zeros(s.keep_row.shape, F32)
    s.keep_row[: dm.images, : dm.seq] = kept
    columns = jnp.transpose(s.keep_row[...])
    for image in range(dm.images):
        rows = slice(image * dm.pad_seq, (image + 1) * dm.pad_seq)
        s.columns[rows, 0:1] = columns[: dm.pad_seq, image : image + 1]


def own_shard(dm, master, net, s):
    z, y, x = net.place
    if dm.shard_rows > dm.block_rows * dm.slots:
        s.rows[...] = jnp.zeros(s.rows.shape, F32)
    for layer in range(dm.layers):
        for j in range(dm.block_rows):
            s.rows[j * dm.slots : (j + 1) * dm.slots, :] = master[0, layer, j]
        s.gath[layer, z, y, x] = s.rows[...].astype(BF16)


def step_kernel(dm, names, hidden, keep_mask, cotangent, slot_block, master, vectors, acts, grad_in, matrix, vec_out, *scratch):
    s = Refs()
    for name, ref in zip(names, scratch):
        setattr(s, name, ref)
    net = Net(dm, s)
    first = net.core == 0
    tokens = Tokens(dm, net, s)
    sent = []
    barrier = pltpu.get_barrier_semaphore()
    net.greet(barrier)
    load = tokens.load(hidden)
    own_shard(dm, master, net, s)
    net.met(barrier)
    moved = [[] for _ in range(dm.layers)]
    gathers = [gather_steps(dm, 0, net, s, moved[0])]
    next(gathers[0])
    pack_vectors(dm, vectors, first, s)
    other_vec = net.send(s.vec_own, s.vec_in, net.sibling())
    sent.append(other_vec)
    prepare_codes(dm, slot_block, s)
    prepare_keep(dm, keep_mask, first, s)
    wait_all(load)
    load_tokens(dm, s.tok_in, s.hid)
    load = tokens.load(cotangent)
    other_vec.wait_recv()
    s.vec[...] = s.vec_own[...] + s.vec_in[...]
    for _ in gathers[0]:
        if _ == "sent" and dm.layers > 1:
            gathers.append(gather_steps(dm, 1, net, s, moved[1]))
            next(gathers[1])

    def share(layer):
        cols, units = dm.half_cols, dm.half_units
        parts = permute_in(dm, layer, net.core, s)
        copies = []

        def push(ref, start, count):
            rows = ref.at[layer, pl.ds(pl.multiple_of(start, 16), count)]
            copies.append(net.send(rows, rows, net.sibling()))

        for _ in parts:
            for kind in range(3):
                push(s.w_qkv, kind * HEADS * HD + net.core * cols, cols)
            push(s.w_out, net.core * cols, cols)
        push(s.w_up, net.core * units, units)
        push(s.w_down, net.core * units, units)
        sent.extend(copies)
        return copies

    weights = share(0)
    for layer in range(dm.layers):
        following = gathers[layer + 1] if layer + 1 < len(gathers) else None

        def tick(name):
            if name == "norm":
                for copy in weights[:3]:
                    copy.wait_recv()
            if name == "attend":
                weights[3].wait_recv()
            if name == "mid":
                weights[4].wait_recv()
            if name == "up":
                weights[5].wait_recv()
            if following:
                event = next(following, None)
                if event == "sent" and layer + 2 < dm.layers:
                    gathers.append(gather_steps(dm, layer + 2, net, s, moved[layer + 2]))
                    next(gathers[layer + 2])

        for name, phase in FORWARD:
            phase(dm, layer, s)
            tick(name)
        if following:
            for _ in following:
                pass
            weights = share(layer + 1)
    for image in range(dm.images):
        rows = slice(image * dm.pad_seq, image * dm.pad_seq + dm.seq)
        s.tok_out[image] = s.hid[rows, :] * s.columns[rows, 0:1]
    store = tokens.store(acts)
    wait_all(load)
    load_tokens(dm, s.tok_in, s.hid, s.columns)


    def put_rows(layer, value):
        s.rows[...] = value
        for j in range(dm.block_rows):
            matrix[0, layer, j] = s.rows[j * dm.slots : (j + 1) * dm.slots, :]

    def put_vectors(layer):
        for r in range(vec_out.shape[1]):
            vec_out[0, r, layer : layer + 1, :] = s.vec_sum[layer, r : r + 1, :]

    depth = dm.axes[0]
    scatters, totals, shared = {}, {}, {}

    def push(layer, start, count):
        rows = pl.ds(start, count)
        copy = net.send(s.grads.at[1 - net.core, rows], s.grads_in.at[rows], net.sibling())
        shared.setdefault(layer, []).append(copy)

    def advance(steps, layer, count=1):
        if layer in steps:
            for _ in range(count):
                next(steps[layer], None)

    def scatter(layer):
        for copy in shared[layer]:
            copy.wait_recv()
        for copy in moved[layer]:
            copy.wait_send()
        fill = permute_out(dm, layer, net.core, s)
        scatters[layer] = scatter_steps(dm, layer, net, s, sent, fill, put_rows)
        advance(scatters, layer)

    def tick(layer, name):
        above = layer + 1
        if name == "units":
            if above in scatters:
                pl.semaphore_wait(s.core_credit, 1)
            push(layer, dm.natural, 2 * dm.half_units)
        if name in ("units", "down", "mid", "out"):
            advance(scatters, above)
        if name == "mid":
            advance(totals, above)
        if name in ("attend", "attended"):
            advance(scatters, above, depth // 2)
        if name == "rows":
            push(layer, 0, dm.natural)
        if name == "more" and layer == 0:
            scatter(layer)
            advance(scatters, layer, depth - 1)
        if name == "project" and layer == 0:
            advance(scatters, layer)
        if name == "end":
            totals[layer] = vector_steps(dm, layer, net, s, first, sent)
            advance(totals, layer)
            for copy in shared[layer]:
                copy.wait_send()
        if name == "end" and layer > 0:
            scatter(layer)
            advance(totals, layer)
            advance(scatters, layer, depth - 1)
            pl.semaphore_signal(s.core_credit, inc=1, device_id=net.sibling(), device_id_type=MESH)

    for layer in reversed(range(dm.layers)):
        for name, phase in BACKWARD:
            phase(dm, layer, s)
            tick(layer, name)
    wait_all(store)
    for image in range(dm.images):
        rows = slice(image * dm.pad_seq, image * dm.pad_seq + dm.seq)
        s.tok_out[image] = s.hid[rows, :]
    store = tokens.store(grad_in)
    advance(totals, 0)
    advance(scatters, 0, depth - 1)
    for layer in reversed(range(1, dm.layers)):
        advance(totals, layer)
        put_vectors(layer)
        advance(scatters, layer)
    advance(totals, 0)
    advance(scatters, 0, depth)
    advance(totals, 0)
    put_vectors(0)
    advance(scatters, 0)
    wait_all(store)
    for copy in sent:
        copy.wait_send()
    assert net.used <= copies_needed(dm)


def run_step(dm, hidden_in, keep_mask, cotangent, slot_block, master, vector_master):
    shapes = scratch_shapes(dm)
    out_shape = (
        jax.ShapeDtypeStruct(hidden_in.shape, F32),
        jax.ShapeDtypeStruct(hidden_in.shape, F32),
        jax.ShapeDtypeStruct(master.shape, F32),
        jax.ShapeDtypeStruct(vector_master.shape, F32),
    )
    full, far = pl.BlockSpec(memory_space=pltpu.VMEM), pl.BlockSpec(memory_space=pl.ANY)
    return pl.pallas_call(
        functools.partial(step_kernel, dm, tuple(shapes)),
        out_shape=out_shape,
        in_specs=[far, full, far, full, full, full],
        out_specs=[far, far, full, full],
        scratch_shapes=list(shapes.values()),
        compiler_params=pltpu.CompilerParams(
            vmem_limit_bytes=63 * 2**20, collective_id=0, has_side_effects=True
        ),
    )(hidden_in, keep_mask, cotangent, slot_block, master, vector_master)


def adam_step(weight, grad_sum, first_old, second_old, rate, decay):
    first_new = BETA_ONE * first_old + (1.0 - BETA_ONE) * grad_sum
    second_new = BETA_TWO * second_old + (1.0 - BETA_TWO) * grad_sum * grad_sum
    first_hat = first_new / (1.0 - BETA_ONE**STEP)
    second_hat = second_new / (1.0 - BETA_TWO**STEP)
    return (
        second_new,
        weight - rate * (first_hat / (jnp.sqrt(second_hat) + EPS_ADAM) + decay * weight),
    )


def shards(
    hidden_in, keep_mask, cotangent, slot_block, master, moment_one, moment_two, vector_master, vector_one, vector_two
):
    images, seq, width = hidden_in.shape
    halves, ranks = lax.axis_size("mp"), lax.axis_size("dp")
    dm = Dims(
        master.shape[1], images // halves, seq, width, halves, ranks, slot_block.shape[1], master.shape[3]
    )
    activations, input_grad, matrix_grad, vector_grad = run_step(
        dm,
        hidden_in.swapaxes(0, 1),
        keep_mask,
        cotangent.swapaxes(0, 1),
        slot_block,
        master.swapaxes(2, 3),
        vector_master.swapaxes(1, 2),
    )
    activations, input_grad = activations.swapaxes(0, 1), input_grad.swapaxes(0, 1)
    matrix_grad, vector_grad = matrix_grad.swapaxes(2, 3), vector_grad.swapaxes(1, 2)
    matrix_two, matrix_new = adam_step(
        master, matrix_grad, moment_one, moment_two, RATE_MATRIX, DECAY_MATRIX
    )
    vector_two_new, vector_new = adam_step(
        vector_master, vector_grad, vector_one, vector_two, RATE_VECTOR, 0.0
    )
    return (
        activations,
        input_grad,
        matrix_grad,
        matrix_two,
        matrix_new,
        vector_grad,
        vector_two_new,
        vector_new,
    )


def solution(mesh):
    images, rows, copied = P("dp", None, None), P("mp", None, "dp", None, None), P("mp", None, None, None)
    return jax.shard_map(
        shards,
        mesh=mesh,
        in_specs=(images, P("dp", None), images, P(), rows, rows, rows, copied, copied, copied),
        out_specs=(images, images, rows, rows, rows, copied, copied, copied),
        check_vma=False,
    )
```

```python
import functools

import jax
import jax.numpy as jnp
from jax import lax
from jax.experimental import pallas as pl
from jax.experimental.pallas import tpu as pltpu
from jax.sharding import PartitionSpec as P

HEADS = 6
HD = 64
FF = 1536
STEP = 10

EPS_NORM = 1e-06
BETA_ONE = 0.9
BETA_TWO = 0.999
RATE_MATRIX = 0.003
RATE_VECTOR = 0.01
DECAY_MATRIX = 0.05
EPS_ADAM = 1e-08
NEG_FILL = -1e30

F32 = jnp.float32
MESH = pl.DeviceIdType.MESH
BF16 = jnp.bfloat16


def dot_nn(left, right):
    return lax.dot_general(left, right, (((1,), (0,)), ((), ())), preferred_element_type=F32)


def dot_nt(left, right):
    return lax.dot_general(left, right, (((1,), (1,)), ((), ())), preferred_element_type=F32)


def dot_tn(left, right):
    return lax.dot_general(left, right, (((0,), (0,)), ((), ())), preferred_element_type=F32)


def fold_rows(values):
    rows, cols = values.shape
    return jnp.sum(values.reshape(rows // 8, 8, cols), 0)


def loop(count, body, unroll=True):
    lax.fori_loop(0, count, lambda i, c: (body(i), c)[1], 0, unroll=unroll)


def gelu_pair(u):
    cdf = 0.5 + 0.5 * lax.erf(u * (0.5**0.5))
    slope = cdf + u * (jnp.exp(-0.5 * u * u) * 0.3989422804014327)
    return u * cdf, slope


class Dims:
    def __init__(self, layers, images, seq, width, halves, ranks, blocks, block_rows):
        self.layers, self.images, self.seq, self.width = layers, images, seq, width
        self.halves, self.ranks, self.blocks, self.block_rows = halves, ranks, blocks, block_rows
        self.pad_seq = -(-seq // 16) * 16
        self.tokens = images * self.pad_seq
        self.slots = blocks // ranks
        side = 1
        while side**3 * 8 <= ranks:
            side *= 2
        self.axes = (ranks // (side * side), side, side)
        self.shard_rows = -(-block_rows * self.slots // 16) * 16
        self.first_rows = -(-self.shard_rows // 32) * 16
        self.groups = block_rows // 2 if 2 * self.slots % 16 == 0 else 1
        self.group = self.shard_rows // self.groups
        self.group_js = block_rows // self.groups
        self.keys = ranks * self.group
        self.half_cols = HEADS * HD // halves
        self.half_units = FF // halves
        self.natural = 4 * self.half_cols
        self.unit_blocks = self.half_units // block_rows
        self.group_units = self.group_js * self.unit_blocks
        self.half_rows = self.natural + 2 * self.half_units


def divide(values, number):
    return jnp.floor((values.astype(F32) + 0.5) * (1.0 / number))


def one_hot(rows, codes, axis):
    start, count = rows
    shape = (count, codes.shape[1]) if axis == 0 else (codes.shape[0], count)
    here = lax.broadcasted_iota(jnp.int32, shape, axis) + start
    return (here == codes.astype(jnp.int32)).astype(F32).astype(BF16)


def permute_in(dm, layer, half, s):
    cols, units = dm.half_cols, dm.half_units
    shards = [
        s.gath[layer, :, :, :, g * dm.group : (g + 1) * dm.group, :].reshape(dm.keys, dm.width)
        for g in range(dm.groups)
    ]
    code = jnp.concatenate([s.codes[layer, z] for z in range(dm.axes[0])], 1)
    for kind in range(4):
        total = None
        for g in range(dm.groups):
            part = dot_nn(one_hot((kind * cols, cols), code[g : g + 1, :], 0), shards[g])
            total = part if total is None else total + part
        total = total.astype(BF16)
        if kind < 3:
            s.w_qkv[layer, pl.ds(pl.multiple_of(kind * HEADS * HD + half * cols, 16), cols), :] = total
        else:
            s.w_out[layer, pl.ds(pl.multiple_of(half * cols, 16), cols), :] = total
    yield
    tile = min(256, dm.group_units)
    for g in range(dm.groups):
        for target, first in ((s.w_up, 0), (s.w_down, dm.group_units)):
            for start in range(0, dm.group_units, tile):
                chosen = one_hot((first + start, tile), code[dm.groups : dm.groups + 1, :], 0)
                at = pl.multiple_of(half * units + g * dm.group_units + start, 16)
                target[layer, pl.ds(at, tile), :] = dot_nn(chosen, shards[g]).astype(BF16)


def permute_out(dm, layer, half, s):
    natural, units, size = dm.natural, dm.half_units, dm.group_units

    def add(start, count):
        rows = slice(start, start + count)
        total = s.grads[half, rows, :].astype(F32) + s.grads_in[rows, :].astype(F32)
        s.grads_in[rows, :] = total.astype(BF16)

    for start in range(0, dm.half_rows, 256):
        add(start, min(256, dm.half_rows - start))
    per = dm.axes[1] * dm.axes[2] * dm.group

    def piece(z):
        codes = jnp.transpose(s.codes[layer, z])
        for g in range(dm.groups):
            up, down = natural + g * size, natural + units + g * size
            both = jnp.concatenate([s.grads_in[up : up + size, :], s.grads_in[down : down + size, :]], 0)
            rows = dot_nn(one_hot((0, natural), codes[:, g : g + 1], 1), s.grads_in[:natural, :])
            rows = rows + dot_nn(one_hot((0, 2 * size), codes[:, dm.groups : dm.groups + 1], 1), both)
            s.gath[layer, z, :, :, g * dm.group : (g + 1) * dm.group, :] = rows.astype(BF16).reshape(
                dm.axes[1], dm.axes[2], dm.group, dm.width
            )

    return piece


def prepare_codes(dm, slot_block, s):
    layers, blocks, group = dm.layers, dm.blocks, dm.group
    block = slot_block[...].astype(F32)
    high = divide(block, 16)
    zero = jnp.zeros((16 - 2 * layers, blocks), F32)
    halves = jnp.concatenate([high, block - 16.0 * high, zero], 0).astype(BF16)
    first = dm.natural // dm.block_rows
    per = dm.keys // dm.axes[0]
    size = per * max(1, 768 // per)
    for start in range(0, dm.keys, size):
        size = min(size, dm.keys - start)

        def place(shape):
            key = lax.broadcasted_iota(jnp.int32, shape, 1) + start
            rank = divide(key, group)
            inside = key.astype(F32) - rank * group
            odd = divide(inside, dm.slots)
            return rank * dm.slots + inside - odd * dm.slots, odd, inside >= dm.group_js * dm.slots

        slot, _, _ = place((blocks, size))
        same = slot == lax.broadcasted_iota(jnp.int32, (blocks, size), 0).astype(F32)
        parts = dot_nn(halves, same.astype(F32).astype(BF16))
        _, odd, padding = place((1, size))
        for layer in range(layers):
            block = 16.0 * parts[layer : layer + 1] + parts[layers + layer : layers + layer + 1]
            rows = []
            for g in range(dm.groups):
                at = block * dm.block_rows + g * dm.group_js + odd
                rows.append(jnp.where(padding | (block >= first), -1.0, at))
            inner = block - first
            at = odd * dm.unit_blocks + inner
            at = jnp.where(inner < dm.unit_blocks, at, at - dm.unit_blocks + dm.group_units)
            rows.append(jnp.where(padding | (inner < 0), -1.0, at))
            rows.append(jnp.zeros((8 - len(rows), size), F32))
            rows = jnp.concatenate(rows, 0)
            for z in range(start // per, (start + size) // per):
                s.codes[layer, z] = rows[:, z * per - start : (z + 1) * per - start]


def unit_order(dm):
    units = dm.half_units
    here = lax.broadcasted_iota(jnp.int32, (units, units), 1)
    inner = divide(here, dm.unit_blocks)
    source = (here.astype(F32) - inner * dm.unit_blocks) * dm.block_rows + inner
    same = source == lax.broadcasted_iota(jnp.int32, (units, units), 0).astype(F32)
    return same.astype(F32).astype(BF16)


def reorder(dot, row, order):
    high = row.astype(BF16)
    rest = row - high.astype(F32)
    middle = rest.astype(BF16)
    low = (rest - middle.astype(F32)).astype(BF16)
    parts = [high.astype(F32), middle.astype(F32), low.astype(F32)]
    parts.append(jnp.zeros((13, row.shape[1]), F32))
    out = dot(jnp.concatenate(parts, 0).astype(BF16), order)
    return out[0:1] + (out[1:2] + out[2:3])


def pack_vectors(dm, vectors, first, s):
    cols, units, width = dm.half_cols, dm.half_units, dm.width
    wide = HEADS * HD
    order = unit_order(dm)
    for layer in range(dm.layers):
        rows = jnp.concatenate([vectors[0, r, layer : layer + 1, :] for r in range(6)], 0)
        flat = rows[0:1]
        q, v = flat[:, :cols], flat[:, cols : 2 * cols]
        none, mid = jnp.zeros((1, cols), F32), jnp.zeros((1, wide), F32)
        tail = jnp.zeros((1, FF - 3 * wide), F32)
        zero_half = jnp.concatenate([q, none, mid, v, none, tail], 1)
        one_half = jnp.concatenate([none, q, mid, none, v, tail], 1)
        s.vec_own[layer, 0:1, :] = jnp.where(first, zero_half, one_half)
        up = reorder(dot_nn, jnp.concatenate([rows[1:2], rows[2:3]], 1), order)
        none = jnp.zeros((1, units), F32)
        s.vec_own[layer, 1:2, :] = jnp.where(
            first, jnp.concatenate([up, none], 1), jnp.concatenate([none, up], 1)
        )
        own = jnp.concatenate([rows[3:6], jnp.zeros((3, FF - width), F32)], 1)
        none = jnp.zeros((3, FF), F32)
        s.vec_own[layer, 2:5, :] = jnp.where(first, own, none)
        s.vec_own[layer, 5:8, :] = jnp.where(first, none, own)


def unpack_vectors(dm, packed, first):
    cols, units, width = dm.half_cols, dm.half_units, dm.width
    wide = HEADS * HD
    flat = packed[0:1]
    zero_half = jnp.concatenate([flat[:, :cols], flat[:, 2 * wide : 2 * wide + cols]], 1)
    one_half = jnp.concatenate([flat[:, cols : 2 * cols], flat[:, 2 * wide + cols : 3 * wide]], 1)
    flat = packed[1:2]
    up = reorder(dot_nt, jnp.where(first, flat[:, :units], flat[:, units:]), unit_order(dm))
    own = jnp.where(first, packed[2:5, :width], packed[5:8, :width])
    return jnp.concatenate(
        [
            jnp.where(first, zero_half, one_half),
            up[:, :width],
            up[:, width:],
            own,
            jnp.zeros((2, width), F32),
        ],
        0,
    )


NORM_ROWS = 208


def norm_forward(dm, layer, source, gain, shift, low_out, hat_out, devs, place):
    def chunk(i):
        rows = pl.ds(pl.multiple_of(i * NORM_ROWS, NORM_ROWS), NORM_ROWS)
        values = source[rows, :]
        centred = values - jnp.mean(values, -1, keepdims=True)
        inv = lax.rsqrt(jnp.mean(centred * centred, -1, keepdims=True) + EPS_NORM)
        hat = centred * inv
        hat_out[layer, rows, :] = hat
        devs[layer, rows, place : place + 1] = inv
        low_out[layer, rows, :] = (hat * gain + shift).astype(BF16)

    loop(dm.tokens // NORM_ROWS, chunk)


def norm_backward(dm, layer, grad, into, gain, hat_in, devs, place):
    def chunk(i, carry):
        rows = pl.ds(pl.multiple_of(i * NORM_ROWS, NORM_ROWS), NORM_ROWS)
        out, hat, inv = grad[rows, :], hat_in[layer, rows, :], devs[layer, rows, place : place + 1]
        scaled = out * gain
        first = jnp.mean(scaled, -1, keepdims=True)
        second = jnp.mean(scaled * hat, -1, keepdims=True)
        into[rows, :] = into[rows, :] + inv * (scaled - first - hat * second)
        return carry[0] + fold_rows(out * hat), carry[1] + fold_rows(out)

    zero = jnp.zeros((8, dm.width), F32)
    gains, shifts = lax.fori_loop(0, dm.tokens // NORM_ROWS, chunk, (zero, zero), unroll=True)
    return jnp.sum(gains, 0, keepdims=True), jnp.sum(shifts, 0, keepdims=True)


def lane_halves():
    lane = lax.broadcasted_iota(jnp.int32, (1, 2 * HD), 1)
    return (lane < HD).astype(F32).astype(BF16), (lane >= HD).astype(F32).astype(BF16)


def image_rows(dm, image):
    return pl.ds(pl.multiple_of(image * dm.pad_seq, 16), dm.pad_seq)


def vector_row(dm, layer, s, row, count=None):
    return s.vec[layer, row : row + 1, : count or dm.width]


def forward_norm_a(dm, layer, s):
    gain, shift = vector_row(dm, layer, s, 2), vector_row(dm, layer, s, 3)
    norm_forward(dm, layer, s.hid, gain, shift, s.low_a, s.hat_a, s.devs, 0)


def forward_project(dm, layer, s):
    wide = HEADS * HD

    def project(image):
        rows = image_rows(dm, image)
        source = s.low_a[layer, rows, :]
        for kind in range(3):
            cols = slice(kind * wide, (kind + 1) * wide)
            value = dot_nt(source, s.w_qkv[layer, cols, :]) + s.vec[layer, 0:1, cols]
            s.qkv[layer, rows, cols] = value.astype(BF16)

    loop(dm.images, project)


def forward_attend(dm, layer, s):
    wide = HEADS * HD

    halves = lane_halves()

    def attend(image):
        rows = image_rows(dm, image)
        keep = s.columns[rows, 0:1]
        for pair in range(HEADS // 2):
            cols = slice(pair * 2 * HD, (pair + 1) * 2 * HD)
            q, k, v = (s.qkv[layer, rows, n * wide + cols.start : n * wide + cols.stop] for n in range(3))
            out = None
            for side, lanes in enumerate(halves):
                scores = dot_nt(k * lanes, q)
                scores = jnp.where(keep > 0, scores * HD ** (-0.5), NEG_FILL)
                exponent = jnp.exp(scores - jnp.max(scores, 0, keepdims=True))
                probs = (exponent * (1.0 / jnp.sum(exponent, 0, keepdims=True))).astype(BF16)
                s.probs[layer, image * HEADS + 2 * pair + side] = probs
                part = dot_tn(probs, v * lanes)
                out = part if out is None else out + part
            s.att[layer, rows, cols] = out.astype(BF16)

    loop(dm.images, attend)


def forward_out(dm, layer, s):
    bias = vector_row(dm, layer, s, 4)

    def out_project(image):
        rows = image_rows(dm, image)
        s.mid[rows, :] = s.hid[rows, :] + (dot_nn(s.att[layer, rows, :], s.w_out[layer]) + bias)

    loop(dm.images, out_project)


def forward_norm_b(dm, layer, s):
    gain, shift = vector_row(dm, layer, s, 5), vector_row(dm, layer, s, 6)
    norm_forward(dm, layer, s.mid, gain, shift, s.low_b, s.hat_b, s.devs, 1)


def forward_up(dm, layer, s):
    tile = 256

    def up(image):
        rows = image_rows(dm, image)
        source = s.low_b[layer, rows, :]
        for number in range(FF // tile):
            cols = slice(number * tile, (number + 1) * tile)
            u = dot_nt(source, s.w_up[layer, cols, :]) + s.vec[layer, 1:2, cols]
            act, slope = gelu_pair(u)
            s.act[layer, rows, cols] = act.astype(BF16)
            s.slope[layer, rows, cols] = slope.astype(BF16)

    loop(dm.images, up)


def forward_down(dm, layer, s):
    bias = vector_row(dm, layer, s, 7)

    def down(image):
        rows = image_rows(dm, image)
        s.hid[rows, :] = s.mid[rows, :] + (dot_nn(s.act[layer, rows, :], s.w_down[layer]) + bias)

    loop(dm.images, down)


FORWARD = (
    ("norm", forward_norm_a),
    ("project", forward_project),
    ("attend", forward_attend),
    ("out", forward_out),
    ("mid", forward_norm_b),
    ("up", forward_up),
    ("down", forward_down),
)


def low_and_sum(dm, source, target):
    def chunk(i, carry):
        rows = pl.ds(pl.multiple_of(i * NORM_ROWS, NORM_ROWS), NORM_ROWS)
        low = source[rows, :].astype(BF16)
        target[rows, :] = low
        return carry + fold_rows(low.astype(F32))

    total = lax.fori_loop(0, dm.tokens // NORM_ROWS, chunk, jnp.zeros((8, dm.width), F32), unroll=True)
    return jnp.sum(total, 0, keepdims=True)


def column_sums(dm, read, cols):
    def chunk(i, carry):
        rows = pl.ds(pl.multiple_of(i * NORM_ROWS, NORM_ROWS), NORM_ROWS)
        return carry + fold_rows(read(rows).astype(F32))

    total = lax.fori_loop(0, dm.tokens // NORM_ROWS, chunk, jnp.zeros((8, cols), F32), unroll=True)
    return jnp.sum(total, 0, keepdims=True)


def backward_start(dm, layer, s):
    s.vec_grad[layer, 7:8, : dm.width] = low_and_sum(dm, s.hid, s.low_g)


def backward_units(dm, layer, s):
    tile, units = 256, dm.half_units
    per_half = units // tile

    def unit_tile(number):
        cols = pl.ds(pl.multiple_of(number * tile, tile), tile)
        grad = dot_nt(s.low_g[...], s.w_down[layer, cols, :])
        grad = (grad * s.slope[layer, :, cols].astype(F32)).astype(BF16)
        s.slope[layer, :, cols] = grad
        half, at = number // per_half, pl.multiple_of((number % per_half) * tile, tile)
        s.grads[half, pl.ds(dm.natural + units + at, tile), :] = dot_tn(
            s.act[layer, :, cols], s.low_g[...]
        ).astype(BF16)
        s.grads[half, pl.ds(dm.natural + at, tile), :] = dot_tn(grad, s.low_b[layer]).astype(BF16)

    loop(FF // tile, unit_tile)


def backward_up_sums(dm, layer, s):
    s.vec_grad[layer, 1:2, :] = column_sums(dm, lambda rows: s.slope[layer, rows, :], FF)


def backward_down(dm, layer, s):
    def down(image):
        rows = image_rows(dm, image)
        s.mid[rows, :] = dot_nn(s.slope[layer, rows, :], s.w_up[layer])

    loop(dm.images, down)


def backward_norm_b(dm, layer, s):
    width = dm.width
    gain = vector_row(dm, layer, s, 5)
    gains, shifts = norm_backward(dm, layer, s.mid, s.hid, gain, s.hat_b, s.devs, 1)
    s.vec_grad[layer, 5:6, :width] = gains
    s.vec_grad[layer, 6:7, :width] = shifts
    s.vec_grad[layer, 4:5, :width] = low_and_sum(dm, s.hid, s.low_g)


def backward_out(dm, layer, s):
    cols = dm.half_cols
    value = dot_tn(s.att[layer], s.low_g[...]).astype(BF16)
    for half in range(dm.halves):
        s.grads[half, 3 * cols : dm.natural, :] = value[half * cols : (half + 1) * cols]

    def out_project(image):
        rows = image_rows(dm, image)
        s.att[layer, rows, :] = dot_nt(s.low_g[rows, :], s.w_out[layer]).astype(BF16)

    loop(dm.images, out_project)


def backward_attend(dm, layer, s, part):
    wide = HEADS * HD
    half = dm.images // 2

    halves = lane_halves()

    def attend(image):
        rows = image_rows(dm, image)
        keep = s.columns[rows, 0:1] * HD ** (-0.5)
        for pair in range(HEADS // 2):
            cols = slice(pair * 2 * HD, (pair + 1) * 2 * HD)
            q, k, v = (s.qkv[layer, rows, n * wide + cols.start : n * wide + cols.stop] for n in range(3))
            out = s.att[layer, rows, cols]
            parts = None
            for side, lanes in enumerate(halves):
                probs = s.probs[layer, image * HEADS + 2 * pair + side]
                grad = dot_nt(v * lanes, out)
                wide_probs = probs.astype(F32)
                total = jnp.sum(wide_probs * grad, 0, keepdims=True)
                raw = (wide_probs * (grad - total) * keep).astype(BF16)
                found = dot_tn(raw, k * lanes), dot_nn(raw, q * lanes), dot_nn(probs, out * lanes)
                parts = found if parts is None else [p + f for p, f in zip(parts, found)]
            for n, part in enumerate(parts):
                s.qkv[layer, rows, n * wide + cols.start : n * wide + cols.stop] = part.astype(BF16)

    loop(half, lambda i: attend(part * half + i))


def backward_rows(dm, layer, s):
    wide, cols = HEADS * HD, dm.half_cols
    for kind in range(3):
        value = dot_tn(s.qkv[layer, :, kind * wide : (kind + 1) * wide], s.low_a[layer]).astype(BF16)
        for half in range(dm.halves):
            s.grads[half, kind * cols : (kind + 1) * cols, :] = value[half * cols : (half + 1) * cols]


def backward_sums(dm, layer, s):
    wide = 3 * HEADS * HD
    s.vec_grad[layer, 0:1, :wide] = column_sums(dm, lambda rows: s.qkv[layer, rows, :], wide)


def backward_project(dm, layer, s):
    def project(image):
        rows = image_rows(dm, image)
        s.mid[rows, :] = dot_nn(s.qkv[layer, rows, :], s.w_qkv[layer])

    loop(dm.images, project)


def backward_norm_a(dm, layer, s):
    width = dm.width
    gain = vector_row(dm, layer, s, 2)
    gains, shifts = norm_backward(dm, layer, s.mid, s.hid, gain, s.hat_a, s.devs, 0)
    s.vec_grad[layer, 2:3, :width] = gains
    s.vec_grad[layer, 3:4, :width] = shifts


BACKWARD = (
    ("start", backward_start),
    ("units", backward_units),
    ("sums", backward_up_sums),
    ("down", backward_down),
    ("mid", backward_norm_b),
    ("out", backward_out),
    ("attend", functools.partial(backward_attend, part=0)),
    ("attended", functools.partial(backward_attend, part=1)),
    ("rows", backward_rows),
    ("more", backward_sums),
    ("project", backward_project),
    ("end", backward_norm_a),
)


class Net:
    def __init__(self, dm, s):
        self.dm, self.s, self.keys = dm, s, {}
        self.rank, self.core = lax.axis_index("dp"), lax.axis_index("mp")
        _, rows, cols = dm.axes
        self.place = (self.rank // (rows * cols), (self.rank // cols) % rows, self.rank % cols)

    def device(self, *offsets):
        z, y, x = ((here + o) % size for here, o, size in zip(self.place, offsets, self.dm.axes))
        return ((z * self.dm.axes[1] + y) * self.dm.axes[2] + x, self.core)

    def sibling(self):
        return (self.rank, 1 - self.core)

    def on_axis(self, axis, offset):
        return self.device(*(offset if axis == k else 0 for k in range(3)))

    def along(self, axis, offset):
        return (self.place[axis] + offset) % self.dm.axes[axis]

    def partners(self):
        depth = self.dm.axes[0]
        found = [self.sibling()]
        found += [self.device(o, 0, 0) for o in range(1, depth)]
        return found + [self.device(0, *o) for o in self.plane()]

    def plane(self):
        _, rows, cols = self.dm.axes
        return [(p, q) for p in range(rows) for q in range(cols) if p or q]

    def greet(self, semaphore):
        for partner in self.partners():
            pl.semaphore_signal(semaphore, inc=1, device_id=partner, device_id_type=MESH)

    def met(self, semaphore):
        pl.semaphore_wait(semaphore, len(self.partners()))

    def copy(self, key, layer, source, target, device):
        name, count, index = key
        if name not in self.keys:
            used = sum(n for _, n in self.keys.values()) * self.dm.layers
            self.keys[name] = (used, count)
        first, known = self.keys[name]
        assert known == count
        number = first + layer * count + index
        return pltpu.make_async_remote_copy(
            src_ref=source,
            dst_ref=target,
            send_sem=self.s.send_sems.at[number],
            recv_sem=self.s.recv_sems.at[number],
            device_id=device,
            device_id_type=MESH,
        )


def copies_needed(dm):
    depth, rows, cols = dm.axes
    cross = depth * (cols + rows - 2)
    vectors = 1 + (depth - 1) + (rows * cols - 1)
    return dm.layers * (depth - 1 + 2 * cross + 6 + 2 + vectors + 1 + 2 * dm.images)


def start_all(copies):
    for copy in copies:
        copy.start()


def wait_all(copies):
    for copy in copies:
        copy.wait()


class Gather:
    def __init__(self, dm, net, s, layer):
        self.dm, self.net, self.layer, self.buf = dm, net, layer, s.gath.at[layer]
        self.head = pl.ds(0, dm.first_rows)
        self.tail = pl.ds(dm.first_rows, dm.shard_rows - dm.first_rows)
        depth = dm.axes[0]
        self.order = sorted(range(1, depth), key=lambda o: min(o, depth - o))

    def keys(self, name, piece, number):
        _, rows, cols = self.dm.axes
        count = rows + cols - 2
        return (name, self.dm.axes[0] * count, piece * count + number)

    def one(self, offset):
        ref = self.buf.at[self.net.place]
        key = ("one", self.dm.axes[0] - 1, offset - 1)
        return [self.net.copy(key, self.layer, ref, ref, self.net.on_axis(0, offset))]

    def pairs(self, name, piece, pairs):
        copies = []
        for ref, axis in pairs:
            for o in range(1, self.dm.axes[axis]):
                key = self.keys(name, piece, len(copies))
                copies.append(self.net.copy(key, self.layer, ref, ref, self.net.on_axis(axis, o)))
        return copies

    def two(self, piece):
        at, (_, y, x) = self.net.along(0, -piece), self.net.place
        return self.pairs(
            "two", piece, [(self.buf.at[at, y, x, self.head], 2), (self.buf.at[at, y, x, self.tail], 1)]
        )

    def three(self, piece):
        at, (_, y, x) = self.net.along(0, -piece), self.net.place
        return self.pairs(
            "three", piece, [(self.buf.at[at, y, :, self.head], 1), (self.buf.at[at, :, x, self.tail], 2)]
        )

    def begin(self):
        for offset in range(1, self.dm.axes[0]):
            start_all(self.one(offset))
        start_all(self.two(0))

    def steps(self):
        found = []
        before = 0
        for piece in self.order + [None]:

            def step(before=before, piece=piece):
                if piece is not None:
                    wait_all(self.one(piece))
                    start_all(self.two(piece))
                wait_all(self.two(before))
                start_all(self.three(before))

            found.append(step)
            before = piece
        return found

    def end(self):
        for piece in range(self.dm.axes[0]):
            wait_all(self.three(piece))


class Scatter:
    def __init__(self, dm, net, s, layer):
        self.dm, self.net, self.s, self.layer, self.buf = dm, net, s, layer, s.gath.at[layer]
        self.head = pl.ds(0, dm.first_rows)
        self.tail = pl.ds(dm.first_rows, dm.shard_rows - dm.first_rows)

    def pairs(self, name, piece, parts):
        copies = []
        _, rows, cols = self.dm.axes
        count = rows + cols - 2
        for axis, make in parts:
            for o in range(1, self.dm.axes[axis]):
                key = (name, self.dm.axes[0] * count, piece * count + len(copies))
                source, target = make(self.net.along(axis, o), o - 1)
                copies.append(self.net.copy(key, 0, source, target, self.net.on_axis(axis, o)))
        return copies

    def one(self, piece):
        at, s, buf = self.net.along(0, piece), self.s, self.buf
        return self.pairs(
            "three",
            piece,
            [
                (1, lambda to, n: (buf.at[at, to, :, self.head], s.one_a.at[piece, n])),
                (2, lambda to, n: (buf.at[at, :, to, self.tail], s.one_b.at[piece, n])),
            ],
        )

    def two(self, piece):
        at, s, buf, (_, y, x) = self.net.along(0, piece), self.s, self.buf, self.net.place
        return self.pairs(
            "two",
            piece,
            [
                (2, lambda to, n: (buf.at[at, y, to, self.head], s.two_a.at[piece, n])),
                (1, lambda to, n: (buf.at[at, to, x, self.tail], s.two_b.at[piece, n])),
            ],
        )

    def three(self, piece):
        _, y, x = self.net.place
        source = self.buf.at[self.net.along(0, piece), y, x]
        target = self.s.three.at[self.layer, piece - 1]
        key = ("one", self.dm.axes[0] - 1, piece - 1)
        turn = self.dm.layers - 1 - self.layer
        return self.net.copy(key, turn, source, target, self.net.device(piece, 0, 0))

    def add(self, at, parts):
        value = self.buf[at].astype(F32)
        for part in parts:
            value = value + part.astype(F32)
        self.buf[at] = value.astype(BF16)

    def second(self, piece):
        _, rows, cols = self.dm.axes
        at, s, (_, y, x) = self.net.along(0, piece), self.s, self.net.place
        wait_all(self.one(piece))
        self.add((at, y, slice(None), self.head), [s.one_a[piece, o] for o in range(rows - 1)])
        self.add((at, slice(None), x, self.tail), [s.one_b[piece, o] for o in range(cols - 1)])
        start_all(self.two(piece))

    def third(self, piece):
        _, rows, cols = self.dm.axes
        at, s, (_, y, x) = self.net.along(0, piece), self.s, self.net.place
        wait_all(self.two(piece))
        self.add((at, y, x, self.head), [s.two_a[piece, o] for o in range(cols - 1)])
        self.add((at, y, x, self.tail), [s.two_b[piece, o] for o in range(rows - 1)])

        @pl.when(piece > 0)
        def _():
            self.three(piece).start()

    def end(self):
        value = self.buf[self.net.place].astype(F32)
        for piece in range(1, self.dm.axes[0]):
            self.three(piece).wait()
            value = value + self.s.three[self.layer, piece - 1].astype(F32)
        return value


class Totals:
    def __init__(self, dm, net, s, layer, first):
        self.dm, self.net, self.s, self.layer, self.first = dm, net, s, layer, first

    def across(self):
        s, layer = self.s, self.layer
        copy = self.net.copy(
            ("cores", 1, 0), layer, s.vec_grad.at[layer], s.vec_back.at[layer], self.net.sibling()
        )
        return [copy]

    def plane(self):
        _, y, x = self.net.place
        here = self.s.vec_p.at[self.layer, y * self.dm.axes[2] + x]
        offsets = self.net.plane()
        return [
            self.net.copy(("plane", len(offsets), n), self.layer, here, here, self.net.device(0, *o))
            for n, o in enumerate(offsets)
        ]

    def depth(self):
        here = self.s.vec_z.at[self.layer, self.net.place[0]]
        size = self.dm.axes[0]
        return [
            self.net.copy(("depth", size - 1, o - 1), self.layer, here, here, self.net.on_axis(0, o))
            for o in range(1, size)
        ]

    def begin(self):
        start_all(self.across())

    def second(self):
        s, layer, (_, y, x) = self.s, self.layer, self.net.place
        wait_all(self.across())
        value = unpack_vectors(self.dm, s.vec_grad[layer] + s.vec_back[layer], self.first)
        s.vec_p[layer, y * self.dm.axes[2] + x] = value
        start_all(self.plane())

    def third(self):
        s, layer = self.s, self.layer
        wait_all(self.plane())
        value = s.vec_p[layer, 0]
        for o in range(1, self.dm.axes[1] * self.dm.axes[2]):
            value = value + s.vec_p[layer, o]
        s.vec_z[layer, self.net.place[0]] = value
        start_all(self.depth())

    def end(self):
        wait_all(self.depth())
        value = self.s.vec_z[self.layer, 0]
        for o in range(1, self.dm.axes[0]):
            value = value + self.s.vec_z[self.layer, o]
        return value


class Refs:
    pass


def scratch_shapes(dm):
    layers, tokens, width, wide = dm.layers, dm.tokens, dm.width, HEADS * HD
    depth, rows, cols = dm.axes
    head, tail = dm.first_rows, dm.shard_rows - dm.first_rows
    vmem, copies = pltpu.VMEM, copies_needed(dm)
    return dict(
        hid=vmem((tokens, width), F32),
        mid=vmem((tokens, width), F32),
        columns=vmem((tokens, 8), F32),
        devs=vmem((layers, tokens, 8), F32),
        low_a=vmem((layers, tokens, width), BF16),
        low_b=vmem((layers, tokens, width), BF16),
        low_g=vmem((tokens, width), BF16),
        hat_a=vmem((layers, tokens, width), F32),
        hat_b=vmem((layers, tokens, width), F32),
        qkv=vmem((layers, tokens, 3 * wide), BF16),
        probs=vmem((layers, dm.images * HEADS, dm.pad_seq, dm.pad_seq), BF16),
        att=vmem((layers, tokens, wide), BF16),
        act=vmem((layers, tokens, FF), BF16),
        slope=vmem((layers, tokens, FF), BF16),
        w_qkv=vmem((layers, 3 * wide, width), BF16),
        w_out=vmem((layers, wide, width), BF16),
        w_up=vmem((layers, FF, width), BF16),
        w_down=vmem((layers, FF, width), BF16),
        grads=vmem((dm.halves, dm.half_rows, width), BF16),
        grads_in=vmem((dm.half_rows, width), BF16),
        gath=vmem((layers, depth, rows, cols, dm.shard_rows, width), BF16),
        one_a=vmem((depth, rows - 1, cols, head, width), BF16),
        one_b=vmem((depth, cols - 1, rows, tail, width), BF16),
        two_a=vmem((depth, cols - 1, head, width), BF16),
        two_b=vmem((depth, rows - 1, tail, width), BF16),
        three=vmem((layers, depth - 1, dm.shard_rows, width), BF16),
        rows=vmem((dm.shard_rows, width), F32),
        tok_in=vmem((dm.images, dm.seq, width), F32),
        tok_out=vmem((dm.images, dm.seq, width), F32),
        codes=vmem((layers, depth, 8, dm.keys // depth), F32),
        vec_own=vmem((layers, 8, FF), F32),
        vec=vmem((layers, 8, FF), F32),
        vec_grad=vmem((layers, 8, FF), F32),
        vec_in=vmem((layers, 8, FF), F32),
        vec_back=vmem((layers, 8, FF), F32),
        vec_z=vmem((layers, depth, 8, width), F32),
        vec_p=vmem((layers, rows * cols, 8, width), F32),
        vec_sum=vmem((layers, 8, width), F32),
        keep_row=vmem((8, -(-dm.pad_seq // 128) * 128), F32),
        send_sems=pltpu.SemaphoreType.DMA((copies,)),
        recv_sems=pltpu.SemaphoreType.DMA((copies,)),
        load_sems=pltpu.SemaphoreType.DMA((dm.images,)),
        store_sems=pltpu.SemaphoreType.DMA((dm.images,)),
        credit=pltpu.SemaphoreType.REGULAR,
        core_credit=pltpu.SemaphoreType.REGULAR,
    )


def load_tokens(dm, source, target, scale=None):
    tail = dm.pad_seq - 16
    for image in range(dm.images):
        start = image * dm.pad_seq
        target[start + tail : start + dm.pad_seq, :] = jnp.zeros((16, dm.width), F32)
        value = source[image]
        if scale is not None:
            value = value * scale[start : start + dm.seq, 0:1]
        target[start : start + dm.seq, :] = value


class Tokens:
    def __init__(self, dm, net, s):
        self.dm, self.net, self.s = dm, net, s

    def image(self, ref, number):
        return ref.at[:, self.net.core * self.dm.images + number]

    def load(self, ref):
        sems = self.s.load_sems
        return [
            pltpu.make_async_copy(self.image(ref, i), self.s.tok_in.at[i], sems.at[i])
            for i in range(self.dm.images)
        ]

    def store(self, ref, turn):
        copies = []
        for i in range(self.dm.images):
            source, target = self.s.tok_out.at[i], self.image(ref, i)
            copies.append(pltpu.make_async_copy(source, target, self.s.store_sems.at[i]))
            key = ("tokens", self.dm.images, i)
            copies.append(self.net.copy(key, turn, source, target, self.net.sibling()))
        return copies


def prepare_keep(dm, keep_mask, first, s):
    kept = keep_mask[...].astype(F32)
    kept = jnp.where(first, kept[: dm.images], kept[dm.images :])
    s.keep_row[...] = jnp.zeros(s.keep_row.shape, F32)
    s.keep_row[: dm.images, : dm.seq] = kept
    columns = jnp.transpose(s.keep_row[...])
    for image in range(dm.images):
        rows = slice(image * dm.pad_seq, (image + 1) * dm.pad_seq)
        s.columns[rows, 0:1] = columns[: dm.pad_seq, image : image + 1]


def own_shard(dm, master, net, s):
    z, y, x = net.place
    if dm.shard_rows > dm.block_rows * dm.slots:
        s.rows[...] = jnp.zeros(s.rows.shape, F32)
    for layer in range(dm.layers):
        for j in range(dm.block_rows):
            s.rows[j * dm.slots : (j + 1) * dm.slots, :] = master[0, layer, j]
        s.gath[layer, z, y, x] = s.rows[...].astype(BF16)


def step_kernel(dm, names, hidden, keep_mask, cotangent, slot_block, master, vectors, acts, grad_in, matrix, vec_out, *scratch):
    s = Refs()
    for name, ref in zip(names, scratch):
        setattr(s, name, ref)
    net = Net(dm, s)
    first = net.core == 0
    tokens = Tokens(dm, net, s)
    cols, units, depth = dm.half_cols, dm.half_units, dm.axes[0]
    assert dm.layers == 2
    gathers = [Gather(dm, net, s, layer) for layer in range(dm.layers)]
    barrier = pltpu.get_barrier_semaphore()
    net.greet(barrier)
    start_all(tokens.load(hidden))
    own_shard(dm, master, net, s)
    net.met(barrier)
    gathers[0].begin()
    pack_vectors(dm, vectors, first, s)
    other_vec = net.copy(("vectors", 1, 0), 0, s.vec_own, s.vec_in, net.sibling())
    other_vec.start()
    prepare_codes(dm, slot_block, s)
    prepare_keep(dm, keep_mask, first, s)
    wait_all(tokens.load(hidden))
    load_tokens(dm, s.tok_in, s.hid)
    start_all(tokens.load(cotangent))
    other_vec.wait()
    s.vec[...] = s.vec_own[...] + s.vec_in[...]
    for step in gathers[0].steps():
        step()
    gathers[1].begin()
    steps = gathers[1].steps()

    def weights(layer):
        parts = [(s.w_qkv, kind * HEADS * HD + net.core * cols, cols) for kind in range(3)]
        parts += [(s.w_out, net.core * cols, cols), (s.w_up, net.core * units, units)]
        parts.append((s.w_down, net.core * units, units))
        copies = []
        for ref, start, count in parts:
            rows = ref.at[layer, pl.ds(pl.multiple_of(start, 16), count)]
            key = ("weights", len(parts), len(copies))
            copies.append(net.copy(key, layer, rows, rows, net.sibling()))
        return copies

    def forward(layer):
        shares = weights(layer)
        for name, phase in FORWARD:
            phase(dm, layer, s)
            if name == "norm":
                Gather(dm, net, s, layer).end()
                parts = permute_in(dm, layer, net.core, s)
                next(parts)
                start_all(shares[:4])
                next(parts, None)
                start_all(shares[4:])
                wait_all(shares[:3])
            if name == "attend":
                shares[3].wait()
            if name == "mid":
                shares[4].wait()
            if name == "up":
                shares[5].wait()
            if name in ("norm", "project", "attend", "mid"):
                now = [steps.pop(0)]
                if name == "mid":
                    now, steps[:] = now + steps, []

                @pl.when(layer + 1 < dm.layers)
                def _(now=now):
                    for step in now:
                        step()

    lax.fori_loop(0, dm.layers, lambda i, c: (forward(i), c)[1], 0)
    for image in range(dm.images):
        rows = slice(image * dm.pad_seq, image * dm.pad_seq + dm.seq)
        s.tok_out[image] = s.hid[rows, :] * s.columns[rows, 0:1]
    start_all(tokens.store(acts, 0))
    wait_all(tokens.load(cotangent))
    load_tokens(dm, s.tok_in, s.hid, s.columns)

    def put_rows(layer):
        s.rows[...] = Scatter(dm, net, s, layer).end()
        for j in range(dm.block_rows):
            matrix[0, layer, j] = s.rows[j * dm.slots : (j + 1) * dm.slots, :]

    def put_vectors(layer):
        value = Totals(dm, net, s, layer, first).end()
        for r in range(vec_out.shape[1]):
            vec_out[0, r, layer : layer + 1, :] = value[r : r + 1]

    def share(layer, number):
        rows = (pl.ds(dm.natural, 2 * units), pl.ds(0, dm.natural))[number]
        source = s.grads.at[1 - net.core, rows]
        return net.copy(("shares", 2, number), layer, source, s.grads_in.at[rows], net.sibling())

    def backward(turn):
        layer = dm.layers - 1 - turn
        later = turn > 0
        before = Scatter(dm, net, s, 1)
        totals_before = Totals(dm, net, s, 1, first)

        def when_later(body, *args):
            pl.when(later)(lambda: body(*args))

        order = list(range(depth - 1, -1, -1))
        for name, phase in BACKWARD:
            phase(dm, layer, s)
            if name == "start":
                when_later(totals_before.second)
            if name == "units":
                when_later(pl.semaphore_wait, s.core_credit, 1)
                share(layer, 0).start()
            if name in ("units", "down", "mid", "out"):
                count = -(-depth // 4)
                now, order = order[:count], order[count:]
                for piece in now:
                    when_later(before.second, piece)
            if name == "out":
                order = list(range(depth - 1, -1, -1))
            if name in ("attend", "attended"):
                count = depth // 2
                now, order = order[:count], order[count:]
                for piece in now:
                    when_later(before.third, piece)
            if name == "attended":
                when_later(net.greet, s.credit)
                when_later(totals_before.third)
            if name == "rows":
                share(layer, 1).start()
            if name == "more":
                wait_all([share(layer, 0), share(layer, 1)])
                fill = permute_out(dm, layer, net.core, s)
                when_later(net.met, s.credit)
                scatter = Scatter(dm, net, s, layer)

                def piece_out(number, carry):
                    piece = depth - 1 - number
                    fill(net.along(0, piece))
                    start_all(scatter.one(piece))
                    return carry

                lax.fori_loop(0, depth, piece_out, 0)

                @pl.when(layer > 0)
                def _():
                    pl.semaphore_signal(
                        s.core_credit, inc=1, device_id=net.sibling(), device_id_type=MESH
                    )
        Totals(dm, net, s, layer, first).begin()

    lax.fori_loop(0, dm.layers, lambda i, c: (backward(i), c)[1], 0)
    wait_all(tokens.store(acts, 0))
    for image in range(dm.images):
        rows = slice(image * dm.pad_seq, image * dm.pad_seq + dm.seq)
        s.tok_out[image] = s.hid[rows, :]
    start_all(tokens.store(grad_in, 1))
    scatter, totals = Scatter(dm, net, s, 0), Totals(dm, net, s, 0, first)
    totals.second()
    loop(depth, lambda n: scatter.second(depth - 1 - n))
    put_vectors(1)
    put_rows(1)
    totals.third()
    loop(depth, lambda n: scatter.third(depth - 1 - n))
    put_vectors(0)
    put_rows(0)
    wait_all(tokens.store(grad_in, 1))


def run_step(dm, hidden_in, keep_mask, cotangent, slot_block, master, vector_master):
    shapes = scratch_shapes(dm)
    out_shape = (
        jax.ShapeDtypeStruct(hidden_in.shape, F32),
        jax.ShapeDtypeStruct(hidden_in.shape, F32),
        jax.ShapeDtypeStruct(master.shape, F32),
        jax.ShapeDtypeStruct(vector_master.shape, F32),
    )
    full, far = pl.BlockSpec(memory_space=pltpu.VMEM), pl.BlockSpec(memory_space=pl.ANY)
    return pl.pallas_call(
        functools.partial(step_kernel, dm, tuple(shapes)),
        out_shape=out_shape,
        in_specs=[far, full, far, full, full, full],
        out_specs=[far, far, full, full],
        scratch_shapes=list(shapes.values()),
        compiler_params=pltpu.CompilerParams(
            vmem_limit_bytes=63 * 2**20, collective_id=0, has_side_effects=True
        ),
    )(hidden_in, keep_mask, cotangent, slot_block, master, vector_master)


def adam_step(weight, grad_sum, first_old, second_old, rate, decay):
    first_new = BETA_ONE * first_old + (1.0 - BETA_ONE) * grad_sum
    second_new = BETA_TWO * second_old + (1.0 - BETA_TWO) * grad_sum * grad_sum
    first_hat = first_new / (1.0 - BETA_ONE**STEP)
    second_hat = second_new / (1.0 - BETA_TWO**STEP)
    return (
        second_new,
        weight - rate * (first_hat / (jnp.sqrt(second_hat) + EPS_ADAM) + decay * weight),
    )


def finish_kernel(parts, *refs):
    large, matrix, vector = refs[:2], refs[2:6], refs[6:10]
    large_out, matrix_out, vector_out = refs[10:12], refs[12:15], refs[15:18]
    stage, matrix_in, vector_in, matrix_done, vector_done, stage_sems, load_sems, store_sems = refs[18:]
    loads, stores = [], []
    rows_all = stage.shape[1]
    size = -(-rows_all // parts)
    for start in range(0, rows_all, size):
        for number, (source, target) in enumerate(zip(large, large_out)):
            rows = pl.ds(start, min(size, rows_all - start))
            held, sem = stage.at[number, rows], stage_sems.at[len(loads)]
            loads.append(pltpu.make_async_copy(source.at[rows], held, sem))
            stores.append(pltpu.make_async_copy(held, target.at[rows], sem))
    matrix_loads = [
        pltpu.make_async_copy(ref, matrix_in.at[n], load_sems.at[n]) for n, ref in enumerate(matrix)
    ]
    vector_loads = [
        pltpu.make_async_copy(ref, vector_in.at[n], load_sems.at[4 + n]) for n, ref in enumerate(vector)
    ]
    results = [
        pltpu.make_async_copy(matrix_done.at[n], ref, store_sems.at[n])
        for n, ref in enumerate(matrix_out)
    ]
    results += [
        pltpu.make_async_copy(vector_done.at[n], ref, store_sems.at[3 + n])
        for n, ref in enumerate(vector_out)
    ]
    start_all(vector_loads + matrix_loads + loads)
    wait_all(vector_loads + matrix_loads)

    def adam(held, done, at, rate, decay):
        grad, weight, one, two = (held[(n, *at)] for n in range(4))
        done[(0, *at)] = grad
        done[(1, *at)], done[(2, *at)] = adam_step(weight, grad, one, two, rate, decay)

    for layer in range(matrix_in.shape[2]):
        adam(matrix_in, matrix_done, (0, layer), RATE_MATRIX, DECAY_MATRIX)
    adam(vector_in, vector_done, (0,), RATE_VECTOR, 0.0)
    start_all(results)
    for load, store in zip(loads, stores):
        load.wait()
        store.start()
    wait_all(stores + results)


def run_finish(acts, grad_in, matrix, vector):
    parts = 1
    far = pl.BlockSpec(memory_space=pl.ANY)
    shapes = [acts, grad_in] + [matrix[0]] * 3 + [vector[0]] * 3
    return pl.pallas_call(
        functools.partial(finish_kernel, parts),
        out_shape=tuple(jax.ShapeDtypeStruct(a.shape, F32) for a in shapes),
        in_specs=[far] * 10,
        out_specs=[far] * 8,
        scratch_shapes=[
            pltpu.VMEM((2, *acts.shape), F32),
            pltpu.VMEM((4, *matrix[0].shape), F32),
            pltpu.VMEM((4, *vector[0].shape), F32),
            pltpu.VMEM((3, *matrix[0].shape), F32),
            pltpu.VMEM((3, *vector[0].shape), F32),
            pltpu.SemaphoreType.DMA((2 * parts,)),
            pltpu.SemaphoreType.DMA((8,)),
            pltpu.SemaphoreType.DMA((6,)),
        ],
        compiler_params=pltpu.CompilerParams(vmem_limit_bytes=63 * 2**20),
    )(acts, grad_in, *matrix, *vector)


def shards(
    hidden_in, keep_mask, cotangent, slot_block, master, moment_one, moment_two, vector_master, vector_one, vector_two
):
    images, seq, width = hidden_in.shape
    halves, ranks = lax.axis_size("mp"), lax.axis_size("dp")
    dm = Dims(
        master.shape[1], images // halves, seq, width, halves, ranks, slot_block.shape[1], master.shape[3]
    )
    matrix = [array.swapaxes(2, 3) for array in (master, moment_one, moment_two)]
    vector = [array.swapaxes(1, 2) for array in (vector_master, vector_one, vector_two)]
    acts, grad_in, matrix_grad, vector_grad = run_step(
        dm, hidden_in.swapaxes(0, 1), keep_mask, cotangent.swapaxes(0, 1), slot_block, matrix[0], vector[0]
    )
    results = run_finish(acts, grad_in, [matrix_grad] + matrix, [vector_grad] + vector)
    return tuple(
        array.swapaxes(*axes)
        for array, axes in zip(results, [(0, 1)] * 2 + [(2, 3)] * 3 + [(1, 2)] * 3)
    )


def solution(mesh):
    images, rows, copied = P("dp", None, None), P("mp", None, "dp", None, None), P("mp", None, None, None)
    return jax.shard_map(
        shards,
        mesh=mesh,
        in_specs=(images, P("dp", None), images, P(), rows, rows, rows, copied, copied, copied),
        out_specs=(images, images, rows, rows, rows, copied, copied, copied),
        check_vma=False,
    )
```

```python
import functools

import jax
import jax.numpy as jnp
from jax import lax
from jax.experimental import pallas as pl
from jax.experimental.pallas import tpu as pltpu
from jax.sharding import PartitionSpec as P

HEADS = 6
HD = 64
FF = 1536
STEP = 10

EPS_NORM = 1e-06
BETA_ONE = 0.9
BETA_TWO = 0.999
RATE_MATRIX = 0.003
RATE_VECTOR = 0.01
DECAY_MATRIX = 0.05
EPS_ADAM = 1e-08
NEG_FILL = -1e30

F32 = jnp.float32
MESH = pl.DeviceIdType.MESH
BF16 = jnp.bfloat16


def dot_nn(left, right):
    return lax.dot_general(left, right, (((1,), (0,)), ((), ())), preferred_element_type=F32)


def dot_nt(left, right):
    return lax.dot_general(left, right, (((1,), (1,)), ((), ())), preferred_element_type=F32)


def dot_tn(left, right):
    return lax.dot_general(left, right, (((0,), (0,)), ((), ())), preferred_element_type=F32)


def fold_rows(values):
    rows, cols = values.shape
    return jnp.sum(values.reshape(rows // 8, 8, cols), 0)


def loop(count, body, unroll=True):
    lax.fori_loop(0, count, lambda i, c: (body(i), c)[1], 0, unroll=unroll)


def gelu_pair(u):
    cdf = 0.5 + 0.5 * lax.erf(u * (0.5**0.5))
    slope = cdf + u * (jnp.exp(-0.5 * u * u) * 0.3989422804014327)
    return u * cdf, slope


class Dims:
    def __init__(self, layers, images, seq, width, halves, ranks, blocks, block_rows):
        self.layers, self.images, self.seq, self.width = layers, images, seq, width
        self.halves, self.ranks, self.blocks, self.block_rows = halves, ranks, blocks, block_rows
        self.pad_seq = -(-seq // 16) * 16
        self.tokens = images * self.pad_seq
        self.slots = blocks // ranks
        side = 1
        while side**3 * 8 <= ranks:
            side *= 2
        self.axes = (ranks // (side * side), side, side)
        self.shard_rows = -(-block_rows * self.slots // 16) * 16
        self.last_rows = 16 * (self.shard_rows // 144)
        self.most_rows = self.shard_rows - self.last_rows
        self.first_rows = -(-self.most_rows // 32) * 16
        self.groups = block_rows // 2 if 2 * self.slots % 16 == 0 else 1
        self.group = self.shard_rows // self.groups
        self.group_js = block_rows // self.groups
        self.keys = ranks * self.group
        self.half_cols = HEADS * HD // halves
        self.half_units = FF // halves
        self.natural = 4 * self.half_cols
        self.unit_blocks = self.half_units // block_rows
        self.kind_blocks = self.half_cols // block_rows
        self.first_unit = 4 * self.kind_blocks


def divide(values, number):
    return jnp.floor((values.astype(F32) + 0.5) * (1.0 / number))


def one_hot(rows, codes, axis):
    start, count = rows
    shape = (count, codes.shape[1]) if axis == 0 else (codes.shape[0], count)
    here = lax.broadcasted_iota(jnp.int32, shape, axis) + start
    return (here == codes.astype(jnp.int32)).astype(F32).astype(BF16)


def permute_in(dm, layer, half, s):
    cols, units, some = dm.half_cols, dm.half_units, dm.unit_blocks
    shards = [
        s.gath[layer, :, :, :, g * dm.group : (g + 1) * dm.group, :].reshape(dm.keys, dm.width)
        for g in range(dm.groups)
    ]
    code = jnp.concatenate([s.codes[layer, z] for z in range(dm.axes[0])], 1)[0:1]
    count = dm.first_unit
    starts = [odd * dm.blocks for odd in range(dm.group_js)]
    chosen = jnp.concatenate([one_hot((start, count), code, 0) for start in starts], 0)
    attention = []
    for g in range(dm.groups):
        rows = dot_nn(chosen, shards[g]).astype(BF16)
        attention += [rows[n * count : (n + 1) * count] for n in range(dm.group_js)]
    order = row_order(dm, cols, dm.kind_blocks)
    for kind in range(4):
        part = slice(kind * dm.kind_blocks, (kind + 1) * dm.kind_blocks)
        rows = dot_nn(order, jnp.concatenate([rows[part] for rows in attention], 0)).astype(BF16)
        if kind < 3:
            s.w_qkv[layer, pl.ds(pl.multiple_of(kind * HEADS * HD + half * cols, 16), cols), :] = rows
        else:
            s.w_out[layer, pl.ds(pl.multiple_of(half * cols, 16), cols), :] = rows
    yield
    for odd, start in enumerate(starts):
        chosen = one_hot((start + count, 2 * some), code, 0)
        for g in range(dm.groups):
            rows = dot_nn(chosen, shards[g]).astype(BF16)
            at = half * units + (g * dm.group_js + odd) * some
            at = pl.ds(pl.multiple_of(at, 16), some)
            s.w_up[layer, at, :] = rows[:some]
            s.w_down[layer, at, :] = rows[some:]


def put_grads(dm, s, kind, rows):
    cols, size = dm.half_cols, dm.kind_blocks
    order = row_order(dm, cols, size)
    for half in range(dm.halves):
        found = dot_tn(order, rows[half * cols : (half + 1) * cols]).astype(BF16)
        for j in range(dm.block_rows):
            s.grads[half, j // dm.group_js, j % dm.group_js, kind * size : (kind + 1) * size, :] = found[
                j * size : (j + 1) * size
            ]


def permute_out(dm, layer, half, s):
    for g in range(dm.groups):
        for odd in range(dm.group_js):
            total = s.grads[half, g, odd].astype(F32) + s.grads_in[g, odd].astype(F32)
            s.grads_in[g, odd] = total.astype(BF16)

    def pieces(places):
        codes = [jnp.transpose(s.codes[layer, z])[:, 0:1] for z in places]
        chosen = one_hot((0, dm.group_js * dm.blocks), jnp.concatenate(codes, 0), 1)
        size = chosen.shape[0] // len(places)
        for g in range(dm.groups):
            grads = s.grads_in[g].reshape(dm.group_js * dm.blocks, dm.width)
            rows = dot_nn(chosen, grads).astype(BF16)
            for n, z in enumerate(places):
                s.gath[layer, z, :, :, g * dm.group : (g + 1) * dm.group, :] = rows[
                    n * size : (n + 1) * size
                ].reshape(dm.axes[1], dm.axes[2], dm.group, dm.width)

    return pieces


def prepare_codes(dm, slot_block, s):
    layers, blocks, group = dm.layers, dm.blocks, dm.group
    block = slot_block[...].astype(F32)
    high = divide(block, 16)
    zero = jnp.zeros((16 - 2 * layers, blocks), F32)
    halves = jnp.concatenate([high, block - 16.0 * high, zero], 0).astype(BF16)
    per = dm.keys // dm.axes[0]
    size = per * max(1, 768 // per)
    for start in range(0, dm.keys, size):
        size = min(size, dm.keys - start)

        def place(shape):
            key = lax.broadcasted_iota(jnp.int32, shape, 1) + start
            rank = divide(key, group)
            inside = key.astype(F32) - rank * group
            odd = divide(inside, dm.slots)
            return rank * dm.slots + inside - odd * dm.slots, odd, inside >= dm.group_js * dm.slots

        slot, _, _ = place((blocks, size))
        same = slot == lax.broadcasted_iota(jnp.int32, (blocks, size), 0).astype(F32)
        parts = dot_nn(halves, same.astype(F32).astype(BF16))
        _, odd, padding = place((1, size))
        for layer in range(layers):
            block = 16.0 * parts[layer : layer + 1] + parts[layers + layer : layers + layer + 1]
            row = jnp.where(padding, -1.0, odd * blocks + block)
            rows = jnp.concatenate([row, jnp.zeros((7, size), F32)], 0)
            for z in range(start // per, (start + size) // per):
                s.codes[layer, z] = rows[:, z * per - start : (z + 1) * per - start]


def row_order(dm, rows, blocks):
    here = lax.broadcasted_iota(jnp.int32, (rows, rows), 1)
    inner = divide(here, blocks)
    source = (here.astype(F32) - inner * blocks) * dm.block_rows + inner
    same = source == lax.broadcasted_iota(jnp.int32, (rows, rows), 0).astype(F32)
    return same.astype(F32).astype(BF16)


def unit_order(dm):
    return row_order(dm, dm.half_units, dm.unit_blocks)


def reorder(dot, row, order):
    high = row.astype(BF16)
    rest = row - high.astype(F32)
    middle = rest.astype(BF16)
    low = (rest - middle.astype(F32)).astype(BF16)
    parts = [high.astype(F32), middle.astype(F32), low.astype(F32)]
    parts.append(jnp.zeros((13, row.shape[1]), F32))
    out = dot(jnp.concatenate(parts, 0).astype(BF16), order)
    return out[0:1] + (out[1:2] + out[2:3])


def pack_vectors(dm, vectors, first, s):
    cols, units, width = dm.half_cols, dm.half_units, dm.width
    wide = HEADS * HD
    order = unit_order(dm)
    for layer in range(dm.layers):
        rows = jnp.concatenate([vectors[0, r, layer : layer + 1, :] for r in range(6)], 0)
        flat = rows[0:1]
        q, v = flat[:, :cols], flat[:, cols : 2 * cols]
        none, mid = jnp.zeros((1, cols), F32), jnp.zeros((1, wide), F32)
        tail = jnp.zeros((1, FF - 3 * wide), F32)
        zero_half = jnp.concatenate([q, none, mid, v, none, tail], 1)
        one_half = jnp.concatenate([none, q, mid, none, v, tail], 1)
        s.vec_own[layer, 0:1, :] = jnp.where(first, zero_half, one_half)
        up = reorder(dot_nn, jnp.concatenate([rows[1:2], rows[2:3]], 1), order)
        none = jnp.zeros((1, units), F32)
        s.vec_own[layer, 1:2, :] = jnp.where(
            first, jnp.concatenate([up, none], 1), jnp.concatenate([none, up], 1)
        )
        own = jnp.concatenate([rows[3:6], jnp.zeros((3, FF - width), F32)], 1)
        none = jnp.zeros((3, FF), F32)
        s.vec_own[layer, 2:5, :] = jnp.where(first, own, none)
        s.vec_own[layer, 5:8, :] = jnp.where(first, none, own)


def unpack_vectors(dm, packed, first):
    cols, units, width = dm.half_cols, dm.half_units, dm.width
    wide = HEADS * HD
    flat = packed[0:1]
    zero_half = jnp.concatenate([flat[:, :cols], flat[:, 2 * wide : 2 * wide + cols]], 1)
    one_half = jnp.concatenate([flat[:, cols : 2 * cols], flat[:, 2 * wide + cols : 3 * wide]], 1)
    flat = packed[1:2]
    up = reorder(dot_nt, jnp.where(first, flat[:, :units], flat[:, units:]), unit_order(dm))
    own = jnp.where(first, packed[2:5, :width], packed[5:8, :width])
    return jnp.concatenate(
        [
            jnp.where(first, zero_half, one_half),
            up[:, :width],
            up[:, width:],
            own,
            jnp.zeros((2, width), F32),
        ],
        0,
    )


NORM_ROWS = 208


def norm_forward(dm, layer, source, gain, shift, low_out, hat_out, devs, place):
    def chunk(i):
        rows = pl.ds(pl.multiple_of(i * NORM_ROWS, NORM_ROWS), NORM_ROWS)
        values = source[rows, :]
        centred = values - jnp.mean(values, -1, keepdims=True)
        inv = lax.rsqrt(jnp.mean(centred * centred, -1, keepdims=True) + EPS_NORM)
        hat = centred * inv
        hat_out[layer, rows, :] = hat
        devs[layer, rows, place : place + 1] = inv
        low_out[layer, rows, :] = (hat * gain + shift).astype(BF16)

    loop(dm.tokens // NORM_ROWS, chunk)


def norm_backward(dm, layer, grad, into, gain, hat_in, devs, place):
    def chunk(i, carry):
        rows = pl.ds(pl.multiple_of(i * NORM_ROWS, NORM_ROWS), NORM_ROWS)
        out, hat, inv = grad[rows, :], hat_in[layer, rows, :], devs[layer, rows, place : place + 1]
        scaled = out * gain
        first = jnp.mean(scaled, -1, keepdims=True)
        second = jnp.mean(scaled * hat, -1, keepdims=True)
        into[rows, :] = into[rows, :] + inv * (scaled - first - hat * second)
        return carry[0] + fold_rows(out * hat), carry[1] + fold_rows(out)

    zero = jnp.zeros((8, dm.width), F32)
    gains, shifts = lax.fori_loop(0, dm.tokens // NORM_ROWS, chunk, (zero, zero), unroll=True)
    return jnp.sum(gains, 0, keepdims=True), jnp.sum(shifts, 0, keepdims=True)


def lane_halves():
    lane = lax.broadcasted_iota(jnp.int32, (1, 2 * HD), 1)
    return (lane < HD).astype(F32).astype(BF16), (lane >= HD).astype(F32).astype(BF16)


def image_rows(dm, image):
    return pl.ds(pl.multiple_of(image * dm.pad_seq, 16), dm.pad_seq)


def vector_row(dm, layer, s, row, count=None):
    return s.vec[layer, row : row + 1, : count or dm.width]


def forward_norm_a(dm, layer, s):
    gain, shift = vector_row(dm, layer, s, 2), vector_row(dm, layer, s, 3)
    norm_forward(dm, layer, s.hid, gain, shift, s.low_a, s.hat_a, s.devs, 0)


def forward_project(dm, layer, s):
    wide = HEADS * HD

    def project(image):
        rows = image_rows(dm, image)
        source = s.low_a[layer, rows, :]
        for kind in range(3):
            cols = slice(kind * wide, (kind + 1) * wide)
            value = dot_nt(source, s.w_qkv[layer, cols, :]) + s.vec[layer, 0:1, cols]
            s.qkv[layer, rows, cols] = value.astype(BF16)

    loop(dm.images, project)


def forward_attend(dm, layer, s):
    wide = HEADS * HD

    halves = lane_halves()

    def attend(image):
        rows = image_rows(dm, image)
        keep = s.columns[rows, 0:1]
        for pair in range(HEADS // 2):
            cols = slice(pair * 2 * HD, (pair + 1) * 2 * HD)
            q, k, v = (s.qkv[layer, rows, n * wide + cols.start : n * wide + cols.stop] for n in range(3))
            out = None
            for side, lanes in enumerate(halves):
                scores = dot_nt(k * lanes, q)
                scores = jnp.where(keep > 0, scores * HD ** (-0.5), NEG_FILL)
                exponent = jnp.exp(scores - jnp.max(scores, 0, keepdims=True))
                probs = (exponent * (1.0 / jnp.sum(exponent, 0, keepdims=True))).astype(BF16)
                s.probs[layer, image * HEADS + 2 * pair + side] = probs
                part = dot_tn(probs, v * lanes)
                out = part if out is None else out + part
            s.att[layer, rows, cols] = out.astype(BF16)

    loop(dm.images, attend)


def forward_out(dm, layer, s):
    bias = vector_row(dm, layer, s, 4)

    def out_project(image):
        rows = image_rows(dm, image)
        s.mid[rows, :] = s.hid[rows, :] + (dot_nn(s.att[layer, rows, :], s.w_out[layer]) + bias)

    loop(dm.images, out_project)


def forward_norm_b(dm, layer, s):
    gain, shift = vector_row(dm, layer, s, 5), vector_row(dm, layer, s, 6)
    norm_forward(dm, layer, s.mid, gain, shift, s.low_b, s.hat_b, s.devs, 1)


def forward_up(dm, layer, s):
    tile = 256

    def up(image):
        rows = image_rows(dm, image)
        source = s.low_b[layer, rows, :]
        for number in range(FF // tile):
            cols = slice(number * tile, (number + 1) * tile)
            u = dot_nt(source, s.w_up[layer, cols, :]) + s.vec[layer, 1:2, cols]
            act, slope = gelu_pair(u)
            s.act[layer, rows, cols] = act.astype(BF16)
            s.slope[layer, rows, cols] = slope.astype(BF16)

    loop(dm.images, up)


def forward_down(dm, layer, s):
    bias = vector_row(dm, layer, s, 7)

    def down(image):
        rows = image_rows(dm, image)
        s.hid[rows, :] = s.mid[rows, :] + (dot_nn(s.act[layer, rows, :], s.w_down[layer]) + bias)

    loop(dm.images, down)


FORWARD = (
    ("norm", forward_norm_a),
    ("project", forward_project),
    ("attend", forward_attend),
    ("out", forward_out),
    ("mid", forward_norm_b),
    ("up", forward_up),
    ("down", forward_down),
)


def low_and_sum(dm, source, target):
    def chunk(i, carry):
        rows = pl.ds(pl.multiple_of(i * NORM_ROWS, NORM_ROWS), NORM_ROWS)
        low = source[rows, :].astype(BF16)
        target[rows, :] = low
        return carry + fold_rows(low.astype(F32))

    total = lax.fori_loop(0, dm.tokens // NORM_ROWS, chunk, jnp.zeros((8, dm.width), F32), unroll=True)
    return jnp.sum(total, 0, keepdims=True)


def column_sums(dm, read, cols):
    def chunk(i, carry):
        rows = pl.ds(pl.multiple_of(i * NORM_ROWS, NORM_ROWS), NORM_ROWS)
        return carry + fold_rows(read(rows).astype(F32))

    total = lax.fori_loop(0, dm.tokens // NORM_ROWS, chunk, jnp.zeros((8, cols), F32), unroll=True)
    return jnp.sum(total, 0, keepdims=True)


def backward_start(dm, layer, s):
    s.vec_grad[layer, 7:8, : dm.width] = low_and_sum(dm, s.hid, s.low_g)


def backward_units(dm, layer, s):
    tile, some = 2 * dm.unit_blocks, dm.unit_blocks
    per_half = dm.half_units // tile

    def unit_tile(number):
        cols = pl.ds(pl.multiple_of(number * tile, tile), tile)
        grad = dot_nt(s.low_g[...], s.w_down[layer, cols, :])
        grad = (grad * s.slope[layer, :, cols].astype(F32)).astype(BF16)
        s.slope[layer, :, cols] = grad
        half, first = number // per_half, (number % per_half) * 2
        down = dot_tn(s.act[layer, :, cols], s.low_g[...]).astype(BF16)
        up = dot_tn(grad, s.low_b[layer]).astype(BF16)
        for n in range(2):
            g, odd = (first + n) // dm.group_js, (first + n) % dm.group_js
            for value, start in ((up, dm.first_unit), (down, dm.first_unit + some)):
                s.grads[half, g, odd, start : start + some, :] = value[n * some : (n + 1) * some]

    loop(FF // tile, unit_tile)


def backward_up_sums(dm, layer, s):
    s.vec_grad[layer, 1:2, :] = column_sums(dm, lambda rows: s.slope[layer, rows, :], FF)


def backward_down(dm, layer, s):
    def down(image):
        rows = image_rows(dm, image)
        s.mid[rows, :] = dot_nn(s.slope[layer, rows, :], s.w_up[layer])

    loop(dm.images, down)


def backward_norm_b(dm, layer, s):
    width = dm.width
    gain = vector_row(dm, layer, s, 5)
    gains, shifts = norm_backward(dm, layer, s.mid, s.hid, gain, s.hat_b, s.devs, 1)
    s.vec_grad[layer, 5:6, :width] = gains
    s.vec_grad[layer, 6:7, :width] = shifts
    s.vec_grad[layer, 4:5, :width] = low_and_sum(dm, s.hid, s.low_g)


def backward_out(dm, layer, s):
    put_grads(dm, s, 3, dot_tn(s.att[layer], s.low_g[...]).astype(BF16))

    def out_project(image):
        rows = image_rows(dm, image)
        s.att[layer, rows, :] = dot_nt(s.low_g[rows, :], s.w_out[layer]).astype(BF16)

    loop(dm.images, out_project)


def backward_attend(dm, layer, s, part):
    wide = HEADS * HD
    half = dm.images // 2

    halves = lane_halves()

    def attend(image):
        rows = image_rows(dm, image)
        keep = s.columns[rows, 0:1] * HD ** (-0.5)
        for pair in range(HEADS // 2):
            cols = slice(pair * 2 * HD, (pair + 1) * 2 * HD)
            q, k, v = (s.qkv[layer, rows, n * wide + cols.start : n * wide + cols.stop] for n in range(3))
            out = s.att[layer, rows, cols]
            parts = None
            for side, lanes in enumerate(halves):
                probs = s.probs[layer, image * HEADS + 2 * pair + side]
                grad = dot_nt(v * lanes, out)
                wide_probs = probs.astype(F32)
                total = jnp.sum(wide_probs * grad, 0, keepdims=True)
                raw = (wide_probs * (grad - total) * keep).astype(BF16)
                found = dot_tn(raw, k * lanes), dot_nn(raw, q * lanes), dot_nn(probs, out * lanes)
                parts = found if parts is None else [p + f for p, f in zip(parts, found)]
            for n, part in enumerate(parts):
                s.qkv[layer, rows, n * wide + cols.start : n * wide + cols.stop] = part.astype(BF16)

    loop(half, lambda i: attend(part * half + i))


def backward_rows(dm, layer, s):
    wide = HEADS * HD
    for kind in range(3):
        value = dot_tn(s.qkv[layer, :, kind * wide : (kind + 1) * wide], s.low_a[layer])
        put_grads(dm, s, kind, value.astype(BF16))


def backward_sums(dm, layer, s):
    wide = 3 * HEADS * HD
    s.vec_grad[layer, 0:1, :wide] = column_sums(dm, lambda rows: s.qkv[layer, rows, :], wide)


def backward_project(dm, layer, s):
    def project(image):
        rows = image_rows(dm, image)
        s.mid[rows, :] = dot_nn(s.qkv[layer, rows, :], s.w_qkv[layer])

    loop(dm.images, project)


def backward_norm_a(dm, layer, s):
    width = dm.width
    gain = vector_row(dm, layer, s, 2)
    gains, shifts = norm_backward(dm, layer, s.mid, s.hid, gain, s.hat_a, s.devs, 0)
    s.vec_grad[layer, 2:3, :width] = gains
    s.vec_grad[layer, 3:4, :width] = shifts


BACKWARD = (
    ("start", backward_start),
    ("units", backward_units),
    ("sums", backward_up_sums),
    ("down", backward_down),
    ("mid", backward_norm_b),
    ("out", backward_out),
    ("attend", functools.partial(backward_attend, part=0)),
    ("attended", functools.partial(backward_attend, part=1)),
    ("rows", backward_rows),
    ("more", backward_sums),
    ("project", backward_project),
    ("end", backward_norm_a),
)


class Net:
    def __init__(self, dm, s):
        self.dm, self.s, self.keys = dm, s, {}
        self.rank, self.core = lax.axis_index("dp"), lax.axis_index("mp")
        _, rows, cols = dm.axes
        self.place = (self.rank // (rows * cols), (self.rank // cols) % rows, self.rank % cols)

    def device(self, *offsets):
        z, y, x = ((here + o) % size for here, o, size in zip(self.place, offsets, self.dm.axes))
        return ((z * self.dm.axes[1] + y) * self.dm.axes[2] + x, self.core)

    def sibling(self):
        return (self.rank, 1 - self.core)

    def on_axis(self, axis, offset):
        return self.device(*(offset if axis == k else 0 for k in range(3)))

    def along(self, axis, offset):
        return (self.place[axis] + offset) % self.dm.axes[axis]

    def partners(self):
        depth = self.dm.axes[0]
        found = [self.sibling()]
        found += [self.device(o, 0, 0) for o in range(1, depth)]
        return found + [self.device(0, *o) for o in self.plane()]

    def plane(self):
        _, rows, cols = self.dm.axes
        return [(p, q) for p in range(rows) for q in range(cols) if p or q]

    def greet(self, semaphore):
        for partner in self.partners():
            pl.semaphore_signal(semaphore, inc=1, device_id=partner, device_id_type=MESH)

    def met(self, semaphore):
        pl.semaphore_wait(semaphore, len(self.partners()))

    def copy(self, key, layer, source, target, device):
        name, count, index = key
        if name not in self.keys:
            used = sum(n for _, n in self.keys.values()) * self.dm.layers
            self.keys[name] = (used, count)
        first, known = self.keys[name]
        assert known == count
        number = first + layer * count + index
        return pltpu.make_async_remote_copy(
            src_ref=source,
            dst_ref=target,
            send_sem=self.s.send_sems.at[number],
            recv_sem=self.s.recv_sems.at[number],
            device_id=device,
            device_id_type=MESH,
        )


def copies_needed(dm):
    depth, rows, cols = dm.axes
    cross = depth * (cols + rows - 2)
    vectors = 1 + (depth - 1) + (rows * cols - 1)
    ends = depth - 1 + rows * cols - 1
    return dm.layers * (depth - 1 + 2 * cross + ends + 6 + 2 + vectors + 1 + 2 * dm.images)


def start_all(copies):
    for copy in copies:
        copy.start()


def wait_all(copies):
    for copy in copies:
        copy.wait()


class Parts:
    def __init__(self, dm, net, s, layer):
        self.dm, self.net, self.s, self.layer, self.buf = dm, net, s, layer, s.gath.at[layer]
        self.most = pl.ds(0, dm.most_rows)
        self.head = pl.ds(0, dm.first_rows)
        self.tail = pl.ds(dm.first_rows, dm.most_rows - dm.first_rows)
        self.last = pl.ds(dm.most_rows, dm.last_rows)

    def pairs(self, name, layer, piece, parts):
        copies = []
        _, rows, cols = self.dm.axes
        count = rows + cols - 2
        for axis, make in parts:
            for o in range(1, self.dm.axes[axis]):
                key = (name, self.dm.axes[0] * count, piece * count + len(copies))
                source, target = make(self.net.along(axis, o), o - 1)
                copies.append(
                    self.net.copy(key, layer, source, target, self.net.on_axis(axis, o))
                )
        return copies

    def plane(self, layer, make):
        offsets = self.net.plane()
        copies = []
        for n, (p, q) in enumerate(offsets):
            source, target = make(self.net.along(1, p), self.net.along(2, q), n)
            copies.append(
                self.net.copy(
                    ("ends", len(offsets), n), layer, source, target, self.net.device(0, p, q)
                )
            )
        return copies


class Gather(Parts):
    def __init__(self, dm, net, s, layer):
        super().__init__(dm, net, s, layer)
        depth = dm.axes[0]
        self.order = sorted(range(1, depth), key=lambda o: min(o, depth - o))

    def one(self, offset):
        ref = self.buf.at[(*self.net.place, self.most)]
        key = ("one", self.dm.axes[0] - 1, offset - 1)
        return [self.net.copy(key, self.layer, ref, ref, self.net.on_axis(0, offset))]

    def two(self, piece):
        at, (_, y, x) = self.net.along(0, -piece), self.net.place
        a, b = self.buf.at[at, y, x, self.head], self.buf.at[at, y, x, self.tail]
        return self.pairs(
            "two", self.layer, piece, [(2, lambda to, n: (a, a)), (1, lambda to, n: (b, b))]
        )

    def three(self, piece):
        at, (_, y, x) = self.net.along(0, -piece), self.net.place
        a, b = self.buf.at[at, y, :, self.head], self.buf.at[at, :, x, self.tail]
        return self.pairs(
            "three", self.layer, piece, [(1, lambda to, n: (a, a)), (2, lambda to, n: (b, b))]
        )

    def near(self):
        if not self.dm.last_rows:
            return []
        ref = self.buf.at[(*self.net.place, self.last)]
        return self.plane(self.layer, lambda y, x, n: (ref, ref))

    def far(self):
        if not self.dm.last_rows:
            return []
        ref = self.buf.at[self.net.place[0], :, :, self.last]
        size = self.dm.axes[0]
        return [
            self.net.copy(("far", size - 1, o - 1), self.layer, ref, ref, self.net.on_axis(0, o))
            for o in range(1, size)
        ]

    def begin(self):
        for offset in range(1, self.dm.axes[0]):
            start_all(self.one(offset))
        start_all(self.two(0))
        start_all(self.near())

    def steps(self):
        found = []
        before = 0
        for number, piece in enumerate(self.order + [None]):

            def step(before=before, piece=piece, number=number):
                if piece is not None:
                    wait_all(self.one(piece))
                    start_all(self.two(piece))
                wait_all(self.two(before))
                start_all(self.three(before))
                if number == 0:
                    wait_all(self.near())
                    start_all(self.far())

            found.append(step)
            before = piece
        return found

    def end(self):
        for piece in range(self.dm.axes[0]):
            wait_all(self.three(piece))
        wait_all(self.far())


class Scatter(Parts):
    def one(self, piece):
        at, s, buf = self.net.along(0, piece), self.s, self.buf
        return self.pairs(
            "three",
            0,
            piece,
            [
                (1, lambda to, n: (buf.at[at, to, :, self.head], s.one_a.at[piece, n])),
                (2, lambda to, n: (buf.at[at, :, to, self.tail], s.one_b.at[piece, n])),
            ],
        )

    def two(self, piece):
        at, s, buf, (_, y, x) = self.net.along(0, piece), self.s, self.buf, self.net.place
        return self.pairs(
            "two",
            0,
            piece,
            [
                (2, lambda to, n: (buf.at[at, y, to, self.head], s.two_a.at[piece, n])),
                (1, lambda to, n: (buf.at[at, to, x, self.tail], s.two_b.at[piece, n])),
            ],
        )

    def three(self, piece):
        _, y, x = self.net.place
        source = self.buf.at[self.net.along(0, piece), y, x, self.most]
        target = self.s.three.at[self.layer, piece - 1]
        key = ("one", self.dm.axes[0] - 1, piece - 1)
        turn = self.dm.layers - 1 - self.layer
        return self.net.copy(key, turn, source, target, self.net.device(piece, 0, 0))

    def far(self, piece):
        source = self.buf.at[self.net.along(0, piece), :, :, self.last]
        key = ("far", self.dm.axes[0] - 1, piece - 1)
        return self.net.copy(key, 0, source, self.s.far.at[piece - 1], self.net.device(piece, 0, 0))

    def near(self):
        z = self.net.place[0]
        return self.plane(0, lambda y, x, n: (self.buf.at[z, y, x, self.last], self.s.near.at[n]))

    def add(self, at, parts):
        value = self.buf[at].astype(F32)
        for part in parts:
            value = value + part.astype(F32)
        self.buf[at] = value.astype(BF16)

    def begin(self, piece):
        if self.dm.last_rows:

            @pl.when(piece > 0)
            def _():
                self.far(piece).start()

        start_all(self.one(piece))

    def second(self, piece):
        _, rows, cols = self.dm.axes
        at, s, (_, y, x) = self.net.along(0, piece), self.s, self.net.place
        wait_all(self.one(piece))
        self.add((at, y, slice(None), self.head), [s.one_a[piece, o] for o in range(rows - 1)])
        self.add((at, slice(None), x, self.tail), [s.one_b[piece, o] for o in range(cols - 1)])
        start_all(self.two(piece))

    def third(self, piece):
        _, rows, cols = self.dm.axes
        at, s, (_, y, x) = self.net.along(0, piece), self.s, self.net.place
        wait_all(self.two(piece))
        self.add((at, y, x, self.head), [s.two_a[piece, o] for o in range(cols - 1)])
        self.add((at, y, x, self.tail), [s.two_b[piece, o] for o in range(rows - 1)])

        @pl.when(piece > 0)
        def _():
            self.three(piece).start()

    def second_last(self):
        if self.dm.last_rows:
            pieces = range(1, self.dm.axes[0])
            wait_all([self.far(piece) for piece in pieces])
            z = self.net.place[0]
            at = (z, slice(None), slice(None), self.last)
            self.add(at, [self.s.far[piece - 1] for piece in pieces])
            start_all(self.near())

    def third_last(self):
        if self.dm.last_rows:
            copies = self.near()
            wait_all(copies)
            self.add((*self.net.place, self.last), [self.s.near[n] for n in range(len(copies))])

    def end(self):
        value = self.buf[(*self.net.place, self.most)].astype(F32)
        for piece in range(1, self.dm.axes[0]):
            self.three(piece).wait()
            value = value + self.s.three[self.layer, piece - 1].astype(F32)
        self.s.rows[self.most, :] = value
        if self.dm.last_rows:
            self.s.rows[self.last, :] = self.buf[(*self.net.place, self.last)].astype(F32)


class Totals:
    def __init__(self, dm, net, s, layer, first):
        self.dm, self.net, self.s, self.layer, self.first = dm, net, s, layer, first

    def across(self):
        s, layer = self.s, self.layer
        copy = self.net.copy(
            ("cores", 1, 0), layer, s.vec_grad.at[layer], s.vec_back.at[layer], self.net.sibling()
        )
        return [copy]

    def plane(self):
        _, y, x = self.net.place
        here = self.s.vec_p.at[self.layer, y * self.dm.axes[2] + x]
        offsets = self.net.plane()
        return [
            self.net.copy(("plane", len(offsets), n), self.layer, here, here, self.net.device(0, *o))
            for n, o in enumerate(offsets)
        ]

    def depth(self):
        here = self.s.vec_z.at[self.layer, self.net.place[0]]
        size = self.dm.axes[0]
        return [
            self.net.copy(("depth", size - 1, o - 1), self.layer, here, here, self.net.on_axis(0, o))
            for o in range(1, size)
        ]

    def begin(self):
        start_all(self.across())

    def second(self):
        s, layer, (_, y, x) = self.s, self.layer, self.net.place
        wait_all(self.across())
        value = unpack_vectors(self.dm, s.vec_grad[layer] + s.vec_back[layer], self.first)
        s.vec_p[layer, y * self.dm.axes[2] + x] = value
        start_all(self.plane())

    def third(self):
        s, layer = self.s, self.layer
        wait_all(self.plane())
        value = s.vec_p[layer, 0]
        for o in range(1, self.dm.axes[1] * self.dm.axes[2]):
            value = value + s.vec_p[layer, o]
        s.vec_z[layer, self.net.place[0]] = value
        start_all(self.depth())

    def end(self):
        wait_all(self.depth())
        value = self.s.vec_z[self.layer, 0]
        for o in range(1, self.dm.axes[0]):
            value = value + self.s.vec_z[self.layer, o]
        return value


class Refs:
    pass


def scratch_shapes(dm):
    layers, tokens, width, wide = dm.layers, dm.tokens, dm.width, HEADS * HD
    depth, rows, cols = dm.axes
    head, tail = dm.first_rows, dm.most_rows - dm.first_rows
    vmem, copies = pltpu.VMEM, copies_needed(dm)
    return dict(
        hid=vmem((tokens, width), F32),
        mid=vmem((tokens, width), F32),
        columns=vmem((tokens, 8), F32),
        devs=vmem((layers, tokens, 8), F32),
        low_a=vmem((layers, tokens, width), BF16),
        low_b=vmem((layers, tokens, width), BF16),
        low_g=vmem((tokens, width), BF16),
        hat_a=vmem((layers, tokens, width), F32),
        hat_b=vmem((layers, tokens, width), F32),
        qkv=vmem((layers, tokens, 3 * wide), BF16),
        probs=vmem((layers, dm.images * HEADS, dm.pad_seq, dm.pad_seq), BF16),
        att=vmem((layers, tokens, wide), BF16),
        act=vmem((layers, tokens, FF), BF16),
        slope=vmem((layers, tokens, FF), BF16),
        w_qkv=vmem((layers, 3 * wide, width), BF16),
        w_out=vmem((layers, wide, width), BF16),
        w_up=vmem((layers, FF, width), BF16),
        w_down=vmem((layers, FF, width), BF16),
        grads=vmem((dm.halves, dm.groups, dm.group_js, dm.blocks, width), BF16),
        grads_in=vmem((dm.groups, dm.group_js, dm.blocks, width), BF16),
        gath=vmem((layers, depth, rows, cols, dm.shard_rows, width), BF16),
        one_a=vmem((depth, rows - 1, cols, head, width), BF16),
        one_b=vmem((depth, cols - 1, rows, tail, width), BF16),
        two_a=vmem((depth, cols - 1, head, width), BF16),
        two_b=vmem((depth, rows - 1, tail, width), BF16),
        three=vmem((layers, depth - 1, dm.most_rows, width), BF16),
        far=vmem((depth - 1, rows, cols, max(16, dm.last_rows), width), BF16),
        near=vmem((rows * cols - 1, max(16, dm.last_rows), width), BF16),
        rows=vmem((dm.shard_rows, width), F32),
        tok_in=vmem((dm.images, dm.seq, width), F32),
        tok_out=vmem((dm.images, dm.seq, width), F32),
        codes=vmem((layers, depth, 8, dm.keys // depth), F32),
        vec_own=vmem((layers, 8, FF), F32),
        vec=vmem((layers, 8, FF), F32),
        vec_grad=vmem((layers, 8, FF), F32),
        vec_in=vmem((layers, 8, FF), F32),
        vec_back=vmem((layers, 8, FF), F32),
        vec_z=vmem((layers, depth, 8, width), F32),
        vec_p=vmem((layers, rows * cols, 8, width), F32),
        vec_sum=vmem((layers, 8, width), F32),
        keep_row=vmem((8, -(-dm.pad_seq // 128) * 128), F32),
        send_sems=pltpu.SemaphoreType.DMA((copies,)),
        recv_sems=pltpu.SemaphoreType.DMA((copies,)),
        load_sems=pltpu.SemaphoreType.DMA((dm.images,)),
        store_sems=pltpu.SemaphoreType.DMA((dm.images,)),
        credit=pltpu.SemaphoreType.REGULAR,
        core_credit=pltpu.SemaphoreType.REGULAR,
    )


def load_tokens(dm, source, target, scale=None):
    tail = dm.pad_seq - 16
    for image in range(dm.images):
        start = image * dm.pad_seq
        target[start + tail : start + dm.pad_seq, :] = jnp.zeros((16, dm.width), F32)
        value = source[image]
        if scale is not None:
            value = value * scale[start : start + dm.seq, 0:1]
        target[start : start + dm.seq, :] = value


class Tokens:
    def __init__(self, dm, net, s):
        self.dm, self.net, self.s = dm, net, s

    def image(self, ref, number):
        return ref.at[:, self.net.core * self.dm.images + number]

    def load(self, ref):
        sems = self.s.load_sems
        return [
            pltpu.make_async_copy(self.image(ref, i), self.s.tok_in.at[i], sems.at[i])
            for i in range(self.dm.images)
        ]

    def store(self, ref, turn):
        copies = []
        for i in range(self.dm.images):
            source, target = self.s.tok_out.at[i], self.image(ref, i)
            copies.append(pltpu.make_async_copy(source, target, self.s.store_sems.at[i]))
            key = ("tokens", self.dm.images, i)
            copies.append(self.net.copy(key, turn, source, target, self.net.sibling()))
        return copies


def prepare_keep(dm, keep_mask, first, s):
    kept = keep_mask[...].astype(F32)
    kept = jnp.where(first, kept[: dm.images], kept[dm.images :])
    s.keep_row[...] = jnp.zeros(s.keep_row.shape, F32)
    s.keep_row[: dm.images, : dm.seq] = kept
    columns = jnp.transpose(s.keep_row[...])
    for image in range(dm.images):
        rows = slice(image * dm.pad_seq, (image + 1) * dm.pad_seq)
        s.columns[rows, 0:1] = columns[: dm.pad_seq, image : image + 1]


def own_shard(dm, master, net, s):
    z, y, x = net.place
    if dm.shard_rows > dm.block_rows * dm.slots:
        s.rows[...] = jnp.zeros(s.rows.shape, F32)
    for layer in range(dm.layers):
        for j in range(dm.block_rows):
            s.rows[j * dm.slots : (j + 1) * dm.slots, :] = master[0, layer, j]
        s.gath[layer, z, y, x] = s.rows[...].astype(BF16)


def step_kernel(dm, names, hidden, keep_mask, cotangent, slot_block, master, vectors, acts, grad_in, matrix, vec_out, *scratch):
    s = Refs()
    for name, ref in zip(names, scratch):
        setattr(s, name, ref)
    net = Net(dm, s)
    first = net.core == 0
    tokens = Tokens(dm, net, s)
    cols, units, depth = dm.half_cols, dm.half_units, dm.axes[0]
    assert dm.layers == 2
    gathers = [Gather(dm, net, s, layer) for layer in range(dm.layers)]
    barrier = pltpu.get_barrier_semaphore()
    net.greet(barrier)
    start_all(tokens.load(hidden))
    own_shard(dm, master, net, s)
    net.met(barrier)
    gathers[0].begin()
    pack_vectors(dm, vectors, first, s)
    other_vec = net.copy(("vectors", 1, 0), 0, s.vec_own, s.vec_in, net.sibling())
    other_vec.start()
    prepare_codes(dm, slot_block, s)
    prepare_keep(dm, keep_mask, first, s)
    wait_all(tokens.load(hidden))
    load_tokens(dm, s.tok_in, s.hid)
    start_all(tokens.load(cotangent))
    other_vec.wait()
    s.vec[...] = s.vec_own[...] + s.vec_in[...]
    for step in gathers[0].steps():
        step()
    gathers[1].begin()
    steps = gathers[1].steps()

    def weights(layer):
        parts = [(s.w_qkv, kind * HEADS * HD + net.core * cols, cols) for kind in range(3)]
        parts += [(s.w_out, net.core * cols, cols), (s.w_up, net.core * units, units)]
        parts.append((s.w_down, net.core * units, units))
        copies = []
        for ref, start, count in parts:
            rows = ref.at[layer, pl.ds(pl.multiple_of(start, 16), count)]
            key = ("weights", len(parts), len(copies))
            copies.append(net.copy(key, layer, rows, rows, net.sibling()))
        return copies

    def forward(layer):
        shares = weights(layer)
        for name, phase in FORWARD:
            phase(dm, layer, s)
            if name == "norm":
                Gather(dm, net, s, layer).end()
                parts = permute_in(dm, layer, net.core, s)
                next(parts)
                start_all(shares[:4])
                next(parts, None)
                start_all(shares[4:])
                wait_all(shares[:3])
            if name == "attend":
                shares[3].wait()
            if name == "mid":
                shares[4].wait()
            if name == "up":
                shares[5].wait()
            if name in ("norm", "project", "attend", "mid"):
                now = [steps.pop(0)]
                if name == "mid":
                    now, steps[:] = now + steps, []

                @pl.when(layer + 1 < dm.layers)
                def _(now=now):
                    for step in now:
                        step()

    lax.fori_loop(0, dm.layers, lambda i, c: (forward(i), c)[1], 0)
    for image in range(dm.images):
        rows = slice(image * dm.pad_seq, image * dm.pad_seq + dm.seq)
        s.tok_out[image] = s.hid[rows, :] * s.columns[rows, 0:1]
    start_all(tokens.store(acts, 0))
    wait_all(tokens.load(cotangent))
    load_tokens(dm, s.tok_in, s.hid, s.columns)

    def put_rows(layer):
        Scatter(dm, net, s, layer).end()
        for j in range(dm.block_rows):
            matrix[0, layer, j] = s.rows[j * dm.slots : (j + 1) * dm.slots, :]

    def put_vectors(layer):
        value = Totals(dm, net, s, layer, first).end()
        for r in range(vec_out.shape[1]):
            vec_out[0, r, layer : layer + 1, :] = value[r : r + 1]

    def share(layer, number):
        start = dm.first_unit
        rows = (pl.ds(start, dm.blocks - start), pl.ds(0, start))[number]
        source, target = s.grads.at[1 - net.core, :, :, rows], s.grads_in.at[:, :, rows]
        return net.copy(("shares", 2, number), layer, source, target, net.sibling())

    def backward(turn):
        layer = dm.layers - 1 - turn
        later = turn > 0
        before = Scatter(dm, net, s, 1)
        totals_before = Totals(dm, net, s, 1, first)

        def when_later(body, *args):
            pl.when(later)(lambda: body(*args))

        order = list(range(depth - 1, -1, -1))
        for name, phase in BACKWARD:
            phase(dm, layer, s)
            if name == "start":
                when_later(totals_before.second)
            if name == "units":
                when_later(pl.semaphore_wait, s.core_credit, 1)
                share(layer, 0).start()
            if name in ("units", "mid", "attend"):
                count = depth // 2 if name == "units" else depth // 4
                now, order = order[:count], order[count:]
                for piece in now:
                    when_later(before.second, piece)
            if name == "down":
                when_later(before.second_last)
            if name == "attended":
                when_later(before.third_last)
                for piece in range(depth - 1, -1, -1):
                    when_later(before.third, piece)
                when_later(net.greet, s.credit)
                when_later(totals_before.third)
            if name == "rows":
                share(layer, 1).start()
            if name == "project":
                wait_all([share(layer, 0), share(layer, 1)])
                fill = permute_out(dm, layer, net.core, s)
                when_later(net.met, s.credit)
                scatter = Scatter(dm, net, s, layer)

                def pieces_out(number, carry):
                    pieces = [depth - 1 - 2 * number, depth - 2 - 2 * number]
                    fill([net.along(0, piece) for piece in pieces])
                    for piece in pieces:
                        scatter.begin(piece)
                    return carry

                lax.fori_loop(0, depth // 2, pieces_out, 0)

                @pl.when(layer > 0)
                def _():
                    pl.semaphore_signal(
                        s.core_credit, inc=1, device_id=net.sibling(), device_id_type=MESH
                    )
        Totals(dm, net, s, layer, first).begin()

    lax.fori_loop(0, dm.layers, lambda i, c: (backward(i), c)[1], 0)
    wait_all(tokens.store(acts, 0))
    for image in range(dm.images):
        rows = slice(image * dm.pad_seq, image * dm.pad_seq + dm.seq)
        s.tok_out[image] = s.hid[rows, :]
    start_all(tokens.store(grad_in, 1))
    scatter, totals = Scatter(dm, net, s, 0), Totals(dm, net, s, 0, first)
    totals.second()
    loop(depth, lambda n: scatter.second(depth - 1 - n))
    scatter.second_last()
    put_vectors(1)
    put_rows(1)
    totals.third()
    loop(depth, lambda n: scatter.third(depth - 1 - n))
    scatter.third_last()
    put_vectors(0)
    put_rows(0)
    wait_all(tokens.store(grad_in, 1))


def run_step(dm, hidden_in, keep_mask, cotangent, slot_block, master, vector_master):
    shapes = scratch_shapes(dm)
    out_shape = (
        jax.ShapeDtypeStruct(hidden_in.shape, F32),
        jax.ShapeDtypeStruct(hidden_in.shape, F32),
        jax.ShapeDtypeStruct(master.shape, F32),
        jax.ShapeDtypeStruct(vector_master.shape, F32),
    )
    full, far = pl.BlockSpec(memory_space=pltpu.VMEM), pl.BlockSpec(memory_space=pl.ANY)
    return pl.pallas_call(
        functools.partial(step_kernel, dm, tuple(shapes)),
        out_shape=out_shape,
        in_specs=[far, full, far, full, full, full],
        out_specs=[far, far, full, full],
        scratch_shapes=list(shapes.values()),
        compiler_params=pltpu.CompilerParams(
            vmem_limit_bytes=63 * 2**20, collective_id=0, has_side_effects=True
        ),
    )(hidden_in, keep_mask, cotangent, slot_block, master, vector_master)


def adam_step(weight, grad_sum, first_old, second_old, rate, decay):
    first_new = BETA_ONE * first_old + (1.0 - BETA_ONE) * grad_sum
    second_new = BETA_TWO * second_old + (1.0 - BETA_TWO) * grad_sum * grad_sum
    first_hat = first_new / (1.0 - BETA_ONE**STEP)
    second_hat = second_new / (1.0 - BETA_TWO**STEP)
    return (
        second_new,
        weight - rate * (first_hat / (jnp.sqrt(second_hat) + EPS_ADAM) + decay * weight),
    )


def finish_kernel(parts, *refs):
    large, matrix, vector = refs[:2], refs[2:6], refs[6:10]
    large_out, matrix_out, vector_out = refs[10:12], refs[12:15], refs[15:18]
    stage, matrix_in, vector_in, matrix_done, vector_done, stage_sems, load_sems, store_sems = refs[18:]
    loads, stores = [], []
    rows_all = stage.shape[1]
    size = -(-rows_all // parts)
    for start in range(0, rows_all, size):
        for number, (source, target) in enumerate(zip(large, large_out)):
            rows = pl.ds(start, min(size, rows_all - start))
            held, sem = stage.at[number, rows], stage_sems.at[len(loads)]
            loads.append(pltpu.make_async_copy(source.at[rows], held, sem))
            stores.append(pltpu.make_async_copy(held, target.at[rows], sem))
    matrix_loads = [
        pltpu.make_async_copy(ref, matrix_in.at[n], load_sems.at[n]) for n, ref in enumerate(matrix)
    ]
    vector_loads = [
        pltpu.make_async_copy(ref, vector_in.at[n], load_sems.at[4 + n]) for n, ref in enumerate(vector)
    ]
    results = [
        pltpu.make_async_copy(matrix_done.at[n], ref, store_sems.at[n])
        for n, ref in enumerate(matrix_out)
    ]
    results += [
        pltpu.make_async_copy(vector_done.at[n], ref, store_sems.at[3 + n])
        for n, ref in enumerate(vector_out)
    ]
    start_all(vector_loads + matrix_loads + loads)
    wait_all(vector_loads + matrix_loads)

    def adam(held, done, at, rate, decay):
        grad, weight, one, two = (held[(n, *at)] for n in range(4))
        done[(0, *at)] = grad
        done[(1, *at)], done[(2, *at)] = adam_step(weight, grad, one, two, rate, decay)

    for layer in range(matrix_in.shape[2]):
        adam(matrix_in, matrix_done, (0, layer), RATE_MATRIX, DECAY_MATRIX)
    adam(vector_in, vector_done, (0,), RATE_VECTOR, 0.0)
    start_all(results)
    for load, store in zip(loads, stores):
        load.wait()
        store.start()
    wait_all(stores + results)


def run_finish(acts, grad_in, matrix, vector):
    parts = 1
    far = pl.BlockSpec(memory_space=pl.ANY)
    shapes = [acts, grad_in] + [matrix[0]] * 3 + [vector[0]] * 3
    return pl.pallas_call(
        functools.partial(finish_kernel, parts),
        out_shape=tuple(jax.ShapeDtypeStruct(a.shape, F32) for a in shapes),
        in_specs=[far] * 10,
        out_specs=[far] * 8,
        scratch_shapes=[
            pltpu.VMEM((2, *acts.shape), F32),
            pltpu.VMEM((4, *matrix[0].shape), F32),
            pltpu.VMEM((4, *vector[0].shape), F32),
            pltpu.VMEM((3, *matrix[0].shape), F32),
            pltpu.VMEM((3, *vector[0].shape), F32),
            pltpu.SemaphoreType.DMA((2 * parts,)),
            pltpu.SemaphoreType.DMA((8,)),
            pltpu.SemaphoreType.DMA((6,)),
        ],
        compiler_params=pltpu.CompilerParams(vmem_limit_bytes=63 * 2**20),
    )(acts, grad_in, *matrix, *vector)


def shards(
    hidden_in, keep_mask, cotangent, slot_block, master, moment_one, moment_two, vector_master, vector_one, vector_two
):
    images, seq, width = hidden_in.shape
    halves, ranks = lax.axis_size("mp"), lax.axis_size("dp")
    dm = Dims(
        master.shape[1], images // halves, seq, width, halves, ranks, slot_block.shape[1], master.shape[3]
    )
    matrix = [array.swapaxes(2, 3) for array in (master, moment_one, moment_two)]
    vector = [array.swapaxes(1, 2) for array in (vector_master, vector_one, vector_two)]
    acts, grad_in, matrix_grad, vector_grad = run_step(
        dm, hidden_in.swapaxes(0, 1), keep_mask, cotangent.swapaxes(0, 1), slot_block, matrix[0], vector[0]
    )
    results = run_finish(acts, grad_in, [matrix_grad] + matrix, [vector_grad] + vector)
    return tuple(
        array.swapaxes(*axes)
        for array, axes in zip(results, [(0, 1)] * 2 + [(2, 3)] * 3 + [(1, 2)] * 3)
    )


def solution(mesh):
    images, rows, copied = P("dp", None, None), P("mp", None, "dp", None, None), P("mp", None, None, None)
    return jax.shard_map(
        shards,
        mesh=mesh,
        in_specs=(images, P("dp", None), images, P(), rows, rows, rows, copied, copied, copied),
        out_specs=(images, images, rows, rows, rows, copied, copied, copied),
        check_vma=False,
    )
```

```python
import functools

import jax
import jax.numpy as jnp
from jax import lax
from jax.experimental import pallas as pl
from jax.experimental.pallas import tpu as pltpu
from jax.sharding import PartitionSpec as P

HEADS = 6
HD = 64
FF = 1536
STEP = 10

EPS_NORM = 1e-06
BETA_ONE = 0.9
BETA_TWO = 0.999
RATE_MATRIX = 0.003
RATE_VECTOR = 0.01
DECAY_MATRIX = 0.05
EPS_ADAM = 1e-08
NEG_FILL = -1e30
LOG2_E = 1.4426950408889634

F32 = jnp.float32
MESH = pl.DeviceIdType.MESH
BF16 = jnp.bfloat16


def dot_nn(left, right):
    return lax.dot_general(left, right, (((1,), (0,)), ((), ())), preferred_element_type=F32)


def dot_nt(left, right):
    return lax.dot_general(left, right, (((1,), (1,)), ((), ())), preferred_element_type=F32)


def dot_tn(left, right):
    return lax.dot_general(left, right, (((0,), (0,)), ((), ())), preferred_element_type=F32)


def fold_rows(values):
    rows, cols = values.shape
    return jnp.sum(values.reshape(rows // 8, 8, cols), 0)


def loop(count, body, unroll=True):
    lax.fori_loop(0, count, lambda i, c: (body(i), c)[1], 0, unroll=unroll)


def gelu_pair(u):
    cdf = 0.5 + 0.5 * lax.erf(u * (0.5**0.5))
    slope = cdf + u * (jnp.exp(-0.5 * u * u) * 0.3989422804014327)
    return u * cdf, slope


class Dims:
    def __init__(self, layers, images, seq, width, halves, ranks, blocks, block_rows):
        self.layers, self.images, self.seq, self.width = layers, images, seq, width
        self.halves, self.ranks, self.blocks, self.block_rows = halves, ranks, blocks, block_rows
        self.pad_seq = -(-seq // 16) * 16
        self.tokens = images * self.pad_seq
        self.slots = blocks // ranks
        side = 1
        while side**3 * 8 <= ranks:
            side *= 2
        self.axes = (ranks // (side * side), side, side)
        self.shard_rows = -(-block_rows * self.slots // 16) * 16
        self.last_rows = 16 * (self.shard_rows // 144)
        self.most_rows = self.shard_rows - self.last_rows
        self.first_rows = -(-self.most_rows // 32) * 16
        self.groups = block_rows // 2 if 2 * self.slots % 16 == 0 else 1
        self.group = self.shard_rows // self.groups
        self.group_js = block_rows // self.groups
        self.keys = ranks * self.group
        self.half_cols = HEADS * HD // halves
        self.half_units = FF // halves
        self.natural = 4 * self.half_cols
        self.unit_blocks = self.half_units // block_rows
        self.kind_blocks = self.half_cols // block_rows
        self.first_unit = 4 * self.kind_blocks


def divide(values, number):
    return jnp.floor((values.astype(F32) + 0.5) * (1.0 / number))


def one_hot(rows, codes, axis):
    start, count = rows
    shape = (count, codes.shape[1]) if axis == 0 else (codes.shape[0], count)
    here = lax.broadcasted_iota(jnp.int32, shape, axis) + start
    return (here == codes.astype(jnp.int32)).astype(F32).astype(BF16)


def permute_in(dm, layer, half, s):
    cols, units, some = dm.half_cols, dm.half_units, dm.unit_blocks
    shards = [
        s.gath[layer, :, :, :, g * dm.group : (g + 1) * dm.group, :].reshape(dm.keys, dm.width)
        for g in range(dm.groups)
    ]
    code = jnp.concatenate([s.codes[layer, z] for z in range(dm.axes[0])], 1)[0:1]
    count = dm.first_unit
    starts = [odd * dm.blocks for odd in range(dm.group_js)]
    chosen = jnp.concatenate([one_hot((start, count), code, 0) for start in starts], 0)
    attention = []
    for g in range(dm.groups):
        rows = dot_nn(chosen, shards[g]).astype(BF16)
        attention += [rows[n * count : (n + 1) * count] for n in range(dm.group_js)]
    order = row_order(dm, cols, dm.kind_blocks)
    for kind in range(4):
        part = slice(kind * dm.kind_blocks, (kind + 1) * dm.kind_blocks)
        rows = dot_nn(order, jnp.concatenate([rows[part] for rows in attention], 0)).astype(BF16)
        if kind < 3:
            s.w_qkv[layer, pl.ds(pl.multiple_of(kind * HEADS * HD + half * cols, 16), cols), :] = rows
        else:
            s.w_out[layer, pl.ds(pl.multiple_of(half * cols, 16), cols), :] = rows
    yield
    for odd, start in enumerate(starts):
        chosen = one_hot((start + count, 2 * some), code, 0)
        for g in range(dm.groups):
            rows = dot_nn(chosen, shards[g]).astype(BF16)
            at = half * units + (g * dm.group_js + odd) * some
            at = pl.ds(pl.multiple_of(at, 16), some)
            s.w_up[layer, at, :] = rows[:some]
            s.w_down[layer, at, :] = rows[some:]


def put_grads(dm, s, kind, rows):
    cols, size = dm.half_cols, dm.kind_blocks
    order = row_order(dm, cols, size)
    for half in range(dm.halves):
        found = dot_tn(order, rows[half * cols : (half + 1) * cols]).astype(BF16)
        for j in range(dm.block_rows):
            s.grads[half, j // dm.group_js, j % dm.group_js, kind * size : (kind + 1) * size, :] = found[
                j * size : (j + 1) * size
            ]


def permute_out(dm, layer, half, s):
    for g in range(dm.groups):
        for odd in range(dm.group_js):
            total = s.grads[half, g, odd].astype(F32) + s.grads_in[g, odd].astype(F32)
            s.grads_in[g, odd] = total.astype(BF16)

    def pieces(places):
        codes = [jnp.transpose(s.codes[layer, z])[:, 0:1] for z in places]
        chosen = one_hot((0, dm.group_js * dm.blocks), jnp.concatenate(codes, 0), 1)
        size = chosen.shape[0] // len(places)
        for g in range(dm.groups):
            grads = s.grads_in[g].reshape(dm.group_js * dm.blocks, dm.width)
            rows = dot_nn(chosen, grads).astype(BF16)
            for n, z in enumerate(places):
                s.gath[layer, z, :, :, g * dm.group : (g + 1) * dm.group, :] = rows[
                    n * size : (n + 1) * size
                ].reshape(dm.axes[1], dm.axes[2], dm.group, dm.width)

    return pieces


def prepare_codes(dm, slot_block, s):
    layers, blocks, group = dm.layers, dm.blocks, dm.group
    block = slot_block[...].astype(F32)
    high = divide(block, 16)
    zero = jnp.zeros((16 - 2 * layers, blocks), F32)
    halves = jnp.concatenate([high, block - 16.0 * high, zero], 0).astype(BF16)
    per = dm.keys // dm.axes[0]
    size = per * max(1, 768 // per)
    for start in range(0, dm.keys, size):
        size = min(size, dm.keys - start)

        def place(shape):
            key = lax.broadcasted_iota(jnp.int32, shape, 1) + start
            rank = divide(key, group)
            inside = key.astype(F32) - rank * group
            odd = divide(inside, dm.slots)
            return rank * dm.slots + inside - odd * dm.slots, odd, inside >= dm.group_js * dm.slots

        slot, _, _ = place((blocks, size))
        same = slot == lax.broadcasted_iota(jnp.int32, (blocks, size), 0).astype(F32)
        parts = dot_nn(halves, same.astype(F32).astype(BF16))
        _, odd, padding = place((1, size))
        for layer in range(layers):
            block = 16.0 * parts[layer : layer + 1] + parts[layers + layer : layers + layer + 1]
            row = jnp.where(padding, -1.0, odd * blocks + block)
            rows = jnp.concatenate([row, jnp.zeros((7, size), F32)], 0)
            for z in range(start // per, (start + size) // per):
                s.codes[layer, z] = rows[:, z * per - start : (z + 1) * per - start]


def row_order(dm, rows, blocks):
    here = lax.broadcasted_iota(jnp.int32, (rows, rows), 1)
    inner = divide(here, blocks)
    source = (here.astype(F32) - inner * blocks) * dm.block_rows + inner
    same = source == lax.broadcasted_iota(jnp.int32, (rows, rows), 0).astype(F32)
    return same.astype(F32).astype(BF16)


def unit_order(dm):
    return row_order(dm, dm.half_units, dm.unit_blocks)


def reorder(dot, row, order):
    high = row.astype(BF16)
    rest = row - high.astype(F32)
    middle = rest.astype(BF16)
    low = (rest - middle.astype(F32)).astype(BF16)
    parts = [high.astype(F32), middle.astype(F32), low.astype(F32)]
    parts.append(jnp.zeros((13, row.shape[1]), F32))
    out = dot(jnp.concatenate(parts, 0).astype(BF16), order)
    return out[0:1] + (out[1:2] + out[2:3])


def pack_vectors(dm, vectors, first, s):
    cols, units, width = dm.half_cols, dm.half_units, dm.width
    wide = HEADS * HD
    order = unit_order(dm)
    for layer in range(dm.layers):
        rows = jnp.concatenate([vectors[0, r, layer : layer + 1, :] for r in range(6)], 0)
        flat = rows[0:1]
        q, v = flat[:, :cols], flat[:, cols : 2 * cols]
        none, mid = jnp.zeros((1, cols), F32), jnp.zeros((1, wide), F32)
        tail = jnp.zeros((1, FF - 3 * wide), F32)
        zero_half = jnp.concatenate([q, none, mid, v, none, tail], 1)
        one_half = jnp.concatenate([none, q, mid, none, v, tail], 1)
        s.vec_own[layer, 0:1, :] = jnp.where(first, zero_half, one_half)
        up = reorder(dot_nn, jnp.concatenate([rows[1:2], rows[2:3]], 1), order)
        none = jnp.zeros((1, units), F32)
        s.vec_own[layer, 1:2, :] = jnp.where(
            first, jnp.concatenate([up, none], 1), jnp.concatenate([none, up], 1)
        )
        own = jnp.concatenate([rows[3:6], jnp.zeros((3, FF - width), F32)], 1)
        none = jnp.zeros((3, FF), F32)
        s.vec_own[layer, 2:5, :] = jnp.where(first, own, none)
        s.vec_own[layer, 5:8, :] = jnp.where(first, none, own)


def unpack_vectors(dm, packed, first):
    cols, units, width = dm.half_cols, dm.half_units, dm.width
    wide = HEADS * HD
    flat = packed[0:1]
    zero_half = jnp.concatenate([flat[:, :cols], flat[:, 2 * wide : 2 * wide + cols]], 1)
    one_half = jnp.concatenate([flat[:, cols : 2 * cols], flat[:, 2 * wide + cols : 3 * wide]], 1)
    flat = packed[1:2]
    up = reorder(dot_nt, jnp.where(first, flat[:, :units], flat[:, units:]), unit_order(dm))
    own = jnp.where(first, packed[2:5, :width], packed[5:8, :width])
    return jnp.concatenate(
        [
            jnp.where(first, zero_half, one_half),
            up[:, :width],
            up[:, width:],
            own,
            jnp.zeros((2, width), F32),
        ],
        0,
    )


NORM_ROWS = 208


def norm_forward(dm, layer, source, gain, shift, low_out, hat_out, devs, place):
    def chunk(i):
        rows = pl.ds(pl.multiple_of(i * NORM_ROWS, NORM_ROWS), NORM_ROWS)
        values = source[rows, :]
        centred = values - jnp.mean(values, -1, keepdims=True)
        inv = lax.rsqrt(jnp.mean(centred * centred, -1, keepdims=True) + EPS_NORM)
        hat = centred * inv
        hat_out[layer, rows, :] = hat
        devs[layer, rows, place : place + 1] = inv
        low_out[layer, rows, :] = (hat * gain + shift).astype(BF16)

    loop(dm.tokens // NORM_ROWS, chunk)


def norm_backward(dm, layer, grad, into, gain, hat_in, devs, place):
    def chunk(i, carry):
        rows = pl.ds(pl.multiple_of(i * NORM_ROWS, NORM_ROWS), NORM_ROWS)
        out, hat, inv = grad[rows, :], hat_in[layer, rows, :], devs[layer, rows, place : place + 1]
        scaled = out * gain
        first = jnp.mean(scaled, -1, keepdims=True)
        second = jnp.mean(scaled * hat, -1, keepdims=True)
        into[rows, :] = into[rows, :] + inv * (scaled - first - hat * second)
        return carry[0] + fold_rows(out * hat), carry[1] + fold_rows(out)

    zero = jnp.zeros((8, dm.width), F32)
    gains, shifts = lax.fori_loop(0, dm.tokens // NORM_ROWS, chunk, (zero, zero), unroll=True)
    return jnp.sum(gains, 0, keepdims=True), jnp.sum(shifts, 0, keepdims=True)


def lane_halves():
    lane = lax.broadcasted_iota(jnp.int32, (1, 2 * HD), 1)
    return (lane < HD).astype(F32).astype(BF16), (lane >= HD).astype(F32).astype(BF16)


def image_rows(dm, image):
    return pl.ds(pl.multiple_of(image * dm.pad_seq, 16), dm.pad_seq)


def vector_row(dm, layer, s, row, count=None):
    return s.vec[layer, row : row + 1, : count or dm.width]


def forward_norm_a(dm, layer, s):
    gain, shift = vector_row(dm, layer, s, 2), vector_row(dm, layer, s, 3)
    norm_forward(dm, layer, s.hid, gain, shift, s.low_a, s.hat_a, s.devs, 0)


def forward_project(dm, layer, s):
    wide = HEADS * HD

    def project(image):
        rows = image_rows(dm, image)
        source = s.low_a[layer, rows, :]
        for kind in range(3):
            cols = slice(kind * wide, (kind + 1) * wide)
            value = dot_nt(source, s.w_qkv[layer, cols, :]) + s.vec[layer, 0:1, cols]
            s.qkv[layer, rows, cols] = value.astype(BF16)

    loop(dm.images, project)


def forward_attend(dm, layer, s):
    wide = HEADS * HD

    halves = lane_halves()

    def attend(image):
        rows = image_rows(dm, image)
        keep = s.columns[rows, 0:1]
        for pair in range(HEADS // 2):
            cols = slice(pair * 2 * HD, (pair + 1) * 2 * HD)
            q, k, v = (s.qkv[layer, rows, n * wide + cols.start : n * wide + cols.stop] for n in range(3))
            out = None
            for side, lanes in enumerate(halves):
                scores = dot_nt(k * lanes, q)
                scores = jnp.where(keep > 0, scores * (HD ** (-0.5) * LOG2_E), NEG_FILL)
                exponent = jnp.exp2(scores - jnp.max(scores, 0, keepdims=True))
                probs = (exponent * (1.0 / jnp.sum(exponent, 0, keepdims=True))).astype(BF16)
                s.probs[layer, image * HEADS + 2 * pair + side] = probs
                part = dot_tn(probs, v * lanes)
                out = part if out is None else out + part
            s.att[layer, rows, cols] = out.astype(BF16)

    loop(dm.images, attend)


def forward_out(dm, layer, s):
    bias = vector_row(dm, layer, s, 4)

    def out_project(image):
        rows = image_rows(dm, image)
        s.mid[rows, :] = s.hid[rows, :] + (dot_nn(s.att[layer, rows, :], s.w_out[layer]) + bias)

    loop(dm.images, out_project)


def forward_norm_b(dm, layer, s):
    gain, shift = vector_row(dm, layer, s, 5), vector_row(dm, layer, s, 6)
    norm_forward(dm, layer, s.mid, gain, shift, s.low_b, s.hat_b, s.devs, 1)


def forward_up(dm, layer, s):
    tile = 256

    def up(image):
        rows = image_rows(dm, image)
        source = s.low_b[layer, rows, :]
        for number in range(FF // tile):
            cols = slice(number * tile, (number + 1) * tile)
            u = dot_nt(source, s.w_up[layer, cols, :]) + s.vec[layer, 1:2, cols]
            act, slope = gelu_pair(u)
            s.act[layer, rows, cols] = act.astype(BF16)
            s.slope[layer, rows, cols] = slope.astype(BF16)

    loop(dm.images, up)


def forward_down(dm, layer, s):
    bias = vector_row(dm, layer, s, 7)

    def down(image):
        rows = image_rows(dm, image)
        s.hid[rows, :] = s.mid[rows, :] + (dot_nn(s.act[layer, rows, :], s.w_down[layer]) + bias)

    loop(dm.images, down)


FORWARD = (
    ("norm", forward_norm_a),
    ("project", forward_project),
    ("attend", forward_attend),
    ("out", forward_out),
    ("mid", forward_norm_b),
    ("up", forward_up),
    ("down", forward_down),
)


def low_and_sum(dm, source, target):
    def chunk(i, carry):
        rows = pl.ds(pl.multiple_of(i * NORM_ROWS, NORM_ROWS), NORM_ROWS)
        low = source[rows, :].astype(BF16)
        target[rows, :] = low
        return carry + fold_rows(low.astype(F32))

    total = lax.fori_loop(0, dm.tokens // NORM_ROWS, chunk, jnp.zeros((8, dm.width), F32), unroll=True)
    return jnp.sum(total, 0, keepdims=True)


def column_sums(dm, read, cols):
    def chunk(i, carry):
        rows = pl.ds(pl.multiple_of(i * NORM_ROWS, NORM_ROWS), NORM_ROWS)
        return carry + fold_rows(read(rows).astype(F32))

    total = lax.fori_loop(0, dm.tokens // NORM_ROWS, chunk, jnp.zeros((8, cols), F32), unroll=True)
    return jnp.sum(total, 0, keepdims=True)


def backward_start(dm, layer, s):
    s.vec_grad[layer, 7:8, : dm.width] = low_and_sum(dm, s.hid, s.low_g)


def backward_units(dm, layer, s):
    tile, some = 2 * dm.unit_blocks, dm.unit_blocks
    per_half = dm.half_units // tile

    def unit_tile(number):
        cols = pl.ds(pl.multiple_of(number * tile, tile), tile)
        grad = dot_nt(s.low_g[...], s.w_down[layer, cols, :])
        grad = (grad * s.slope[layer, :, cols].astype(F32)).astype(BF16)
        s.slope[layer, :, cols] = grad
        half, first = number // per_half, (number % per_half) * 2
        down = dot_tn(s.act[layer, :, cols], s.low_g[...]).astype(BF16)
        up = dot_tn(grad, s.low_b[layer]).astype(BF16)
        for n in range(2):
            g, odd = (first + n) // dm.group_js, (first + n) % dm.group_js
            for value, start in ((up, dm.first_unit), (down, dm.first_unit + some)):
                s.grads[half, g, odd, start : start + some, :] = value[n * some : (n + 1) * some]

    loop(FF // tile, unit_tile)


def backward_up_sums(dm, layer, s):
    s.vec_grad[layer, 1:2, :] = column_sums(dm, lambda rows: s.slope[layer, rows, :], FF)


def backward_down(dm, layer, s):
    def down(image):
        rows = image_rows(dm, image)
        s.mid[rows, :] = dot_nn(s.slope[layer, rows, :], s.w_up[layer])

    loop(dm.images, down)


def backward_norm_b(dm, layer, s):
    width = dm.width
    gain = vector_row(dm, layer, s, 5)
    gains, shifts = norm_backward(dm, layer, s.mid, s.hid, gain, s.hat_b, s.devs, 1)
    s.vec_grad[layer, 5:6, :width] = gains
    s.vec_grad[layer, 6:7, :width] = shifts
    s.vec_grad[layer, 4:5, :width] = low_and_sum(dm, s.hid, s.low_g)


def backward_out(dm, layer, s):
    put_grads(dm, s, 3, dot_tn(s.att[layer], s.low_g[...]).astype(BF16))

    def out_project(image):
        rows = image_rows(dm, image)
        s.att[layer, rows, :] = dot_nt(s.low_g[rows, :], s.w_out[layer]).astype(BF16)

    loop(dm.images, out_project)


def backward_attend(dm, layer, s, part):
    wide = HEADS * HD
    half = dm.images // 2

    halves = lane_halves()

    def attend(image):
        rows = image_rows(dm, image)
        keep = s.columns[rows, 0:1] * HD ** (-0.5)
        for pair in range(HEADS // 2):
            cols = slice(pair * 2 * HD, (pair + 1) * 2 * HD)
            q, k, v = (s.qkv[layer, rows, n * wide + cols.start : n * wide + cols.stop] for n in range(3))
            out = s.att[layer, rows, cols]
            parts = None
            for side, lanes in enumerate(halves):
                probs = s.probs[layer, image * HEADS + 2 * pair + side]
                grad = dot_nt(v * lanes, out)
                wide_probs = probs.astype(F32)
                total = jnp.sum(wide_probs * grad, 0, keepdims=True)
                raw = (wide_probs * (grad - total) * keep).astype(BF16)
                found = dot_tn(raw, k * lanes), dot_nn(raw, q * lanes), dot_nn(probs, out * lanes)
                parts = found if parts is None else [p + f for p, f in zip(parts, found)]
            for n, part in enumerate(parts):
                s.qkv[layer, rows, n * wide + cols.start : n * wide + cols.stop] = part.astype(BF16)

    loop(half, lambda i: attend(part * half + i))


def backward_rows(dm, layer, s):
    wide = HEADS * HD
    for kind in range(3):
        value = dot_tn(s.qkv[layer, :, kind * wide : (kind + 1) * wide], s.low_a[layer])
        put_grads(dm, s, kind, value.astype(BF16))


def backward_sums(dm, layer, s):
    wide = 3 * HEADS * HD
    s.vec_grad[layer, 0:1, :wide] = column_sums(dm, lambda rows: s.qkv[layer, rows, :], wide)


def backward_project(dm, layer, s):
    def project(image):
        rows = image_rows(dm, image)
        s.mid[rows, :] = dot_nn(s.qkv[layer, rows, :], s.w_qkv[layer])

    loop(dm.images, project)


def backward_norm_a(dm, layer, s):
    width = dm.width
    gain = vector_row(dm, layer, s, 2)
    gains, shifts = norm_backward(dm, layer, s.mid, s.hid, gain, s.hat_a, s.devs, 0)
    s.vec_grad[layer, 2:3, :width] = gains
    s.vec_grad[layer, 3:4, :width] = shifts


BACKWARD = (
    ("start", backward_start),
    ("units", backward_units),
    ("sums", backward_up_sums),
    ("down", backward_down),
    ("mid", backward_norm_b),
    ("out", backward_out),
    ("attend", functools.partial(backward_attend, part=0)),
    ("attended", functools.partial(backward_attend, part=1)),
    ("rows", backward_rows),
    ("more", backward_sums),
    ("project", backward_project),
    ("end", backward_norm_a),
)


class Net:
    def __init__(self, dm, s):
        self.dm, self.s, self.keys = dm, s, {}
        self.rank, self.core = lax.axis_index("dp"), lax.axis_index("mp")
        _, rows, cols = dm.axes
        self.place = (self.rank // (rows * cols), (self.rank // cols) % rows, self.rank % cols)

    def device(self, *offsets):
        z, y, x = ((here + o) % size for here, o, size in zip(self.place, offsets, self.dm.axes))
        return ((z * self.dm.axes[1] + y) * self.dm.axes[2] + x, self.core)

    def sibling(self):
        return (self.rank, 1 - self.core)

    def on_axis(self, axis, offset):
        return self.device(*(offset if axis == k else 0 for k in range(3)))

    def along(self, axis, offset):
        return (self.place[axis] + offset) % self.dm.axes[axis]

    def partners(self):
        depth = self.dm.axes[0]
        found = [self.sibling()]
        found += [self.device(o, 0, 0) for o in range(1, depth)]
        return found + [self.device(0, *o) for o in self.plane()]

    def plane(self):
        _, rows, cols = self.dm.axes
        return [(p, q) for p in range(rows) for q in range(cols) if p or q]

    def greet(self, semaphore):
        for partner in self.partners():
            pl.semaphore_signal(semaphore, inc=1, device_id=partner, device_id_type=MESH)

    def met(self, semaphore):
        pl.semaphore_wait(semaphore, len(self.partners()))

    def copy(self, key, layer, source, target, device):
        name, count, index = key
        if name not in self.keys:
            used = sum(n for _, n in self.keys.values()) * self.dm.layers
            self.keys[name] = (used, count)
        first, known = self.keys[name]
        assert known == count
        number = first + layer * count + index
        return pltpu.make_async_remote_copy(
            src_ref=source,
            dst_ref=target,
            send_sem=self.s.send_sems.at[number],
            recv_sem=self.s.recv_sems.at[number],
            device_id=device,
            device_id_type=MESH,
        )


def copies_needed(dm):
    depth, rows, cols = dm.axes
    cross = depth * (cols + rows - 2)
    vectors = 1 + (depth - 1) + (rows * cols - 1)
    ends = depth - 1 + rows * cols - 1
    return dm.layers * (depth - 1 + 2 * cross + ends + 6 + 2 + vectors + 1 + 2 * dm.images)


def start_all(copies):
    for copy in copies:
        copy.start()


def wait_all(copies):
    for copy in copies:
        copy.wait()


class Parts:
    def __init__(self, dm, net, s, layer):
        self.dm, self.net, self.s, self.layer, self.buf = dm, net, s, layer, s.gath.at[layer]
        self.most = pl.ds(0, dm.most_rows)
        self.head = pl.ds(0, dm.first_rows)
        self.tail = pl.ds(dm.first_rows, dm.most_rows - dm.first_rows)
        self.last = pl.ds(dm.most_rows, dm.last_rows)

    def pairs(self, name, layer, piece, parts):
        copies = []
        _, rows, cols = self.dm.axes
        count = rows + cols - 2
        for axis, make in parts:
            for o in range(1, self.dm.axes[axis]):
                key = (name, self.dm.axes[0] * count, piece * count + len(copies))
                source, target = make(self.net.along(axis, o), o - 1)
                copies.append(
                    self.net.copy(key, layer, source, target, self.net.on_axis(axis, o))
                )
        return copies

    def plane(self, layer, make):
        offsets = self.net.plane()
        copies = []
        for n, (p, q) in enumerate(offsets):
            source, target = make(self.net.along(1, p), self.net.along(2, q), n)
            copies.append(
                self.net.copy(
                    ("ends", len(offsets), n), layer, source, target, self.net.device(0, p, q)
                )
            )
        return copies


class Gather(Parts):
    def one(self, offset):
        ref = self.buf.at[(*self.net.place, self.most)]
        key = ("one", self.dm.axes[0] - 1, offset - 1)
        return [self.net.copy(key, self.layer, ref, ref, self.net.on_axis(0, offset))]

    def two(self, piece):
        at, (_, y, x) = self.net.along(0, -piece), self.net.place
        a, b = self.buf.at[at, y, x, self.head], self.buf.at[at, y, x, self.tail]
        return self.pairs(
            "two", self.layer, piece, [(2, lambda to, n: (a, a)), (1, lambda to, n: (b, b))]
        )

    def three(self, piece):
        at, (_, y, x) = self.net.along(0, -piece), self.net.place
        a, b = self.buf.at[at, y, :, self.head], self.buf.at[at, :, x, self.tail]
        return self.pairs(
            "three", self.layer, piece, [(1, lambda to, n: (a, a)), (2, lambda to, n: (b, b))]
        )

    def near(self):
        if not self.dm.last_rows:
            return []
        ref = self.buf.at[(*self.net.place, self.last)]
        return self.plane(self.layer, lambda y, x, n: (ref, ref))

    def far(self):
        if not self.dm.last_rows:
            return []
        ref = self.buf.at[self.net.place[0], :, :, self.last]
        size = self.dm.axes[0]
        return [
            self.net.copy(("far", size - 1, o - 1), self.layer, ref, ref, self.net.on_axis(0, o))
            for o in range(1, size)
        ]

    def along_depth(self):
        for offset in range(1, self.dm.axes[0]):
            start_all(self.one(offset))

    def begin(self):
        start_all(self.two(0))
        start_all(self.near())

    def cross(self, piece):
        wait_all(self.one(piece))
        start_all(self.two(piece))

    def spread(self, piece):
        wait_all(self.two(piece))
        start_all(self.three(piece))

    def spread_last(self):
        wait_all(self.near())
        start_all(self.far())

    def end(self):
        for piece in range(self.dm.axes[0]):
            wait_all(self.three(piece))
        wait_all(self.far())


class Scatter(Parts):
    def one(self, piece):
        at, s, buf = self.net.along(0, piece), self.s, self.buf
        return self.pairs(
            "three",
            0,
            piece,
            [
                (1, lambda to, n: (buf.at[at, to, :, self.head], s.one_a.at[piece, n])),
                (2, lambda to, n: (buf.at[at, :, to, self.tail], s.one_b.at[piece, n])),
            ],
        )

    def two(self, piece):
        at, s, buf, (_, y, x) = self.net.along(0, piece), self.s, self.buf, self.net.place
        return self.pairs(
            "two",
            0,
            piece,
            [
                (2, lambda to, n: (buf.at[at, y, to, self.head], s.two_a.at[piece, n])),
                (1, lambda to, n: (buf.at[at, to, x, self.tail], s.two_b.at[piece, n])),
            ],
        )

    def three(self, piece):
        _, y, x = self.net.place
        source = self.buf.at[self.net.along(0, piece), y, x, self.most]
        target = self.s.three.at[self.layer, piece - 1]
        key = ("one", self.dm.axes[0] - 1, piece - 1)
        turn = self.dm.layers - 1 - self.layer
        return self.net.copy(key, turn, source, target, self.net.device(piece, 0, 0))

    def far(self, piece):
        source = self.buf.at[self.net.along(0, piece), :, :, self.last]
        key = ("far", self.dm.axes[0] - 1, piece - 1)
        return self.net.copy(key, 0, source, self.s.far.at[piece - 1], self.net.device(piece, 0, 0))

    def near(self):
        z = self.net.place[0]
        return self.plane(0, lambda y, x, n: (self.buf.at[z, y, x, self.last], self.s.near.at[n]))

    def add(self, at, parts):
        value = self.buf[at].astype(F32)
        for part in parts:
            value = value + part.astype(F32)
        self.buf[at] = value.astype(BF16)

    def begin(self, piece):
        if self.dm.last_rows:

            @pl.when(piece > 0)
            def _():
                self.far(piece).start()

        start_all(self.one(piece))

    def second(self, piece):
        _, rows, cols = self.dm.axes
        at, s, (_, y, x) = self.net.along(0, piece), self.s, self.net.place
        wait_all(self.one(piece))
        self.add((at, y, slice(None), self.head), [s.one_a[piece, o] for o in range(rows - 1)])
        self.add((at, slice(None), x, self.tail), [s.one_b[piece, o] for o in range(cols - 1)])
        start_all(self.two(piece))

    def third(self, piece):
        _, rows, cols = self.dm.axes
        at, s, (_, y, x) = self.net.along(0, piece), self.s, self.net.place
        wait_all(self.two(piece))
        self.add((at, y, x, self.head), [s.two_a[piece, o] for o in range(cols - 1)])
        self.add((at, y, x, self.tail), [s.two_b[piece, o] for o in range(rows - 1)])

        @pl.when(piece > 0)
        def _():
            self.three(piece).start()

    def second_last(self):
        if self.dm.last_rows:
            pieces = range(1, self.dm.axes[0])
            wait_all([self.far(piece) for piece in pieces])
            z = self.net.place[0]
            at = (z, slice(None), slice(None), self.last)
            self.add(at, [self.s.far[piece - 1] for piece in pieces])
            start_all(self.near())

    def third_last(self):
        if self.dm.last_rows:
            copies = self.near()
            wait_all(copies)
            self.add((*self.net.place, self.last), [self.s.near[n] for n in range(len(copies))])

    def end(self):
        value = self.buf[(*self.net.place, self.most)].astype(F32)
        for piece in range(1, self.dm.axes[0]):
            self.three(piece).wait()
            value = value + self.s.three[self.layer, piece - 1].astype(F32)
        self.s.rows[self.most, :] = value
        if self.dm.last_rows:
            self.s.rows[self.last, :] = self.buf[(*self.net.place, self.last)].astype(F32)


class Totals:
    def __init__(self, dm, net, s, layer, first):
        self.dm, self.net, self.s, self.layer, self.first = dm, net, s, layer, first

    def across(self):
        s, layer = self.s, self.layer
        copy = self.net.copy(
            ("cores", 1, 0), layer, s.vec_grad.at[layer], s.vec_back.at[layer], self.net.sibling()
        )
        return [copy]

    def plane(self):
        _, y, x = self.net.place
        here = self.s.vec_p.at[self.layer, y * self.dm.axes[2] + x]
        offsets = self.net.plane()
        return [
            self.net.copy(("plane", len(offsets), n), self.layer, here, here, self.net.device(0, *o))
            for n, o in enumerate(offsets)
        ]

    def depth(self):
        here = self.s.vec_z.at[self.layer, self.net.place[0]]
        size = self.dm.axes[0]
        return [
            self.net.copy(("depth", size - 1, o - 1), self.layer, here, here, self.net.on_axis(0, o))
            for o in range(1, size)
        ]

    def begin(self):
        start_all(self.across())

    def second(self):
        s, layer, (_, y, x) = self.s, self.layer, self.net.place
        wait_all(self.across())
        value = unpack_vectors(self.dm, s.vec_grad[layer] + s.vec_back[layer], self.first)
        s.vec_p[layer, y * self.dm.axes[2] + x] = value
        start_all(self.plane())

    def third(self):
        s, layer = self.s, self.layer
        wait_all(self.plane())
        value = s.vec_p[layer, 0]
        for o in range(1, self.dm.axes[1] * self.dm.axes[2]):
            value = value + s.vec_p[layer, o]
        s.vec_z[layer, self.net.place[0]] = value
        start_all(self.depth())

    def end(self):
        wait_all(self.depth())
        value = self.s.vec_z[self.layer, 0]
        for o in range(1, self.dm.axes[0]):
            value = value + self.s.vec_z[self.layer, o]
        return value


class Refs:
    pass


def scratch_shapes(dm):
    layers, tokens, width, wide = dm.layers, dm.tokens, dm.width, HEADS * HD
    depth, rows, cols = dm.axes
    head, tail = dm.first_rows, dm.most_rows - dm.first_rows
    vmem, copies = pltpu.VMEM, copies_needed(dm)
    return dict(
        hid=vmem((tokens, width), F32),
        mid=vmem((tokens, width), F32),
        columns=vmem((tokens, 8), F32),
        devs=vmem((layers, tokens, 8), F32),
        low_a=vmem((layers, tokens, width), BF16),
        low_b=vmem((layers, tokens, width), BF16),
        low_g=vmem((tokens, width), BF16),
        hat_a=vmem((layers, tokens, width), F32),
        hat_b=vmem((layers, tokens, width), F32),
        qkv=vmem((layers, tokens, 3 * wide), BF16),
        probs=vmem((layers, dm.images * HEADS, dm.pad_seq, dm.pad_seq), BF16),
        att=vmem((layers, tokens, wide), BF16),
        act=vmem((layers, tokens, FF), BF16),
        slope=vmem((layers, tokens, FF), BF16),
        w_qkv=vmem((layers, 3 * wide, width), BF16),
        w_out=vmem((layers, wide, width), BF16),
        w_up=vmem((layers, FF, width), BF16),
        w_down=vmem((layers, FF, width), BF16),
        grads=vmem((dm.halves, dm.groups, dm.group_js, dm.blocks, width), BF16),
        grads_in=vmem((dm.groups, dm.group_js, dm.blocks, width), BF16),
        gath=vmem((layers, depth, rows, cols, dm.shard_rows, width), BF16),
        one_a=vmem((depth, rows - 1, cols, head, width), BF16),
        one_b=vmem((depth, cols - 1, rows, tail, width), BF16),
        two_a=vmem((depth, cols - 1, head, width), BF16),
        two_b=vmem((depth, rows - 1, tail, width), BF16),
        three=vmem((layers, depth - 1, dm.most_rows, width), BF16),
        far=vmem((depth - 1, rows, cols, max(16, dm.last_rows), width), BF16),
        near=vmem((rows * cols - 1, max(16, dm.last_rows), width), BF16),
        rows=vmem((dm.shard_rows, width), F32),
        tok_in=vmem((dm.images, dm.seq, width), F32),
        tok_out=vmem((dm.images, dm.seq, width), F32),
        codes=vmem((layers, depth, 8, dm.keys // depth), F32),
        vec_own=vmem((layers, 8, FF), F32),
        vec=vmem((layers, 8, FF), F32),
        vec_grad=vmem((layers, 8, FF), F32),
        vec_in=vmem((layers, 8, FF), F32),
        vec_back=vmem((layers, 8, FF), F32),
        vec_z=vmem((layers, depth, 8, width), F32),
        vec_p=vmem((layers, rows * cols, 8, width), F32),
        vec_sum=vmem((layers, 8, width), F32),
        keep_row=vmem((8, -(-dm.pad_seq // 128) * 128), F32),
        send_sems=pltpu.SemaphoreType.DMA((copies,)),
        recv_sems=pltpu.SemaphoreType.DMA((copies,)),
        load_sems=pltpu.SemaphoreType.DMA((dm.images,)),
        store_sems=pltpu.SemaphoreType.DMA((dm.images,)),
        credit=pltpu.SemaphoreType.REGULAR,
        core_credit=pltpu.SemaphoreType.REGULAR,
    )


def load_tokens(dm, source, target, scale=None):
    tail = dm.pad_seq - 16
    for image in range(dm.images):
        start = image * dm.pad_seq
        target[start + tail : start + dm.pad_seq, :] = jnp.zeros((16, dm.width), F32)
        value = source[image]
        if scale is not None:
            value = value * scale[start : start + dm.seq, 0:1]
        target[start : start + dm.seq, :] = value


class Tokens:
    def __init__(self, dm, net, s):
        self.dm, self.net, self.s = dm, net, s

    def image(self, ref, number):
        return ref.at[:, self.net.core * self.dm.images + number]

    def load(self, ref):
        sems = self.s.load_sems
        return [
            pltpu.make_async_copy(self.image(ref, i), self.s.tok_in.at[i], sems.at[i])
            for i in range(self.dm.images)
        ]

    def store(self, ref, turn):
        copies = []
        for i in range(self.dm.images):
            source, target = self.s.tok_out.at[i], self.image(ref, i)
            copies.append(pltpu.make_async_copy(source, target, self.s.store_sems.at[i]))
            key = ("tokens", self.dm.images, i)
            copies.append(self.net.copy(key, turn, source, target, self.net.sibling()))
        return copies


def prepare_keep(dm, keep_mask, first, s):
    kept = keep_mask[...].astype(F32)
    kept = jnp.where(first, kept[: dm.images], kept[dm.images :])
    s.keep_row[...] = jnp.zeros(s.keep_row.shape, F32)
    s.keep_row[: dm.images, : dm.seq] = kept
    columns = jnp.transpose(s.keep_row[...])
    for image in range(dm.images):
        rows = slice(image * dm.pad_seq, (image + 1) * dm.pad_seq)
        s.columns[rows, 0:1] = columns[: dm.pad_seq, image : image + 1]


def own_shard(dm, master, net, s):
    z, y, x = net.place
    if dm.shard_rows > dm.block_rows * dm.slots:
        s.rows[...] = jnp.zeros(s.rows.shape, F32)
    for layer in range(dm.layers):
        for j in range(dm.block_rows):
            s.rows[j * dm.slots : (j + 1) * dm.slots, :] = master[0, layer, j]
        s.gath[layer, z, y, x] = s.rows[...].astype(BF16)


def step_kernel(dm, names, hidden, keep_mask, cotangent, slot_block, master, vectors, acts, grad_in, matrix, vec_out, *scratch):
    s = Refs()
    for name, ref in zip(names, scratch):
        setattr(s, name, ref)
    net = Net(dm, s)
    first = net.core == 0
    tokens = Tokens(dm, net, s)
    cols, units, depth = dm.half_cols, dm.half_units, dm.axes[0]
    assert dm.layers == 2
    gathers = [Gather(dm, net, s, layer) for layer in range(dm.layers)]
    barrier = pltpu.get_barrier_semaphore()
    net.greet(barrier)
    start_all(tokens.load(hidden))
    own_shard(dm, master, net, s)
    net.met(barrier)
    gathers[0].along_depth()
    gathers[0].begin()
    pack_vectors(dm, vectors, first, s)
    other_vec = net.copy(("vectors", 1, 0), 0, s.vec_own, s.vec_in, net.sibling())
    other_vec.start()
    prepare_codes(dm, slot_block, s)
    prepare_keep(dm, keep_mask, first, s)
    wait_all(tokens.load(hidden))
    load_tokens(dm, s.tok_in, s.hid)
    start_all(tokens.load(cotangent))
    other_vec.wait()
    s.vec[...] = s.vec_own[...] + s.vec_in[...]
    gathers[0].spread(0)
    gathers[0].spread_last()
    for piece in range(1, depth):
        gathers[0].cross(piece)
        if piece > 1:
            gathers[0].spread(piece - 1)
    gathers[1].along_depth()
    gathers[0].spread(depth - 1)
    gathers[1].begin()

    def weights(layer):
        parts = [(s.w_qkv, kind * HEADS * HD + net.core * cols, cols) for kind in range(3)]
        parts += [(s.w_out, net.core * cols, cols), (s.w_up, net.core * units, units)]
        parts.append((s.w_down, net.core * units, units))
        copies = []
        for ref, start, count in parts:
            rows = ref.at[layer, pl.ds(pl.multiple_of(start, 16), count)]
            key = ("weights", len(parts), len(copies))
            copies.append(net.copy(key, layer, rows, rows, net.sibling()))
        return copies

    def forward(layer):
        shares = weights(layer)
        for name, phase in FORWARD:
            phase(dm, layer, s)
            if name == "norm":

                more = layer + 1 < dm.layers
                pl.when(more)(lambda: gathers[1].cross(1))
                Gather(dm, net, s, layer).end()

                @pl.when(more)
                def _():
                    gathers[1].spread(0)
                    gathers[1].spread_last()
                    for piece in range(2, depth // 2 + 1):
                        gathers[1].cross(piece)

                parts = permute_in(dm, layer, net.core, s)
                next(parts)
                start_all(shares[:4])
                next(parts, None)
                start_all(shares[4:])

                @pl.when(more)
                def _():
                    for piece in range(depth // 2 + 1, depth):
                        gathers[1].cross(piece)
                    for piece in range(1, depth // 2):
                        gathers[1].spread(piece)

                wait_all(shares[:3])
            if name == "attend":
                shares[3].wait()
            if name == "mid":
                shares[4].wait()
            if name == "up":
                shares[5].wait()
            if name in ("project", "attend"):
                some = depth // 4
                pieces = range(depth // 2, depth - some) if name == "project" else range(depth - some, depth)

                @pl.when(layer + 1 < dm.layers)
                def _(pieces=pieces):
                    for piece in pieces:
                        gathers[1].spread(piece)

    lax.fori_loop(0, dm.layers, lambda i, c: (forward(i), c)[1], 0)
    for image in range(dm.images):
        rows = slice(image * dm.pad_seq, image * dm.pad_seq + dm.seq)
        s.tok_out[image] = s.hid[rows, :] * s.columns[rows, 0:1]
    start_all(tokens.store(acts, 0))
    wait_all(tokens.load(cotangent))
    load_tokens(dm, s.tok_in, s.hid, s.columns)

    def put_rows(layer):
        Scatter(dm, net, s, layer).end()
        for j in range(dm.block_rows):
            matrix[0, layer, j] = s.rows[j * dm.slots : (j + 1) * dm.slots, :]

    def put_vectors(layer):
        value = Totals(dm, net, s, layer, first).end()
        for r in range(vec_out.shape[1]):
            vec_out[0, r, layer : layer + 1, :] = value[r : r + 1]

    def share(layer, number):
        start = dm.first_unit
        rows = (pl.ds(start, dm.blocks - start), pl.ds(0, start))[number]
        source, target = s.grads.at[1 - net.core, :, :, rows], s.grads_in.at[:, :, rows]
        return net.copy(("shares", 2, number), layer, source, target, net.sibling())

    def backward(turn):
        layer = dm.layers - 1 - turn
        later = turn > 0
        before = Scatter(dm, net, s, 1)
        totals_before = Totals(dm, net, s, 1, first)

        def when_later(body, *args):
            pl.when(later)(lambda: body(*args))

        order = list(range(depth - 1, -1, -1))
        for name, phase in BACKWARD:
            phase(dm, layer, s)
            if name == "start":
                for piece in range(depth // 2 - 1, -1, -1):
                    when_later(before.begin, piece)
            if name == "units":
                when_later(pl.semaphore_wait, s.core_credit, 1)
                share(layer, 0).start()
            if name in ("units", "mid", "attend"):
                count = depth // 2 if name == "units" else depth // 4
                now, order = order[:count], order[count:]
                for piece in now:
                    when_later(before.second, piece)
            if name == "units":
                when_later(totals_before.second)
            if name == "down":
                when_later(before.second_last)
            if name == "attended":
                when_later(before.third_last)
                for piece in range(depth - 1, -1, -1):
                    when_later(before.third, piece)
                when_later(net.greet, s.credit)
                when_later(totals_before.third)
            if name == "rows":
                share(layer, 1).start()
            if name == "project":
                wait_all([share(layer, 0), share(layer, 1)])
                fill = permute_out(dm, layer, net.core, s)
                when_later(net.met, s.credit)
                scatter = Scatter(dm, net, s, layer)

                for number in range(depth // 2):
                    pieces = [depth - 1 - 2 * number, depth - 2 - 2 * number]
                    fill([net.along(0, piece) for piece in pieces])
                    for piece in pieces if number < depth // 4 else []:
                        scatter.begin(piece)

                @pl.when(layer > 0)
                def _():
                    pl.semaphore_signal(
                        s.core_credit, inc=1, device_id=net.sibling(), device_id_type=MESH
                    )
        Totals(dm, net, s, layer, first).begin()

    lax.fori_loop(0, dm.layers, lambda i, c: (backward(i), c)[1], 0)
    wait_all(tokens.store(acts, 0))
    for image in range(dm.images):
        rows = slice(image * dm.pad_seq, image * dm.pad_seq + dm.seq)
        s.tok_out[image] = s.hid[rows, :]
    start_all(tokens.store(grad_in, 1))
    scatter, totals = Scatter(dm, net, s, 0), Totals(dm, net, s, 0, first)
    events = [(totals.second,)]
    for piece in range(depth - 1, -1, -1):
        events.append((scatter.second, piece))
        if piece == depth // 2:
            events.append((totals.third,))
        if piece >= depth // 2:
            events.append((scatter.begin, piece - depth // 2))
        if piece < depth - 1:
            events.append((scatter.third, piece + 1))
    for event, *args in events:
        event(*args)
    scatter.second_last()
    scatter.third(0)
    scatter.third_last()
    put_vectors(1)
    put_rows(1)
    put_vectors(0)
    put_rows(0)
    wait_all(tokens.store(grad_in, 1))


def run_step(dm, hidden_in, keep_mask, cotangent, slot_block, master, vector_master):
    shapes = scratch_shapes(dm)
    out_shape = (
        jax.ShapeDtypeStruct(hidden_in.shape, F32),
        jax.ShapeDtypeStruct(hidden_in.shape, F32),
        jax.ShapeDtypeStruct(master.shape, F32),
        jax.ShapeDtypeStruct(vector_master.shape, F32),
    )
    full, far = pl.BlockSpec(memory_space=pltpu.VMEM), pl.BlockSpec(memory_space=pl.ANY)
    return pl.pallas_call(
        functools.partial(step_kernel, dm, tuple(shapes)),
        out_shape=out_shape,
        in_specs=[far, full, far, full, full, full],
        out_specs=[far, far, full, full],
        scratch_shapes=list(shapes.values()),
        compiler_params=pltpu.CompilerParams(
            vmem_limit_bytes=63 * 2**20, collective_id=0, has_side_effects=True
        ),
    )(hidden_in, keep_mask, cotangent, slot_block, master, vector_master)


def adam_step(weight, grad_sum, first_old, second_old, rate, decay):
    first_new = BETA_ONE * first_old + (1.0 - BETA_ONE) * grad_sum
    second_new = BETA_TWO * second_old + (1.0 - BETA_TWO) * grad_sum * grad_sum
    first_hat = first_new / (1.0 - BETA_ONE**STEP)
    second_hat = second_new / (1.0 - BETA_TWO**STEP)
    return (
        second_new,
        weight - rate * (first_hat / (jnp.sqrt(second_hat) + EPS_ADAM) + decay * weight),
    )


def finish_kernel(parts, *refs):
    large, matrix, vector = refs[:2], refs[2:6], refs[6:10]
    large_out, matrix_out, vector_out = refs[10:12], refs[12:15], refs[15:18]
    stage, matrix_in, vector_in, matrix_done, vector_done, stage_sems, load_sems, store_sems = refs[18:]
    loads, stores = [], []
    rows_all = stage.shape[1]
    size = -(-rows_all // parts)
    for start in range(0, rows_all, size):
        for number, (source, target) in enumerate(zip(large, large_out)):
            rows = pl.ds(start, min(size, rows_all - start))
            held, sem = stage.at[number, rows], stage_sems.at[len(loads)]
            loads.append(pltpu.make_async_copy(source.at[rows], held, sem))
            stores.append(pltpu.make_async_copy(held, target.at[rows], sem))
    matrix_loads = [
        pltpu.make_async_copy(ref, matrix_in.at[n], load_sems.at[n]) for n, ref in enumerate(matrix)
    ]
    vector_loads = [
        pltpu.make_async_copy(ref, vector_in.at[n], load_sems.at[4 + n]) for n, ref in enumerate(vector)
    ]
    results = [
        pltpu.make_async_copy(matrix_done.at[n], ref, store_sems.at[n])
        for n, ref in enumerate(matrix_out)
    ]
    results += [
        pltpu.make_async_copy(vector_done.at[n], ref, store_sems.at[3 + n])
        for n, ref in enumerate(vector_out)
    ]
    start_all(vector_loads + matrix_loads + loads)
    wait_all(vector_loads + matrix_loads)

    def adam(held, done, at, rate, decay):
        grad, weight, one, two = (held[(n, *at)] for n in range(4))
        done[(0, *at)] = grad
        done[(1, *at)], done[(2, *at)] = adam_step(weight, grad, one, two, rate, decay)

    for layer in range(matrix_in.shape[2]):
        adam(matrix_in, matrix_done, (0, layer), RATE_MATRIX, DECAY_MATRIX)
    adam(vector_in, vector_done, (0,), RATE_VECTOR, 0.0)
    start_all(results)
    for load, store in zip(loads, stores):
        load.wait()
        store.start()
    wait_all(stores + results)


def run_finish(acts, grad_in, matrix, vector):
    parts = 1
    far = pl.BlockSpec(memory_space=pl.ANY)
    shapes = [acts, grad_in] + [matrix[0]] * 3 + [vector[0]] * 3
    return pl.pallas_call(
        functools.partial(finish_kernel, parts),
        out_shape=tuple(jax.ShapeDtypeStruct(a.shape, F32) for a in shapes),
        in_specs=[far] * 10,
        out_specs=[far] * 8,
        scratch_shapes=[
            pltpu.VMEM((2, *acts.shape), F32),
            pltpu.VMEM((4, *matrix[0].shape), F32),
            pltpu.VMEM((4, *vector[0].shape), F32),
            pltpu.VMEM((3, *matrix[0].shape), F32),
            pltpu.VMEM((3, *vector[0].shape), F32),
            pltpu.SemaphoreType.DMA((2 * parts,)),
            pltpu.SemaphoreType.DMA((8,)),
            pltpu.SemaphoreType.DMA((6,)),
        ],
        compiler_params=pltpu.CompilerParams(vmem_limit_bytes=63 * 2**20),
    )(acts, grad_in, *matrix, *vector)


def shards(
    hidden_in, keep_mask, cotangent, slot_block, master, moment_one, moment_two, vector_master, vector_one, vector_two
):
    images, seq, width = hidden_in.shape
    halves, ranks = lax.axis_size("mp"), lax.axis_size("dp")
    dm = Dims(
        master.shape[1], images // halves, seq, width, halves, ranks, slot_block.shape[1], master.shape[3]
    )
    matrix = [array.swapaxes(2, 3) for array in (master, moment_one, moment_two)]
    vector = [array.swapaxes(1, 2) for array in (vector_master, vector_one, vector_two)]
    acts, grad_in, matrix_grad, vector_grad = run_step(
        dm, hidden_in.swapaxes(0, 1), keep_mask, cotangent.swapaxes(0, 1), slot_block, matrix[0], vector[0]
    )
    results = run_finish(acts, grad_in, [matrix_grad] + matrix, [vector_grad] + vector)
    return tuple(
        array.swapaxes(*axes)
        for array, axes in zip(results, [(0, 1)] * 2 + [(2, 3)] * 3 + [(1, 2)] * 3)
    )


def solution(mesh):
    images, rows, copied = P("dp", None, None), P("mp", None, "dp", None, None), P("mp", None, None, None)
    return jax.shard_map(
        shards,
        mesh=mesh,
        in_specs=(images, P("dp", None), images, P(), rows, rows, rows, copied, copied, copied),
        out_specs=(images, images, rows, rows, rows, copied, copied, copied),
        check_vma=False,
    )
```

```python
import functools

import jax
import jax.numpy as jnp
from jax import lax
from jax.experimental import pallas as pl
from jax.experimental.pallas import tpu as pltpu
from jax.sharding import PartitionSpec as P

HEADS = 6
HD = 64
FF = 1536
STEP = 10

EPS_NORM = 1e-06
BETA_ONE = 0.9
BETA_TWO = 0.999
RATE_MATRIX = 0.003
RATE_VECTOR = 0.01
DECAY_MATRIX = 0.05
EPS_ADAM = 1e-08
NEG_FILL = -1e30
LOG2_E = 1.4426950408889634

F32 = jnp.float32
MESH = pl.DeviceIdType.MESH
BF16 = jnp.bfloat16


def dot_nn(left, right):
    return lax.dot_general(left, right, (((1,), (0,)), ((), ())), preferred_element_type=F32)


def dot_nt(left, right):
    return lax.dot_general(left, right, (((1,), (1,)), ((), ())), preferred_element_type=F32)


def dot_tn(left, right):
    return lax.dot_general(left, right, (((0,), (0,)), ((), ())), preferred_element_type=F32)


def fold_rows(values):
    rows, cols = values.shape
    return jnp.sum(values.reshape(rows // 8, 8, cols), 0)


def loop(count, body, unroll=True):
    lax.fori_loop(0, count, lambda i, c: (body(i), c)[1], 0, unroll=unroll)


def gelu_pair(u):
    cdf = 0.5 + 0.5 * lax.erf(u * (0.5**0.5))
    slope = cdf + u * (jnp.exp(-0.5 * u * u) * 0.3989422804014327)
    return u * cdf, slope


class Dims:
    def __init__(self, layers, images, seq, width, halves, ranks, blocks, block_rows):
        self.layers, self.images, self.seq, self.width = layers, images, seq, width
        self.halves, self.ranks, self.blocks, self.block_rows = halves, ranks, blocks, block_rows
        self.pad_seq = -(-seq // 16) * 16
        self.tokens = images * self.pad_seq
        self.slots = blocks // ranks
        side = 1
        while side**3 * 8 <= ranks:
            side *= 2
        self.axes = (ranks // (side * side), side, side)
        self.shard_rows = -(-block_rows * self.slots // 16) * 16
        self.last_rows = 16 * (self.shard_rows // 144)
        self.most_rows = self.shard_rows - self.last_rows
        self.first_rows = -(-self.most_rows // 32) * 16
        self.groups = block_rows // 2 if 2 * self.slots % 16 == 0 else 1
        self.group = self.shard_rows // self.groups
        self.group_js = block_rows // self.groups
        self.keys = ranks * self.group
        self.half_cols = HEADS * HD // halves
        self.half_units = FF // halves
        self.natural = 4 * self.half_cols
        self.unit_blocks = self.half_units // block_rows
        self.kind_blocks = self.half_cols // block_rows
        self.first_unit = 4 * self.kind_blocks


def divide(values, number):
    return jnp.floor((values.astype(F32) + 0.5) * (1.0 / number))


def one_hot(rows, codes, axis):
    start, count = rows
    shape = (count, codes.shape[1]) if axis == 0 else (codes.shape[0], count)
    here = lax.broadcasted_iota(jnp.int32, shape, axis) + start
    return (here == codes.astype(jnp.int32)).astype(F32).astype(BF16)


def permute_in(dm, layer, half, s):
    cols, units, some = dm.half_cols, dm.half_units, dm.unit_blocks
    shards = [
        s.gath[layer, :, :, :, g * dm.group : (g + 1) * dm.group, :].reshape(dm.keys, dm.width)
        for g in range(dm.groups)
    ]
    code = jnp.concatenate([s.codes[layer, z] for z in range(dm.axes[0])], 1)[0:1]
    count = dm.first_unit
    starts = [odd * dm.blocks for odd in range(dm.group_js)]
    chosen = jnp.concatenate([one_hot((start, count), code, 0) for start in starts], 0)
    attention = []
    for g in range(dm.groups):
        rows = dot_nn(chosen, shards[g]).astype(BF16)
        attention += [rows[n * count : (n + 1) * count] for n in range(dm.group_js)]
    order = row_order(dm, cols, dm.kind_blocks)
    for kind in range(4):
        part = slice(kind * dm.kind_blocks, (kind + 1) * dm.kind_blocks)
        rows = dot_nn(order, jnp.concatenate([rows[part] for rows in attention], 0)).astype(BF16)
        if kind < 3:
            s.w_qkv[layer, pl.ds(pl.multiple_of(kind * HEADS * HD + half * cols, 16), cols), :] = rows
        else:
            s.w_out[layer, pl.ds(pl.multiple_of(half * cols, 16), cols), :] = rows
    yield
    for odd, start in enumerate(starts):
        chosen = one_hot((start + count, 2 * some), code, 0)
        for g in range(dm.groups):
            rows = dot_nn(chosen, shards[g]).astype(BF16)
            at = half * units + (g * dm.group_js + odd) * some
            at = pl.ds(pl.multiple_of(at, 16), some)
            s.w_up[layer, at, :] = rows[:some]
            s.w_down[layer, at, :] = rows[some:]


def put_grads(dm, s, kind, rows):
    cols, size = dm.half_cols, dm.kind_blocks
    order = row_order(dm, cols, size)
    for half in range(dm.halves):
        found = dot_tn(order, rows[half * cols : (half + 1) * cols]).astype(BF16)
        for j in range(dm.block_rows):
            s.grads[half, j // dm.group_js, j % dm.group_js, kind * size : (kind + 1) * size, :] = found[
                j * size : (j + 1) * size
            ]


def permute_out(dm, layer, half, s):
    for g in range(dm.groups):
        for odd in range(dm.group_js):
            total = s.grads[half, g, odd].astype(F32) + s.grads_in[g, odd].astype(F32)
            s.grads_in[g, odd] = total.astype(BF16)

    def pieces(places):
        codes = [jnp.transpose(s.codes[layer, z])[:, 0:1] for z in places]
        chosen = one_hot((0, dm.group_js * dm.blocks), jnp.concatenate(codes, 0), 1)
        size = chosen.shape[0] // len(places)
        for g in range(dm.groups):
            grads = s.grads_in[g].reshape(dm.group_js * dm.blocks, dm.width)
            rows = dot_nn(chosen, grads).astype(BF16)
            for n, z in enumerate(places):
                s.gath[layer, z, :, :, g * dm.group : (g + 1) * dm.group, :] = rows[
                    n * size : (n + 1) * size
                ].reshape(dm.axes[1], dm.axes[2], dm.group, dm.width)

    return pieces


def prepare_codes(dm, slot_block, s):
    layers, blocks, group = dm.layers, dm.blocks, dm.group
    block = slot_block[...].astype(F32)
    high = divide(block, 16)
    zero = jnp.zeros((16 - 2 * layers, blocks), F32)
    halves = jnp.concatenate([high, block - 16.0 * high, zero], 0).astype(BF16)
    per = dm.keys // dm.axes[0]
    size = per * max(1, 768 // per)
    for start in range(0, dm.keys, size):
        size = min(size, dm.keys - start)

        def place(shape):
            key = lax.broadcasted_iota(jnp.int32, shape, 1) + start
            rank = divide(key, group)
            inside = key.astype(F32) - rank * group
            odd = divide(inside, dm.slots)
            return rank * dm.slots + inside - odd * dm.slots, odd, inside >= dm.group_js * dm.slots

        slot, _, _ = place((blocks, size))
        same = slot == lax.broadcasted_iota(jnp.int32, (blocks, size), 0).astype(F32)
        parts = dot_nn(halves, same.astype(F32).astype(BF16))
        _, odd, padding = place((1, size))
        for layer in range(layers):
            block = 16.0 * parts[layer : layer + 1] + parts[layers + layer : layers + layer + 1]
            row = jnp.where(padding, -1.0, odd * blocks + block)
            rows = jnp.concatenate([row, jnp.zeros((7, size), F32)], 0)
            for z in range(start // per, (start + size) // per):
                s.codes[layer, z] = rows[:, z * per - start : (z + 1) * per - start]


def row_order(dm, rows, blocks):
    here = lax.broadcasted_iota(jnp.int32, (rows, rows), 1)
    inner = divide(here, blocks)
    source = (here.astype(F32) - inner * blocks) * dm.block_rows + inner
    same = source == lax.broadcasted_iota(jnp.int32, (rows, rows), 0).astype(F32)
    return same.astype(F32).astype(BF16)


def unit_order(dm):
    return row_order(dm, dm.half_units, dm.unit_blocks)


def reorder(dot, row, order):
    high = row.astype(BF16)
    rest = row - high.astype(F32)
    middle = rest.astype(BF16)
    low = (rest - middle.astype(F32)).astype(BF16)
    parts = [high.astype(F32), middle.astype(F32), low.astype(F32)]
    parts.append(jnp.zeros((13, row.shape[1]), F32))
    out = dot(jnp.concatenate(parts, 0).astype(BF16), order)
    return out[0:1] + (out[1:2] + out[2:3])


def pack_vectors(dm, vectors, first, s):
    cols, units, width = dm.half_cols, dm.half_units, dm.width
    wide = HEADS * HD
    order = unit_order(dm)
    for layer in range(dm.layers):
        rows = jnp.concatenate([vectors[0, r, layer : layer + 1, :] for r in range(6)], 0)
        flat = rows[0:1]
        q, v = flat[:, :cols], flat[:, cols : 2 * cols]
        none, mid = jnp.zeros((1, cols), F32), jnp.zeros((1, wide), F32)
        tail = jnp.zeros((1, FF - 3 * wide), F32)
        zero_half = jnp.concatenate([q, none, mid, v, none, tail], 1)
        one_half = jnp.concatenate([none, q, mid, none, v, tail], 1)
        s.vec_own[layer, 0:1, :] = jnp.where(first, zero_half, one_half)
        up = reorder(dot_nn, jnp.concatenate([rows[1:2], rows[2:3]], 1), order)
        none = jnp.zeros((1, units), F32)
        s.vec_own[layer, 1:2, :] = jnp.where(
            first, jnp.concatenate([up, none], 1), jnp.concatenate([none, up], 1)
        )
        own = jnp.concatenate([rows[3:6], jnp.zeros((3, FF - width), F32)], 1)
        none = jnp.zeros((3, FF), F32)
        s.vec_own[layer, 2:5, :] = jnp.where(first, own, none)
        s.vec_own[layer, 5:8, :] = jnp.where(first, none, own)


def unpack_vectors(dm, packed, first):
    cols, units, width = dm.half_cols, dm.half_units, dm.width
    wide = HEADS * HD
    flat = packed[0:1]
    zero_half = jnp.concatenate([flat[:, :cols], flat[:, 2 * wide : 2 * wide + cols]], 1)
    one_half = jnp.concatenate([flat[:, cols : 2 * cols], flat[:, 2 * wide + cols : 3 * wide]], 1)
    flat = packed[1:2]
    up = reorder(dot_nt, jnp.where(first, flat[:, :units], flat[:, units:]), unit_order(dm))
    own = jnp.where(first, packed[2:5, :width], packed[5:8, :width])
    return jnp.concatenate(
        [
            jnp.where(first, zero_half, one_half),
            up[:, :width],
            up[:, width:],
            own,
            jnp.zeros((2, width), F32),
        ],
        0,
    )


NORM_ROWS = 208


def norm_forward(dm, layer, source, gain, shift, low_out, hat_out, devs, place):
    def chunk(i):
        rows = pl.ds(pl.multiple_of(i * NORM_ROWS, NORM_ROWS), NORM_ROWS)
        values = source[rows, :]
        centred = values - jnp.mean(values, -1, keepdims=True)
        inv = lax.rsqrt(jnp.mean(centred * centred, -1, keepdims=True) + EPS_NORM)
        hat = centred * inv
        hat_out[layer, rows, :] = hat
        devs[layer, rows, place : place + 1] = inv
        low_out[layer, rows, :] = (hat * gain + shift).astype(BF16)

    loop(dm.tokens // NORM_ROWS, chunk)


def norm_backward(dm, layer, grad, into, gain, hat_in, devs, place):
    def chunk(i, carry):
        rows = pl.ds(pl.multiple_of(i * NORM_ROWS, NORM_ROWS), NORM_ROWS)
        out, hat, inv = grad[rows, :], hat_in[layer, rows, :], devs[layer, rows, place : place + 1]
        scaled = out * gain
        first = jnp.mean(scaled, -1, keepdims=True)
        second = jnp.mean(scaled * hat, -1, keepdims=True)
        into[rows, :] = into[rows, :] + inv * (scaled - first - hat * second)
        return carry[0] + fold_rows(out * hat), carry[1] + fold_rows(out)

    zero = jnp.zeros((8, dm.width), F32)
    gains, shifts = lax.fori_loop(0, dm.tokens // NORM_ROWS, chunk, (zero, zero), unroll=True)
    return jnp.sum(gains, 0, keepdims=True), jnp.sum(shifts, 0, keepdims=True)


def lane_halves():
    lane = lax.broadcasted_iota(jnp.int32, (1, 2 * HD), 1)
    return (lane < HD).astype(F32).astype(BF16), (lane >= HD).astype(F32).astype(BF16)


def image_rows(dm, image):
    return pl.ds(pl.multiple_of(image * dm.pad_seq, 16), dm.pad_seq)


def vector_row(dm, layer, s, row, count=None):
    return s.vec[layer, row : row + 1, : count or dm.width]


def forward_norm_a(dm, layer, s):
    gain, shift = vector_row(dm, layer, s, 2), vector_row(dm, layer, s, 3)
    norm_forward(dm, layer, s.hid, gain, shift, s.low_a, s.hat_a, s.devs, 0)


def forward_project(dm, layer, s):
    wide = HEADS * HD

    def project(image):
        rows = image_rows(dm, image)
        source = s.low_a[layer, rows, :]
        for kind in range(3):
            cols = slice(kind * wide, (kind + 1) * wide)
            value = dot_nt(source, s.w_qkv[layer, cols, :]) + s.vec[layer, 0:1, cols]
            s.qkv[layer, rows, cols] = value.astype(BF16)

    loop(dm.images, project)


def forward_attend(dm, layer, s):
    wide = HEADS * HD

    halves = lane_halves()

    def attend(image):
        rows = image_rows(dm, image)
        keep = s.columns[rows, 0:1]
        for pair in range(HEADS // 2):
            cols = slice(pair * 2 * HD, (pair + 1) * 2 * HD)
            q, k, v = (s.qkv[layer, rows, n * wide + cols.start : n * wide + cols.stop] for n in range(3))
            out = None
            for side, lanes in enumerate(halves):
                scores = dot_nt(k * lanes, q)
                scores = jnp.where(keep > 0, scores * (HD ** (-0.5) * LOG2_E), NEG_FILL)
                exponent = jnp.exp2(scores - jnp.max(scores, 0, keepdims=True))
                probs = (exponent * (1.0 / jnp.sum(exponent, 0, keepdims=True))).astype(BF16)
                s.probs[layer, image * HEADS + 2 * pair + side] = probs
                part = dot_tn(probs, v * lanes)
                out = part if out is None else out + part
            s.att[layer, rows, cols] = out.astype(BF16)

    loop(dm.images, attend)


def forward_out(dm, layer, s):
    bias = vector_row(dm, layer, s, 4)

    def out_project(image):
        rows = image_rows(dm, image)
        s.mid[rows, :] = s.hid[rows, :] + (dot_nn(s.att[layer, rows, :], s.w_out[layer]) + bias)

    loop(dm.images, out_project)


def forward_norm_b(dm, layer, s):
    gain, shift = vector_row(dm, layer, s, 5), vector_row(dm, layer, s, 6)
    norm_forward(dm, layer, s.mid, gain, shift, s.low_b, s.hat_b, s.devs, 1)


def forward_up(dm, layer, s):
    tile = 256

    def up(image):
        rows = image_rows(dm, image)
        source = s.low_b[layer, rows, :]
        for number in range(FF // tile):
            cols = slice(number * tile, (number + 1) * tile)
            u = dot_nt(source, s.w_up[layer, cols, :]) + s.vec[layer, 1:2, cols]
            act, slope = gelu_pair(u)
            s.act[layer, rows, cols] = act.astype(BF16)
            s.slope[layer, rows, cols] = slope.astype(BF16)

    loop(dm.images, up)


def forward_down(dm, layer, s):
    bias = vector_row(dm, layer, s, 7)

    def down(image):
        rows = image_rows(dm, image)
        s.hid[rows, :] = s.mid[rows, :] + (dot_nn(s.act[layer, rows, :], s.w_down[layer]) + bias)

    loop(dm.images, down)


FORWARD = (
    ("norm", forward_norm_a),
    ("project", forward_project),
    ("attend", forward_attend),
    ("out", forward_out),
    ("mid", forward_norm_b),
    ("up", forward_up),
    ("down", forward_down),
)


def low_and_sum(dm, source, target):
    def chunk(i, carry):
        rows = pl.ds(pl.multiple_of(i * NORM_ROWS, NORM_ROWS), NORM_ROWS)
        low = source[rows, :].astype(BF16)
        target[rows, :] = low
        return carry + fold_rows(low.astype(F32))

    total = lax.fori_loop(0, dm.tokens // NORM_ROWS, chunk, jnp.zeros((8, dm.width), F32), unroll=True)
    return jnp.sum(total, 0, keepdims=True)


def column_sums(dm, read, cols):
    def chunk(i, carry):
        rows = pl.ds(pl.multiple_of(i * NORM_ROWS, NORM_ROWS), NORM_ROWS)
        return carry + fold_rows(read(rows).astype(F32))

    total = lax.fori_loop(0, dm.tokens // NORM_ROWS, chunk, jnp.zeros((8, cols), F32), unroll=True)
    return jnp.sum(total, 0, keepdims=True)


def backward_start(dm, layer, s):
    s.vec_grad[layer, 7:8, : dm.width] = low_and_sum(dm, s.hid, s.low_g)


def backward_units(dm, layer, s):
    tile, some = 2 * dm.unit_blocks, dm.unit_blocks
    per_half = dm.half_units // tile

    def unit_tile(number):
        cols = pl.ds(pl.multiple_of(number * tile, tile), tile)
        grad = dot_nt(s.low_g[...], s.w_down[layer, cols, :])
        grad = (grad * s.slope[layer, :, cols].astype(F32)).astype(BF16)
        s.slope[layer, :, cols] = grad
        half, first = number // per_half, (number % per_half) * 2
        down = dot_tn(s.act[layer, :, cols], s.low_g[...]).astype(BF16)
        up = dot_tn(grad, s.low_b[layer]).astype(BF16)
        for n in range(2):
            g, odd = (first + n) // dm.group_js, (first + n) % dm.group_js
            for value, start in ((up, dm.first_unit), (down, dm.first_unit + some)):
                s.grads[half, g, odd, start : start + some, :] = value[n * some : (n + 1) * some]

    loop(FF // tile, unit_tile)


def backward_up_sums(dm, layer, s):
    s.vec_grad[layer, 1:2, :] = column_sums(dm, lambda rows: s.slope[layer, rows, :], FF)


def backward_down(dm, layer, s):
    def down(image):
        rows = image_rows(dm, image)
        s.mid[rows, :] = dot_nn(s.slope[layer, rows, :], s.w_up[layer])

    loop(dm.images, down)


def backward_norm_b(dm, layer, s):
    width = dm.width
    gain = vector_row(dm, layer, s, 5)
    gains, shifts = norm_backward(dm, layer, s.mid, s.hid, gain, s.hat_b, s.devs, 1)
    s.vec_grad[layer, 5:6, :width] = gains
    s.vec_grad[layer, 6:7, :width] = shifts
    s.vec_grad[layer, 4:5, :width] = low_and_sum(dm, s.hid, s.low_g)


def backward_out(dm, layer, s):
    put_grads(dm, s, 3, dot_tn(s.att[layer], s.low_g[...]).astype(BF16))

    def out_project(image):
        rows = image_rows(dm, image)
        s.att[layer, rows, :] = dot_nt(s.low_g[rows, :], s.w_out[layer]).astype(BF16)

    loop(dm.images, out_project)


def backward_attend(dm, layer, s, part):
    wide = HEADS * HD
    half = dm.images // 2

    halves = lane_halves()

    def attend(image):
        rows = image_rows(dm, image)
        keep = s.columns[rows, 0:1] * HD ** (-0.5)
        for pair in range(HEADS // 2):
            cols = slice(pair * 2 * HD, (pair + 1) * 2 * HD)
            q, k, v = (s.qkv[layer, rows, n * wide + cols.start : n * wide + cols.stop] for n in range(3))
            out = s.att[layer, rows, cols]
            parts = None
            for side, lanes in enumerate(halves):
                probs = s.probs[layer, image * HEADS + 2 * pair + side]
                grad = dot_nt(v * lanes, out)
                wide_probs = probs.astype(F32)
                total = jnp.sum(wide_probs * grad, 0, keepdims=True)
                raw = (wide_probs * (grad - total) * keep).astype(BF16)
                found = dot_tn(raw, k * lanes), dot_nn(raw, q * lanes), dot_nn(probs, out * lanes)
                parts = found if parts is None else [p + f for p, f in zip(parts, found)]
            for n, part in enumerate(parts):
                s.qkv[layer, rows, n * wide + cols.start : n * wide + cols.stop] = part.astype(BF16)

    loop(half, lambda i: attend(part * half + i))


def backward_rows(dm, layer, s):
    wide = HEADS * HD
    for kind in range(3):
        value = dot_tn(s.qkv[layer, :, kind * wide : (kind + 1) * wide], s.low_a[layer])
        put_grads(dm, s, kind, value.astype(BF16))


def backward_sums(dm, layer, s):
    wide = 3 * HEADS * HD
    s.vec_grad[layer, 0:1, :wide] = column_sums(dm, lambda rows: s.qkv[layer, rows, :], wide)


def backward_project(dm, layer, s):
    def project(image):
        rows = image_rows(dm, image)
        s.mid[rows, :] = dot_nn(s.qkv[layer, rows, :], s.w_qkv[layer])

    loop(dm.images, project)


def backward_norm_a(dm, layer, s):
    width = dm.width
    gain = vector_row(dm, layer, s, 2)
    gains, shifts = norm_backward(dm, layer, s.mid, s.hid, gain, s.hat_a, s.devs, 0)
    s.vec_grad[layer, 2:3, :width] = gains
    s.vec_grad[layer, 3:4, :width] = shifts


BACKWARD = (
    ("start", backward_start),
    ("units", backward_units),
    ("sums", backward_up_sums),
    ("down", backward_down),
    ("mid", backward_norm_b),
    ("out", backward_out),
    ("attend", functools.partial(backward_attend, part=0)),
    ("attended", functools.partial(backward_attend, part=1)),
    ("rows", backward_rows),
    ("more", backward_sums),
    ("project", backward_project),
    ("end", backward_norm_a),
)


class Net:
    def __init__(self, dm, s):
        self.dm, self.s, self.keys = dm, s, {}
        self.rank, self.core = lax.axis_index("dp"), lax.axis_index("mp")
        _, rows, cols = dm.axes
        self.place = (self.rank // (rows * cols), (self.rank // cols) % rows, self.rank % cols)

    def device(self, *offsets):
        z, y, x = ((here + o) % size for here, o, size in zip(self.place, offsets, self.dm.axes))
        return ((z * self.dm.axes[1] + y) * self.dm.axes[2] + x, self.core)

    def sibling(self):
        return (self.rank, 1 - self.core)

    def on_axis(self, axis, offset):
        return self.device(*(offset if axis == k else 0 for k in range(3)))

    def along(self, axis, offset):
        return (self.place[axis] + offset) % self.dm.axes[axis]

    def partners(self):
        depth = self.dm.axes[0]
        found = [self.sibling()]
        found += [self.device(o, 0, 0) for o in range(1, depth)]
        return found + [self.device(0, *o) for o in self.plane()]

    def plane(self):
        _, rows, cols = self.dm.axes
        return [(p, q) for p in range(rows) for q in range(cols) if p or q]

    def greet(self, semaphore):
        for partner in self.partners():
            pl.semaphore_signal(semaphore, inc=1, device_id=partner, device_id_type=MESH)

    def met(self, semaphore):
        pl.semaphore_wait(semaphore, len(self.partners()))

    def copy(self, key, layer, source, target, device):
        name, count, index = key
        if name not in self.keys:
            used = sum(n for _, n in self.keys.values()) * self.dm.layers
            self.keys[name] = (used, count)
        first, known = self.keys[name]
        assert known == count
        number = first + layer * count + index
        return pltpu.make_async_remote_copy(
            src_ref=source,
            dst_ref=target,
            send_sem=self.s.send_sems.at[number],
            recv_sem=self.s.recv_sems.at[number],
            device_id=device,
            device_id_type=MESH,
        )


def copies_needed(dm):
    depth, rows, cols = dm.axes
    cross = depth * (cols + rows - 2)
    vectors = 1 + (depth - 1) + (rows * cols - 1)
    ends = depth - 1 + rows * cols - 1
    return dm.layers * (depth - 1 + 2 * cross + ends + 6 + 2 + vectors + 1 + 2 * dm.images)


def start_all(copies):
    for copy in copies:
        copy.start()


def wait_all(copies):
    for copy in copies:
        copy.wait()


class Parts:
    def __init__(self, dm, net, s, layer):
        self.dm, self.net, self.s, self.layer, self.buf = dm, net, s, layer, s.gath.at[layer]
        self.most = pl.ds(0, dm.most_rows)
        self.head = pl.ds(0, dm.first_rows)
        self.tail = pl.ds(dm.first_rows, dm.most_rows - dm.first_rows)
        self.last = pl.ds(dm.most_rows, dm.last_rows)

    def pairs(self, name, layer, piece, parts):
        copies = []
        _, rows, cols = self.dm.axes
        count = rows + cols - 2
        for axis, make in parts:
            for o in range(1, self.dm.axes[axis]):
                key = (name, self.dm.axes[0] * count, piece * count + len(copies))
                source, target = make(self.net.along(axis, o), o - 1)
                copies.append(
                    self.net.copy(key, layer, source, target, self.net.on_axis(axis, o))
                )
        return copies

    def plane(self, layer, make):
        offsets = self.net.plane()
        copies = []
        for n, (p, q) in enumerate(offsets):
            source, target = make(self.net.along(1, p), self.net.along(2, q), n)
            copies.append(
                self.net.copy(
                    ("ends", len(offsets), n), layer, source, target, self.net.device(0, p, q)
                )
            )
        return copies


class Gather(Parts):
    def one(self, offset):
        ref = self.buf.at[(*self.net.place, self.most)]
        key = ("one", self.dm.axes[0] - 1, offset - 1)
        return [self.net.copy(key, self.layer, ref, ref, self.net.on_axis(0, offset))]

    def two(self, piece):
        at, (_, y, x) = self.net.along(0, -piece), self.net.place
        a, b = self.buf.at[at, y, x, self.head], self.buf.at[at, y, x, self.tail]
        return self.pairs(
            "two", self.layer, piece, [(2, lambda to, n: (a, a)), (1, lambda to, n: (b, b))]
        )

    def three(self, piece):
        at, (_, y, x) = self.net.along(0, -piece), self.net.place
        a, b = self.buf.at[at, y, :, self.head], self.buf.at[at, :, x, self.tail]
        return self.pairs(
            "three", self.layer, piece, [(1, lambda to, n: (a, a)), (2, lambda to, n: (b, b))]
        )

    def near(self):
        if not self.dm.last_rows:
            return []
        ref = self.buf.at[(*self.net.place, self.last)]
        return self.plane(self.layer, lambda y, x, n: (ref, ref))

    def far(self):
        if not self.dm.last_rows:
            return []
        ref = self.buf.at[self.net.place[0], :, :, self.last]
        size = self.dm.axes[0]
        return [
            self.net.copy(("far", size - 1, o - 1), self.layer, ref, ref, self.net.on_axis(0, o))
            for o in range(1, size)
        ]

    def along_depth(self):
        for offset in range(1, self.dm.axes[0]):
            start_all(self.one(offset))

    def begin(self):
        start_all(self.two(0))
        start_all(self.near())

    def cross(self, piece):
        wait_all(self.one(piece))
        start_all(self.two(piece))

    def spread(self, piece):
        wait_all(self.two(piece))
        start_all(self.three(piece))

    def spread_last(self):
        wait_all(self.near())
        start_all(self.far())

    def end(self):
        for piece in range(self.dm.axes[0]):
            wait_all(self.three(piece))
        wait_all(self.far())


class Scatter(Parts):
    def one(self, piece):
        at, s, buf = self.net.along(0, piece), self.s, self.buf
        return self.pairs(
            "three",
            0,
            piece,
            [
                (1, lambda to, n: (buf.at[at, to, :, self.head], s.one_a.at[piece, n])),
                (2, lambda to, n: (buf.at[at, :, to, self.tail], s.one_b.at[piece, n])),
            ],
        )

    def two(self, piece):
        at, s, buf, (_, y, x) = self.net.along(0, piece), self.s, self.buf, self.net.place
        return self.pairs(
            "two",
            0,
            piece,
            [
                (2, lambda to, n: (buf.at[at, y, to, self.head], s.two_a.at[piece, n])),
                (1, lambda to, n: (buf.at[at, to, x, self.tail], s.two_b.at[piece, n])),
            ],
        )

    def three(self, piece):
        _, y, x = self.net.place
        source = self.buf.at[self.net.along(0, piece), y, x, self.most]
        target = self.s.three.at[self.layer, piece - 1]
        key = ("one", self.dm.axes[0] - 1, piece - 1)
        turn = self.dm.layers - 1 - self.layer
        return self.net.copy(key, turn, source, target, self.net.device(piece, 0, 0))

    def far(self, piece):
        source = self.buf.at[self.net.along(0, piece), :, :, self.last]
        key = ("far", self.dm.axes[0] - 1, piece - 1)
        return self.net.copy(key, 0, source, self.s.far.at[piece - 1], self.net.device(piece, 0, 0))

    def near(self):
        z = self.net.place[0]
        return self.plane(0, lambda y, x, n: (self.buf.at[z, y, x, self.last], self.s.near.at[n]))

    def add(self, at, parts):
        value = self.buf[at].astype(F32)
        for part in parts:
            value = value + part.astype(F32)
        self.buf[at] = value.astype(BF16)

    def begin(self, piece):
        if self.dm.last_rows:

            @pl.when(piece > 0)
            def _():
                self.far(piece).start()

        start_all(self.one(piece))

    def second(self, piece):
        _, rows, cols = self.dm.axes
        at, s, (_, y, x) = self.net.along(0, piece), self.s, self.net.place
        wait_all(self.one(piece))
        self.add((at, y, slice(None), self.head), [s.one_a[piece, o] for o in range(rows - 1)])
        self.add((at, slice(None), x, self.tail), [s.one_b[piece, o] for o in range(cols - 1)])
        start_all(self.two(piece))

    def third(self, piece):
        _, rows, cols = self.dm.axes
        at, s, (_, y, x) = self.net.along(0, piece), self.s, self.net.place
        wait_all(self.two(piece))
        self.add((at, y, x, self.head), [s.two_a[piece, o] for o in range(cols - 1)])
        self.add((at, y, x, self.tail), [s.two_b[piece, o] for o in range(rows - 1)])

        @pl.when(piece > 0)
        def _():
            self.three(piece).start()

    def second_last(self):
        if self.dm.last_rows:
            pieces = range(1, self.dm.axes[0])
            wait_all([self.far(piece) for piece in pieces])
            z = self.net.place[0]
            at = (z, slice(None), slice(None), self.last)
            self.add(at, [self.s.far[piece - 1] for piece in pieces])
            start_all(self.near())

    def third_last(self):
        if self.dm.last_rows:
            copies = self.near()
            wait_all(copies)
            self.add((*self.net.place, self.last), [self.s.near[n] for n in range(len(copies))])

    def end(self):
        value = self.buf[(*self.net.place, self.most)].astype(F32)
        for piece in range(1, self.dm.axes[0]):
            self.three(piece).wait()
            value = value + self.s.three[self.layer, piece - 1].astype(F32)
        self.s.rows[self.most, :] = value
        if self.dm.last_rows:
            self.s.rows[self.last, :] = self.buf[(*self.net.place, self.last)].astype(F32)


class Totals:
    def __init__(self, dm, net, s, layer, first):
        self.dm, self.net, self.s, self.layer, self.first = dm, net, s, layer, first

    def across(self):
        s, layer = self.s, self.layer
        copy = self.net.copy(
            ("cores", 1, 0), layer, s.vec_grad.at[layer], s.vec_back.at[layer], self.net.sibling()
        )
        return [copy]

    def plane(self):
        _, y, x = self.net.place
        here = self.s.vec_p.at[self.layer, y * self.dm.axes[2] + x]
        offsets = self.net.plane()
        return [
            self.net.copy(("plane", len(offsets), n), self.layer, here, here, self.net.device(0, *o))
            for n, o in enumerate(offsets)
        ]

    def depth(self):
        here = self.s.vec_z.at[self.layer, self.net.place[0]]
        size = self.dm.axes[0]
        return [
            self.net.copy(("depth", size - 1, o - 1), self.layer, here, here, self.net.on_axis(0, o))
            for o in range(1, size)
        ]

    def begin(self):
        start_all(self.across())

    def second(self):
        s, layer, (_, y, x) = self.s, self.layer, self.net.place
        wait_all(self.across())
        value = unpack_vectors(self.dm, s.vec_grad[layer] + s.vec_back[layer], self.first)
        s.vec_p[layer, y * self.dm.axes[2] + x] = value
        start_all(self.plane())

    def third(self):
        s, layer = self.s, self.layer
        wait_all(self.plane())
        value = s.vec_p[layer, 0]
        for o in range(1, self.dm.axes[1] * self.dm.axes[2]):
            value = value + s.vec_p[layer, o]
        s.vec_z[layer, self.net.place[0]] = value
        start_all(self.depth())

    def end(self):
        wait_all(self.depth())
        value = self.s.vec_z[self.layer, 0]
        for o in range(1, self.dm.axes[0]):
            value = value + self.s.vec_z[self.layer, o]
        return value


class Refs:
    pass


def scratch_shapes(dm, operands=None):
    layers, tokens, width, wide = dm.layers, dm.tokens, dm.width, HEADS * HD
    depth, rows, cols = dm.axes
    head, tail = dm.first_rows, dm.most_rows - dm.first_rows
    vmem, copies = pltpu.VMEM, copies_needed(dm)
    return dict(
        hid=vmem((tokens, width), F32),
        mid=vmem((tokens, width), F32),
        columns=vmem((tokens, 8), F32),
        devs=vmem((layers, tokens, 8), F32),
        low_a=vmem((layers, tokens, width), BF16),
        low_b=vmem((layers, tokens, width), BF16),
        low_g=vmem((tokens, width), BF16),
        hat_a=vmem((layers, tokens, width), F32),
        hat_b=vmem((layers, tokens, width), F32),
        qkv=vmem((layers, tokens, 3 * wide), BF16),
        probs=vmem((layers, dm.images * HEADS, dm.pad_seq, dm.pad_seq), BF16),
        att=vmem((layers, tokens, wide), BF16),
        act=vmem((layers, tokens, FF), BF16),
        slope=vmem((layers, tokens, FF), BF16),
        w_qkv=vmem((layers, 3 * wide, width), BF16),
        w_out=vmem((layers, wide, width), BF16),
        w_up=vmem((layers, FF, width), BF16),
        w_down=vmem((layers, FF, width), BF16),
        grads=vmem((dm.halves, dm.groups, dm.group_js, dm.blocks, width), BF16),
        grads_in=vmem((dm.groups, dm.group_js, dm.blocks, width), BF16),
        gath=vmem((layers, depth, rows, cols, dm.shard_rows, width), BF16),
        one_a=vmem((depth, rows - 1, cols, head, width), BF16),
        one_b=vmem((depth, cols - 1, rows, tail, width), BF16),
        two_a=vmem((depth, cols - 1, head, width), BF16),
        two_b=vmem((depth, rows - 1, tail, width), BF16),
        three=vmem((layers, depth - 1, dm.most_rows, width), BF16),
        far=vmem((depth - 1, rows, cols, max(16, dm.last_rows), width), BF16),
        near=vmem((rows * cols - 1, max(16, dm.last_rows), width), BF16),
        rows=vmem((dm.shard_rows, width), F32),
        tok_in=vmem((dm.images, dm.seq, width), F32),
        tok_out=vmem((dm.images, dm.seq, width), F32),
        codes=vmem((layers, depth, 8, dm.keys // depth), F32),
        vec_own=vmem((layers, 8, FF), F32),
        vec=vmem((layers, 8, FF), F32),
        vec_grad=vmem((layers, 8, FF), F32),
        vec_in=vmem((layers, 8, FF), F32),
        vec_back=vmem((layers, 8, FF), F32),
        vec_z=vmem((layers, depth, 8, width), F32),
        vec_p=vmem((layers, rows * cols, 8, width), F32),
        vec_sum=vmem((layers, 8, width), F32),
        keep_row=vmem((8, -(-dm.pad_seq // 128) * 128), F32),
        send_sems=pltpu.SemaphoreType.DMA((copies,)),
        recv_sems=pltpu.SemaphoreType.DMA((copies,)),
        load_sems=pltpu.SemaphoreType.DMA((dm.images,)),
        input_sems=pltpu.SemaphoreType.DMA((4,)),
        **{name: vmem(array.shape, array.dtype) for name, array in (operands or {}).items()},
        store_sems=pltpu.SemaphoreType.DMA((dm.images,)),
        credit=pltpu.SemaphoreType.REGULAR,
        core_credit=pltpu.SemaphoreType.REGULAR,
    )


def load_tokens(dm, source, target, scale=None):
    tail = dm.pad_seq - 16
    for image in range(dm.images):
        start = image * dm.pad_seq
        target[start + tail : start + dm.pad_seq, :] = jnp.zeros((16, dm.width), F32)
        value = source[image]
        if scale is not None:
            value = value * scale[start : start + dm.seq, 0:1]
        target[start : start + dm.seq, :] = value


class Tokens:
    def __init__(self, dm, net, s):
        self.dm, self.net, self.s = dm, net, s

    def image(self, ref, number):
        return ref.at[:, self.net.core * self.dm.images + number]

    def load(self, ref):
        sems = self.s.load_sems
        return [
            pltpu.make_async_copy(self.image(ref, i), self.s.tok_in.at[i], sems.at[i])
            for i in range(self.dm.images)
        ]

    def store(self, ref, turn):
        copies = []
        for i in range(self.dm.images):
            source, target = self.s.tok_out.at[i], self.image(ref, i)
            copies.append(pltpu.make_async_copy(source, target, self.s.store_sems.at[i]))
            key = ("tokens", self.dm.images, i)
            copies.append(self.net.copy(key, turn, source, target, self.net.sibling()))
        return copies


def prepare_keep(dm, keep_mask, first, s):
    kept = keep_mask[...].astype(F32)
    kept = jnp.where(first, kept[: dm.images], kept[dm.images :])
    s.keep_row[...] = jnp.zeros(s.keep_row.shape, F32)
    s.keep_row[: dm.images, : dm.seq] = kept
    columns = jnp.transpose(s.keep_row[...])
    for image in range(dm.images):
        rows = slice(image * dm.pad_seq, (image + 1) * dm.pad_seq)
        s.columns[rows, 0:1] = columns[: dm.pad_seq, image : image + 1]


def own_shard(dm, master, net, s):
    z, y, x = net.place
    if dm.shard_rows > dm.block_rows * dm.slots:
        s.rows[...] = jnp.zeros(s.rows.shape, F32)
    for layer in range(dm.layers):
        for j in range(dm.block_rows):
            s.rows[j * dm.slots : (j + 1) * dm.slots, :] = master[0, layer, j]
        s.gath[layer, z, y, x] = s.rows[...].astype(BF16)


def step_kernel(dm, names, hidden, keep_far, cotangent, slots_far, master_far, vectors_far, acts, grad_in, matrix, vec_out, *scratch):
    s = Refs()
    for name, ref in zip(names, scratch):
        setattr(s, name, ref)
    master, vectors, slot_block, keep_mask = s.master, s.vectors, s.slot_block, s.keep_mask
    inputs = [
        pltpu.make_async_copy(far, here, s.input_sems.at[n])
        for n, (far, here) in enumerate(
            ((master_far, master), (vectors_far, vectors), (slots_far, slot_block), (keep_far, keep_mask))
        )
    ]
    net = Net(dm, s)
    first = net.core == 0
    tokens = Tokens(dm, net, s)
    cols, units, depth = dm.half_cols, dm.half_units, dm.axes[0]
    assert dm.layers == 2
    gathers = [Gather(dm, net, s, layer) for layer in range(dm.layers)]
    barrier = pltpu.get_barrier_semaphore()
    net.greet(barrier)
    start_all(inputs)
    start_all(tokens.load(hidden))
    inputs[0].wait()
    own_shard(dm, master, net, s)
    net.met(barrier)
    gathers[0].along_depth()
    gathers[0].begin()
    wait_all(inputs[1:])
    pack_vectors(dm, vectors, first, s)
    other_vec = net.copy(("vectors", 1, 0), 0, s.vec_own, s.vec_in, net.sibling())
    other_vec.start()
    prepare_codes(dm, slot_block, s)
    prepare_keep(dm, keep_mask, first, s)
    wait_all(tokens.load(hidden))
    load_tokens(dm, s.tok_in, s.hid)
    start_all(tokens.load(cotangent))
    other_vec.wait()
    s.vec[...] = s.vec_own[...] + s.vec_in[...]
    gathers[0].spread(0)
    gathers[0].spread_last()
    for piece in range(1, depth):
        gathers[0].cross(piece)
        if piece > 1:
            gathers[0].spread(piece - 1)
    gathers[1].along_depth()
    gathers[0].spread(depth - 1)
    gathers[1].begin()

    def weights(layer):
        parts = [(s.w_qkv, kind * HEADS * HD + net.core * cols, cols) for kind in range(3)]
        parts += [(s.w_out, net.core * cols, cols), (s.w_up, net.core * units, units)]
        parts.append((s.w_down, net.core * units, units))
        copies = []
        for ref, start, count in parts:
            rows = ref.at[layer, pl.ds(pl.multiple_of(start, 16), count)]
            key = ("weights", len(parts), len(copies))
            copies.append(net.copy(key, layer, rows, rows, net.sibling()))
        return copies

    def forward(layer):
        shares = weights(layer)
        for name, phase in FORWARD:
            phase(dm, layer, s)
            if name == "norm":

                more = layer + 1 < dm.layers
                pl.when(more)(lambda: gathers[1].cross(1))
                Gather(dm, net, s, layer).end()

                @pl.when(more)
                def _():
                    gathers[1].spread(0)
                    gathers[1].spread_last()
                    for piece in range(2, depth // 2 + 1):
                        gathers[1].cross(piece)

                parts = permute_in(dm, layer, net.core, s)
                next(parts)
                start_all(shares[:4])
                next(parts, None)
                start_all(shares[4:])

                @pl.when(more)
                def _():
                    for piece in range(depth // 2 + 1, depth):
                        gathers[1].cross(piece)
                    for piece in range(1, depth // 2):
                        gathers[1].spread(piece)

                wait_all(shares[:3])
            if name == "attend":
                shares[3].wait()
            if name == "mid":
                shares[4].wait()
            if name == "up":
                shares[5].wait()
            if name in ("project", "attend"):
                some = depth // 4
                pieces = range(depth // 2, depth - some) if name == "project" else range(depth - some, depth)

                @pl.when(layer + 1 < dm.layers)
                def _(pieces=pieces):
                    for piece in pieces:
                        gathers[1].spread(piece)

    lax.fori_loop(0, dm.layers, lambda i, c: (forward(i), c)[1], 0)
    for image in range(dm.images):
        rows = slice(image * dm.pad_seq, image * dm.pad_seq + dm.seq)
        s.tok_out[image] = s.hid[rows, :] * s.columns[rows, 0:1]
    start_all(tokens.store(acts, 0))
    wait_all(tokens.load(cotangent))
    load_tokens(dm, s.tok_in, s.hid, s.columns)

    def put_rows(layer):
        Scatter(dm, net, s, layer).end()
        for j in range(dm.block_rows):
            matrix[0, layer, j] = s.rows[j * dm.slots : (j + 1) * dm.slots, :]

    def put_vectors(layer):
        value = Totals(dm, net, s, layer, first).end()
        for r in range(vec_out.shape[1]):
            vec_out[0, r, layer : layer + 1, :] = value[r : r + 1]

    def share(layer, number):
        start = dm.first_unit
        rows = (pl.ds(start, dm.blocks - start), pl.ds(0, start))[number]
        source, target = s.grads.at[1 - net.core, :, :, rows], s.grads_in.at[:, :, rows]
        return net.copy(("shares", 2, number), layer, source, target, net.sibling())

    def backward(turn):
        layer = dm.layers - 1 - turn
        later = turn > 0
        before = Scatter(dm, net, s, 1)
        totals_before = Totals(dm, net, s, 1, first)

        def when_later(body, *args):
            pl.when(later)(lambda: body(*args))

        order = list(range(depth - 1, -1, -1))
        for name, phase in BACKWARD:
            phase(dm, layer, s)
            if name == "start":
                for piece in range(depth // 2 - 1, -1, -1):
                    when_later(before.begin, piece)
            if name == "units":
                when_later(pl.semaphore_wait, s.core_credit, 1)
                share(layer, 0).start()
            if name in ("units", "down", "out", "attend"):
                now, order = order[: depth // 4], order[depth // 4 :]
                for piece in now:
                    when_later(before.second, piece)
            if name == "units":
                when_later(totals_before.second)
            if name == "down":
                when_later(before.second_last)
            if name == "attended":
                when_later(before.third_last)
                for piece in range(depth - 1, -1, -1):
                    when_later(before.third, piece)
                when_later(net.greet, s.credit)
                when_later(totals_before.third)
            if name == "rows":
                share(layer, 1).start()
            if name == "end":
                Totals(dm, net, s, layer, first).begin()
                wait_all([share(layer, 0), share(layer, 1)])
                fill = permute_out(dm, layer, net.core, s)
                when_later(net.met, s.credit)
                scatter = Scatter(dm, net, s, layer)

                for number in range(depth // 2):
                    pieces = [depth - 1 - 2 * number, depth - 2 - 2 * number]
                    fill([net.along(0, piece) for piece in pieces])
                    for piece in pieces if number < depth // 4 else []:
                        scatter.begin(piece)

                @pl.when(layer > 0)
                def _():
                    pl.semaphore_signal(
                        s.core_credit, inc=1, device_id=net.sibling(), device_id_type=MESH
                    )
    lax.fori_loop(0, dm.layers, lambda i, c: (backward(i), c)[1], 0)
    wait_all(tokens.store(acts, 0))
    for image in range(dm.images):
        rows = slice(image * dm.pad_seq, image * dm.pad_seq + dm.seq)
        s.tok_out[image] = s.hid[rows, :]
    start_all(tokens.store(grad_in, 1))
    scatter, totals = Scatter(dm, net, s, 0), Totals(dm, net, s, 0, first)
    events = [(totals.second,)]
    for piece in range(depth - 1, -1, -1):
        events.append((scatter.second, piece))
        if piece == depth // 2:
            events.append((totals.third,))
        if piece >= depth // 2:
            events.append((scatter.begin, piece - depth // 2))
        if piece < depth - 1:
            events.append((scatter.third, piece + 1))
    for event, *args in events:
        event(*args)
    scatter.second_last()
    scatter.third(0)
    scatter.third_last()
    put_vectors(1)
    put_rows(1)
    put_vectors(0)
    put_rows(0)
    wait_all(tokens.store(grad_in, 1))


def run_step(dm, hidden_in, keep_mask, cotangent, slot_block, master, vector_master):
    operands = dict(
        master=master, vectors=vector_master, slot_block=slot_block, keep_mask=keep_mask
    )
    shapes = scratch_shapes(dm, operands)
    out_shape = (
        jax.ShapeDtypeStruct(hidden_in.shape, F32),
        jax.ShapeDtypeStruct(hidden_in.shape, F32),
        jax.ShapeDtypeStruct(master.shape, F32),
        jax.ShapeDtypeStruct(vector_master.shape, F32),
    )
    full, far = pl.BlockSpec(memory_space=pltpu.VMEM), pl.BlockSpec(memory_space=pl.ANY)
    return pl.pallas_call(
        functools.partial(step_kernel, dm, tuple(shapes)),
        out_shape=out_shape,
        in_specs=[far] * 6,
        out_specs=[far, far, full, full],
        scratch_shapes=list(shapes.values()),
        compiler_params=pltpu.CompilerParams(
            vmem_limit_bytes=63 * 2**20, collective_id=0, has_side_effects=True
        ),
    )(hidden_in, keep_mask, cotangent, slot_block, master, vector_master)


def adam_step(weight, grad_sum, first_old, second_old, rate, decay):
    first_new = BETA_ONE * first_old + (1.0 - BETA_ONE) * grad_sum
    second_new = BETA_TWO * second_old + (1.0 - BETA_TWO) * grad_sum * grad_sum
    first_hat = first_new / (1.0 - BETA_ONE**STEP)
    second_hat = second_new / (1.0 - BETA_TWO**STEP)
    return (
        second_new,
        weight - rate * (first_hat / (jnp.sqrt(second_hat) + EPS_ADAM) + decay * weight),
    )


def finish_kernel(parts, *refs):
    large, matrix, vector = refs[:2], refs[2:6], refs[6:10]
    large_out, matrix_out, vector_out = refs[10:12], refs[12:15], refs[15:18]
    stage, matrix_in, vector_in, matrix_done, vector_done, stage_sems, load_sems, store_sems = refs[18:]
    loads, stores = [], []
    rows_all = stage.shape[1]
    size = -(-rows_all // parts)
    for start in range(0, rows_all, size):
        for number, (source, target) in enumerate(zip(large, large_out)):
            rows = pl.ds(start, min(size, rows_all - start))
            held, sem = stage.at[number, rows], stage_sems.at[len(loads)]
            loads.append(pltpu.make_async_copy(source.at[rows], held, sem))
            stores.append(pltpu.make_async_copy(held, target.at[rows], sem))
    matrix_loads = [
        pltpu.make_async_copy(ref, matrix_in.at[n], load_sems.at[n]) for n, ref in enumerate(matrix)
    ]
    vector_loads = [
        pltpu.make_async_copy(ref, vector_in.at[n], load_sems.at[4 + n]) for n, ref in enumerate(vector)
    ]
    results = [
        pltpu.make_async_copy(matrix_done.at[n], ref, store_sems.at[n])
        for n, ref in enumerate(matrix_out)
    ]
    results += [
        pltpu.make_async_copy(vector_done.at[n], ref, store_sems.at[3 + n])
        for n, ref in enumerate(vector_out)
    ]
    start_all(loads + matrix_loads + vector_loads)
    for load, store in zip(loads, stores):
        load.wait()
        store.start()
    wait_all(matrix_loads + vector_loads)

    def adam(held, done, at, rate, decay):
        grad, weight, one, two = (held[(n, *at)] for n in range(4))
        done[(0, *at)] = grad
        done[(1, *at)], done[(2, *at)] = adam_step(weight, grad, one, two, rate, decay)

    for layer in range(matrix_in.shape[2]):
        adam(matrix_in, matrix_done, (0, layer), RATE_MATRIX, DECAY_MATRIX)
    adam(vector_in, vector_done, (0,), RATE_VECTOR, 0.0)
    start_all(results)
    wait_all(stores + results)


def run_finish(acts, grad_in, matrix, vector):
    parts = 1
    far = pl.BlockSpec(memory_space=pl.ANY)
    shapes = [acts, grad_in] + [matrix[0]] * 3 + [vector[0]] * 3
    return pl.pallas_call(
        functools.partial(finish_kernel, parts),
        out_shape=tuple(jax.ShapeDtypeStruct(a.shape, F32) for a in shapes),
        in_specs=[far] * 10,
        out_specs=[far] * 8,
        scratch_shapes=[
            pltpu.VMEM((2, *acts.shape), F32),
            pltpu.VMEM((4, *matrix[0].shape), F32),
            pltpu.VMEM((4, *vector[0].shape), F32),
            pltpu.VMEM((3, *matrix[0].shape), F32),
            pltpu.VMEM((3, *vector[0].shape), F32),
            pltpu.SemaphoreType.DMA((2 * parts,)),
            pltpu.SemaphoreType.DMA((8,)),
            pltpu.SemaphoreType.DMA((6,)),
        ],
        compiler_params=pltpu.CompilerParams(vmem_limit_bytes=63 * 2**20),
    )(acts, grad_in, *matrix, *vector)


def shards(
    hidden_in, keep_mask, cotangent, slot_block, master, moment_one, moment_two, vector_master, vector_one, vector_two
):
    images, seq, width = hidden_in.shape
    halves, ranks = lax.axis_size("mp"), lax.axis_size("dp")
    dm = Dims(
        master.shape[1], images // halves, seq, width, halves, ranks, slot_block.shape[1], master.shape[3]
    )
    matrix = [array.swapaxes(2, 3) for array in (master, moment_one, moment_two)]
    vector = [array.swapaxes(1, 2) for array in (vector_master, vector_one, vector_two)]
    acts, grad_in, matrix_grad, vector_grad = run_step(
        dm, hidden_in.swapaxes(0, 1), keep_mask, cotangent.swapaxes(0, 1), slot_block, matrix[0], vector[0]
    )
    results = run_finish(acts, grad_in, [matrix_grad] + matrix, [vector_grad] + vector)
    return tuple(
        array.swapaxes(*axes)
        for array, axes in zip(results, [(0, 1)] * 2 + [(2, 3)] * 3 + [(1, 2)] * 3)
    )


def solution(mesh):
    images, rows, copied = P("dp", None, None), P("mp", None, "dp", None, None), P("mp", None, None, None)
    return jax.shard_map(
        shards,
        mesh=mesh,
        in_specs=(images, P("dp", None), images, P(), rows, rows, rows, copied, copied, copied),
        out_specs=(images, images, rows, rows, rows, copied, copied, copied),
        check_vma=False,
    )
```

```python
import functools

import jax
import jax.numpy as jnp
from jax import lax
from jax.experimental import pallas as pl
from jax.experimental.pallas import tpu as pltpu
from jax.sharding import PartitionSpec as P

HEADS = 6
HD = 64
FF = 1536
STEP = 10

EPS_NORM = 1e-06
BETA_ONE = 0.9
BETA_TWO = 0.999
RATE_MATRIX = 0.003
RATE_VECTOR = 0.01
DECAY_MATRIX = 0.05
EPS_ADAM = 1e-08
NEG_FILL = -1e30
LOG2_E = 1.4426950408889634

F32 = jnp.float32
MESH = pl.DeviceIdType.MESH
BF16 = jnp.bfloat16


def dot_nn(left, right):
    return lax.dot_general(left, right, (((1,), (0,)), ((), ())), preferred_element_type=F32)


def dot_nt(left, right):
    return lax.dot_general(left, right, (((1,), (1,)), ((), ())), preferred_element_type=F32)


def dot_tn(left, right):
    return lax.dot_general(left, right, (((0,), (0,)), ((), ())), preferred_element_type=F32)


def fold_rows(values):
    rows, cols = values.shape
    return jnp.sum(values.reshape(rows // 8, 8, cols), 0)


def loop(count, body, unroll=True):
    lax.fori_loop(0, count, lambda i, c: (body(i), c)[1], 0, unroll=unroll)


def gelu_pair(u):
    cdf = 0.5 + 0.5 * lax.erf(u * (0.5**0.5))
    slope = cdf + u * (jnp.exp(-0.5 * u * u) * 0.3989422804014327)
    return u * cdf, slope


class Dims:
    def __init__(self, layers, images, seq, width, halves, ranks, blocks, block_rows):
        self.layers, self.images, self.seq, self.width = layers, images, seq, width
        self.halves, self.ranks, self.blocks, self.block_rows = halves, ranks, blocks, block_rows
        self.pad_seq = -(-seq // 16) * 16
        self.tokens = images * self.pad_seq
        self.slots = blocks // ranks
        side = 1
        while side**3 * 8 <= ranks:
            side *= 2
        self.axes = (ranks // (side * side), side, side)
        self.shard_rows = -(-block_rows * self.slots // 16) * 16
        self.last_rows = 16 * (self.shard_rows // 144)
        self.most_rows = self.shard_rows - self.last_rows
        self.first_rows = -(-self.most_rows // 32) * 16
        self.groups = block_rows // 2 if 2 * self.slots % 16 == 0 else 1
        self.group = self.shard_rows // self.groups
        self.group_js = block_rows // self.groups
        self.keys = ranks * self.group
        self.half_cols = HEADS * HD // halves
        self.half_units = FF // halves
        self.natural = 4 * self.half_cols
        self.unit_blocks = self.half_units // block_rows
        self.kind_blocks = self.half_cols // block_rows
        self.first_unit = 4 * self.kind_blocks


def divide(values, number):
    return jnp.floor((values.astype(F32) + 0.5) * (1.0 / number))


def one_hot(rows, codes, axis):
    start, count = rows
    shape = (count, codes.shape[1]) if axis == 0 else (codes.shape[0], count)
    here = lax.broadcasted_iota(jnp.int32, shape, axis) + start
    return (here == codes.astype(jnp.int32)).astype(F32).astype(BF16)


def permute_in(dm, layer, half, s):
    cols, units, some = dm.half_cols, dm.half_units, dm.unit_blocks
    shards = [
        s.gath[layer, :, :, :, g * dm.group : (g + 1) * dm.group, :].reshape(dm.keys, dm.width)
        for g in range(dm.groups)
    ]
    code = jnp.concatenate([s.codes[layer, z] for z in range(dm.axes[0])], 1)[0:1]
    count = dm.first_unit
    starts = [odd * dm.blocks for odd in range(dm.group_js)]
    chosen = jnp.concatenate([one_hot((start, count), code, 0) for start in starts], 0)
    attention = []
    for g in range(dm.groups):
        rows = dot_nn(chosen, shards[g]).astype(BF16)
        attention += [rows[n * count : (n + 1) * count] for n in range(dm.group_js)]
    order = row_order(dm, cols, dm.kind_blocks)
    for kind in range(4):
        part = slice(kind * dm.kind_blocks, (kind + 1) * dm.kind_blocks)
        rows = dot_nn(order, jnp.concatenate([rows[part] for rows in attention], 0)).astype(BF16)
        if kind < 3:
            s.w_qkv[layer, pl.ds(pl.multiple_of(kind * HEADS * HD + half * cols, 16), cols), :] = rows
        else:
            s.w_out[layer, pl.ds(pl.multiple_of(half * cols, 16), cols), :] = rows
    yield
    for odd, start in enumerate(starts):
        chosen = one_hot((start + count, 2 * some), code, 0)
        for g in range(dm.groups):
            rows = dot_nn(chosen, shards[g]).astype(BF16)
            at = half * units + (g * dm.group_js + odd) * some
            at = pl.ds(pl.multiple_of(at, 16), some)
            s.w_up[layer, at, :] = rows[:some]
            s.w_down[layer, at, :] = rows[some:]


def put_grads(dm, s, kind, rows):
    cols, size = dm.half_cols, dm.kind_blocks
    order = row_order(dm, cols, size)
    for half in range(dm.halves):
        found = dot_tn(order, rows[half * cols : (half + 1) * cols]).astype(BF16)
        for j in range(dm.block_rows):
            s.grads[half, j // dm.group_js, j % dm.group_js, kind * size : (kind + 1) * size, :] = found[
                j * size : (j + 1) * size
            ]


def permute_out(dm, layer, half, s):
    for g in range(dm.groups):
        for odd in range(dm.group_js):
            total = s.grads[half, g, odd].astype(F32) + s.grads_in[g, odd].astype(F32)
            s.grads_in[g, odd] = total.astype(BF16)

    def pieces(places):
        codes = [jnp.transpose(s.codes[layer, z])[:, 0:1] for z in places]
        chosen = one_hot((0, dm.group_js * dm.blocks), jnp.concatenate(codes, 0), 1)
        size = chosen.shape[0] // len(places)
        for g in range(dm.groups):
            grads = s.grads_in[g].reshape(dm.group_js * dm.blocks, dm.width)
            rows = dot_nn(chosen, grads).astype(BF16)
            for n, z in enumerate(places):
                s.gath[layer, z, :, :, g * dm.group : (g + 1) * dm.group, :] = rows[
                    n * size : (n + 1) * size
                ].reshape(dm.axes[1], dm.axes[2], dm.group, dm.width)

    return pieces


def prepare_codes(dm, slot_block, s):
    layers, blocks, group = dm.layers, dm.blocks, dm.group
    block = slot_block[...].astype(F32)
    high = divide(block, 16)
    zero = jnp.zeros((16 - 2 * layers, blocks), F32)
    halves = jnp.concatenate([high, block - 16.0 * high, zero], 0).astype(BF16)
    per = dm.keys // dm.axes[0]
    size = per * max(1, 768 // per)
    for start in range(0, dm.keys, size):
        size = min(size, dm.keys - start)

        def place(shape):
            key = lax.broadcasted_iota(jnp.int32, shape, 1) + start
            rank = divide(key, group)
            inside = key.astype(F32) - rank * group
            odd = divide(inside, dm.slots)
            return rank * dm.slots + inside - odd * dm.slots, odd, inside >= dm.group_js * dm.slots

        slot, _, _ = place((blocks, size))
        same = slot == lax.broadcasted_iota(jnp.int32, (blocks, size), 0).astype(F32)
        parts = dot_nn(halves, same.astype(F32).astype(BF16))
        _, odd, padding = place((1, size))
        for layer in range(layers):
            block = 16.0 * parts[layer : layer + 1] + parts[layers + layer : layers + layer + 1]
            row = jnp.where(padding, -1.0, odd * blocks + block)
            rows = jnp.concatenate([row, jnp.zeros((7, size), F32)], 0)
            for z in range(start // per, (start + size) // per):
                s.codes[layer, z] = rows[:, z * per - start : (z + 1) * per - start]


def row_order(dm, rows, blocks):
    here = lax.broadcasted_iota(jnp.int32, (rows, rows), 1)
    inner = divide(here, blocks)
    source = (here.astype(F32) - inner * blocks) * dm.block_rows + inner
    same = source == lax.broadcasted_iota(jnp.int32, (rows, rows), 0).astype(F32)
    return same.astype(F32).astype(BF16)


def unit_order(dm):
    return row_order(dm, dm.half_units, dm.unit_blocks)


def reorder(dot, row, order):
    high = row.astype(BF16)
    rest = row - high.astype(F32)
    middle = rest.astype(BF16)
    low = (rest - middle.astype(F32)).astype(BF16)
    parts = [high.astype(F32), middle.astype(F32), low.astype(F32)]
    parts.append(jnp.zeros((13, row.shape[1]), F32))
    out = dot(jnp.concatenate(parts, 0).astype(BF16), order)
    return out[0:1] + (out[1:2] + out[2:3])


def pack_vectors(dm, vectors, first, s):
    cols, units, width = dm.half_cols, dm.half_units, dm.width
    wide = HEADS * HD
    order = unit_order(dm)
    for layer in range(dm.layers):
        rows = jnp.concatenate([vectors[0, r, layer : layer + 1, :] for r in range(6)], 0)
        flat = rows[0:1]
        q, v = flat[:, :cols], flat[:, cols : 2 * cols]
        none, mid = jnp.zeros((1, cols), F32), jnp.zeros((1, wide), F32)
        tail = jnp.zeros((1, FF - 3 * wide), F32)
        zero_half = jnp.concatenate([q, none, mid, v, none, tail], 1)
        one_half = jnp.concatenate([none, q, mid, none, v, tail], 1)
        s.vec_own[layer, 0:1, :] = jnp.where(first, zero_half, one_half)
        up = reorder(dot_nn, jnp.concatenate([rows[1:2], rows[2:3]], 1), order)
        none = jnp.zeros((1, units), F32)
        s.vec_own[layer, 1:2, :] = jnp.where(
            first, jnp.concatenate([up, none], 1), jnp.concatenate([none, up], 1)
        )
        own = jnp.concatenate([rows[3:6], jnp.zeros((3, FF - width), F32)], 1)
        none = jnp.zeros((3, FF), F32)
        s.vec_own[layer, 2:5, :] = jnp.where(first, own, none)
        s.vec_own[layer, 5:8, :] = jnp.where(first, none, own)


def unpack_vectors(dm, packed, first):
    cols, units, width = dm.half_cols, dm.half_units, dm.width
    wide = HEADS * HD
    flat = packed[0:1]
    zero_half = jnp.concatenate([flat[:, :cols], flat[:, 2 * wide : 2 * wide + cols]], 1)
    one_half = jnp.concatenate([flat[:, cols : 2 * cols], flat[:, 2 * wide + cols : 3 * wide]], 1)
    flat = packed[1:2]
    up = reorder(dot_nt, jnp.where(first, flat[:, :units], flat[:, units:]), unit_order(dm))
    own = jnp.where(first, packed[2:5, :width], packed[5:8, :width])
    return jnp.concatenate(
        [
            jnp.where(first, zero_half, one_half),
            up[:, :width],
            up[:, width:],
            own,
            jnp.zeros((2, width), F32),
        ],
        0,
    )


NORM_ROWS = 208


def norm_forward(dm, layer, source, gain, shift, low_out, hat_out, devs, place):
    def chunk(i):
        rows = pl.ds(pl.multiple_of(i * NORM_ROWS, NORM_ROWS), NORM_ROWS)
        values = source[rows, :]
        centred = values - jnp.mean(values, -1, keepdims=True)
        inv = lax.rsqrt(jnp.mean(centred * centred, -1, keepdims=True) + EPS_NORM)
        hat = centred * inv
        hat_out[layer, rows, :] = hat
        devs[layer, rows, place : place + 1] = inv
        low_out[layer, rows, :] = (hat * gain + shift).astype(BF16)

    loop(dm.tokens // NORM_ROWS, chunk)


def norm_backward(dm, layer, grad, into, gain, hat_in, devs, place):
    def chunk(i, carry):
        rows = pl.ds(pl.multiple_of(i * NORM_ROWS, NORM_ROWS), NORM_ROWS)
        out, hat, inv = grad[rows, :], hat_in[layer, rows, :], devs[layer, rows, place : place + 1]
        scaled = out * gain
        first = jnp.mean(scaled, -1, keepdims=True)
        second = jnp.mean(scaled * hat, -1, keepdims=True)
        into[rows, :] = into[rows, :] + inv * (scaled - first - hat * second)
        return carry[0] + fold_rows(out * hat), carry[1] + fold_rows(out)

    zero = jnp.zeros((8, dm.width), F32)
    gains, shifts = lax.fori_loop(0, dm.tokens // NORM_ROWS, chunk, (zero, zero), unroll=True)
    return jnp.sum(gains, 0, keepdims=True), jnp.sum(shifts, 0, keepdims=True)


def lane_halves():
    lane = lax.broadcasted_iota(jnp.int32, (1, 2 * HD), 1)
    return (lane < HD).astype(F32).astype(BF16), (lane >= HD).astype(F32).astype(BF16)


def image_rows(dm, image):
    return pl.ds(pl.multiple_of(image * dm.pad_seq, 16), dm.pad_seq)


def vector_row(dm, layer, s, row, count=None):
    return s.vec[layer, row : row + 1, : count or dm.width]


def forward_norm_a(dm, layer, s):
    gain, shift = vector_row(dm, layer, s, 2), vector_row(dm, layer, s, 3)
    norm_forward(dm, layer, s.hid, gain, shift, s.low_a, s.hat_a, s.devs, 0)


def forward_project(dm, layer, s):
    wide = HEADS * HD

    def project(image):
        rows = image_rows(dm, image)
        source = s.low_a[layer, rows, :]
        for kind in range(3):
            cols = slice(kind * wide, (kind + 1) * wide)
            value = dot_nt(source, s.w_qkv[layer, cols, :]) + s.vec[layer, 0:1, cols]
            s.qkv[layer, rows, cols] = value.astype(BF16)

    loop(dm.images, project)


def forward_attend(dm, layer, s):
    wide = HEADS * HD

    halves = lane_halves()

    def attend(image):
        rows = image_rows(dm, image)
        keep = s.columns[rows, 0:1]
        for pair in range(HEADS // 2):
            cols = slice(pair * 2 * HD, (pair + 1) * 2 * HD)
            q, k, v = (s.qkv[layer, rows, n * wide + cols.start : n * wide + cols.stop] for n in range(3))
            out = None
            for side, lanes in enumerate(halves):
                scores = dot_nt(k * lanes, q)
                scores = jnp.where(keep > 0, scores * (HD ** (-0.5) * LOG2_E), NEG_FILL)
                exponent = jnp.exp2(scores - jnp.max(scores, 0, keepdims=True))
                probs = (exponent * (1.0 / jnp.sum(exponent, 0, keepdims=True))).astype(BF16)
                s.probs[layer, image * HEADS + 2 * pair + side] = probs
                part = dot_tn(probs, v * lanes)
                out = part if out is None else out + part
            s.att[layer, rows, cols] = out.astype(BF16)

    loop(dm.images, attend)


def forward_out(dm, layer, s):
    bias = vector_row(dm, layer, s, 4)

    def out_project(image):
        rows = image_rows(dm, image)
        s.mid[rows, :] = s.hid[rows, :] + (dot_nn(s.att[layer, rows, :], s.w_out[layer]) + bias)

    loop(dm.images, out_project)


def forward_norm_b(dm, layer, s):
    gain, shift = vector_row(dm, layer, s, 5), vector_row(dm, layer, s, 6)
    norm_forward(dm, layer, s.mid, gain, shift, s.low_b, s.hat_b, s.devs, 1)


def forward_up(dm, layer, s):
    tile = 256

    def up(image):
        rows = image_rows(dm, image)
        source = s.low_b[layer, rows, :]
        for number in range(FF // tile):
            cols = slice(number * tile, (number + 1) * tile)
            u = dot_nt(source, s.w_up[layer, cols, :]) + s.vec[layer, 1:2, cols]
            act, slope = gelu_pair(u)
            s.act[layer, rows, cols] = act.astype(BF16)
            s.slope[layer, rows, cols] = slope.astype(BF16)

    loop(dm.images, up)


def forward_down(dm, layer, s):
    bias = vector_row(dm, layer, s, 7)

    def down(image):
        rows = image_rows(dm, image)
        s.hid[rows, :] = s.mid[rows, :] + (dot_nn(s.act[layer, rows, :], s.w_down[layer]) + bias)

    loop(dm.images, down)


FORWARD = (
    ("norm", forward_norm_a),
    ("project", forward_project),
    ("attend", forward_attend),
    ("out", forward_out),
    ("mid", forward_norm_b),
    ("up", forward_up),
    ("down", forward_down),
)


def low_and_sum(dm, source, target):
    def chunk(i, carry):
        rows = pl.ds(pl.multiple_of(i * NORM_ROWS, NORM_ROWS), NORM_ROWS)
        low = source[rows, :].astype(BF16)
        target[rows, :] = low
        return carry + fold_rows(low.astype(F32))

    total = lax.fori_loop(0, dm.tokens // NORM_ROWS, chunk, jnp.zeros((8, dm.width), F32), unroll=True)
    return jnp.sum(total, 0, keepdims=True)


def column_sums(dm, read, cols):
    def chunk(i, carry):
        rows = pl.ds(pl.multiple_of(i * NORM_ROWS, NORM_ROWS), NORM_ROWS)
        return carry + fold_rows(read(rows).astype(F32))

    total = lax.fori_loop(0, dm.tokens // NORM_ROWS, chunk, jnp.zeros((8, cols), F32), unroll=True)
    return jnp.sum(total, 0, keepdims=True)


def backward_start(dm, layer, s):
    s.vec_grad[layer, 7:8, : dm.width] = low_and_sum(dm, s.hid, s.low_g)


def backward_units(dm, layer, s):
    tile, some = 2 * dm.unit_blocks, dm.unit_blocks
    per_half = dm.half_units // tile

    def unit_tile(number):
        cols = pl.ds(pl.multiple_of(number * tile, tile), tile)
        grad = dot_nt(s.low_g[...], s.w_down[layer, cols, :])
        grad = (grad * s.slope[layer, :, cols].astype(F32)).astype(BF16)
        s.slope[layer, :, cols] = grad
        s.vec_grad[layer, 1:2, cols] = jnp.sum(fold_rows(grad.astype(F32)), 0, keepdims=True)
        half, first = number // per_half, (number % per_half) * 2
        down = dot_tn(s.act[layer, :, cols], s.low_g[...]).astype(BF16)
        up = dot_tn(grad, s.low_b[layer]).astype(BF16)
        for n in range(2):
            g, odd = (first + n) // dm.group_js, (first + n) % dm.group_js
            for value, start in ((up, dm.first_unit), (down, dm.first_unit + some)):
                s.grads[half, g, odd, start : start + some, :] = value[n * some : (n + 1) * some]

    loop(FF // tile, unit_tile)


def backward_down(dm, layer, s):
    def down(image):
        rows = image_rows(dm, image)
        s.mid[rows, :] = dot_nn(s.slope[layer, rows, :], s.w_up[layer])

    loop(dm.images, down)


def backward_norm_b(dm, layer, s):
    width = dm.width
    gain = vector_row(dm, layer, s, 5)
    gains, shifts = norm_backward(dm, layer, s.mid, s.hid, gain, s.hat_b, s.devs, 1)
    s.vec_grad[layer, 5:6, :width] = gains
    s.vec_grad[layer, 6:7, :width] = shifts
    s.vec_grad[layer, 4:5, :width] = low_and_sum(dm, s.hid, s.low_g)


def backward_out(dm, layer, s):
    put_grads(dm, s, 3, dot_tn(s.att[layer], s.low_g[...]).astype(BF16))

    def out_project(image):
        rows = image_rows(dm, image)
        s.att[layer, rows, :] = dot_nt(s.low_g[rows, :], s.w_out[layer]).astype(BF16)

    loop(dm.images, out_project)


def backward_attend(dm, layer, s, part):
    wide = HEADS * HD
    half = dm.images // 2

    halves = lane_halves()

    def attend(image):
        rows = image_rows(dm, image)
        keep = s.columns[rows, 0:1] * HD ** (-0.5)
        for pair in range(HEADS // 2):
            cols = slice(pair * 2 * HD, (pair + 1) * 2 * HD)
            q, k, v = (s.qkv[layer, rows, n * wide + cols.start : n * wide + cols.stop] for n in range(3))
            out = s.att[layer, rows, cols]
            parts = None
            for side, lanes in enumerate(halves):
                probs = s.probs[layer, image * HEADS + 2 * pair + side]
                grad = dot_nt(v * lanes, out)
                wide_probs = probs.astype(F32)
                total = jnp.sum(wide_probs * grad, 0, keepdims=True)
                raw = (wide_probs * (grad - total) * keep).astype(BF16)
                found = dot_tn(raw, k * lanes), dot_nn(raw, q * lanes), dot_nn(probs, out * lanes)
                parts = found if parts is None else [p + f for p, f in zip(parts, found)]
            for n, part in enumerate(parts):
                s.qkv[layer, rows, n * wide + cols.start : n * wide + cols.stop] = part.astype(BF16)

    loop(half, lambda i: attend(part * half + i))


def backward_rows(dm, layer, s):
    wide = HEADS * HD
    for kind in range(3):
        value = dot_tn(s.qkv[layer, :, kind * wide : (kind + 1) * wide], s.low_a[layer])
        put_grads(dm, s, kind, value.astype(BF16))


def backward_sums(dm, layer, s):
    wide = HEADS * HD
    for start in (0, 2 * wide):
        cols = slice(start, start + wide)
        s.vec_grad[layer, 0:1, cols] = column_sums(dm, lambda rows: s.qkv[layer, rows, cols], wide)


def backward_project(dm, layer, s):
    def project(image):
        rows = image_rows(dm, image)
        s.mid[rows, :] = dot_nn(s.qkv[layer, rows, :], s.w_qkv[layer])

    loop(dm.images, project)


def backward_norm_a(dm, layer, s):
    width = dm.width
    gain = vector_row(dm, layer, s, 2)
    gains, shifts = norm_backward(dm, layer, s.mid, s.hid, gain, s.hat_a, s.devs, 0)
    s.vec_grad[layer, 2:3, :width] = gains
    s.vec_grad[layer, 3:4, :width] = shifts


BACKWARD = (
    ("start", backward_start),
    ("units", backward_units),
    ("down", backward_down),
    ("mid", backward_norm_b),
    ("out", backward_out),
    ("attend", functools.partial(backward_attend, part=0)),
    ("attended", functools.partial(backward_attend, part=1)),
    ("rows", backward_rows),
    ("more", backward_sums),
    ("project", backward_project),
    ("end", backward_norm_a),
)


class Net:
    def __init__(self, dm, s):
        self.dm, self.s, self.keys = dm, s, {}
        self.rank, self.core = lax.axis_index("dp"), lax.axis_index("mp")
        _, rows, cols = dm.axes
        self.place = (self.rank // (rows * cols), (self.rank // cols) % rows, self.rank % cols)

    def device(self, *offsets):
        z, y, x = ((here + o) % size for here, o, size in zip(self.place, offsets, self.dm.axes))
        return ((z * self.dm.axes[1] + y) * self.dm.axes[2] + x, self.core)

    def sibling(self):
        return (self.rank, 1 - self.core)

    def on_axis(self, axis, offset):
        return self.device(*(offset if axis == k else 0 for k in range(3)))

    def along(self, axis, offset):
        return (self.place[axis] + offset) % self.dm.axes[axis]

    def partners(self):
        depth = self.dm.axes[0]
        found = [self.sibling()]
        found += [self.device(o, 0, 0) for o in range(1, depth)]
        return found + [self.device(0, *o) for o in self.plane()]

    def plane(self):
        _, rows, cols = self.dm.axes
        return [(p, q) for p in range(rows) for q in range(cols) if p or q]

    def greet(self, semaphore):
        for partner in self.partners():
            pl.semaphore_signal(semaphore, inc=1, device_id=partner, device_id_type=MESH)

    def met(self, semaphore):
        pl.semaphore_wait(semaphore, len(self.partners()))

    def copy(self, key, layer, source, target, device):
        name, count, index = key
        if name not in self.keys:
            used = sum(n for _, n in self.keys.values()) * self.dm.layers
            self.keys[name] = (used, count)
        first, known = self.keys[name]
        assert known == count
        number = first + layer * count + index
        return pltpu.make_async_remote_copy(
            src_ref=source,
            dst_ref=target,
            send_sem=self.s.send_sems.at[number],
            recv_sem=self.s.recv_sems.at[number],
            device_id=device,
            device_id_type=MESH,
        )


def copies_needed(dm):
    depth, rows, cols = dm.axes
    cross = depth * (cols + rows - 2)
    vectors = 1 + (depth - 1) + (rows * cols - 1)
    ends = depth - 1 + rows * cols - 1
    return dm.layers * (depth - 1 + 2 * cross + ends + 6 + 2 + vectors + 1 + 2 * dm.images)


def start_all(copies):
    for copy in copies:
        copy.start()


def wait_all(copies):
    for copy in copies:
        copy.wait()


class Parts:
    def __init__(self, dm, net, s, layer):
        self.dm, self.net, self.s, self.layer, self.buf = dm, net, s, layer, s.gath.at[layer]
        self.most = pl.ds(0, dm.most_rows)
        self.head = pl.ds(0, dm.first_rows)
        self.tail = pl.ds(dm.first_rows, dm.most_rows - dm.first_rows)
        self.last = pl.ds(dm.most_rows, dm.last_rows)

    def pairs(self, name, layer, piece, parts):
        copies = []
        _, rows, cols = self.dm.axes
        count = rows + cols - 2
        for axis, make in parts:
            for o in range(1, self.dm.axes[axis]):
                key = (name, self.dm.axes[0] * count, piece * count + len(copies))
                source, target = make(self.net.along(axis, o), o - 1)
                copies.append(
                    self.net.copy(key, layer, source, target, self.net.on_axis(axis, o))
                )
        return copies

    def plane(self, layer, make):
        offsets = self.net.plane()
        copies = []
        for n, (p, q) in enumerate(offsets):
            source, target = make(self.net.along(1, p), self.net.along(2, q), n)
            copies.append(
                self.net.copy(
                    ("ends", len(offsets), n), layer, source, target, self.net.device(0, p, q)
                )
            )
        return copies


class Gather(Parts):
    def one(self, offset):
        ref = self.buf.at[(*self.net.place, self.most)]
        key = ("one", self.dm.axes[0] - 1, offset - 1)
        return [self.net.copy(key, self.layer, ref, ref, self.net.on_axis(0, offset))]

    def two(self, piece):
        at, (_, y, x) = self.net.along(0, -piece), self.net.place
        a, b = self.buf.at[at, y, x, self.head], self.buf.at[at, y, x, self.tail]
        return self.pairs(
            "two", self.layer, piece, [(2, lambda to, n: (a, a)), (1, lambda to, n: (b, b))]
        )

    def three(self, piece):
        at, (_, y, x) = self.net.along(0, -piece), self.net.place
        a, b = self.buf.at[at, y, :, self.head], self.buf.at[at, :, x, self.tail]
        return self.pairs(
            "three", self.layer, piece, [(1, lambda to, n: (a, a)), (2, lambda to, n: (b, b))]
        )

    def near(self):
        if not self.dm.last_rows:
            return []
        ref = self.buf.at[(*self.net.place, self.last)]
        return self.plane(self.layer, lambda y, x, n: (ref, ref))

    def far(self):
        if not self.dm.last_rows:
            return []
        ref = self.buf.at[self.net.place[0], :, :, self.last]
        size = self.dm.axes[0]
        return [
            self.net.copy(("far", size - 1, o - 1), self.layer, ref, ref, self.net.on_axis(0, o))
            for o in range(1, size)
        ]

    def along_depth(self):
        for offset in range(1, self.dm.axes[0]):
            start_all(self.one(offset))

    def begin(self):
        start_all(self.two(0))
        start_all(self.near())

    def cross(self, piece):
        wait_all(self.one(piece))
        start_all(self.two(piece))

    def spread(self, piece):
        wait_all(self.two(piece))
        start_all(self.three(piece))

    def spread_last(self):
        wait_all(self.near())
        start_all(self.far())

    def end(self):
        for piece in range(self.dm.axes[0]):
            wait_all(self.three(piece))
        wait_all(self.far())


class Scatter(Parts):
    def one(self, piece):
        at, s, buf = self.net.along(0, piece), self.s, self.buf
        return self.pairs(
            "three",
            0,
            piece,
            [
                (1, lambda to, n: (buf.at[at, to, :, self.head], s.one_a.at[piece, n])),
                (2, lambda to, n: (buf.at[at, :, to, self.tail], s.one_b.at[piece, n])),
            ],
        )

    def two(self, piece):
        at, s, buf, (_, y, x) = self.net.along(0, piece), self.s, self.buf, self.net.place
        return self.pairs(
            "two",
            0,
            piece,
            [
                (2, lambda to, n: (buf.at[at, y, to, self.head], s.two_a.at[piece, n])),
                (1, lambda to, n: (buf.at[at, to, x, self.tail], s.two_b.at[piece, n])),
            ],
        )

    def three(self, piece):
        _, y, x = self.net.place
        source = self.buf.at[self.net.along(0, piece), y, x, self.most]
        target = self.s.three.at[self.layer, piece - 1]
        key = ("one", self.dm.axes[0] - 1, piece - 1)
        turn = self.dm.layers - 1 - self.layer
        return self.net.copy(key, turn, source, target, self.net.device(piece, 0, 0))

    def far(self, piece):
        source = self.buf.at[self.net.along(0, piece), :, :, self.last]
        key = ("far", self.dm.axes[0] - 1, piece - 1)
        return self.net.copy(key, 0, source, self.s.far.at[piece - 1], self.net.device(piece, 0, 0))

    def near(self):
        z = self.net.place[0]
        return self.plane(0, lambda y, x, n: (self.buf.at[z, y, x, self.last], self.s.near.at[n]))

    def add(self, at, parts):
        value = self.buf[at].astype(F32)
        for part in parts:
            value = value + part.astype(F32)
        self.buf[at] = value.astype(BF16)

    def begin(self, piece):
        if self.dm.last_rows:

            @pl.when(piece > 0)
            def _():
                self.far(piece).start()

        start_all(self.one(piece))

    def second(self, piece):
        _, rows, cols = self.dm.axes
        at, s, (_, y, x) = self.net.along(0, piece), self.s, self.net.place
        wait_all(self.one(piece))
        self.add((at, y, slice(None), self.head), [s.one_a[piece, o] for o in range(rows - 1)])
        self.add((at, slice(None), x, self.tail), [s.one_b[piece, o] for o in range(cols - 1)])
        start_all(self.two(piece))

    def third(self, piece):
        _, rows, cols = self.dm.axes
        at, s, (_, y, x) = self.net.along(0, piece), self.s, self.net.place
        wait_all(self.two(piece))
        self.add((at, y, x, self.head), [s.two_a[piece, o] for o in range(cols - 1)])
        self.add((at, y, x, self.tail), [s.two_b[piece, o] for o in range(rows - 1)])

        @pl.when(piece > 0)
        def _():
            self.three(piece).start()

    def second_last(self):
        if self.dm.last_rows:
            pieces = range(1, self.dm.axes[0])
            wait_all([self.far(piece) for piece in pieces])
            z = self.net.place[0]
            at = (z, slice(None), slice(None), self.last)
            self.add(at, [self.s.far[piece - 1] for piece in pieces])
            start_all(self.near())

    def third_last(self):
        if self.dm.last_rows:
            copies = self.near()
            wait_all(copies)
            self.add((*self.net.place, self.last), [self.s.near[n] for n in range(len(copies))])

    def end(self):
        value = self.buf[(*self.net.place, self.most)].astype(F32)
        for piece in range(1, self.dm.axes[0]):
            self.three(piece).wait()
            value = value + self.s.three[self.layer, piece - 1].astype(F32)
        self.s.rows[self.most, :] = value
        if self.dm.last_rows:
            self.s.rows[self.last, :] = self.buf[(*self.net.place, self.last)].astype(F32)


class Totals:
    def __init__(self, dm, net, s, layer, first):
        self.dm, self.net, self.s, self.layer, self.first = dm, net, s, layer, first

    def across(self):
        s, layer = self.s, self.layer
        copy = self.net.copy(
            ("cores", 1, 0), layer, s.vec_grad.at[layer], s.vec_back.at[layer], self.net.sibling()
        )
        return [copy]

    def plane(self):
        _, y, x = self.net.place
        here = self.s.vec_p.at[self.layer, y * self.dm.axes[2] + x]
        offsets = self.net.plane()
        return [
            self.net.copy(("plane", len(offsets), n), self.layer, here, here, self.net.device(0, *o))
            for n, o in enumerate(offsets)
        ]

    def depth(self):
        here = self.s.vec_z.at[self.layer, self.net.place[0]]
        size = self.dm.axes[0]
        return [
            self.net.copy(("depth", size - 1, o - 1), self.layer, here, here, self.net.on_axis(0, o))
            for o in range(1, size)
        ]

    def begin(self):
        start_all(self.across())

    def second(self):
        s, layer, (_, y, x) = self.s, self.layer, self.net.place
        wait_all(self.across())
        value = unpack_vectors(self.dm, s.vec_grad[layer] + s.vec_back[layer], self.first)
        s.vec_p[layer, y * self.dm.axes[2] + x] = value
        start_all(self.plane())

    def third(self):
        s, layer = self.s, self.layer
        wait_all(self.plane())
        value = s.vec_p[layer, 0]
        for o in range(1, self.dm.axes[1] * self.dm.axes[2]):
            value = value + s.vec_p[layer, o]
        s.vec_z[layer, self.net.place[0]] = value
        start_all(self.depth())

    def end(self):
        wait_all(self.depth())
        value = self.s.vec_z[self.layer, 0]
        for o in range(1, self.dm.axes[0]):
            value = value + self.s.vec_z[self.layer, o]
        return value


class Refs:
    pass


def scratch_shapes(dm, operands=None):
    layers, tokens, width, wide = dm.layers, dm.tokens, dm.width, HEADS * HD
    depth, rows, cols = dm.axes
    head, tail = dm.first_rows, dm.most_rows - dm.first_rows
    vmem, copies = pltpu.VMEM, copies_needed(dm)
    return dict(
        hid=vmem((tokens, width), F32),
        mid=vmem((tokens, width), F32),
        columns=vmem((tokens, 8), F32),
        devs=vmem((layers, tokens, 8), F32),
        low_a=vmem((layers, tokens, width), BF16),
        low_b=vmem((layers, tokens, width), BF16),
        low_g=vmem((tokens, width), BF16),
        hat_a=vmem((layers, tokens, width), F32),
        hat_b=vmem((layers, tokens, width), F32),
        qkv=vmem((layers, tokens, 3 * wide), BF16),
        probs=vmem((layers, dm.images * HEADS, dm.pad_seq, dm.pad_seq), BF16),
        att=vmem((layers, tokens, wide), BF16),
        act=vmem((layers, tokens, FF), BF16),
        slope=vmem((layers, tokens, FF), BF16),
        w_qkv=vmem((layers, 3 * wide, width), BF16),
        w_out=vmem((layers, wide, width), BF16),
        w_up=vmem((layers, FF, width), BF16),
        w_down=vmem((layers, FF, width), BF16),
        grads=vmem((dm.halves, dm.groups, dm.group_js, dm.blocks, width), BF16),
        grads_in=vmem((dm.groups, dm.group_js, dm.blocks, width), BF16),
        gath=vmem((layers, depth, rows, cols, dm.shard_rows, width), BF16),
        one_a=vmem((depth, rows - 1, cols, head, width), BF16),
        one_b=vmem((depth, cols - 1, rows, tail, width), BF16),
        two_a=vmem((depth, cols - 1, head, width), BF16),
        two_b=vmem((depth, rows - 1, tail, width), BF16),
        three=vmem((layers, depth - 1, dm.most_rows, width), BF16),
        far=vmem((depth - 1, rows, cols, max(16, dm.last_rows), width), BF16),
        near=vmem((rows * cols - 1, max(16, dm.last_rows), width), BF16),
        rows=vmem((dm.shard_rows, width), F32),
        tok_in=vmem((dm.images, dm.seq, width), F32),
        tok_out=vmem((dm.images, dm.seq, width), F32),
        codes=vmem((layers, depth, 8, dm.keys // depth), F32),
        vec_own=vmem((layers, 8, FF), F32),
        vec=vmem((layers, 8, FF), F32),
        vec_grad=vmem((layers, 8, FF), F32),
        vec_in=vmem((layers, 8, FF), F32),
        vec_back=vmem((layers, 8, FF), F32),
        vec_z=vmem((layers, depth, 8, width), F32),
        vec_p=vmem((layers, rows * cols, 8, width), F32),
        vec_sum=vmem((layers, 8, width), F32),
        keep_row=vmem((8, -(-dm.pad_seq // 128) * 128), F32),
        send_sems=pltpu.SemaphoreType.DMA((copies,)),
        recv_sems=pltpu.SemaphoreType.DMA((copies,)),
        load_sems=pltpu.SemaphoreType.DMA((dm.images,)),
        input_sems=pltpu.SemaphoreType.DMA((4,)),
        **{name: vmem(array.shape, array.dtype) for name, array in (operands or {}).items()},
        store_sems=pltpu.SemaphoreType.DMA((dm.images,)),
        credit=pltpu.SemaphoreType.REGULAR,
        core_credit=pltpu.SemaphoreType.REGULAR,
    )


def load_tokens(dm, source, target, scale=None):
    tail = dm.pad_seq - 16
    for image in range(dm.images):
        start = image * dm.pad_seq
        target[start + tail : start + dm.pad_seq, :] = jnp.zeros((16, dm.width), F32)
        value = source[image]
        if scale is not None:
            value = value * scale[start : start + dm.seq, 0:1]
        target[start : start + dm.seq, :] = value


class Tokens:
    def __init__(self, dm, net, s):
        self.dm, self.net, self.s = dm, net, s

    def image(self, ref, number):
        return ref.at[:, self.net.core * self.dm.images + number]

    def load(self, ref):
        sems = self.s.load_sems
        return [
            pltpu.make_async_copy(self.image(ref, i), self.s.tok_in.at[i], sems.at[i])
            for i in range(self.dm.images)
        ]

    def store(self, ref, turn):
        copies = []
        for i in range(self.dm.images):
            source, target = self.s.tok_out.at[i], self.image(ref, i)
            copies.append(pltpu.make_async_copy(source, target, self.s.store_sems.at[i]))
            key = ("tokens", self.dm.images, i)
            copies.append(self.net.copy(key, turn, source, target, self.net.sibling()))
        return copies


def prepare_keep(dm, keep_mask, first, s):
    kept = keep_mask[...].astype(F32)
    kept = jnp.where(first, kept[: dm.images], kept[dm.images :])
    s.keep_row[...] = jnp.zeros(s.keep_row.shape, F32)
    s.keep_row[: dm.images, : dm.seq] = kept
    columns = jnp.transpose(s.keep_row[...])
    for image in range(dm.images):
        rows = slice(image * dm.pad_seq, (image + 1) * dm.pad_seq)
        s.columns[rows, 0:1] = columns[: dm.pad_seq, image : image + 1]


def own_shard(dm, master, net, s):
    z, y, x = net.place
    if dm.shard_rows > dm.block_rows * dm.slots:
        s.rows[...] = jnp.zeros(s.rows.shape, F32)
    for layer in range(dm.layers):
        for j in range(dm.block_rows):
            s.rows[j * dm.slots : (j + 1) * dm.slots, :] = master[0, layer, j]
        s.gath[layer, z, y, x] = s.rows[...].astype(BF16)


def step_kernel(dm, names, hidden, keep_far, cotangent, slots_far, master_far, vectors_far, acts, grad_in, matrix, vec_out, *scratch):
    s = Refs()
    for name, ref in zip(names, scratch):
        setattr(s, name, ref)
    master, vectors, slot_block, keep_mask = s.master, s.vectors, s.slot_block, s.keep_mask
    inputs = [
        pltpu.make_async_copy(far, here, s.input_sems.at[n])
        for n, (far, here) in enumerate(
            ((master_far, master), (vectors_far, vectors), (slots_far, slot_block), (keep_far, keep_mask))
        )
    ]
    net = Net(dm, s)
    first = net.core == 0
    tokens = Tokens(dm, net, s)
    cols, units, depth = dm.half_cols, dm.half_units, dm.axes[0]
    assert dm.layers == 2
    gathers = [Gather(dm, net, s, layer) for layer in range(dm.layers)]
    barrier = pltpu.get_barrier_semaphore()
    net.greet(barrier)
    start_all(inputs)
    start_all(tokens.load(hidden))
    inputs[0].wait()
    own_shard(dm, master, net, s)
    net.met(barrier)
    gathers[0].along_depth()
    gathers[0].begin()
    wait_all(inputs[1:])
    pack_vectors(dm, vectors, first, s)
    other_vec = net.copy(("vectors", 1, 0), 0, s.vec_own, s.vec_in, net.sibling())
    other_vec.start()
    prepare_codes(dm, slot_block, s)
    gathers[0].spread(0)
    prepare_keep(dm, keep_mask, first, s)
    gathers[0].spread_last()
    gathers[0].cross(1)
    wait_all(tokens.load(hidden))
    load_tokens(dm, s.tok_in, s.hid)
    start_all(tokens.load(cotangent))
    other_vec.wait()
    s.vec[...] = s.vec_own[...] + s.vec_in[...]
    for piece in range(2, depth):
        gathers[0].cross(piece)
        gathers[0].spread(piece - 1)
    gathers[1].along_depth()
    gathers[0].spread(depth - 1)
    gathers[1].begin()

    def weights(layer):
        parts = [(s.w_qkv, kind * HEADS * HD + net.core * cols, cols) for kind in range(3)]
        parts += [(s.w_out, net.core * cols, cols), (s.w_up, net.core * units, units)]
        parts.append((s.w_down, net.core * units, units))
        copies = []
        for ref, start, count in parts:
            rows = ref.at[layer, pl.ds(pl.multiple_of(start, 16), count)]
            key = ("weights", len(parts), len(copies))
            copies.append(net.copy(key, layer, rows, rows, net.sibling()))
        return copies

    def forward(layer):
        shares = weights(layer)
        for name, phase in FORWARD:
            phase(dm, layer, s)
            if name == "norm":

                more = layer + 1 < dm.layers
                pl.when(more)(lambda: gathers[1].cross(1))
                Gather(dm, net, s, layer).end()

                @pl.when(more)
                def _():
                    gathers[1].spread(0)
                    gathers[1].spread_last()
                    for piece in range(2, depth // 2 + 1):
                        gathers[1].cross(piece)

                parts = permute_in(dm, layer, net.core, s)
                next(parts)
                start_all(shares[:4])
                next(parts, None)
                start_all(shares[4:])

                @pl.when(more)
                def _():
                    for piece in range(depth // 2 + 1, depth):
                        gathers[1].cross(piece)
                    for piece in range(1, depth // 2):
                        gathers[1].spread(piece)

                wait_all(shares[:3])
            if name == "attend":
                shares[3].wait()
            if name == "mid":
                shares[4].wait()
            if name == "up":
                shares[5].wait()
            if name in ("project", "attend"):
                some = depth // 4
                pieces = range(depth // 2, depth - some) if name == "project" else range(depth - some, depth)

                @pl.when(layer + 1 < dm.layers)
                def _(pieces=pieces):
                    for piece in pieces:
                        gathers[1].spread(piece)

    lax.fori_loop(0, dm.layers, lambda i, c: (forward(i), c)[1], 0)
    for image in range(dm.images):
        rows = slice(image * dm.pad_seq, image * dm.pad_seq + dm.seq)
        s.tok_out[image] = s.hid[rows, :] * s.columns[rows, 0:1]
    start_all(tokens.store(acts, 0))
    wait_all(tokens.load(cotangent))
    load_tokens(dm, s.tok_in, s.hid, s.columns)

    def put_rows(layer):
        Scatter(dm, net, s, layer).end()
        for j in range(dm.block_rows):
            matrix[0, layer, j] = s.rows[j * dm.slots : (j + 1) * dm.slots, :]

    def put_vectors(layer):
        value = Totals(dm, net, s, layer, first).end()
        for r in range(vec_out.shape[1]):
            vec_out[0, r, layer : layer + 1, :] = value[r : r + 1]

    def share(layer, number):
        start = dm.first_unit
        rows = (pl.ds(start, dm.blocks - start), pl.ds(0, start))[number]
        source, target = s.grads.at[1 - net.core, :, :, rows], s.grads_in.at[:, :, rows]
        return net.copy(("shares", 2, number), layer, source, target, net.sibling())

    def backward(turn):
        layer = dm.layers - 1 - turn
        later = turn > 0
        before = Scatter(dm, net, s, 1)
        totals_before = Totals(dm, net, s, 1, first)

        def when_later(body, *args):
            pl.when(later)(lambda: body(*args))

        order = list(range(depth - 1, -1, -1))
        for name, phase in BACKWARD:
            phase(dm, layer, s)
            if name == "start":
                for piece in range(depth // 2 - 1, -1, -1):
                    when_later(before.begin, piece)
            if name == "units":
                when_later(pl.semaphore_wait, s.core_credit, 1)
                share(layer, 0).start()
            if name in ("units", "down", "out", "attend"):
                now, order = order[: depth // 4], order[depth // 4 :]
                for piece in now:
                    when_later(before.second, piece)
            if name == "units":
                when_later(totals_before.second)
            if name == "down":
                when_later(before.second_last)
            if name == "attended":
                when_later(before.third_last)
                for piece in range(depth - 1, -1, -1):
                    when_later(before.third, piece)
                when_later(net.greet, s.credit)
                when_later(totals_before.third)
            if name == "rows":
                share(layer, 1).start()
            if name == "end":
                Totals(dm, net, s, layer, first).begin()
                wait_all([share(layer, 0), share(layer, 1)])
                fill = permute_out(dm, layer, net.core, s)
                when_later(net.met, s.credit)
                scatter = Scatter(dm, net, s, layer)

                for number in range(depth // 2):
                    pieces = [depth - 1 - 2 * number, depth - 2 - 2 * number]
                    fill([net.along(0, piece) for piece in pieces])
                    for piece in pieces if number < depth // 4 else []:
                        scatter.begin(piece)

                @pl.when(layer > 0)
                def _():
                    pl.semaphore_signal(
                        s.core_credit, inc=1, device_id=net.sibling(), device_id_type=MESH
                    )
    lax.fori_loop(0, dm.layers, lambda i, c: (backward(i), c)[1], 0)
    wait_all(tokens.store(acts, 0))
    for image in range(dm.images):
        rows = slice(image * dm.pad_seq, image * dm.pad_seq + dm.seq)
        s.tok_out[image] = s.hid[rows, :]
    start_all(tokens.store(grad_in, 1))
    scatter, totals = Scatter(dm, net, s, 0), Totals(dm, net, s, 0, first)
    events = [(totals.second,)]
    for piece in range(depth - 1, -1, -1):
        events.append((scatter.second, piece))
        if piece == depth // 2:
            events.append((totals.third,))
        if piece >= depth // 2:
            events.append((scatter.begin, piece - depth // 2))
        if piece < depth - 1:
            events.append((scatter.third, piece + 1))
    for event, *args in events:
        event(*args)
    scatter.second_last()
    scatter.third(0)
    scatter.third_last()
    put_vectors(1)
    put_rows(1)
    put_vectors(0)
    put_rows(0)
    wait_all(tokens.store(grad_in, 1))


def run_step(dm, hidden_in, keep_mask, cotangent, slot_block, master, vector_master):
    operands = dict(
        master=master, vectors=vector_master, slot_block=slot_block, keep_mask=keep_mask
    )
    shapes = scratch_shapes(dm, operands)
    out_shape = (
        jax.ShapeDtypeStruct(hidden_in.shape, F32),
        jax.ShapeDtypeStruct(hidden_in.shape, F32),
        jax.ShapeDtypeStruct(master.shape, F32),
        jax.ShapeDtypeStruct(vector_master.shape, F32),
    )
    full, far = pl.BlockSpec(memory_space=pltpu.VMEM), pl.BlockSpec(memory_space=pl.ANY)
    return pl.pallas_call(
        functools.partial(step_kernel, dm, tuple(shapes)),
        out_shape=out_shape,
        in_specs=[far] * 6,
        out_specs=[far, far, full, full],
        scratch_shapes=list(shapes.values()),
        compiler_params=pltpu.CompilerParams(
            vmem_limit_bytes=63 * 2**20, collective_id=0, has_side_effects=True
        ),
    )(hidden_in, keep_mask, cotangent, slot_block, master, vector_master)


def adam_step(weight, grad_sum, first_old, second_old, rate, decay):
    first_new = BETA_ONE * first_old + (1.0 - BETA_ONE) * grad_sum
    second_new = BETA_TWO * second_old + (1.0 - BETA_TWO) * grad_sum * grad_sum
    first_hat = first_new / (1.0 - BETA_ONE**STEP)
    second_hat = second_new / (1.0 - BETA_TWO**STEP)
    return (
        second_new,
        weight - rate * (first_hat / (jnp.sqrt(second_hat) + EPS_ADAM) + decay * weight),
    )


def finish_kernel(parts, *refs):
    large, matrix, vector = refs[:2], refs[2:6], refs[6:10]
    large_out, matrix_out, vector_out = refs[10:12], refs[12:15], refs[15:18]
    stage, matrix_in, vector_in, matrix_done, vector_done, stage_sems, load_sems, store_sems = refs[18:]
    loads, stores = [], []
    rows_all = stage.shape[1]
    size = -(-rows_all // parts)
    for start in range(0, rows_all, size):
        for number, (source, target) in enumerate(zip(large, large_out)):
            rows = pl.ds(start, min(size, rows_all - start))
            held, sem = stage.at[number, rows], stage_sems.at[len(loads)]
            loads.append(pltpu.make_async_copy(source.at[rows], held, sem))
            stores.append(pltpu.make_async_copy(held, target.at[rows], sem))
    matrix_loads = [
        pltpu.make_async_copy(ref, matrix_in.at[n], load_sems.at[n]) for n, ref in enumerate(matrix)
    ]
    vector_loads = [
        pltpu.make_async_copy(ref, vector_in.at[n], load_sems.at[4 + n]) for n, ref in enumerate(vector)
    ]
    results = [
        pltpu.make_async_copy(matrix_done.at[n], ref, store_sems.at[n])
        for n, ref in enumerate(matrix_out)
    ]
    results += [
        pltpu.make_async_copy(vector_done.at[n], ref, store_sems.at[3 + n])
        for n, ref in enumerate(vector_out)
    ]
    start_all(loads + matrix_loads + vector_loads)
    for load, store in zip(loads, stores):
        load.wait()
        store.start()
    wait_all(matrix_loads + vector_loads)

    def adam(held, done, at, rate, decay):
        grad, weight, one, two = (held[(n, *at)] for n in range(4))
        done[(0, *at)] = grad
        done[(1, *at)], done[(2, *at)] = adam_step(weight, grad, one, two, rate, decay)

    for layer in range(matrix_in.shape[2]):
        adam(matrix_in, matrix_done, (0, layer), RATE_MATRIX, DECAY_MATRIX)
    adam(vector_in, vector_done, (0,), RATE_VECTOR, 0.0)
    start_all(results)
    wait_all(stores + results)


def run_finish(acts, grad_in, matrix, vector):
    parts = 1
    far = pl.BlockSpec(memory_space=pl.ANY)
    shapes = [acts, grad_in] + [matrix[0]] * 3 + [vector[0]] * 3
    return pl.pallas_call(
        functools.partial(finish_kernel, parts),
        out_shape=tuple(jax.ShapeDtypeStruct(a.shape, F32) for a in shapes),
        in_specs=[far] * 10,
        out_specs=[far] * 8,
        scratch_shapes=[
            pltpu.VMEM((2, *acts.shape), F32),
            pltpu.VMEM((4, *matrix[0].shape), F32),
            pltpu.VMEM((4, *vector[0].shape), F32),
            pltpu.VMEM((3, *matrix[0].shape), F32),
            pltpu.VMEM((3, *vector[0].shape), F32),
            pltpu.SemaphoreType.DMA((2 * parts,)),
            pltpu.SemaphoreType.DMA((8,)),
            pltpu.SemaphoreType.DMA((6,)),
        ],
        compiler_params=pltpu.CompilerParams(vmem_limit_bytes=63 * 2**20),
    )(acts, grad_in, *matrix, *vector)


def shards(
    hidden_in, keep_mask, cotangent, slot_block, master, moment_one, moment_two, vector_master, vector_one, vector_two
):
    images, seq, width = hidden_in.shape
    halves, ranks = lax.axis_size("mp"), lax.axis_size("dp")
    dm = Dims(
        master.shape[1], images // halves, seq, width, halves, ranks, slot_block.shape[1], master.shape[3]
    )
    matrix = [array.swapaxes(2, 3) for array in (master, moment_one, moment_two)]
    vector = [array.swapaxes(1, 2) for array in (vector_master, vector_one, vector_two)]
    acts, grad_in, matrix_grad, vector_grad = run_step(
        dm, hidden_in.swapaxes(0, 1), keep_mask, cotangent.swapaxes(0, 1), slot_block, matrix[0], vector[0]
    )
    results = run_finish(acts, grad_in, [matrix_grad] + matrix, [vector_grad] + vector)
    return tuple(
        array.swapaxes(*axes)
        for array, axes in zip(results, [(0, 1)] * 2 + [(2, 3)] * 3 + [(1, 2)] * 3)
    )


def solution(mesh):
    images, rows, copied = P("dp", None, None), P("mp", None, "dp", None, None), P("mp", None, None, None)
    return jax.shard_map(
        shards,
        mesh=mesh,
        in_specs=(images, P("dp", None), images, P(), rows, rows, rows, copied, copied, copied),
        out_specs=(images, images, rows, rows, rows, copied, copied, copied),
        check_vma=False,
    )
```

```python
import functools

import jax
import jax.numpy as jnp
from jax import lax
from jax.experimental import pallas as pl
from jax.experimental.pallas import tpu as pltpu
from jax.sharding import PartitionSpec as P

HEADS = 6
HD = 64
FF = 1536
STEP = 10

EPS_NORM = 1e-06
BETA_ONE = 0.9
BETA_TWO = 0.999
RATE_MATRIX = 0.003
RATE_VECTOR = 0.01
DECAY_MATRIX = 0.05
EPS_ADAM = 1e-08
NEG_FILL = -1e30
LOG2_E = 1.4426950408889634

F32 = jnp.float32
MESH = pl.DeviceIdType.MESH
BF16 = jnp.bfloat16


def dot_nn(left, right):
    return lax.dot_general(left, right, (((1,), (0,)), ((), ())), preferred_element_type=F32)


def dot_nt(left, right):
    return lax.dot_general(left, right, (((1,), (1,)), ((), ())), preferred_element_type=F32)


def dot_tn(left, right):
    return lax.dot_general(left, right, (((0,), (0,)), ((), ())), preferred_element_type=F32)


def fold_rows(values):
    rows, cols = values.shape
    return jnp.sum(values.reshape(rows // 8, 8, cols), 0)


def loop(count, body, unroll=True):
    lax.fori_loop(0, count, lambda i, c: (body(i), c)[1], 0, unroll=unroll)


def gelu_pair(u):
    cdf = 0.5 + 0.5 * lax.erf(u * (0.5**0.5))
    slope = cdf + u * (jnp.exp(-0.5 * u * u) * 0.3989422804014327)
    return u * cdf, slope


class Dims:
    def __init__(self, layers, images, seq, width, halves, ranks, blocks, block_rows):
        self.layers, self.images, self.seq, self.width = layers, images, seq, width
        self.halves, self.ranks, self.blocks, self.block_rows = halves, ranks, blocks, block_rows
        self.pad_seq = -(-seq // 16) * 16
        self.tokens = images * self.pad_seq
        self.slots = blocks // ranks
        side = 1
        while side**3 * 8 <= ranks:
            side *= 2
        self.axes = (ranks // (side * side), side, side)
        self.shard_rows = -(-block_rows * self.slots // 16) * 16
        self.last_rows = 16 * (self.shard_rows // 144)
        self.most_rows = self.shard_rows - self.last_rows
        self.first_rows = -(-self.most_rows // 32) * 16
        self.groups = block_rows // 2 if 2 * self.slots % 16 == 0 else 1
        self.group = self.shard_rows // self.groups
        self.group_js = block_rows // self.groups
        self.keys = ranks * self.group
        self.half_cols = HEADS * HD // halves
        self.half_units = FF // halves
        self.natural = 4 * self.half_cols
        self.unit_blocks = self.half_units // block_rows
        self.kind_blocks = self.half_cols // block_rows
        self.first_unit = 4 * self.kind_blocks


def divide(values, number):
    return jnp.floor((values.astype(F32) + 0.5) * (1.0 / number))


def one_hot(rows, codes, axis):
    start, count = rows
    shape = (count, codes.shape[1]) if axis == 0 else (codes.shape[0], count)
    here = lax.broadcasted_iota(jnp.int32, shape, axis) + start
    return (here == codes.astype(jnp.int32)).astype(F32).astype(BF16)


def permute_in(dm, layer, half, s):
    cols, units, some = dm.half_cols, dm.half_units, dm.unit_blocks
    shards = [
        s.gath[layer, :, :, :, g * dm.group : (g + 1) * dm.group, :].reshape(dm.keys, dm.width)
        for g in range(dm.groups)
    ]
    code = jnp.concatenate([s.codes[layer, z] for z in range(dm.axes[0])], 1)[0:1]
    count = dm.first_unit
    starts = [odd * dm.blocks for odd in range(dm.group_js)]
    chosen = jnp.concatenate([one_hot((start, count), code, 0) for start in starts], 0)
    attention = []
    for g in range(dm.groups):
        rows = dot_nn(chosen, shards[g]).astype(BF16)
        attention += [rows[n * count : (n + 1) * count] for n in range(dm.group_js)]
    order = row_order(dm, cols, dm.kind_blocks)
    for kind in range(4):
        part = slice(kind * dm.kind_blocks, (kind + 1) * dm.kind_blocks)
        rows = dot_nn(order, jnp.concatenate([rows[part] for rows in attention], 0)).astype(BF16)
        if kind < 3:
            s.w_qkv[layer, pl.ds(pl.multiple_of(kind * HEADS * HD + half * cols, 16), cols), :] = rows
        else:
            s.w_out[layer, pl.ds(pl.multiple_of(half * cols, 16), cols), :] = rows
    yield
    for odd, start in enumerate(starts):
        chosen = one_hot((start + count, 2 * some), code, 0)
        for g in range(dm.groups):
            rows = dot_nn(chosen, shards[g]).astype(BF16)
            at = half * units + (g * dm.group_js + odd) * some
            at = pl.ds(pl.multiple_of(at, 16), some)
            s.w_up[layer, at, :] = rows[:some]
            s.w_down[layer, at, :] = rows[some:]


def put_grads(dm, s, kind, rows):
    cols, size = dm.half_cols, dm.kind_blocks
    order = row_order(dm, cols, size)
    for half in range(dm.halves):
        found = dot_tn(order, rows[half * cols : (half + 1) * cols]).astype(BF16)
        for j in range(dm.block_rows):
            s.grads[half, j // dm.group_js, j % dm.group_js, kind * size : (kind + 1) * size, :] = found[
                j * size : (j + 1) * size
            ]


def permute_out(dm, layer, half, s):
    for g in range(dm.groups):
        for odd in range(dm.group_js):
            total = s.grads[half, g, odd].astype(F32) + s.grads_in[g, odd].astype(F32)
            s.grads_in[g, odd] = total.astype(BF16)

    def pieces(places):
        codes = [jnp.transpose(s.codes[layer, z])[:, 0:1] for z in places]
        chosen = one_hot((0, dm.group_js * dm.blocks), jnp.concatenate(codes, 0), 1)
        size = chosen.shape[0] // len(places)
        for g in range(dm.groups):
            grads = s.grads_in[g].reshape(dm.group_js * dm.blocks, dm.width)
            rows = dot_nn(chosen, grads).astype(BF16)
            for n, z in enumerate(places):
                s.gath[layer, z, :, :, g * dm.group : (g + 1) * dm.group, :] = rows[
                    n * size : (n + 1) * size
                ].reshape(dm.axes[1], dm.axes[2], dm.group, dm.width)

    return pieces


def prepare_codes(dm, slot_block, s):
    layers, blocks, group = dm.layers, dm.blocks, dm.group
    block = slot_block[...].astype(F32)
    high = divide(block, 16)
    zero = jnp.zeros((16 - 2 * layers, blocks), F32)
    halves = jnp.concatenate([high, block - 16.0 * high, zero], 0).astype(BF16)
    per = dm.keys // dm.axes[0]
    size = per * max(1, 768 // per)
    for start in range(0, dm.keys, size):
        size = min(size, dm.keys - start)

        def place(shape):
            key = lax.broadcasted_iota(jnp.int32, shape, 1) + start
            rank = divide(key, group)
            inside = key.astype(F32) - rank * group
            odd = divide(inside, dm.slots)
            return rank * dm.slots + inside - odd * dm.slots, odd, inside >= dm.group_js * dm.slots

        slot, _, _ = place((blocks, size))
        same = slot == lax.broadcasted_iota(jnp.int32, (blocks, size), 0).astype(F32)
        parts = dot_nn(halves, same.astype(F32).astype(BF16))
        _, odd, padding = place((1, size))
        for layer in range(layers):
            block = 16.0 * parts[layer : layer + 1] + parts[layers + layer : layers + layer + 1]
            row = jnp.where(padding, -1.0, odd * blocks + block)
            rows = jnp.concatenate([row, jnp.zeros((7, size), F32)], 0)
            for z in range(start // per, (start + size) // per):
                s.codes[layer, z] = rows[:, z * per - start : (z + 1) * per - start]


def row_order(dm, rows, blocks):
    here = lax.broadcasted_iota(jnp.int32, (rows, rows), 1)
    inner = divide(here, blocks)
    source = (here.astype(F32) - inner * blocks) * dm.block_rows + inner
    same = source == lax.broadcasted_iota(jnp.int32, (rows, rows), 0).astype(F32)
    return same.astype(F32).astype(BF16)


def unit_order(dm):
    return row_order(dm, dm.half_units, dm.unit_blocks)


def reorder(dot, row, order):
    high = row.astype(BF16)
    rest = row - high.astype(F32)
    middle = rest.astype(BF16)
    low = (rest - middle.astype(F32)).astype(BF16)
    parts = [high.astype(F32), middle.astype(F32), low.astype(F32)]
    parts.append(jnp.zeros((13, row.shape[1]), F32))
    out = dot(jnp.concatenate(parts, 0).astype(BF16), order)
    return out[0:1] + (out[1:2] + out[2:3])


def pack_vectors(dm, vectors, first, s):
    cols, units, width = dm.half_cols, dm.half_units, dm.width
    wide = HEADS * HD
    order = unit_order(dm)
    for layer in range(dm.layers):
        rows = jnp.concatenate([vectors[0, r, layer : layer + 1, :] for r in range(6)], 0)
        flat = rows[0:1]
        q, v = flat[:, :cols], flat[:, cols : 2 * cols]
        none, mid = jnp.zeros((1, cols), F32), jnp.zeros((1, wide), F32)
        tail = jnp.zeros((1, FF - 3 * wide), F32)
        zero_half = jnp.concatenate([q, none, mid, v, none, tail], 1)
        one_half = jnp.concatenate([none, q, mid, none, v, tail], 1)
        s.vec_own[layer, 0:1, :] = jnp.where(first, zero_half, one_half)
        up = reorder(dot_nn, jnp.concatenate([rows[1:2], rows[2:3]], 1), order)
        none = jnp.zeros((1, units), F32)
        s.vec_own[layer, 1:2, :] = jnp.where(
            first, jnp.concatenate([up, none], 1), jnp.concatenate([none, up], 1)
        )
        own = jnp.concatenate([rows[3:6], jnp.zeros((3, FF - width), F32)], 1)
        none = jnp.zeros((3, FF), F32)
        s.vec_own[layer, 2:5, :] = jnp.where(first, own, none)
        s.vec_own[layer, 5:8, :] = jnp.where(first, none, own)


def unpack_vectors(dm, packed, first):
    cols, units, width = dm.half_cols, dm.half_units, dm.width
    wide = HEADS * HD
    flat = packed[0:1]
    zero_half = jnp.concatenate([flat[:, :cols], flat[:, 2 * wide : 2 * wide + cols]], 1)
    one_half = jnp.concatenate([flat[:, cols : 2 * cols], flat[:, 2 * wide + cols : 3 * wide]], 1)
    flat = packed[1:2]
    up = reorder(dot_nt, jnp.where(first, flat[:, :units], flat[:, units:]), unit_order(dm))
    own = jnp.where(first, packed[2:5, :width], packed[5:8, :width])
    return jnp.concatenate(
        [
            jnp.where(first, zero_half, one_half),
            up[:, :width],
            up[:, width:],
            own,
            jnp.zeros((2, width), F32),
        ],
        0,
    )


NORM_ROWS = 208


def norm_forward(dm, layer, source, gain, shift, low_out, hat_out, devs, place):
    def chunk(i):
        rows = pl.ds(pl.multiple_of(i * NORM_ROWS, NORM_ROWS), NORM_ROWS)
        values = source[rows, :]
        centred = values - jnp.mean(values, -1, keepdims=True)
        inv = lax.rsqrt(jnp.mean(centred * centred, -1, keepdims=True) + EPS_NORM)
        hat = centred * inv
        hat_out[layer, rows, :] = hat
        devs[layer, rows, place : place + 1] = inv
        low_out[layer, rows, :] = (hat * gain + shift).astype(BF16)

    loop(dm.tokens // NORM_ROWS, chunk)


def norm_backward(dm, layer, grad, into, gain, hat_in, devs, place):
    def chunk(i, carry):
        rows = pl.ds(pl.multiple_of(i * NORM_ROWS, NORM_ROWS), NORM_ROWS)
        out, hat, inv = grad[rows, :], hat_in[layer, rows, :], devs[layer, rows, place : place + 1]
        scaled = out * gain
        first = jnp.mean(scaled, -1, keepdims=True)
        second = jnp.mean(scaled * hat, -1, keepdims=True)
        into[rows, :] = into[rows, :] + inv * (scaled - first - hat * second)
        return carry[0] + fold_rows(out * hat), carry[1] + fold_rows(out)

    zero = jnp.zeros((8, dm.width), F32)
    gains, shifts = lax.fori_loop(0, dm.tokens // NORM_ROWS, chunk, (zero, zero), unroll=True)
    return jnp.sum(gains, 0, keepdims=True), jnp.sum(shifts, 0, keepdims=True)


def lane_halves():
    lane = lax.broadcasted_iota(jnp.int32, (1, 2 * HD), 1)
    return (lane < HD).astype(F32).astype(BF16), (lane >= HD).astype(F32).astype(BF16)


def image_rows(dm, image):
    return pl.ds(pl.multiple_of(image * dm.pad_seq, 16), dm.pad_seq)


def vector_row(dm, layer, s, row, count=None):
    return s.vec[layer, row : row + 1, : count or dm.width]


def forward_norm_a(dm, layer, s):
    gain, shift = vector_row(dm, layer, s, 2), vector_row(dm, layer, s, 3)
    norm_forward(dm, layer, s.hid, gain, shift, s.low_a, s.hat_a, s.devs, 0)


def forward_project(dm, layer, s):
    wide = HEADS * HD

    def project(image):
        rows = image_rows(dm, image)
        source = s.low_a[layer, rows, :]
        for kind in range(3):
            cols = slice(kind * wide, (kind + 1) * wide)
            value = dot_nt(source, s.w_qkv[layer, cols, :]) + s.vec[layer, 0:1, cols]
            s.qkv[layer, rows, cols] = value.astype(BF16)

    loop(dm.images, project)


def forward_attend(dm, layer, s):
    wide = HEADS * HD

    halves = lane_halves()

    def attend(image):
        rows = image_rows(dm, image)
        keep = s.columns[rows, 0:1]
        for pair in range(HEADS // 2):
            cols = slice(pair * 2 * HD, (pair + 1) * 2 * HD)
            q, k, v = (s.qkv[layer, rows, n * wide + cols.start : n * wide + cols.stop] for n in range(3))
            out = None
            for side, lanes in enumerate(halves):
                scores = dot_nt(k * lanes, q)
                scores = jnp.where(keep > 0, scores * (HD ** (-0.5) * LOG2_E), NEG_FILL)
                exponent = jnp.exp2(scores - jnp.max(scores, 0, keepdims=True))
                probs = (exponent * (1.0 / jnp.sum(exponent, 0, keepdims=True))).astype(BF16)
                s.probs[layer, image * HEADS + 2 * pair + side] = probs
                part = dot_tn(probs, v * lanes)
                out = part if out is None else out + part
            s.att[layer, rows, cols] = out.astype(BF16)

    loop(dm.images, attend)


def forward_out(dm, layer, s):
    bias = vector_row(dm, layer, s, 4)

    def out_project(image):
        rows = image_rows(dm, image)
        s.mid[rows, :] = s.hid[rows, :] + (dot_nn(s.att[layer, rows, :], s.w_out[layer]) + bias)

    loop(dm.images, out_project)


def forward_norm_b(dm, layer, s):
    gain, shift = vector_row(dm, layer, s, 5), vector_row(dm, layer, s, 6)
    norm_forward(dm, layer, s.mid, gain, shift, s.low_b, s.hat_b, s.devs, 1)


def forward_up(dm, layer, s):
    tile = 256

    def up(image):
        rows = image_rows(dm, image)
        source = s.low_b[layer, rows, :]
        for number in range(FF // tile):
            cols = slice(number * tile, (number + 1) * tile)
            u = dot_nt(source, s.w_up[layer, cols, :]) + s.vec[layer, 1:2, cols]
            act, slope = gelu_pair(u)
            s.act[layer, rows, cols] = act.astype(BF16)
            s.slope[layer, rows, cols] = slope.astype(BF16)

    loop(dm.images, up)


def forward_down(dm, layer, s):
    bias = vector_row(dm, layer, s, 7)

    def down(image):
        rows = image_rows(dm, image)
        s.hid[rows, :] = s.mid[rows, :] + (dot_nn(s.act[layer, rows, :], s.w_down[layer]) + bias)

    loop(dm.images, down)


FORWARD = (
    ("norm", forward_norm_a),
    ("project", forward_project),
    ("attend", forward_attend),
    ("out", forward_out),
    ("mid", forward_norm_b),
    ("up", forward_up),
    ("down", forward_down),
)


def low_and_sum(dm, source, target):
    def chunk(i, carry):
        rows = pl.ds(pl.multiple_of(i * NORM_ROWS, NORM_ROWS), NORM_ROWS)
        low = source[rows, :].astype(BF16)
        target[rows, :] = low
        return carry + fold_rows(low.astype(F32))

    total = lax.fori_loop(0, dm.tokens // NORM_ROWS, chunk, jnp.zeros((8, dm.width), F32), unroll=True)
    return jnp.sum(total, 0, keepdims=True)


def backward_start(dm, layer, s):
    s.vec_grad[layer, 7:8, : dm.width] = low_and_sum(dm, s.hid, s.low_g)


def backward_units(dm, layer, s):
    tile, some = 2 * dm.unit_blocks, dm.unit_blocks
    per_half = dm.half_units // tile

    def unit_tile(number):
        cols = pl.ds(pl.multiple_of(number * tile, tile), tile)
        grad = dot_nt(s.low_g[...], s.w_down[layer, cols, :])
        grad = (grad * s.slope[layer, :, cols].astype(F32)).astype(BF16)
        s.slope[layer, :, cols] = grad
        s.vec_grad[layer, 1:2, cols] = jnp.sum(fold_rows(grad.astype(F32)), 0, keepdims=True)
        half, first = number // per_half, (number % per_half) * 2
        down = dot_tn(s.act[layer, :, cols], s.low_g[...]).astype(BF16)
        up = dot_tn(grad, s.low_b[layer]).astype(BF16)
        for n in range(2):
            g, odd = (first + n) // dm.group_js, (first + n) % dm.group_js
            for value, start in ((up, dm.first_unit), (down, dm.first_unit + some)):
                s.grads[half, g, odd, start : start + some, :] = value[n * some : (n + 1) * some]

    loop(FF // tile, unit_tile)


def backward_down(dm, layer, s):
    def down(image):
        rows = image_rows(dm, image)
        s.mid[rows, :] = dot_nn(s.slope[layer, rows, :], s.w_up[layer])

    loop(dm.images, down)


def backward_norm_b(dm, layer, s):
    width = dm.width
    gain = vector_row(dm, layer, s, 5)
    gains, shifts = norm_backward(dm, layer, s.mid, s.hid, gain, s.hat_b, s.devs, 1)
    s.vec_grad[layer, 5:6, :width] = gains
    s.vec_grad[layer, 6:7, :width] = shifts
    s.vec_grad[layer, 4:5, :width] = low_and_sum(dm, s.hid, s.low_g)


def backward_out(dm, layer, s):
    put_grads(dm, s, 3, dot_tn(s.att[layer], s.low_g[...]).astype(BF16))

    def out_project(image):
        rows = image_rows(dm, image)
        s.att[layer, rows, :] = dot_nt(s.low_g[rows, :], s.w_out[layer]).astype(BF16)

    loop(dm.images, out_project)


def backward_attend(dm, layer, s, part):
    wide = HEADS * HD
    half = dm.images // 2

    halves = lane_halves()

    def attend(image):
        rows = image_rows(dm, image)
        keep = s.columns[rows, 0:1] * HD ** (-0.5)
        for pair in range(HEADS // 2):
            cols = slice(pair * 2 * HD, (pair + 1) * 2 * HD)
            q, k, v = (s.qkv[layer, rows, n * wide + cols.start : n * wide + cols.stop] for n in range(3))
            out = s.att[layer, rows, cols]
            parts = None
            for side, lanes in enumerate(halves):
                probs = s.probs[layer, image * HEADS + 2 * pair + side]
                grad = dot_nt(v * lanes, out)
                wide_probs = probs.astype(F32)
                total = jnp.sum(wide_probs * grad, 0, keepdims=True)
                raw = (wide_probs * (grad - total) * keep).astype(BF16)
                found = dot_tn(raw, k * lanes), dot_nn(raw, q * lanes), dot_nn(probs, out * lanes)
                parts = found if parts is None else [p + f for p, f in zip(parts, found)]
            for n, part in enumerate(parts):
                s.qkv[layer, rows, n * wide + cols.start : n * wide + cols.stop] = part.astype(BF16)

    loop(half, lambda i: attend(part * half + i))


def backward_rows(dm, layer, s):
    wide = HEADS * HD
    for kind in range(3):
        cols = slice(kind * wide, (kind + 1) * wide)
        grad = s.qkv[layer, :, cols]
        if kind != 1:
            s.vec_grad[layer, 0:1, cols] = jnp.sum(fold_rows(grad.astype(F32)), 0, keepdims=True)
        value = dot_tn(grad, s.low_a[layer])
        put_grads(dm, s, kind, value.astype(BF16))


def backward_project(dm, layer, s):
    def project(image):
        rows = image_rows(dm, image)
        s.mid[rows, :] = dot_nn(s.qkv[layer, rows, :], s.w_qkv[layer])

    loop(dm.images, project)


def backward_norm_a(dm, layer, s):
    width = dm.width
    gain = vector_row(dm, layer, s, 2)
    gains, shifts = norm_backward(dm, layer, s.mid, s.hid, gain, s.hat_a, s.devs, 0)
    s.vec_grad[layer, 2:3, :width] = gains
    s.vec_grad[layer, 3:4, :width] = shifts


BACKWARD = (
    ("start", backward_start),
    ("units", backward_units),
    ("down", backward_down),
    ("mid", backward_norm_b),
    ("out", backward_out),
    ("attend", functools.partial(backward_attend, part=0)),
    ("attended", functools.partial(backward_attend, part=1)),
    ("rows", backward_rows),
    ("project", backward_project),
    ("end", backward_norm_a),
)


class Net:
    def __init__(self, dm, s):
        self.dm, self.s, self.keys = dm, s, {}
        self.rank, self.core = lax.axis_index("dp"), lax.axis_index("mp")
        _, rows, cols = dm.axes
        self.place = (self.rank // (rows * cols), (self.rank // cols) % rows, self.rank % cols)

    def device(self, *offsets):
        z, y, x = ((here + o) % size for here, o, size in zip(self.place, offsets, self.dm.axes))
        return ((z * self.dm.axes[1] + y) * self.dm.axes[2] + x, self.core)

    def sibling(self):
        return (self.rank, 1 - self.core)

    def on_axis(self, axis, offset):
        return self.device(*(offset if axis == k else 0 for k in range(3)))

    def along(self, axis, offset):
        return (self.place[axis] + offset) % self.dm.axes[axis]

    def partners(self):
        depth = self.dm.axes[0]
        found = [self.sibling()]
        found += [self.device(o, 0, 0) for o in range(1, depth)]
        return found + [self.device(0, *o) for o in self.plane()]

    def plane(self):
        _, rows, cols = self.dm.axes
        return [(p, q) for p in range(rows) for q in range(cols) if p or q]

    def greet(self, semaphore):
        for partner in self.partners():
            pl.semaphore_signal(semaphore, inc=1, device_id=partner, device_id_type=MESH)

    def met(self, semaphore):
        pl.semaphore_wait(semaphore, len(self.partners()))

    def copy(self, key, layer, source, target, device):
        name, count, index = key
        if name not in self.keys:
            used = sum(n for _, n in self.keys.values()) * self.dm.layers
            self.keys[name] = (used, count)
        first, known = self.keys[name]
        assert known == count
        number = first + layer * count + index
        return pltpu.make_async_remote_copy(
            src_ref=source,
            dst_ref=target,
            send_sem=self.s.send_sems.at[number],
            recv_sem=self.s.recv_sems.at[number],
            device_id=device,
            device_id_type=MESH,
        )


def copies_needed(dm):
    depth, rows, cols = dm.axes
    cross = depth * (cols + rows - 2)
    vectors = 1 + (depth - 1) + (rows * cols - 1)
    ends = depth - 1 + rows * cols - 1
    return dm.layers * (depth - 1 + 2 * cross + ends + 6 + 2 + vectors + 1 + 2 * dm.images)


def start_all(copies):
    for copy in copies:
        copy.start()


def wait_all(copies):
    for copy in copies:
        copy.wait()


class Parts:
    def __init__(self, dm, net, s, layer):
        self.dm, self.net, self.s, self.layer, self.buf = dm, net, s, layer, s.gath.at[layer]
        self.most = pl.ds(0, dm.most_rows)
        self.head = pl.ds(0, dm.first_rows)
        self.tail = pl.ds(dm.first_rows, dm.most_rows - dm.first_rows)
        self.last = pl.ds(dm.most_rows, dm.last_rows)

    def pairs(self, name, layer, piece, parts):
        copies = []
        _, rows, cols = self.dm.axes
        count = rows + cols - 2
        for axis, make in parts:
            for o in range(1, self.dm.axes[axis]):
                key = (name, self.dm.axes[0] * count, piece * count + len(copies))
                source, target = make(self.net.along(axis, o), o - 1)
                copies.append(
                    self.net.copy(key, layer, source, target, self.net.on_axis(axis, o))
                )
        return copies

    def plane(self, layer, make):
        offsets = self.net.plane()
        copies = []
        for n, (p, q) in enumerate(offsets):
            source, target = make(self.net.along(1, p), self.net.along(2, q), n)
            copies.append(
                self.net.copy(
                    ("ends", len(offsets), n), layer, source, target, self.net.device(0, p, q)
                )
            )
        return copies


class Gather(Parts):
    def one(self, offset):
        ref = self.buf.at[(*self.net.place, self.most)]
        key = ("one", self.dm.axes[0] - 1, offset - 1)
        return [self.net.copy(key, self.layer, ref, ref, self.net.on_axis(0, offset))]

    def two(self, piece):
        at, (_, y, x) = self.net.along(0, -piece), self.net.place
        a, b = self.buf.at[at, y, x, self.head], self.buf.at[at, y, x, self.tail]
        return self.pairs(
            "two", self.layer, piece, [(2, lambda to, n: (a, a)), (1, lambda to, n: (b, b))]
        )

    def three(self, piece):
        at, (_, y, x) = self.net.along(0, -piece), self.net.place
        a, b = self.buf.at[at, y, :, self.head], self.buf.at[at, :, x, self.tail]
        return self.pairs(
            "three", self.layer, piece, [(1, lambda to, n: (a, a)), (2, lambda to, n: (b, b))]
        )

    def near(self):
        if not self.dm.last_rows:
            return []
        ref = self.buf.at[(*self.net.place, self.last)]
        return self.plane(self.layer, lambda y, x, n: (ref, ref))

    def far(self):
        if not self.dm.last_rows:
            return []
        ref = self.buf.at[self.net.place[0], :, :, self.last]
        size = self.dm.axes[0]
        return [
            self.net.copy(("far", size - 1, o - 1), self.layer, ref, ref, self.net.on_axis(0, o))
            for o in range(1, size)
        ]

    def along_depth(self):
        for offset in range(1, self.dm.axes[0]):
            start_all(self.one(offset))

    def begin(self):
        start_all(self.two(0))
        start_all(self.near())

    def cross(self, piece):
        wait_all(self.one(piece))
        start_all(self.two(piece))

    def spread(self, piece):
        wait_all(self.two(piece))
        start_all(self.three(piece))

    def spread_last(self):
        wait_all(self.near())
        start_all(self.far())

    def end(self):
        for piece in range(self.dm.axes[0]):
            wait_all(self.three(piece))
        wait_all(self.far())


class Scatter(Parts):
    def one(self, piece):
        at, s, buf = self.net.along(0, piece), self.s, self.buf
        return self.pairs(
            "three",
            0,
            piece,
            [
                (1, lambda to, n: (buf.at[at, to, :, self.head], s.one_a.at[piece, n])),
                (2, lambda to, n: (buf.at[at, :, to, self.tail], s.one_b.at[piece, n])),
            ],
        )

    def two(self, piece):
        at, s, buf, (_, y, x) = self.net.along(0, piece), self.s, self.buf, self.net.place
        return self.pairs(
            "two",
            0,
            piece,
            [
                (2, lambda to, n: (buf.at[at, y, to, self.head], s.two_a.at[piece, n])),
                (1, lambda to, n: (buf.at[at, to, x, self.tail], s.two_b.at[piece, n])),
            ],
        )

    def three(self, piece):
        _, y, x = self.net.place
        source = self.buf.at[self.net.along(0, piece), y, x, self.most]
        target = self.s.three.at[self.layer, piece - 1]
        key = ("one", self.dm.axes[0] - 1, piece - 1)
        turn = self.dm.layers - 1 - self.layer
        return self.net.copy(key, turn, source, target, self.net.device(piece, 0, 0))

    def far(self, piece):
        source = self.buf.at[self.net.along(0, piece), :, :, self.last]
        key = ("far", self.dm.axes[0] - 1, piece - 1)
        return self.net.copy(key, 0, source, self.s.far.at[piece - 1], self.net.device(piece, 0, 0))

    def near(self):
        z = self.net.place[0]
        return self.plane(0, lambda y, x, n: (self.buf.at[z, y, x, self.last], self.s.near.at[n]))

    def add(self, at, parts):
        value = self.buf[at].astype(F32)
        for part in parts:
            value = value + part.astype(F32)
        self.buf[at] = value.astype(BF16)

    def begin(self, piece):
        if self.dm.last_rows:

            @pl.when(piece > 0)
            def _():
                self.far(piece).start()

        start_all(self.one(piece))

    def second(self, piece):
        _, rows, cols = self.dm.axes
        at, s, (_, y, x) = self.net.along(0, piece), self.s, self.net.place
        wait_all(self.one(piece))
        self.add((at, y, slice(None), self.head), [s.one_a[piece, o] for o in range(rows - 1)])
        self.add((at, slice(None), x, self.tail), [s.one_b[piece, o] for o in range(cols - 1)])
        start_all(self.two(piece))

    def third(self, piece):
        _, rows, cols = self.dm.axes
        at, s, (_, y, x) = self.net.along(0, piece), self.s, self.net.place
        wait_all(self.two(piece))
        self.add((at, y, x, self.head), [s.two_a[piece, o] for o in range(cols - 1)])
        self.add((at, y, x, self.tail), [s.two_b[piece, o] for o in range(rows - 1)])

        @pl.when(piece > 0)
        def _():
            self.three(piece).start()

    def second_last(self):
        if self.dm.last_rows:
            pieces = range(1, self.dm.axes[0])
            wait_all([self.far(piece) for piece in pieces])
            z = self.net.place[0]
            at = (z, slice(None), slice(None), self.last)
            self.add(at, [self.s.far[piece - 1] for piece in pieces])
            start_all(self.near())

    def third_last(self):
        if self.dm.last_rows:
            copies = self.near()
            wait_all(copies)
            self.add((*self.net.place, self.last), [self.s.near[n] for n in range(len(copies))])

    def end(self):
        value = self.buf[(*self.net.place, self.most)].astype(F32)
        for piece in range(1, self.dm.axes[0]):
            self.three(piece).wait()
            value = value + self.s.three[self.layer, piece - 1].astype(F32)
        self.s.rows[self.most, :] = value
        if self.dm.last_rows:
            self.s.rows[self.last, :] = self.buf[(*self.net.place, self.last)].astype(F32)


class Totals:
    def __init__(self, dm, net, s, layer, first):
        self.dm, self.net, self.s, self.layer, self.first = dm, net, s, layer, first

    def across(self):
        s, layer = self.s, self.layer
        copy = self.net.copy(
            ("cores", 1, 0), layer, s.vec_grad.at[layer], s.vec_back.at[layer], self.net.sibling()
        )
        return [copy]

    def plane(self):
        _, y, x = self.net.place
        here = self.s.vec_p.at[self.layer, y * self.dm.axes[2] + x]
        offsets = self.net.plane()
        return [
            self.net.copy(("plane", len(offsets), n), self.layer, here, here, self.net.device(0, *o))
            for n, o in enumerate(offsets)
        ]

    def depth(self):
        here = self.s.vec_z.at[self.layer, self.net.place[0]]
        size = self.dm.axes[0]
        return [
            self.net.copy(("depth", size - 1, o - 1), self.layer, here, here, self.net.on_axis(0, o))
            for o in range(1, size)
        ]

    def begin(self):
        start_all(self.across())

    def second(self):
        s, layer, (_, y, x) = self.s, self.layer, self.net.place
        wait_all(self.across())
        value = unpack_vectors(self.dm, s.vec_grad[layer] + s.vec_back[layer], self.first)
        s.vec_p[layer, y * self.dm.axes[2] + x] = value
        start_all(self.plane())

    def third(self):
        s, layer = self.s, self.layer
        wait_all(self.plane())
        value = s.vec_p[layer, 0]
        for o in range(1, self.dm.axes[1] * self.dm.axes[2]):
            value = value + s.vec_p[layer, o]
        s.vec_z[layer, self.net.place[0]] = value
        start_all(self.depth())

    def end(self):
        wait_all(self.depth())
        value = self.s.vec_z[self.layer, 0]
        for o in range(1, self.dm.axes[0]):
            value = value + self.s.vec_z[self.layer, o]
        return value


class Refs:
    pass


def scratch_shapes(dm, operands=None):
    layers, tokens, width, wide = dm.layers, dm.tokens, dm.width, HEADS * HD
    depth, rows, cols = dm.axes
    head, tail = dm.first_rows, dm.most_rows - dm.first_rows
    vmem, copies = pltpu.VMEM, copies_needed(dm)
    return dict(
        hid=vmem((tokens, width), F32),
        mid=vmem((tokens, width), F32),
        columns=vmem((tokens, 8), F32),
        devs=vmem((layers, tokens, 8), F32),
        low_a=vmem((layers, tokens, width), BF16),
        low_b=vmem((layers, tokens, width), BF16),
        low_g=vmem((tokens, width), BF16),
        hat_a=vmem((layers, tokens, width), F32),
        hat_b=vmem((layers, tokens, width), F32),
        qkv=vmem((layers, tokens, 3 * wide), BF16),
        probs=vmem((layers, dm.images * HEADS, dm.pad_seq, dm.pad_seq), BF16),
        att=vmem((layers, tokens, wide), BF16),
        act=vmem((layers, tokens, FF), BF16),
        slope=vmem((layers, tokens, FF), BF16),
        w_qkv=vmem((layers, 3 * wide, width), BF16),
        w_out=vmem((layers, wide, width), BF16),
        w_up=vmem((layers, FF, width), BF16),
        w_down=vmem((layers, FF, width), BF16),
        grads=vmem((dm.halves, dm.groups, dm.group_js, dm.blocks, width), BF16),
        grads_in=vmem((dm.groups, dm.group_js, dm.blocks, width), BF16),
        gath=vmem((layers, depth, rows, cols, dm.shard_rows, width), BF16),
        one_a=vmem((depth, rows - 1, cols, head, width), BF16),
        one_b=vmem((depth, cols - 1, rows, tail, width), BF16),
        two_a=vmem((depth, cols - 1, head, width), BF16),
        two_b=vmem((depth, rows - 1, tail, width), BF16),
        three=vmem((layers, depth - 1, dm.most_rows, width), BF16),
        far=vmem((depth - 1, rows, cols, max(16, dm.last_rows), width), BF16),
        near=vmem((rows * cols - 1, max(16, dm.last_rows), width), BF16),
        rows=vmem((dm.shard_rows, width), F32),
        tok_in=vmem((dm.images, dm.seq, width), F32),
        tok_out=vmem((dm.images, dm.seq, width), F32),
        codes=vmem((layers, depth, 8, dm.keys // depth), F32),
        vec_own=vmem((layers, 8, FF), F32),
        vec=vmem((layers, 8, FF), F32),
        vec_grad=vmem((layers, 8, FF), F32),
        vec_in=vmem((layers, 8, FF), F32),
        vec_back=vmem((layers, 8, FF), F32),
        vec_z=vmem((layers, depth, 8, width), F32),
        vec_p=vmem((layers, rows * cols, 8, width), F32),
        vec_sum=vmem((layers, 8, width), F32),
        keep_row=vmem((8, -(-dm.pad_seq // 128) * 128), F32),
        send_sems=pltpu.SemaphoreType.DMA((copies,)),
        recv_sems=pltpu.SemaphoreType.DMA((copies,)),
        load_sems=pltpu.SemaphoreType.DMA((dm.images,)),
        input_sems=pltpu.SemaphoreType.DMA((4,)),
        **{name: vmem(array.shape, array.dtype) for name, array in (operands or {}).items()},
        store_sems=pltpu.SemaphoreType.DMA((dm.images,)),
        credit=pltpu.SemaphoreType.REGULAR,
        core_credit=pltpu.SemaphoreType.REGULAR,
    )


def load_tokens(dm, source, target, scale=None):
    tail = dm.pad_seq - 16
    for image in range(dm.images):
        start = image * dm.pad_seq
        target[start + tail : start + dm.pad_seq, :] = jnp.zeros((16, dm.width), F32)
        value = source[image]
        if scale is not None:
            value = value * scale[start : start + dm.seq, 0:1]
        target[start : start + dm.seq, :] = value


class Tokens:
    def __init__(self, dm, net, s):
        self.dm, self.net, self.s = dm, net, s

    def image(self, ref, number):
        return ref.at[:, self.net.core * self.dm.images + number]

    def load(self, ref):
        sems = self.s.load_sems
        return [
            pltpu.make_async_copy(self.image(ref, i), self.s.tok_in.at[i], sems.at[i])
            for i in range(self.dm.images)
        ]

    def store(self, ref, turn):
        copies = []
        for i in range(self.dm.images):
            source, target = self.s.tok_out.at[i], self.image(ref, i)
            copies.append(pltpu.make_async_copy(source, target, self.s.store_sems.at[i]))
            key = ("tokens", self.dm.images, i)
            copies.append(self.net.copy(key, turn, source, target, self.net.sibling()))
        return copies


def prepare_keep(dm, keep_mask, first, s):
    kept = keep_mask[...].astype(F32)
    kept = jnp.where(first, kept[: dm.images], kept[dm.images :])
    s.keep_row[...] = jnp.zeros(s.keep_row.shape, F32)
    s.keep_row[: dm.images, : dm.seq] = kept
    columns = jnp.transpose(s.keep_row[...])
    for image in range(dm.images):
        rows = slice(image * dm.pad_seq, (image + 1) * dm.pad_seq)
        s.columns[rows, 0:1] = columns[: dm.pad_seq, image : image + 1]


def own_shard(dm, master, net, s):
    z, y, x = net.place
    if dm.shard_rows > dm.block_rows * dm.slots:
        s.rows[...] = jnp.zeros(s.rows.shape, F32)
    for layer in range(dm.layers):
        for j in range(dm.block_rows):
            s.rows[j * dm.slots : (j + 1) * dm.slots, :] = master[0, layer, j]
        s.gath[layer, z, y, x] = s.rows[...].astype(BF16)


def step_kernel(dm, names, hidden, keep_far, cotangent, slots_far, master_far, vectors_far, acts, grad_in, matrix, vec_out, *scratch):
    s = Refs()
    for name, ref in zip(names, scratch):
        setattr(s, name, ref)
    master, vectors, slot_block, keep_mask = s.master, s.vectors, s.slot_block, s.keep_mask
    inputs = [
        pltpu.make_async_copy(far, here, s.input_sems.at[n])
        for n, (far, here) in enumerate(
            ((master_far, master), (vectors_far, vectors), (slots_far, slot_block), (keep_far, keep_mask))
        )
    ]
    net = Net(dm, s)
    first = net.core == 0
    tokens = Tokens(dm, net, s)
    cols, units, depth = dm.half_cols, dm.half_units, dm.axes[0]
    assert dm.layers == 2
    gathers = [Gather(dm, net, s, layer) for layer in range(dm.layers)]
    barrier = pltpu.get_barrier_semaphore()
    net.greet(barrier)
    start_all(inputs)
    start_all(tokens.load(hidden))
    inputs[0].wait()
    own_shard(dm, master, net, s)
    net.met(barrier)
    gathers[0].along_depth()
    gathers[0].begin()
    wait_all(inputs[1:])
    pack_vectors(dm, vectors, first, s)
    other_vec = net.copy(("vectors", 1, 0), 0, s.vec_own, s.vec_in, net.sibling())
    other_vec.start()
    prepare_codes(dm, slot_block, s)
    gathers[0].spread(0)
    prepare_keep(dm, keep_mask, first, s)
    gathers[0].spread_last()
    gathers[0].cross(1)
    wait_all(tokens.load(hidden))
    load_tokens(dm, s.tok_in, s.hid)
    start_all(tokens.load(cotangent))
    other_vec.wait()
    s.vec[...] = s.vec_own[...] + s.vec_in[...]
    for piece in range(2, depth):
        gathers[0].cross(piece)
        gathers[0].spread(piece - 1)
    gathers[1].along_depth()
    gathers[0].spread(depth - 1)
    gathers[1].begin()

    def weights(layer):
        parts = [(s.w_qkv, kind * HEADS * HD + net.core * cols, cols) for kind in range(3)]
        parts += [(s.w_out, net.core * cols, cols), (s.w_up, net.core * units, units)]
        parts.append((s.w_down, net.core * units, units))
        copies = []
        for ref, start, count in parts:
            rows = ref.at[layer, pl.ds(pl.multiple_of(start, 16), count)]
            key = ("weights", len(parts), len(copies))
            copies.append(net.copy(key, layer, rows, rows, net.sibling()))
        return copies

    def forward(layer):
        shares = weights(layer)
        for name, phase in FORWARD:
            phase(dm, layer, s)
            if name == "norm":

                more = layer + 1 < dm.layers
                pl.when(more)(lambda: gathers[1].cross(1))
                Gather(dm, net, s, layer).end()

                @pl.when(more)
                def _():
                    gathers[1].spread(0)
                    gathers[1].spread_last()
                    for piece in range(2, depth // 2 + 1):
                        gathers[1].cross(piece)

                parts = permute_in(dm, layer, net.core, s)
                next(parts)
                start_all(shares[:4])
                next(parts, None)
                start_all(shares[4:])

                @pl.when(more)
                def _():
                    for piece in range(depth // 2 + 1, depth):
                        gathers[1].cross(piece)
                    for piece in range(1, depth // 2):
                        gathers[1].spread(piece)

                wait_all(shares[:3])
            if name == "attend":
                shares[3].wait()
            if name == "mid":
                shares[4].wait()
            if name == "up":
                shares[5].wait()
            if name in ("project", "attend"):
                some = depth // 4
                pieces = range(depth // 2, depth - some) if name == "project" else range(depth - some, depth)

                @pl.when(layer + 1 < dm.layers)
                def _(pieces=pieces):
                    for piece in pieces:
                        gathers[1].spread(piece)

    lax.fori_loop(0, dm.layers, lambda i, c: (forward(i), c)[1], 0)
    for image in range(dm.images):
        rows = slice(image * dm.pad_seq, image * dm.pad_seq + dm.seq)
        s.tok_out[image] = s.hid[rows, :] * s.columns[rows, 0:1]
    start_all(tokens.store(acts, 0))
    wait_all(tokens.load(cotangent))
    load_tokens(dm, s.tok_in, s.hid, s.columns)

    def put_rows(layer):
        Scatter(dm, net, s, layer).end()
        for j in range(dm.block_rows):
            matrix[0, layer, j] = s.rows[j * dm.slots : (j + 1) * dm.slots, :]

    def put_vectors(layer):
        value = Totals(dm, net, s, layer, first).end()
        for r in range(vec_out.shape[1]):
            vec_out[0, r, layer : layer + 1, :] = value[r : r + 1]

    def share(layer, number):
        start = dm.first_unit
        rows = (pl.ds(start, dm.blocks - start), pl.ds(0, start))[number]
        source, target = s.grads.at[1 - net.core, :, :, rows], s.grads_in.at[:, :, rows]
        return net.copy(("shares", 2, number), layer, source, target, net.sibling())

    def backward(turn):
        layer = dm.layers - 1 - turn
        later = turn > 0
        before = Scatter(dm, net, s, 1)
        totals_before = Totals(dm, net, s, 1, first)

        def when_later(body, *args):
            pl.when(later)(lambda: body(*args))

        order = list(range(depth - 1, -1, -1))
        for name, phase in BACKWARD:
            phase(dm, layer, s)
            if name == "start":
                for piece in range(depth // 2 - 1, -1, -1):
                    when_later(before.begin, piece)
            if name == "units":
                when_later(pl.semaphore_wait, s.core_credit, 1)
                share(layer, 0).start()
            if name in ("units", "down", "out", "attend"):
                now, order = order[: depth // 4], order[depth // 4 :]
                for piece in now:
                    when_later(before.second, piece)
            if name == "units":
                when_later(totals_before.second)
            if name == "down":
                when_later(before.second_last)
            if name == "attended":
                when_later(before.third_last)
                for piece in range(depth - 1, -1, -1):
                    when_later(before.third, piece)
                when_later(net.greet, s.credit)
                when_later(totals_before.third)
            if name == "rows":
                share(layer, 1).start()
            if name == "end":
                Totals(dm, net, s, layer, first).begin()
                wait_all([share(layer, 0), share(layer, 1)])
                fill = permute_out(dm, layer, net.core, s)
                when_later(net.met, s.credit)
                scatter = Scatter(dm, net, s, layer)

                for number in range(depth // 2):
                    pieces = [depth - 1 - 2 * number, depth - 2 - 2 * number]
                    fill([net.along(0, piece) for piece in pieces])
                    for piece in pieces if number < depth // 4 else []:
                        scatter.begin(piece)

                @pl.when(layer > 0)
                def _():
                    pl.semaphore_signal(
                        s.core_credit, inc=1, device_id=net.sibling(), device_id_type=MESH
                    )
    lax.fori_loop(0, dm.layers, lambda i, c: (backward(i), c)[1], 0)
    wait_all(tokens.store(acts, 0))
    for image in range(dm.images):
        rows = slice(image * dm.pad_seq, image * dm.pad_seq + dm.seq)
        s.tok_out[image] = s.hid[rows, :]
    start_all(tokens.store(grad_in, 1))
    scatter, totals = Scatter(dm, net, s, 0), Totals(dm, net, s, 0, first)
    events = [(totals.second,)]
    for piece in range(depth - 1, -1, -1):
        events.append((scatter.second, piece))
        if piece == depth // 2:
            events.append((totals.third,))
        if piece >= depth // 2:
            events.append((scatter.begin, piece - depth // 2))
        if piece < depth - 1:
            events.append((scatter.third, piece + 1))
    for event, *args in events:
        event(*args)
    scatter.second_last()
    scatter.third(0)
    scatter.third_last()
    put_vectors(1)
    put_rows(1)
    put_vectors(0)
    put_rows(0)
    wait_all(tokens.store(grad_in, 1))


def run_step(dm, hidden_in, keep_mask, cotangent, slot_block, master, vector_master):
    operands = dict(
        master=master, vectors=vector_master, slot_block=slot_block, keep_mask=keep_mask
    )
    shapes = scratch_shapes(dm, operands)
    out_shape = (
        jax.ShapeDtypeStruct(hidden_in.shape, F32),
        jax.ShapeDtypeStruct(hidden_in.shape, F32),
        jax.ShapeDtypeStruct(master.shape, F32),
        jax.ShapeDtypeStruct(vector_master.shape, F32),
    )
    full, far = pl.BlockSpec(memory_space=pltpu.VMEM), pl.BlockSpec(memory_space=pl.ANY)
    return pl.pallas_call(
        functools.partial(step_kernel, dm, tuple(shapes)),
        out_shape=out_shape,
        in_specs=[far] * 6,
        out_specs=[far, far, full, full],
        scratch_shapes=list(shapes.values()),
        compiler_params=pltpu.CompilerParams(
            vmem_limit_bytes=63 * 2**20, collective_id=0, has_side_effects=True
        ),
    )(hidden_in, keep_mask, cotangent, slot_block, master, vector_master)


def adam_step(weight, grad_sum, first_old, second_old, rate, decay):
    first_new = BETA_ONE * first_old + (1.0 - BETA_ONE) * grad_sum
    second_new = BETA_TWO * second_old + (1.0 - BETA_TWO) * grad_sum * grad_sum
    first_hat = first_new / (1.0 - BETA_ONE**STEP)
    second_hat = second_new / (1.0 - BETA_TWO**STEP)
    return (
        second_new,
        weight - rate * (first_hat / (jnp.sqrt(second_hat) + EPS_ADAM) + decay * weight),
    )


def finish_kernel(parts, *refs):
    large, matrix, vector = refs[:2], refs[2:6], refs[6:10]
    large_out, matrix_out, vector_out = refs[10:12], refs[12:15], refs[15:18]
    stage, matrix_in, vector_in, matrix_done, vector_done, stage_sems, load_sems, store_sems = refs[18:]
    loads, stores = [], []
    rows_all = stage.shape[1]
    size = -(-rows_all // parts)
    for start in range(0, rows_all, size):
        for number, (source, target) in enumerate(zip(large, large_out)):
            rows = pl.ds(start, min(size, rows_all - start))
            held, sem = stage.at[number, rows], stage_sems.at[len(loads)]
            loads.append(pltpu.make_async_copy(source.at[rows], held, sem))
            stores.append(pltpu.make_async_copy(held, target.at[rows], sem))
    matrix_loads = [
        pltpu.make_async_copy(ref, matrix_in.at[n], load_sems.at[n]) for n, ref in enumerate(matrix)
    ]
    vector_loads = [
        pltpu.make_async_copy(ref, vector_in.at[n], load_sems.at[4 + n]) for n, ref in enumerate(vector)
    ]
    results = [
        pltpu.make_async_copy(matrix_done.at[n], ref, store_sems.at[n])
        for n, ref in enumerate(matrix_out)
    ]
    results += [
        pltpu.make_async_copy(vector_done.at[n], ref, store_sems.at[3 + n])
        for n, ref in enumerate(vector_out)
    ]
    start_all(loads + matrix_loads + vector_loads)
    for load, store in zip(loads, stores):
        load.wait()
        store.start()
    wait_all(matrix_loads + vector_loads)

    def adam(held, done, at, rate, decay):
        grad, weight, one, two = (held[(n, *at)] for n in range(4))
        done[(0, *at)] = grad
        done[(1, *at)], done[(2, *at)] = adam_step(weight, grad, one, two, rate, decay)

    for layer in range(matrix_in.shape[2]):
        adam(matrix_in, matrix_done, (0, layer), RATE_MATRIX, DECAY_MATRIX)
    adam(vector_in, vector_done, (0,), RATE_VECTOR, 0.0)
    start_all(results)
    wait_all(stores + results)


def run_finish(acts, grad_in, matrix, vector):
    parts = 1
    far = pl.BlockSpec(memory_space=pl.ANY)
    shapes = [acts, grad_in] + [matrix[0]] * 3 + [vector[0]] * 3
    return pl.pallas_call(
        functools.partial(finish_kernel, parts),
        out_shape=tuple(jax.ShapeDtypeStruct(a.shape, F32) for a in shapes),
        in_specs=[far] * 10,
        out_specs=[far] * 8,
        scratch_shapes=[
            pltpu.VMEM((2, *acts.shape), F32),
            pltpu.VMEM((4, *matrix[0].shape), F32),
            pltpu.VMEM((4, *vector[0].shape), F32),
            pltpu.VMEM((3, *matrix[0].shape), F32),
            pltpu.VMEM((3, *vector[0].shape), F32),
            pltpu.SemaphoreType.DMA((2 * parts,)),
            pltpu.SemaphoreType.DMA((8,)),
            pltpu.SemaphoreType.DMA((6,)),
        ],
        compiler_params=pltpu.CompilerParams(vmem_limit_bytes=63 * 2**20),
    )(acts, grad_in, *matrix, *vector)


def shards(
    hidden_in, keep_mask, cotangent, slot_block, master, moment_one, moment_two, vector_master, vector_one, vector_two
):
    images, seq, width = hidden_in.shape
    halves, ranks = lax.axis_size("mp"), lax.axis_size("dp")
    dm = Dims(
        master.shape[1], images // halves, seq, width, halves, ranks, slot_block.shape[1], master.shape[3]
    )
    matrix = [array.swapaxes(2, 3) for array in (master, moment_one, moment_two)]
    vector = [array.swapaxes(1, 2) for array in (vector_master, vector_one, vector_two)]
    acts, grad_in, matrix_grad, vector_grad = run_step(
        dm, hidden_in.swapaxes(0, 1), keep_mask, cotangent.swapaxes(0, 1), slot_block, matrix[0], vector[0]
    )
    results = run_finish(acts, grad_in, [matrix_grad] + matrix, [vector_grad] + vector)
    return tuple(
        array.swapaxes(*axes)
        for array, axes in zip(results, [(0, 1)] * 2 + [(2, 3)] * 3 + [(1, 2)] * 3)
    )


def solution(mesh):
    images, rows, copied = P("dp", None, None), P("mp", None, "dp", None, None), P("mp", None, None, None)
    return jax.shard_map(
        shards,
        mesh=mesh,
        in_specs=(images, P("dp", None), images, P(), rows, rows, rows, copied, copied, copied),
        out_specs=(images, images, rows, rows, rows, copied, copied, copied),
        check_vma=False,
    )
```
